32 devices in a mesh: pa: 8 (over z, y), sa: 4 (over x, core).
Axes of the slice: x: 2, y: 2, z: 4, core: 2. Of those that a mesh axis runs over, the one named last changes fastest.
Arguments:
- raw_echo: bfloat16 [256, 2, 32768], P('pa', None, 'sa'), may hold values from -6 to 6
- chirp_replica: bfloat16 [2, 1024], replicated, may hold values from -0.125 to 0.125
- azimuth_refs: bfloat16 [64, 2, 512], P('pa'), may hold values from -0.1875 to 0.1875
- migration_index: int32 [4, 8], replicated, may hold values from 0 to 63
- window_start: int32 [1], replicated, may hold values from 0 to 2047
Outputs:
- image: float32 [4, 4096, 2, 256], P('sa', 'pa')
The draws below stay inside these ranges and needn't reach their ends.
All inputs are finite; a program needn't handle non-finite values.
Results may differ from the reference program's by a relative error of at most 0.0029.
Values may be sent and summed in bfloat16 or wider, within the bound.
No kernel may reach another device: no remote copies, remote signals or barrier semaphores. Data moves between devices by JAX's collectives and lax.ppermute only.
A program may use at most 64 MiB of HBM per device.

```python
import math
import jax
import jax.numpy as jnp
from jax import lax

S = 32768
K = 1024
R = 16384
L = 512
RB = 256
PULSES = 256
NREF = 64
W = 4096
BIN_DEV = 512
AB = 256
N_PA = 8
N_SA = 4


def set_ends(entries, key, low, high):
    shape = entries.shape
    index_at = [jax.random.randint(jax.random.fold_in(key, axis), (), 0, shape[axis]) for axis in range(len(shape))]
    entries = entries.at[tuple(index_at)].set(low)
    longest = shape.index(max(shape))
    index_at[longest] = (index_at[longest] + 1) % shape[longest]
    return entries.at[tuple(index_at)].set(high)


def levels(rng, shape, split, low, largest):
    level, own = 1.0, jax.random.fold_in(rng, 6)
    for position, shards_of in split:
        draws = jnp.exp(jax.random.uniform(jax.random.fold_in(own, position), (shards_of,), jnp.float32, low / len(split), largest / len(split)))
        level = level * jnp.repeat(draws, shape[position] // shards_of).reshape([-1 if axis == position else 1 for axis in range(len(shape))])
    return level


def bell_draw(stream_key, dims, width, most, shards=(), dtype=jnp.bfloat16):
    values = jax.random.normal(stream_key, dims, jnp.float32) * width
    if len(shards) > 0:
        values = levels(stream_key, dims, shards, -0.22, 0.18) * values
    return jnp.clip(values, min=-most, max=most).astype(dtype)


def setup_inputs(seed: int = 0) -> dict:
    keys = jax.random.split(jax.random.key(seed), 6)
    return {
        "raw_echo": bell_draw(keys[0], (PULSES, 2, S), 1.0, 6.0, ((0, 8), (2, 4))),
        "chirp_replica": bell_draw(keys[1], (2, K), (2 * K) ** -0.5, 0.125),
        "azimuth_refs": bell_draw(keys[2], (NREF, 2, L), (2 * L) ** -0.5, 0.1875, ((0, 8),)),
        "migration_index": set_ends(jax.random.randint(keys[3], (N_SA, N_PA), 0, NREF), jax.random.fold_in(keys[3], 1), 0, NREF - 1).astype(jnp.int32),
        "window_start": jax.random.randint(keys[4], (1,), 0, R // (2 * N_SA)).astype(jnp.int32),
    }


def toeplitz(diagonal_taps, size):
    span_size = 2 * size - 1
    reversed_taps = diagonal_taps[..., ::-1]
    shifted = jnp.concatenate([reversed_taps[..., size - 1:], reversed_taps[..., :size - 1]], axis=-1)
    reps = (1,) * (shifted.ndim - 1) + (size,)
    tiled_flat = jnp.tile(shifted, reps)[..., : size * (span_size - 1)]
    return tiled_flat.reshape(shifted.shape[:-1] + (size, span_size - 1))[..., :size]


def tap_blocks(tap_values, size):
    block_total = tap_values.shape[1] // size + 1
    padded_taps = jnp.pad(tap_values, ((0, 0), (size, 2 * size)))
    matrices = []
    for offset_block in range(block_total):
        first_tap = offset_block * size + 1
        parts = toeplitz(padded_taps[:, first_tap:first_tap + 2 * size - 1], size)
        real_part = parts[0]
        imag_part = parts[1]
        matrices.append(jnp.stack([jnp.stack([real_part, -imag_part]), jnp.stack([imag_part, real_part])]))
    return jnp.stack(matrices)


def correlate(blocked, matrices, output_count):
    summed = jnp.zeros((blocked.shape[0], 2, output_count, blocked.shape[3]), jnp.float32)
    wide_blocks = blocked.astype(jnp.float32)
    wide_mats = matrices.astype(jnp.float32)
    for offset_block in range(matrices.shape[0]):
        piece_rows = wide_blocks[:, :, offset_block:offset_block + output_count, :]
        summed = summed + jnp.einsum("rcib,cdbn->rdin", piece_rows, wide_mats[offset_block], precision=lax.Precision.HIGHEST)
    return summed


def reference(raw_echo, chirp_replica, azimuth_refs, migration_index, window_start):
    range_mats = tap_blocks(chirp_replica, RB)
    padded = jnp.pad(raw_echo, ((0, 0), (0, 0), (0, K)))
    window = lax.dynamic_slice_in_dim(padded, window_start[0].astype(jnp.int32), R + K, 2)
    group = math.gcd(PULSES, 128)
    grouped = window.reshape(PULSES // group, group, 2, R + K)

    def compress_group(samples):
        blocked = samples.reshape(group, 2, (R + K) // RB, RB)
        focused = correlate(blocked, range_mats, R // RB)
        return focused.astype(jnp.bfloat16).reshape(group, 2, R)

    kept_bins = lax.map(compress_group, grouped).reshape(PULSES, 2, R)
    lines = jnp.transpose(kept_bins, (2, 1, 0)).reshape(N_SA * N_PA, BIN_DEV, 2, PULSES)
    flat_index = migration_index.reshape(N_SA * N_PA)

    def focus_group(inputs):
        range_lines, row_index = inputs
        reference_row = lax.dynamic_index_in_dim(azimuth_refs, row_index.astype(jnp.int32), 0, keepdims=False)
        az_mats = tap_blocks(reference_row, AB)
        block_count = PULSES // AB
        blocked = range_lines.reshape(BIN_DEV, 2, block_count, AB)
        blocked = jnp.pad(blocked, ((0, 0), (0, 0), (1, 1), (0, 0)))
        return correlate(blocked, az_mats, block_count).reshape(BIN_DEV, 2, PULSES)

    focused = lax.map(focus_group, (lines, flat_index))
    return focused.reshape(N_SA, W, 2, PULSES)
```

```python
import jax
import jax.numpy as jnp
from jax import lax
from jax.experimental import pallas as pl
from jax.experimental.pallas import tpu as pltpu
from jax.sharding import PartitionSpec as P

R = 16384
L = 512
LANES = 128
BF = jnp.bfloat16
F32 = jnp.float32


def reversed_lanes(row):
    row_id = lax.broadcasted_iota(jnp.int32, (LANES, LANES), 0)
    col_id = lax.broadcasted_iota(jnp.int32, (LANES, LANES), 1)
    flip = (row_id + col_id == LANES - 1).astype(BF)
    tiles = row.shape[1] // LANES
    pieces = [row[:, t * LANES : (t + 1) * LANES] for t in reversed(range(tiles))]
    return jnp.concatenate([jnp.dot(piece, flip, preferred_element_type=F32) for piece in pieces], axis=1)


def prep_kernel(window_ref, index_ref, chirp_ref, refs_ref, taps_ref, rows_ref):
    taps = chirp_ref.shape[1]
    blocks = taps_ref.shape[0] // LANES
    width = blocks * LANES
    shift = lax.rem(window_ref[0], LANES)
    chirp = jnp.concatenate([chirp_ref[...], jnp.zeros((14, taps), BF)], axis=0)
    flipped = reversed_lanes(chirp)
    padded = jnp.concatenate([jnp.zeros((16, 2 * LANES), F32), flipped], axis=1)
    padded = jnp.concatenate([padded, jnp.zeros((16, width + LANES - padded.shape[1]), F32)], axis=1)
    moved = pltpu.roll(padded, width + LANES - 127 - shift, 1)[:, :width]
    for part in range(2):
        spread = jnp.broadcast_to(moved[part : part + 1], (LANES, width))
        skewed = pltpu.roll(spread, 0, 1, stride=1, stride_axis=0)
        for t in range(blocks):
            first = LANES * (blocks - 1 - t)
            taps_ref[t * LANES : (t + 1) * LANES, part * LANES : (part + 1) * LANES] = skewed[
                :, first : first + LANES
            ].astype(BF)
    own = refs_ref.shape[0]
    sub_index = lax.axis_index("sa")
    first_row = lax.axis_index("pa") * own

    def fill(target, carry):
        local = index_ref[sub_index, target] - first_row
        held = jnp.logical_and(local >= 0, local < own)
        row = refs_ref[jnp.clip(local, 0, own - 1)]
        rows_ref[target] = jnp.where(held, row, jnp.zeros_like(row))
        return carry

    lax.fori_loop(0, rows_ref.shape[0], fill, 0)


def compress_kernel(window_ref, own_ref, near_ref, far_ref, taps_ref, out_ref, held, sems):
    half = far_ref.shape[0]
    span = near_ref.shape[0]
    segment = own_ref.shape[0]
    tail = held.shape[0] - span
    offset = window_ref[0] // LANES
    sub_index = lax.axis_index("sa")

    @pl.when(sub_index == 0)
    def _():
        copy = pltpu.make_async_copy(own_ref.at[pl.ds(offset, span)], held.at[pl.ds(0, span)], sems.at[0])
        copy.start()
        copy.wait()

    @pl.when(sub_index == 1)
    def _():
        first = pltpu.make_async_copy(near_ref, held.at[pl.ds(0, span)], sems.at[0])
        second = pltpu.make_async_copy(own_ref.at[pl.ds(0, tail)], held.at[pl.ds(span, tail)], sems.at[1])
        first.start()
        second.start()
        first.wait()
        second.wait()

    @pl.when(sub_index == 2)
    def _():
        copy = pltpu.make_async_copy(near_ref, held.at[pl.ds(0, span)], sems.at[0])
        copy.start()
        copy.wait()

    @pl.when(sub_index == 3)
    def _():
        first = pltpu.make_async_copy(far_ref, held.at[pl.ds(0, half)], sems.at[0])
        second = pltpu.make_async_copy(near_ref.at[pl.ds(0, tail)], held.at[pl.ds(half, tail)], sems.at[1])
        first.start()
        second.start()
        first.wait()
        second.wait()

    base = jnp.where(sub_index == 1, span - (segment - half) + offset, jnp.where(sub_index == 3, offset, 0))
    rows = held.shape[1]
    tap_blocks = taps_ref.shape[0] // LANES
    even = lax.rem(lax.broadcasted_iota(jnp.int32, (1, 8, LANES), 1), 2) == 0
    group = 8
    for step in range(out_ref.shape[0] // group):
        blocks = [
            held[pl.ds(base + group * step + t, group)].reshape(group * rows, LANES) for t in range(tap_blocks)
        ]
        product = jnp.dot(jnp.concatenate(blocks, axis=1), taps_ref[...], preferred_element_type=F32)
        straight = product[:, :LANES].reshape(-1, 8, LANES)
        crossed = product[:, LANES:].reshape(-1, 8, LANES)
        total = straight + jnp.where(even, pltpu.roll(crossed, 7, 1), -pltpu.roll(crossed, 1, 1))
        out_ref[group * step : group * (step + 1)] = total.astype(BF).reshape(group, rows, LANES)


def azimuth_taps_kernel(rows_ref, out_ref, scratch):
    size = out_ref.shape[0] // 2
    row = jnp.sum(rows_ref[...].astype(F32), axis=0).astype(BF)
    row = jnp.concatenate([row, jnp.zeros((14, row.shape[1]), BF)], axis=0)
    flipped = reversed_lanes(row)
    moved = pltpu.roll(flipped, row.shape[1] - (size - 1), 1)
    parts = []
    for part in range(2):
        spread = jnp.broadcast_to(moved[part : part + 1], (size, row.shape[1]))
        parts.append(pltpu.roll(spread, 0, 1, stride=1, stride_axis=0)[:, :size])
    columns = size // LANES
    for part, pair in enumerate(((parts[0], -parts[1]), (parts[1], parts[0]))):
        for target in range(2):
            for column in range(columns):
                scratch[target * columns + column, pl.ds(part, size, stride=2), :] = pair[target][
                    :, column * LANES : (column + 1) * LANES
                ]
    for column in range(2 * columns):
        out_ref[:, column * LANES : (column + 1) * LANES] = scratch[column].astype(BF)


def azimuth_kernel(lines_ref, taps_ref, out_ref):
    sources, tiles, rows, _ = lines_ref.shape
    pulses = out_ref.shape[2]
    for tile in range(tiles):
        lines = lines_ref[:, tile].reshape(sources * rows, LANES)
        focused = lax.dot_general(
            lines, taps_ref[...], (((0,), (0,)), ((), ())), preferred_element_type=F32
        )
        out_ref[tile * LANES : (tile + 1) * LANES, 0, :] = focused[:, :pulses]
        out_ref[tile * LANES : (tile + 1) * LANES, 1, :] = focused[:, pulses:]


def toeplitz(diagonal_taps, size):
    span_size = 2 * size - 1
    reversed_taps = diagonal_taps[..., ::-1]
    shifted = jnp.concatenate(
        [reversed_taps[..., size - 1 :], reversed_taps[..., : size - 1]], axis=-1
    )
    reps = (1,) * (shifted.ndim - 1) + (size,)
    tiled_flat = jnp.tile(shifted, reps)[..., : size * (span_size - 1)]
    return tiled_flat.reshape(shifted.shape[:-1] + (size, span_size - 1))[..., :size]


def tap_blocks(tap_values, size):
    block_total = tap_values.shape[1] // size + 1
    padded_taps = jnp.pad(tap_values, ((0, 0), (size, 2 * size)))
    matrices = []
    for offset_block in range(block_total):
        first_tap = offset_block * size + 1
        parts = toeplitz(padded_taps[:, first_tap : first_tap + 2 * size - 1], size)
        real_part = parts[0]
        imag_part = parts[1]
        matrices.append(
            jnp.stack([jnp.stack([real_part, -imag_part]), jnp.stack([imag_part, real_part])])
        )
    return jnp.stack(matrices)


def correlate(blocked, matrices, output_count):
    summed = jnp.zeros((blocked.shape[0], 2, output_count, blocked.shape[3]), F32)
    for offset_block in range(matrices.shape[0]):
        piece_rows = blocked[:, :, offset_block : offset_block + output_count, :]
        summed = summed + jnp.einsum(
            "rcib,cdbn->rdin", piece_rows, matrices[offset_block], preferred_element_type=F32
        )
    return summed


def focus_long(range_lines, reference_row):
    block_size = L // 2
    bin_count, _, total_pulses = range_lines.shape
    block_count = total_pulses // block_size
    blocked = range_lines.reshape(bin_count, 2, block_count, block_size)
    blocked = jnp.pad(blocked, ((0, 0), (0, 0), (1, 1), (0, 0)))
    focused = correlate(blocked, tap_blocks(reference_row, block_size), block_count)
    return focused.reshape(1, bin_count, 2, total_pulses)


def call(kernel, outs, specs, flops, moved, scratch=(), vmem=48 * 2**20):
    space = {"s": pltpu.SMEM, "v": pltpu.VMEM, "a": pl.ANY}
    return pl.pallas_call(
        kernel,
        out_shape=outs,
        in_specs=[pl.BlockSpec(memory_space=space[kind]) for kind in specs],
        out_specs=jax.tree.map(lambda _: pl.BlockSpec(memory_space=pltpu.VMEM), outs),
        scratch_shapes=list(scratch),
        compiler_params=pltpu.CompilerParams(vmem_limit_bytes=vmem),
        cost_estimate=pl.CostEstimate(flops=flops, bytes_accessed=moved, transcendentals=0),
    )


def on_device(raw_echo, chirp_replica, azimuth_refs, migration_index, window_start):
    pulses, _, segment = raw_echo.shape
    segment_devices = lax.axis_size("sa")
    pulse_devices = lax.axis_size("pa")
    sub_index = lax.axis_index("sa")
    tap_count = chirp_replica.shape[1]
    kept_width = R // segment_devices
    bin_count = kept_width // pulse_devices
    total_pulses = pulses * pulse_devices
    rows = 2 * pulses
    tiles = segment // LANES
    half = kept_width // LANES
    tap_tiles = tap_count // LANES + 2
    span = half + tap_tiles - 1
    offset = window_start[0] // LANES

    tiled = raw_echo.reshape(pulses, 2, tiles, LANES).transpose(2, 0, 1, 3).reshape(tiles, rows, LANES)
    near_first = jnp.where(sub_index == 0, tiles - span, jnp.where(sub_index == 1, offset, 0))
    near = lax.dynamic_slice_in_dim(tiled, near_first, span, 0)
    far = tiled[tiles - half :]
    near = lax.ppermute(near, "sa", [(0, 1), (1, 2), (2, 3)])
    far = lax.ppermute(far, "sa", [(1, 3)])

    taps, own_rows = call(
        prep_kernel,
        (
            jax.ShapeDtypeStruct((tap_tiles * LANES, 2 * LANES), BF),
            jax.ShapeDtypeStruct((pulse_devices, 2, L), BF),
        ),
        "ssvv",
        10**7,
        10**6,
    )(window_start, migration_index, chirp_replica, azimuth_refs)
    rows_in = lax.all_to_all(own_rows, "pa", split_axis=0, concat_axis=0, tiled=True)

    tail = 16 + tap_tiles - 1
    compressed = call(
        compress_kernel,
        jax.ShapeDtypeStruct((half, rows, LANES), BF),
        "saaav",
        2 * half * rows * tap_tiles * LANES * 2 * LANES,
        4 * 10**6,
        [pltpu.VMEM((span + tail, rows, LANES), BF), pltpu.SemaphoreType.DMA((2,))],
    )(window_start, tiled, near, far, taps)

    if bin_count % LANES or total_pulses != L // 2:
        kept = compressed.reshape(half, pulses, 2, LANES).transpose(0, 3, 2, 1)
        outgoing = kept.reshape(pulse_devices, bin_count, 2, pulses)
        turned = lax.all_to_all(outgoing, "pa", split_axis=0, concat_axis=3, tiled=True)
        reference_row = jnp.sum(rows_in.astype(F32), axis=0).astype(BF)
        return focus_long(turned[0], reference_row)

    azimuth_taps = call(
        azimuth_taps_kernel,
        jax.ShapeDtypeStruct((2 * total_pulses, 2 * total_pulses), BF),
        "v",
        10**6,
        10**6,
        [pltpu.VMEM((2 * total_pulses // LANES, 2 * total_pulses, LANES), F32)],
    )(rows_in)
    outgoing = compressed.reshape(pulse_devices, bin_count // LANES, rows, LANES)
    lines = lax.all_to_all(outgoing, "pa", split_axis=0, concat_axis=0, tiled=True)
    focused = call(
        azimuth_kernel,
        jax.ShapeDtypeStruct((bin_count, 2, total_pulses), F32),
        "vv",
        8 * bin_count * total_pulses * total_pulses,
        2 * 10**6,
    )(lines, azimuth_taps)
    return focused[None]


def solution(mesh):
    placed = (P("pa", None, "sa"), P(), P("pa", None, None), P(), P())
    return jax.shard_map(
        on_device, mesh=mesh, in_specs=placed, out_specs=P("sa", "pa", None, None), check_vma=False
    )
```

```python
import functools

import jax
import jax.numpy as jnp
from jax import lax
from jax.experimental import pallas as pl
from jax.experimental.pallas import tpu as pltpu
from jax.sharding import PartitionSpec as P

R = 16384
L = 512
LANES = 128
BF = jnp.bfloat16
F32 = jnp.float32


def reversed_lanes(row):
    row_id = lax.broadcasted_iota(jnp.int32, (LANES, LANES), 0)
    col_id = lax.broadcasted_iota(jnp.int32, (LANES, LANES), 1)
    flip = (row_id + col_id == LANES - 1).astype(BF)
    tiles = row.shape[1] // LANES
    pieces = [row[:, t * LANES : (t + 1) * LANES] for t in reversed(range(tiles))]
    return jnp.concatenate([jnp.dot(piece, flip, preferred_element_type=F32) for piece in pieces], axis=1)


def retile(source, target, tiles):
    for t in range(tiles):
        target[t] = source[:, :, t * LANES : (t + 1) * LANES]


def send_kernel(part, window_ref, raw_ref, near_ref, far_ref, near_raw, far_raw, sems):
    span, pulses = near_ref.shape[:2]
    half = far_ref.shape[0]
    tiles = raw_ref.shape[2] // LANES
    sub_index = lax.axis_index("sa")
    offset = window_ref[0] // LANES
    first = jnp.where(sub_index == 0, tiles - span, jnp.where(sub_index == 1, offset, 0))
    own = pl.ds(part * pulses, pulses)
    near_from = raw_ref.at[own, :, pl.ds(pl.multiple_of(first * LANES, LANES), span * LANES)]
    far_from = raw_ref.at[own, :, pl.ds((tiles - half) * LANES, half * LANES)]
    near_copy = pltpu.make_async_copy(near_from, near_raw, sems.at[0])
    far_copy = pltpu.make_async_copy(far_from, far_raw, sems.at[1])

    @pl.when(sub_index < 3)
    def _():
        near_copy.start()

    @pl.when(sub_index == 1)
    def _():
        far_copy.start()

    @pl.when(sub_index < 3)
    def _():
        near_copy.wait()
        retile(near_raw, near_ref, span)

    @pl.when(sub_index == 1)
    def _():
        far_copy.wait()
        retile(far_raw, far_ref, half)


def prep_kernel(window_ref, index_ref, chirp_ref, refs_ref, raw_ref, taps_ref, rows_ref, own_ref, own_raw, sem):
    sub_index = lax.axis_index("sa")
    halves, span, pulses = own_ref.shape[:3]
    first_tile = jnp.where(sub_index == 0, window_ref[0] // LANES, 0)
    own_copy = pltpu.make_async_copy(
        raw_ref.at[:, :, pl.ds(pl.multiple_of(first_tile * LANES, LANES), span * LANES)], own_raw, sem
    )

    @pl.when(sub_index < 2)
    def _():
        own_copy.start()

    taps = chirp_ref.shape[1]
    blocks = taps_ref.shape[0] // LANES
    width = blocks * LANES
    shift = lax.rem(window_ref[0], LANES)
    chirp = jnp.concatenate([chirp_ref[...], jnp.zeros((14, taps), BF)], axis=0)
    flipped = reversed_lanes(chirp)
    padded = jnp.concatenate([jnp.zeros((16, 2 * LANES), F32), flipped], axis=1)
    padded = jnp.concatenate([padded, jnp.zeros((16, width + LANES - padded.shape[1]), F32)], axis=1)
    moved = pltpu.roll(padded, width + LANES - 127 - shift, 1)[:, :width]
    for part in range(2):
        spread = jnp.broadcast_to(moved[part : part + 1], (LANES, width))
        skewed = pltpu.roll(spread, 0, 1, stride=1, stride_axis=0)
        for t in range(blocks):
            first = LANES * (blocks - 1 - t)
            taps_ref[t * LANES : (t + 1) * LANES, part * LANES : (part + 1) * LANES] = skewed[
                :, first : first + LANES
            ].astype(BF)
    own = refs_ref.shape[0]
    first_row = lax.axis_index("pa") * own

    def fill(target, carry):
        local = index_ref[sub_index, target] - first_row
        held = jnp.logical_and(local >= 0, local < own)
        row = refs_ref[jnp.clip(local, 0, own - 1)].astype(F32)
        row = jnp.where(held, row, jnp.zeros_like(row))
        pieces = [row[part : part + 1, t * LANES : (t + 1) * LANES] for part in range(2) for t in range(L // LANES)]
        rows_ref[target] = jnp.concatenate(pieces + [jnp.zeros((8, LANES), F32)], axis=0).astype(BF)
        return carry

    lax.fori_loop(0, rows_ref.shape[0], fill, 0)

    @pl.when(sub_index < 2)
    def _():
        own_copy.wait()
        for part in range(halves):
            retile(own_raw.at[pl.ds(part * pulses, pulses)], own_ref.at[part], span)


def compress_kernel(part, window_ref, own_ref, near_ref, far_ref, taps_ref, rows_ref, out_ref, held, taps, sems):
    half = far_ref.shape[0]
    span = near_ref.shape[0]
    tail = held.shape[0] - span
    offset = window_ref[0] // LANES
    sub_index = lax.axis_index("sa")
    taps_copy = pltpu.make_async_copy(taps_ref, taps, sems.at[2])
    taps_copy.start()

    def fetch(*pairs):
        copies = [pltpu.make_async_copy(*pair, sems.at[at]) for at, pair in enumerate(pairs)]
        for copy in copies:
            copy.start()
        for copy in copies:
            copy.wait()

    @pl.when(sub_index == 0)
    def _():
        fetch((own_ref.at[part], held.at[pl.ds(0, span)]))

    @pl.when(sub_index == 1)
    def _():
        fetch((near_ref, held.at[pl.ds(0, span)]), (own_ref.at[part, pl.ds(0, tail)], held.at[pl.ds(span, tail)]))

    @pl.when(sub_index == 2)
    def _():
        fetch((near_ref, held.at[pl.ds(0, span)]))

    @pl.when(sub_index == 3)
    def _():
        fetch((far_ref, held.at[pl.ds(0, half)]), (near_ref.at[pl.ds(0, tail)], held.at[pl.ds(half, tail)]))

    taps_copy.wait()
    base = jnp.where(sub_index == 1, span - half + offset, jnp.where(sub_index == 3, offset, 0))
    rows = held.shape[1]
    tap_tiles = taps.shape[0] // LANES
    even = lax.rem(lax.broadcasted_iota(jnp.int32, (1, 8, LANES), 1), 2) == 0
    targets = out_ref.shape[0]
    per_target = half // targets
    group = 16
    for step in range(half // group):
        blocks = [
            held[pl.ds(base + group * step + t, group)].reshape(group * rows, LANES) for t in range(tap_tiles)
        ]
        product = jnp.dot(jnp.concatenate(blocks, axis=1), taps[...], preferred_element_type=F32)
        straight = product[:, :LANES].reshape(-1, 8, LANES)
        crossed = product[:, LANES:].reshape(-1, 8, LANES)
        total = straight + jnp.where(even, pltpu.roll(crossed, 7, 1), -pltpu.roll(crossed, 1, 1))
        total = total.astype(BF).reshape(group // per_target, per_target * rows, LANES)
        for at in range(group // per_target):
            out_ref[step * (group // per_target) + at, : per_target * rows] = total[at]
    if out_ref.shape[1] > per_target * rows:
        out_ref[:, per_target * rows :] = rows_ref[...]


def azimuth_taps(row, scratch, size):
    row = jnp.concatenate([row, jnp.zeros((14, row.shape[1]), BF)], axis=0)
    flipped = reversed_lanes(row)
    moved = pltpu.roll(flipped, row.shape[1] - (size - 1), 1)
    parts = []
    for part in range(2):
        spread = jnp.broadcast_to(moved[part : part + 1], (size, row.shape[1]))
        parts.append(pltpu.roll(spread, 0, 1, stride=1, stride_axis=0)[:, :size])
    columns = size // LANES
    for part, pair in enumerate(((parts[0], -parts[1]), (parts[1], parts[0]))):
        for target in range(2):
            for column in range(columns):
                scratch[target * columns + column, pl.ds(part, size, stride=2), :] = pair[target][
                    :, column * LANES : (column + 1) * LANES
                ]


def azimuth_product(lines_ref, tile, rows, taps):
    sources = lines_ref.shape[0]
    lines = lines_ref[:, tile * rows : (tile + 1) * rows].reshape(sources * rows, LANES)
    return lax.dot_general(lines, taps, (((0,), (0,)), ((), ())), preferred_element_type=F32)


def azimuth_first_kernel(lines_ref, later_ref, sum_ref, scratch, taps):
    size = scratch.shape[1] // 2
    sources = lines_ref.shape[0]
    tiles = sum_ref.shape[0] // LANES
    rows = (lines_ref.shape[1] - 16) // tiles
    picked = jnp.sum(lines_ref[:, tiles * rows :].astype(F32), axis=0)
    columns = L // LANES
    row = jnp.concatenate(
        [
            jnp.concatenate([picked[part * columns + t : part * columns + t + 1] for t in range(columns)], axis=1)
            for part in range(2)
        ],
        axis=0,
    ).astype(BF)
    azimuth_taps(row, scratch, size)
    for column in range(scratch.shape[0]):
        lanes = slice(column * LANES, (column + 1) * LANES)
        for source in range(sources):
            into = slice(source * rows, (source + 1) * rows)
            start = source * 2 * rows
            taps[into, lanes] = scratch[column, start : start + rows].astype(BF)
            later_ref[into, lanes] = scratch[column, start + rows : start + 2 * rows].astype(BF)
    for tile in range(tiles):
        sum_ref[tile * LANES : (tile + 1) * LANES] = azimuth_product(lines_ref, tile, rows, taps[...])


def azimuth_last_kernel(lines_ref, taps_ref, sum_ref, out_ref):
    pulses = out_ref.shape[2]
    tiles = out_ref.shape[0] // LANES
    rows = lines_ref.shape[1] // tiles
    for tile in range(tiles):
        bins = slice(tile * LANES, (tile + 1) * LANES)
        focused = sum_ref[bins] + azimuth_product(lines_ref, tile, rows, taps_ref[...])
        out_ref[bins, 0, :] = focused[:, :pulses]
        out_ref[bins, 1, :] = focused[:, pulses:]


def toeplitz(diagonal_taps, size):
    span_size = 2 * size - 1
    reversed_taps = diagonal_taps[..., ::-1]
    shifted = jnp.concatenate(
        [reversed_taps[..., size - 1 :], reversed_taps[..., : size - 1]], axis=-1
    )
    reps = (1,) * (shifted.ndim - 1) + (size,)
    tiled_flat = jnp.tile(shifted, reps)[..., : size * (span_size - 1)]
    return tiled_flat.reshape(shifted.shape[:-1] + (size, span_size - 1))[..., :size]


def tap_blocks(tap_values, size):
    block_total = tap_values.shape[1] // size + 1
    padded_taps = jnp.pad(tap_values, ((0, 0), (size, 2 * size)))
    matrices = []
    for offset_block in range(block_total):
        first_tap = offset_block * size + 1
        parts = toeplitz(padded_taps[:, first_tap : first_tap + 2 * size - 1], size)
        real_part = parts[0]
        imag_part = parts[1]
        matrices.append(
            jnp.stack([jnp.stack([real_part, -imag_part]), jnp.stack([imag_part, real_part])])
        )
    return jnp.stack(matrices)


def correlate(blocked, matrices, output_count):
    summed = jnp.zeros((blocked.shape[0], 2, output_count, blocked.shape[3]), F32)
    for offset_block in range(matrices.shape[0]):
        piece_rows = blocked[:, :, offset_block : offset_block + output_count, :]
        summed = summed + jnp.einsum(
            "rcib,cdbn->rdin", piece_rows, matrices[offset_block], preferred_element_type=F32
        )
    return summed


def focus_long(range_lines, reference_row):
    block_size = L // 2
    bin_count, _, total_pulses = range_lines.shape
    block_count = total_pulses // block_size
    blocked = range_lines.reshape(bin_count, 2, block_count, block_size)
    blocked = jnp.pad(blocked, ((0, 0), (0, 0), (1, 1), (0, 0)))
    focused = correlate(blocked, tap_blocks(reference_row, block_size), block_count)
    return focused.reshape(1, bin_count, 2, total_pulses)


def call(kernel, outs, specs, flops, moved, scratch=(), vmem=40 * 2**20):
    space = {"s": pltpu.SMEM, "v": pltpu.VMEM, "a": pl.ANY}
    return pl.pallas_call(
        kernel,
        out_shape=outs,
        in_specs=[pl.BlockSpec(memory_space=space[kind]) for kind in specs],
        out_specs=jax.tree.map(lambda _: pl.BlockSpec(memory_space=pltpu.VMEM), outs),
        scratch_shapes=list(scratch),
        compiler_params=pltpu.CompilerParams(vmem_limit_bytes=vmem),
        cost_estimate=pl.CostEstimate(flops=flops, bytes_accessed=moved, transcendentals=0),
    )


def on_device(raw_echo, chirp_replica, azimuth_refs, migration_index, window_start):
    pulses = raw_echo.shape[0]
    segment_devices = lax.axis_size("sa")
    pulse_devices = lax.axis_size("pa")
    tap_count = chirp_replica.shape[1]
    kept_width = R // segment_devices
    bin_count = kept_width // pulse_devices
    total_pulses = pulses * pulse_devices
    half = kept_width // LANES
    tap_tiles = tap_count // LANES + 2
    span = half + tap_tiles - 1

    parts = 2
    pulses_each = pulses // parts
    rows_each = 2 * pulses_each
    short = bin_count % LANES == 0 and total_pulses == L // 2

    nears, fars = [], []
    turn = window_start
    for part in range(parts):
        near, far = call(
            functools.partial(send_kernel, part),
            (
                jax.ShapeDtypeStruct((span, pulses_each, 2, LANES), BF),
                jax.ShapeDtypeStruct((half, pulses_each, 2, LANES), BF),
            ),
            "sa",
            10**5,
            2 * 10**6,
            [
                pltpu.VMEM((pulses_each, 2, span * LANES), BF),
                pltpu.VMEM((pulses_each, 2, half * LANES), BF),
                pltpu.SemaphoreType.DMA((2,)),
            ],
            60 * 2**20,
        )(turn, raw_echo)
        turn = lax.optimization_barrier((window_start, near))[0]
        near = near.reshape(span, rows_each, LANES)
        far = far.reshape(half, rows_each, LANES)
        nears.append(lax.ppermute(near, "sa", [(0, 1), (1, 2), (2, 3)]))
        fars.append(lax.ppermute(far, "sa", [(1, 3)]))

    taps, own_rows, own = call(
        prep_kernel,
        (
            jax.ShapeDtypeStruct((tap_tiles * LANES, 2 * LANES), BF),
            jax.ShapeDtypeStruct((pulse_devices, 16, LANES), BF),
            jax.ShapeDtypeStruct((parts, span, pulses_each, 2, LANES), BF),
        ),
        "ssvva",
        10**7,
        10**6,
        [pltpu.VMEM((pulses, 2, span * LANES), BF), pltpu.SemaphoreType.DMA],
    )(turn, migration_index, chirp_replica, azimuth_refs, raw_echo)
    own = own.reshape(parts, span, rows_each, LANES)

    tail = 16 + tap_tiles - 1
    targets = pulse_devices if short else 2
    squeezed = []
    turn = window_start
    for part in range(parts):
        extra = 16 if short and part == 0 else 0
        squeezed.append(
            call(
                functools.partial(compress_kernel, part),
                jax.ShapeDtypeStruct((targets, half // targets * rows_each + extra, LANES), BF),
                "saaaav" if extra else "saaaaa",
                2 * half * rows_each * tap_tiles * LANES * 2 * LANES,
                4 * 10**6,
                [
                    pltpu.VMEM((span + tail, rows_each, LANES), BF),
                    pltpu.VMEM((tap_tiles * LANES, 2 * LANES), BF),
                    pltpu.SemaphoreType.DMA((3,)),
                ],
            )(turn, own, nears[part], fars[part], taps, own_rows)
        )
        turn = lax.optimization_barrier((window_start, squeezed[-1]))[0]

    if not short:
        kept = jnp.stack(squeezed).reshape(parts, half, pulses_each, 2, LANES).transpose(1, 4, 3, 0, 2)
        outgoing = kept.reshape(pulse_devices, bin_count, 2, pulses)
        turned = lax.all_to_all(outgoing, "pa", split_axis=0, concat_axis=3, tiled=True)
        rows_in = lax.all_to_all(own_rows, "pa", split_axis=0, concat_axis=0, tiled=True)
        reference_row = jnp.sum(rows_in[:, :8].astype(F32), axis=0).astype(BF).reshape(2, L)
        return focus_long(turned[0], reference_row)

    lines = [lax.all_to_all(part, "pa", split_axis=0, concat_axis=0, tiled=True) for part in squeezed]
    width = 2 * total_pulses
    later_taps, first_sum = call(
        azimuth_first_kernel,
        (jax.ShapeDtypeStruct((width // 2, width), BF), jax.ShapeDtypeStruct((bin_count, width), F32)),
        "v",
        4 * bin_count * total_pulses * total_pulses,
        2 * 10**6,
        [pltpu.VMEM((width // LANES, width, LANES), F32), pltpu.VMEM((width // 2, width), BF)],
    )(lines[0])
    focused = call(
        azimuth_last_kernel,
        jax.ShapeDtypeStruct((bin_count, 2, total_pulses), F32),
        "vvv",
        4 * bin_count * total_pulses * total_pulses,
        2 * 10**6,
    )(lines[1], later_taps, first_sum)
    return focused[None]


def solution(mesh):
    placed = (P("pa", None, "sa"), P(), P("pa", None, None), P(), P())
    return jax.shard_map(
        on_device, mesh=mesh, in_specs=placed, out_specs=P("sa", "pa", None, None), check_vma=False
    )
```

```python
import functools

import jax
import jax.numpy as jnp
from jax import lax
from jax.experimental import pallas as pl
from jax.experimental.pallas import tpu as pltpu
from jax.sharding import PartitionSpec as P

R = 16384
L = 512
LANES = 128
BF = jnp.bfloat16
F32 = jnp.float32


def reversed_lanes(row):
    row_id = lax.broadcasted_iota(jnp.int32, (LANES, LANES), 0)
    col_id = lax.broadcasted_iota(jnp.int32, (LANES, LANES), 1)
    flip = (row_id + col_id == LANES - 1).astype(BF)
    tiles = row.shape[1] // LANES
    pieces = [row[:, t * LANES : (t + 1) * LANES] for t in reversed(range(tiles))]
    return jnp.concatenate([jnp.dot(piece, flip, preferred_element_type=F32) for piece in pieces], axis=1)


def retile(source, target, tiles):
    for t in range(tiles):
        target[t] = source[:, :, t * LANES : (t + 1) * LANES]


def send_kernel(part, window_ref, raw_ref, near_ref, far_ref, near_raw, far_raw, sems):
    span, pulses = near_ref.shape[:2]
    half = far_ref.shape[0]
    tiles = raw_ref.shape[2] // LANES
    sub_index = lax.axis_index("sa")
    offset = window_ref[0] // LANES
    first = jnp.where(sub_index == 0, tiles - span, jnp.where(sub_index == 1, offset, 0))
    own = pl.ds(part * pulses, pulses)
    near_from = raw_ref.at[own, :, pl.ds(pl.multiple_of(first * LANES, LANES), span * LANES)]
    far_from = raw_ref.at[own, :, pl.ds((tiles - half) * LANES, half * LANES)]
    near_copy = pltpu.make_async_copy(near_from, near_raw, sems.at[0])
    far_copy = pltpu.make_async_copy(far_from, far_raw, sems.at[1])

    @pl.when(sub_index < 3)
    def _():
        near_copy.start()

    @pl.when(sub_index == 1)
    def _():
        far_copy.start()

    @pl.when(sub_index < 3)
    def _():
        near_copy.wait()
        retile(near_raw, near_ref, span)

    @pl.when(sub_index == 1)
    def _():
        far_copy.wait()
        retile(far_raw, far_ref, half)


def prep_kernel(window_ref, index_ref, chirp_ref, refs_ref, raw_ref, taps_ref, rows_ref, own_ref, own_raw, sem):
    sub_index = lax.axis_index("sa")
    halves, span, pulses = own_ref.shape[:3]
    first_tile = jnp.where(sub_index == 0, window_ref[0] // LANES, 0)
    own_copy = pltpu.make_async_copy(
        raw_ref.at[:, :, pl.ds(pl.multiple_of(first_tile * LANES, LANES), span * LANES)], own_raw, sem
    )

    @pl.when(sub_index < 2)
    def _():
        own_copy.start()

    taps = chirp_ref.shape[1]
    blocks = taps_ref.shape[0] // LANES
    width = blocks * LANES
    shift = lax.rem(window_ref[0], LANES)
    chirp = jnp.concatenate([chirp_ref[...], jnp.zeros((14, taps), BF)], axis=0)
    flipped = reversed_lanes(chirp)
    padded = jnp.concatenate([jnp.zeros((16, 2 * LANES), F32), flipped], axis=1)
    padded = jnp.concatenate([padded, jnp.zeros((16, width + LANES - padded.shape[1]), F32)], axis=1)
    moved = pltpu.roll(padded, width + LANES - 127 - shift, 1)[:, :width]
    for part in range(2):
        spread = jnp.broadcast_to(moved[part : part + 1], (LANES, width))
        skewed = pltpu.roll(spread, 0, 1, stride=1, stride_axis=0)
        for t in range(blocks):
            first = LANES * (blocks - 1 - t)
            taps_ref[t * LANES : (t + 1) * LANES, part * LANES : (part + 1) * LANES] = skewed[
                :, first : first + LANES
            ].astype(BF)
    own = refs_ref.shape[0]
    first_row = lax.axis_index("pa") * own

    def fill(target, carry):
        local = index_ref[sub_index, target] - first_row
        held = jnp.logical_and(local >= 0, local < own)
        row = refs_ref[jnp.clip(local, 0, own - 1)].astype(F32)
        row = jnp.where(held, row, jnp.zeros_like(row))
        pieces = [row[part : part + 1, t * LANES : (t + 1) * LANES] for part in range(2) for t in range(L // LANES)]
        rows_ref[target] = jnp.concatenate(pieces + [jnp.zeros((8, LANES), F32)], axis=0).astype(BF)
        return carry

    lax.fori_loop(0, rows_ref.shape[0], fill, 0)

    @pl.when(sub_index < 2)
    def _():
        own_copy.wait()
        for part in range(halves):
            retile(own_raw.at[pl.ds(part * pulses, pulses)], own_ref.at[part], span)


def compress_kernel(part, window_ref, own_ref, near_ref, far_ref, taps_ref, rows_ref, out_ref, held, taps, sems):
    half = far_ref.shape[0]
    span = near_ref.shape[0]
    tail = held.shape[0] - span
    offset = window_ref[0] // LANES
    sub_index = lax.axis_index("sa")
    taps_copy = pltpu.make_async_copy(taps_ref, taps, sems.at[2])
    taps_copy.start()

    def fetch(*pairs):
        copies = [pltpu.make_async_copy(*pair, sems.at[at]) for at, pair in enumerate(pairs)]
        for copy in copies:
            copy.start()
        for copy in copies:
            copy.wait()

    @pl.when(sub_index == 0)
    def _():
        fetch((own_ref.at[part], held.at[pl.ds(0, span)]))

    @pl.when(sub_index == 1)
    def _():
        fetch((near_ref, held.at[pl.ds(0, span)]), (own_ref.at[part, pl.ds(0, tail)], held.at[pl.ds(span, tail)]))

    @pl.when(sub_index == 2)
    def _():
        fetch((near_ref, held.at[pl.ds(0, span)]))

    @pl.when(sub_index == 3)
    def _():
        fetch((far_ref, held.at[pl.ds(0, half)]), (near_ref.at[pl.ds(0, tail)], held.at[pl.ds(half, tail)]))

    taps_copy.wait()
    base = jnp.where(sub_index == 1, span - half + offset, jnp.where(sub_index == 3, offset, 0))
    rows = held.shape[1]
    tap_tiles = taps.shape[0] // LANES
    even = lax.rem(lax.broadcasted_iota(jnp.int32, (1, 8, LANES), 1), 2) == 0
    targets = out_ref.shape[0]
    per_target = half // targets
    group = 16
    for step in range(half // group):
        blocks = [
            held[pl.ds(base + group * step + t, group)].reshape(group * rows, LANES) for t in range(tap_tiles)
        ]
        product = jnp.dot(jnp.concatenate(blocks, axis=1), taps[...], preferred_element_type=F32)
        straight = product[:, :LANES].reshape(-1, 8, LANES)
        crossed = product[:, LANES:].reshape(-1, 8, LANES)
        total = straight + jnp.where(even, pltpu.roll(crossed, 7, 1), -pltpu.roll(crossed, 1, 1))
        total = total.astype(BF).reshape(group // per_target, per_target * rows, LANES)
        for at in range(group // per_target):
            out_ref[step * (group // per_target) + at, : per_target * rows] = total[at]
    if out_ref.shape[1] > per_target * rows:
        out_ref[:, per_target * rows :] = rows_ref[...]


def azimuth_taps(row, scratch, size):
    row = jnp.concatenate([row, jnp.zeros((14, row.shape[1]), BF)], axis=0)
    flipped = reversed_lanes(row)
    moved = pltpu.roll(flipped, row.shape[1] - (size - 1), 1)
    parts = []
    for part in range(2):
        spread = jnp.broadcast_to(moved[part : part + 1], (size, row.shape[1]))
        parts.append(pltpu.roll(spread, 0, 1, stride=1, stride_axis=0)[:, :size])
    columns = size // LANES
    for part, pair in enumerate(((parts[0], -parts[1]), (parts[1], parts[0]))):
        for target in range(2):
            for column in range(columns):
                scratch[target * columns + column, pl.ds(part, size, stride=2), :] = pair[target][
                    :, column * LANES : (column + 1) * LANES
                ]


def azimuth_product(lines_ref, tile, rows, taps):
    sources = lines_ref.shape[0]
    lines = lines_ref[:, tile * rows : (tile + 1) * rows].reshape(sources * rows, LANES)
    return lax.dot_general(lines, taps, (((0,), (0,)), ((), ())), preferred_element_type=F32)


def azimuth_first_kernel(lines_ref, later_ref, sum_ref, scratch, taps):
    size = scratch.shape[1] // 2
    sources = lines_ref.shape[0]
    tiles = sum_ref.shape[0] // LANES
    rows = (lines_ref.shape[1] - 16) // tiles
    picked = jnp.sum(lines_ref[:, tiles * rows :].astype(F32), axis=0)
    columns = L // LANES
    row = jnp.concatenate(
        [
            jnp.concatenate([picked[part * columns + t : part * columns + t + 1] for t in range(columns)], axis=1)
            for part in range(2)
        ],
        axis=0,
    ).astype(BF)
    azimuth_taps(row, scratch, size)
    for column in range(scratch.shape[0]):
        lanes = slice(column * LANES, (column + 1) * LANES)
        for source in range(sources):
            into = slice(source * rows, (source + 1) * rows)
            start = source * 2 * rows
            taps[into, lanes] = scratch[column, start : start + rows].astype(BF)
            later_ref[into, lanes] = scratch[column, start + rows : start + 2 * rows].astype(BF)
    for tile in range(tiles):
        sum_ref[tile * LANES : (tile + 1) * LANES] = azimuth_product(lines_ref, tile, rows, taps[...])


def azimuth_last_kernel(lines_ref, taps_ref, sum_ref, out_ref):
    pulses = out_ref.shape[2]
    tiles = out_ref.shape[0] // LANES
    rows = lines_ref.shape[1] // tiles
    for tile in range(tiles):
        bins = slice(tile * LANES, (tile + 1) * LANES)
        focused = sum_ref[bins] + azimuth_product(lines_ref, tile, rows, taps_ref[...])
        out_ref[bins, 0, :] = focused[:, :pulses]
        out_ref[bins, 1, :] = focused[:, pulses:]


def toeplitz(diagonal_taps, size):
    span_size = 2 * size - 1
    reversed_taps = diagonal_taps[..., ::-1]
    shifted = jnp.concatenate(
        [reversed_taps[..., size - 1 :], reversed_taps[..., : size - 1]], axis=-1
    )
    reps = (1,) * (shifted.ndim - 1) + (size,)
    tiled_flat = jnp.tile(shifted, reps)[..., : size * (span_size - 1)]
    return tiled_flat.reshape(shifted.shape[:-1] + (size, span_size - 1))[..., :size]


def tap_blocks(tap_values, size):
    block_total = tap_values.shape[1] // size + 1
    padded_taps = jnp.pad(tap_values, ((0, 0), (size, 2 * size)))
    matrices = []
    for offset_block in range(block_total):
        first_tap = offset_block * size + 1
        parts = toeplitz(padded_taps[:, first_tap : first_tap + 2 * size - 1], size)
        real_part = parts[0]
        imag_part = parts[1]
        matrices.append(
            jnp.stack([jnp.stack([real_part, -imag_part]), jnp.stack([imag_part, real_part])])
        )
    return jnp.stack(matrices)


def correlate(blocked, matrices, output_count):
    summed = jnp.zeros((blocked.shape[0], 2, output_count, blocked.shape[3]), F32)
    for offset_block in range(matrices.shape[0]):
        piece_rows = blocked[:, :, offset_block : offset_block + output_count, :]
        summed = summed + jnp.einsum(
            "rcib,cdbn->rdin", piece_rows, matrices[offset_block], preferred_element_type=F32
        )
    return summed


def focus_long(range_lines, reference_row):
    block_size = L // 2
    bin_count, _, total_pulses = range_lines.shape
    block_count = total_pulses // block_size
    blocked = range_lines.reshape(bin_count, 2, block_count, block_size)
    blocked = jnp.pad(blocked, ((0, 0), (0, 0), (1, 1), (0, 0)))
    focused = correlate(blocked, tap_blocks(reference_row, block_size), block_count)
    return focused.reshape(1, bin_count, 2, total_pulses)


def call(kernel, outs, specs, flops, moved, scratch=(), vmem=40 * 2**20):
    space = {"s": pltpu.SMEM, "v": pltpu.VMEM, "a": pl.ANY, "h": pltpu.HBM}
    return pl.pallas_call(
        kernel,
        out_shape=outs,
        in_specs=[pl.BlockSpec(memory_space=space[kind]) for kind in specs],
        out_specs=jax.tree.map(lambda _: pl.BlockSpec(memory_space=pltpu.VMEM), outs),
        scratch_shapes=list(scratch),
        compiler_params=pltpu.CompilerParams(vmem_limit_bytes=vmem),
        cost_estimate=pl.CostEstimate(flops=flops, bytes_accessed=moved, transcendentals=0),
    )


def on_device(raw_echo, chirp_replica, azimuth_refs, migration_index, window_start):
    pulses = raw_echo.shape[0]
    segment_devices = lax.axis_size("sa")
    pulse_devices = lax.axis_size("pa")
    tap_count = chirp_replica.shape[1]
    kept_width = R // segment_devices
    bin_count = kept_width // pulse_devices
    total_pulses = pulses * pulse_devices
    half = kept_width // LANES
    tap_tiles = tap_count // LANES + 2
    span = half + tap_tiles - 1

    parts = 2
    pulses_each = pulses // parts
    rows_each = 2 * pulses_each
    short = bin_count % LANES == 0 and total_pulses == L // 2

    nears, fars = [], []
    turn = window_start
    for part in range(parts):
        near, far = call(
            functools.partial(send_kernel, part),
            (
                jax.ShapeDtypeStruct((span, pulses_each, 2, LANES), BF),
                jax.ShapeDtypeStruct((half, pulses_each, 2, LANES), BF),
            ),
            "sh",
            1000,
            1000,
            [
                pltpu.VMEM((pulses_each, 2, span * LANES), BF),
                pltpu.VMEM((pulses_each, 2, half * LANES), BF),
                pltpu.SemaphoreType.DMA((2,)),
            ],
            60 * 2**20,
        )(turn, raw_echo)
        turn = lax.optimization_barrier((window_start, near))[0]
        near = near.reshape(span, rows_each, LANES)
        far = far.reshape(half, rows_each, LANES)
        nears.append(lax.ppermute(near, "sa", [(0, 1), (1, 2), (2, 3)]))
        fars.append(lax.ppermute(far, "sa", [(1, 3)]))

    taps, own_rows, own = call(
        prep_kernel,
        (
            jax.ShapeDtypeStruct((tap_tiles * LANES, 2 * LANES), BF),
            jax.ShapeDtypeStruct((pulse_devices, 16, LANES), BF),
            jax.ShapeDtypeStruct((parts, span, pulses_each, 2, LANES), BF),
        ),
        "ssvvh",
        1000,
        1000,
        [pltpu.VMEM((pulses, 2, span * LANES), BF), pltpu.SemaphoreType.DMA],
        60 * 2**20,
    )(turn, migration_index, chirp_replica, azimuth_refs, raw_echo)
    own = own.reshape(parts, span, rows_each, LANES)

    tail = 16 + tap_tiles - 1
    targets = pulse_devices if short else 2
    squeezed = []
    for part in range(parts):
        extra = 16 if short and part == 0 else 0
        squeezed.append(
            call(
                functools.partial(compress_kernel, part),
                jax.ShapeDtypeStruct((targets, half // targets * rows_each + extra, LANES), BF),
                "saaaav" if extra else "saaaaa",
                1000,
                1000,
                [
                    pltpu.VMEM((span + tail, rows_each, LANES), BF),
                    pltpu.VMEM((tap_tiles * LANES, 2 * LANES), BF),
                    pltpu.SemaphoreType.DMA((3,)),
                ],
            )(turn, own, nears[part], fars[part], taps, own_rows)
        )
        turn = lax.optimization_barrier((window_start, squeezed[-1]))[0]

    if not short:
        kept = jnp.stack(squeezed).reshape(parts, half, pulses_each, 2, LANES).transpose(1, 4, 3, 0, 2)
        outgoing = kept.reshape(pulse_devices, bin_count, 2, pulses)
        turned = lax.all_to_all(outgoing, "pa", split_axis=0, concat_axis=3, tiled=True)
        rows_in = lax.all_to_all(own_rows, "pa", split_axis=0, concat_axis=0, tiled=True)
        reference_row = jnp.sum(rows_in[:, :8].astype(F32), axis=0).astype(BF).reshape(2, L)
        return focus_long(turned[0], reference_row)

    lines = [lax.all_to_all(part, "pa", split_axis=0, concat_axis=0, tiled=True) for part in squeezed]
    width = 2 * total_pulses
    later_taps, first_sum = call(
        azimuth_first_kernel,
        (jax.ShapeDtypeStruct((width // 2, width), BF), jax.ShapeDtypeStruct((bin_count, width), F32)),
        "v",
        4 * bin_count * total_pulses * total_pulses,
        2 * 10**6,
        [pltpu.VMEM((width // LANES, width, LANES), F32), pltpu.VMEM((width // 2, width), BF)],
    )(lines[0])
    focused = call(
        azimuth_last_kernel,
        jax.ShapeDtypeStruct((bin_count, 2, total_pulses), F32),
        "vvv",
        4 * bin_count * total_pulses * total_pulses,
        2 * 10**6,
    )(lines[1], later_taps, first_sum)
    return focused[None]


def solution(mesh):
    placed = (P("pa", None, "sa"), P(), P("pa", None, None), P(), P())
    return jax.shard_map(
        on_device, mesh=mesh, in_specs=placed, out_specs=P("sa", "pa", None, None), check_vma=False
    )
```

```python
import functools

import jax
import jax.numpy as jnp
from jax import lax
from jax.experimental import pallas as pl
from jax.experimental.pallas import tpu as pltpu
from jax.sharding import PartitionSpec as P

R = 16384
L = 512
LANES = 128
BF = jnp.bfloat16
F32 = jnp.float32


def reversed_lanes(row):
    row_id = lax.broadcasted_iota(jnp.int32, (LANES, LANES), 0)
    col_id = lax.broadcasted_iota(jnp.int32, (LANES, LANES), 1)
    flip = (row_id + col_id == LANES - 1).astype(BF)
    tiles = row.shape[1] // LANES
    pieces = [row[:, t * LANES : (t + 1) * LANES] for t in reversed(range(tiles))]
    return jnp.concatenate([jnp.dot(piece, flip, preferred_element_type=F32) for piece in pieces], axis=1)


def retile(source, target, tiles):
    for t in range(tiles):
        target[t] = source[:, :, t * LANES : (t + 1) * LANES]


def send_kernel(part, window_ref, raw_ref, near_ref, far_ref, turn_ref, near_raw, far_raw, sems):
    turn_ref[0] = window_ref[0]
    span, pulses = near_ref.shape[:2]
    half = far_ref.shape[0]
    tiles = raw_ref.shape[2] // LANES
    sub_index = lax.axis_index("sa")
    offset = window_ref[0] // LANES
    first = jnp.where(sub_index == 0, tiles - span, jnp.where(sub_index == 1, offset, 0))
    own = pl.ds(part * pulses, pulses)
    near_from = raw_ref.at[own, :, pl.ds(pl.multiple_of(first * LANES, LANES), span * LANES)]
    far_from = raw_ref.at[own, :, pl.ds((tiles - half) * LANES, half * LANES)]
    near_copy = pltpu.make_async_copy(near_from, near_raw, sems.at[0])
    far_copy = pltpu.make_async_copy(far_from, far_raw, sems.at[1])

    @pl.when(sub_index < 3)
    def _():
        near_copy.start()

    @pl.when(sub_index == 1)
    def _():
        far_copy.start()

    @pl.when(sub_index < 3)
    def _():
        near_copy.wait()
        retile(near_raw, near_ref, span)

    @pl.when(sub_index == 1)
    def _():
        far_copy.wait()
        retile(far_raw, far_ref, half)


def prep_kernel(window_ref, index_ref, chirp_ref, refs_ref, raw_ref, taps_ref, rows_ref, own_ref, own_raw, sem):
    sub_index = lax.axis_index("sa")
    halves, span, pulses = own_ref.shape[:3]
    first_tile = jnp.where(sub_index == 0, window_ref[0] // LANES, 0)
    own_copy = pltpu.make_async_copy(
        raw_ref.at[:, :, pl.ds(pl.multiple_of(first_tile * LANES, LANES), span * LANES)], own_raw, sem
    )

    @pl.when(sub_index < 2)
    def _():
        own_copy.start()

    taps = chirp_ref.shape[1]
    blocks = taps_ref.shape[0] // LANES
    width = blocks * LANES
    shift = lax.rem(window_ref[0], LANES)
    chirp = jnp.concatenate([chirp_ref[...], jnp.zeros((14, taps), BF)], axis=0)
    flipped = reversed_lanes(chirp)
    padded = jnp.concatenate([jnp.zeros((16, 2 * LANES), F32), flipped], axis=1)
    padded = jnp.concatenate([padded, jnp.zeros((16, width + LANES - padded.shape[1]), F32)], axis=1)
    moved = pltpu.roll(padded, width + LANES - 127 - shift, 1)[:, :width]
    for part in range(2):
        spread = jnp.broadcast_to(moved[part : part + 1], (LANES, width))
        skewed = pltpu.roll(spread, 0, 1, stride=1, stride_axis=0)
        for t in range(blocks):
            first = LANES * (blocks - 1 - t)
            taps_ref[t * LANES : (t + 1) * LANES, part * LANES : (part + 1) * LANES] = skewed[
                :, first : first + LANES
            ].astype(BF)
    own = refs_ref.shape[0]
    first_row = lax.axis_index("pa") * own

    def fill(target, carry):
        local = index_ref[sub_index, target] - first_row
        held = jnp.logical_and(local >= 0, local < own)
        row = refs_ref[jnp.clip(local, 0, own - 1)].astype(F32)
        row = jnp.where(held, row, jnp.zeros_like(row))
        pieces = [row[part : part + 1, t * LANES : (t + 1) * LANES] for part in range(2) for t in range(L // LANES)]
        rows_ref[target] = jnp.concatenate(pieces + [jnp.zeros((8, LANES), F32)], axis=0).astype(BF)
        return carry

    lax.fori_loop(0, rows_ref.shape[0], fill, 0)

    @pl.when(sub_index < 2)
    def _():
        own_copy.wait()
        for part in range(halves):
            retile(own_raw.at[pl.ds(part * pulses, pulses)], own_ref.at[part], span)


def compress_kernel(part, window_ref, own_ref, near_ref, far_ref, taps_ref, rows_ref, out_ref, held, taps, sems):
    half = far_ref.shape[0]
    span = near_ref.shape[0]
    tail = held.shape[0] - span
    offset = window_ref[0] // LANES
    sub_index = lax.axis_index("sa")
    taps_copy = pltpu.make_async_copy(taps_ref, taps, sems.at[2])
    taps_copy.start()

    def fetch(*pairs):
        copies = [pltpu.make_async_copy(*pair, sems.at[at]) for at, pair in enumerate(pairs)]
        for copy in copies:
            copy.start()
        for copy in copies:
            copy.wait()

    @pl.when(sub_index == 0)
    def _():
        fetch((own_ref.at[part], held.at[pl.ds(0, span)]))

    @pl.when(sub_index == 1)
    def _():
        fetch((near_ref, held.at[pl.ds(0, span)]), (own_ref.at[part, pl.ds(0, tail)], held.at[pl.ds(span, tail)]))

    @pl.when(sub_index == 2)
    def _():
        fetch((near_ref, held.at[pl.ds(0, span)]))

    @pl.when(sub_index == 3)
    def _():
        fetch((far_ref, held.at[pl.ds(0, half)]), (near_ref.at[pl.ds(0, tail)], held.at[pl.ds(half, tail)]))

    taps_copy.wait()
    base = jnp.where(sub_index == 1, span - half + offset, jnp.where(sub_index == 3, offset, 0))
    rows = held.shape[1]
    tap_tiles = taps.shape[0] // LANES
    even = lax.rem(lax.broadcasted_iota(jnp.int32, (1, 8, LANES), 1), 2) == 0
    targets = out_ref.shape[0]
    per_target = half // targets
    group = 16
    for step in range(half // group):
        blocks = [
            held[pl.ds(base + group * step + t, group)].reshape(group * rows, LANES) for t in range(tap_tiles)
        ]
        product = jnp.dot(jnp.concatenate(blocks, axis=1), taps[...], preferred_element_type=F32)
        straight = product[:, :LANES].reshape(-1, 8, LANES)
        crossed = product[:, LANES:].reshape(-1, 8, LANES)
        total = straight + jnp.where(even, pltpu.roll(crossed, 7, 1), -pltpu.roll(crossed, 1, 1))
        total = total.astype(BF).reshape(group // per_target, per_target * rows, LANES)
        for at in range(group // per_target):
            out_ref[step * (group // per_target) + at, : per_target * rows] = total[at]
    if out_ref.shape[1] > per_target * rows:
        out_ref[:, per_target * rows :] = rows_ref[...]


def azimuth_taps(row, scratch, size):
    row = jnp.concatenate([row, jnp.zeros((14, row.shape[1]), BF)], axis=0)
    flipped = reversed_lanes(row)
    moved = pltpu.roll(flipped, row.shape[1] - (size - 1), 1)
    parts = []
    for part in range(2):
        spread = jnp.broadcast_to(moved[part : part + 1], (size, row.shape[1]))
        parts.append(pltpu.roll(spread, 0, 1, stride=1, stride_axis=0)[:, :size])
    columns = size // LANES
    for part, pair in enumerate(((parts[0], -parts[1]), (parts[1], parts[0]))):
        for target in range(2):
            for column in range(columns):
                scratch[target * columns + column, pl.ds(part, size, stride=2), :] = pair[target][
                    :, column * LANES : (column + 1) * LANES
                ]


def azimuth_product(lines_ref, tile, rows, taps):
    sources = lines_ref.shape[0]
    lines = lines_ref[:, tile * rows : (tile + 1) * rows].reshape(sources * rows, LANES)
    return lax.dot_general(lines, taps, (((0,), (0,)), ((), ())), preferred_element_type=F32)


def azimuth_first_kernel(lines_ref, later_ref, sum_ref, scratch, taps):
    size = scratch.shape[1] // 2
    sources = lines_ref.shape[0]
    tiles = sum_ref.shape[0] // LANES
    rows = (lines_ref.shape[1] - 16) // tiles
    picked = jnp.sum(lines_ref[:, tiles * rows :].astype(F32), axis=0)
    columns = L // LANES
    row = jnp.concatenate(
        [
            jnp.concatenate([picked[part * columns + t : part * columns + t + 1] for t in range(columns)], axis=1)
            for part in range(2)
        ],
        axis=0,
    ).astype(BF)
    azimuth_taps(row, scratch, size)
    for column in range(scratch.shape[0]):
        lanes = slice(column * LANES, (column + 1) * LANES)
        for source in range(sources):
            into = slice(source * rows, (source + 1) * rows)
            start = source * 2 * rows
            taps[into, lanes] = scratch[column, start : start + rows].astype(BF)
            later_ref[into, lanes] = scratch[column, start + rows : start + 2 * rows].astype(BF)
    for tile in range(tiles):
        sum_ref[tile * LANES : (tile + 1) * LANES] = azimuth_product(lines_ref, tile, rows, taps[...])


def azimuth_last_kernel(lines_ref, taps_ref, sum_ref, out_ref):
    pulses = out_ref.shape[2]
    tiles = out_ref.shape[0] // LANES
    rows = lines_ref.shape[1] // tiles
    for tile in range(tiles):
        bins = slice(tile * LANES, (tile + 1) * LANES)
        focused = sum_ref[bins] + azimuth_product(lines_ref, tile, rows, taps_ref[...])
        out_ref[bins, 0, :] = focused[:, :pulses]
        out_ref[bins, 1, :] = focused[:, pulses:]


def toeplitz(diagonal_taps, size):
    span_size = 2 * size - 1
    reversed_taps = diagonal_taps[..., ::-1]
    shifted = jnp.concatenate(
        [reversed_taps[..., size - 1 :], reversed_taps[..., : size - 1]], axis=-1
    )
    reps = (1,) * (shifted.ndim - 1) + (size,)
    tiled_flat = jnp.tile(shifted, reps)[..., : size * (span_size - 1)]
    return tiled_flat.reshape(shifted.shape[:-1] + (size, span_size - 1))[..., :size]


def tap_blocks(tap_values, size):
    block_total = tap_values.shape[1] // size + 1
    padded_taps = jnp.pad(tap_values, ((0, 0), (size, 2 * size)))
    matrices = []
    for offset_block in range(block_total):
        first_tap = offset_block * size + 1
        parts = toeplitz(padded_taps[:, first_tap : first_tap + 2 * size - 1], size)
        real_part = parts[0]
        imag_part = parts[1]
        matrices.append(
            jnp.stack([jnp.stack([real_part, -imag_part]), jnp.stack([imag_part, real_part])])
        )
    return jnp.stack(matrices)


def correlate(blocked, matrices, output_count):
    summed = jnp.zeros((blocked.shape[0], 2, output_count, blocked.shape[3]), F32)
    for offset_block in range(matrices.shape[0]):
        piece_rows = blocked[:, :, offset_block : offset_block + output_count, :]
        summed = summed + jnp.einsum(
            "rcib,cdbn->rdin", piece_rows, matrices[offset_block], preferred_element_type=F32
        )
    return summed


def focus_long(range_lines, reference_row):
    block_size = L // 2
    bin_count, _, total_pulses = range_lines.shape
    block_count = total_pulses // block_size
    blocked = range_lines.reshape(bin_count, 2, block_count, block_size)
    blocked = jnp.pad(blocked, ((0, 0), (0, 0), (1, 1), (0, 0)))
    focused = correlate(blocked, tap_blocks(reference_row, block_size), block_count)
    return focused.reshape(1, bin_count, 2, total_pulses)


def call(kernel, outs, specs, flops, moved, scratch=(), vmem=40 * 2**20):
    space = {"s": pltpu.SMEM, "v": pltpu.VMEM, "a": pl.ANY, "h": pltpu.HBM}
    return pl.pallas_call(
        kernel,
        out_shape=outs,
        in_specs=[pl.BlockSpec(memory_space=space[kind]) for kind in specs],
        out_specs=jax.tree.map(
            lambda out: pl.BlockSpec(memory_space=pltpu.SMEM if out.dtype == jnp.int32 else pltpu.VMEM), outs
        ),
        scratch_shapes=list(scratch),
        compiler_params=pltpu.CompilerParams(vmem_limit_bytes=vmem),
        cost_estimate=pl.CostEstimate(flops=flops, bytes_accessed=moved, transcendentals=0),
    )


def on_device(raw_echo, chirp_replica, azimuth_refs, migration_index, window_start):
    pulses = raw_echo.shape[0]
    segment_devices = lax.axis_size("sa")
    pulse_devices = lax.axis_size("pa")
    tap_count = chirp_replica.shape[1]
    kept_width = R // segment_devices
    bin_count = kept_width // pulse_devices
    total_pulses = pulses * pulse_devices
    half = kept_width // LANES
    tap_tiles = tap_count // LANES + 2
    span = half + tap_tiles - 1

    parts = 2
    pulses_each = pulses // parts
    rows_each = 2 * pulses_each
    short = bin_count % LANES == 0 and total_pulses == L // 2

    nears, fars = [], []
    turn = window_start
    for part in range(parts):
        near, far, turn = call(
            functools.partial(send_kernel, part),
            (
                jax.ShapeDtypeStruct((span, pulses_each, 2, LANES), BF),
                jax.ShapeDtypeStruct((half, pulses_each, 2, LANES), BF),
                jax.ShapeDtypeStruct((1,), jnp.int32),
            ),
            "sh",
            1000,
            1000,
            [
                pltpu.VMEM((pulses_each, 2, span * LANES), BF),
                pltpu.VMEM((pulses_each, 2, half * LANES), BF),
                pltpu.SemaphoreType.DMA((2,)),
            ],
            60 * 2**20,
        )(turn, raw_echo)
        near = near.reshape(span, rows_each, LANES)
        far = far.reshape(half, rows_each, LANES)
        nears.append(lax.ppermute(near, "sa", [(0, 1), (1, 2), (2, 3)]))
        fars.append(lax.ppermute(far, "sa", [(1, 3)]))

    taps, own_rows, own = call(
        prep_kernel,
        (
            jax.ShapeDtypeStruct((tap_tiles * LANES, 2 * LANES), BF),
            jax.ShapeDtypeStruct((pulse_devices, 16, LANES), BF),
            jax.ShapeDtypeStruct((parts, span, pulses_each, 2, LANES), BF),
        ),
        "ssvvh",
        1000,
        1000,
        [pltpu.VMEM((pulses, 2, span * LANES), BF), pltpu.SemaphoreType.DMA],
    )(turn, migration_index, chirp_replica, azimuth_refs, raw_echo)
    own = own.reshape(parts, span, rows_each, LANES)

    tail = 16 + tap_tiles - 1
    targets = pulse_devices if short else 2
    squeezed = []
    for part in range(parts):
        extra = 16 if short and part == 0 else 0
        squeezed.append(
            call(
                functools.partial(compress_kernel, part),
                jax.ShapeDtypeStruct((targets, half // targets * rows_each + extra, LANES), BF),
                "saaaav" if extra else "saaaaa",
                1000,
                1000,
                [
                    pltpu.VMEM((span + tail, rows_each, LANES), BF),
                    pltpu.VMEM((tap_tiles * LANES, 2 * LANES), BF),
                    pltpu.SemaphoreType.DMA((3,)),
                ],
            )(turn, own, nears[part], fars[part], taps, own_rows)
        )

    if not short:
        kept = jnp.stack(squeezed).reshape(parts, half, pulses_each, 2, LANES).transpose(1, 4, 3, 0, 2)
        outgoing = kept.reshape(pulse_devices, bin_count, 2, pulses)
        turned = lax.all_to_all(outgoing, "pa", split_axis=0, concat_axis=3, tiled=True)
        rows_in = lax.all_to_all(own_rows, "pa", split_axis=0, concat_axis=0, tiled=True)
        reference_row = jnp.sum(rows_in[:, :8].astype(F32), axis=0).astype(BF).reshape(2, L)
        return focus_long(turned[0], reference_row)

    lines = [lax.all_to_all(part, "pa", split_axis=0, concat_axis=0, tiled=True) for part in squeezed]
    width = 2 * total_pulses
    later_taps, first_sum = call(
        azimuth_first_kernel,
        (jax.ShapeDtypeStruct((width // 2, width), BF), jax.ShapeDtypeStruct((bin_count, width), F32)),
        "v",
        4 * bin_count * total_pulses * total_pulses,
        2 * 10**6,
        [pltpu.VMEM((width // LANES, width, LANES), F32), pltpu.VMEM((width // 2, width), BF)],
    )(lines[0])
    focused = call(
        azimuth_last_kernel,
        jax.ShapeDtypeStruct((bin_count, 2, total_pulses), F32),
        "vvv",
        4 * bin_count * total_pulses * total_pulses,
        2 * 10**6,
    )(lines[1], later_taps, first_sum)
    return focused[None]


def solution(mesh):
    placed = (P("pa", None, "sa"), P(), P("pa", None, None), P(), P())
    return jax.shard_map(
        on_device, mesh=mesh, in_specs=placed, out_specs=P("sa", "pa", None, None), check_vma=False
    )
```

```python
import jax
import jax.numpy as jnp
from jax import lax
from jax.experimental import pallas as pl
from jax.experimental.pallas import tpu as pltpu
from jax.sharding import PartitionSpec as P

R = 16384
L = 512
LANES = 128
BF = jnp.bfloat16
F32 = jnp.float32


def reversed_lanes(row):
    row_id = lax.broadcasted_iota(jnp.int32, (LANES, LANES), 0)
    col_id = lax.broadcasted_iota(jnp.int32, (LANES, LANES), 1)
    flip = (row_id + col_id == LANES - 1).astype(BF)
    tiles = row.shape[1] // LANES
    pieces = [row[:, t * LANES : (t + 1) * LANES] for t in reversed(range(tiles))]
    return jnp.concatenate([jnp.dot(piece, flip, preferred_element_type=F32) for piece in pieces], axis=1)


def retile(source, target, first, tiles):
    shape = target.shape[1:]
    for t in range(tiles):
        target[first + t] = source[:, :, t * LANES : (t + 1) * LANES].reshape(shape)


def copy_all(sems, *pairs):
    copies = [pltpu.make_async_copy(*pair, sems.at[at]) for at, pair in enumerate(pairs)]
    for copy in copies:
        copy.start()
    for copy in copies:
        copy.wait()


def far_kernel(raw_ref, far_ref, turn_ref, sems):
    turn_ref[0] = 0
    width = far_ref.shape[2]

    @pl.when(lax.axis_index("sa") == 1)
    def _():
        copy_all(sems, (raw_ref.at[:, :, pl.ds(raw_ref.shape[2] - width, width)], far_ref))


def near_kernel(turn_in_ref, window_ref, raw_ref, near_ref, turn_ref, natural, held, sems):
    turn_ref[0] = turn_in_ref[0]
    span = near_ref.shape[0]
    tiles = raw_ref.shape[2] // LANES
    sub_index = lax.axis_index("sa")
    offset = window_ref[0] // LANES
    first = jnp.where(sub_index == 0, tiles - span, jnp.where(sub_index == 1, offset, 0))

    @pl.when(sub_index < 3)
    def _():
        copy_all(sems, (raw_ref.at[:, :, pl.ds(pl.multiple_of(first * LANES, LANES), span * LANES)], natural))
        retile(natural, held, 0, span)
        copy_all(sems, (held, near_ref))


def rows_kernel(turn_in_ref, index_ref, refs_ref, rows_ref, turn_ref):
    turn_ref[0] = turn_in_ref[0]
    own = refs_ref.shape[0]
    sub_index = lax.axis_index("sa")
    first_row = lax.axis_index("pa") * own

    def fill(target, carry):
        local = index_ref[sub_index, target] - first_row
        held = jnp.logical_and(local >= 0, local < own)
        row = refs_ref[jnp.clip(local, 0, own - 1)]
        rows_ref[target] = jnp.where(held, row, jnp.zeros_like(row))
        return carry

    lax.fori_loop(0, rows_ref.shape[0], fill, 0)


def range_taps_kernel(turn_in_ref, window_ref, chirp_ref, taps_ref):
    taps = chirp_ref.shape[1]
    blocks = taps_ref.shape[0] // LANES
    width = blocks * LANES
    shift = lax.rem(window_ref[0], LANES)
    chirp = jnp.concatenate([chirp_ref[...], jnp.zeros((14, taps), BF)], axis=0)
    flipped = reversed_lanes(chirp)
    padded = jnp.concatenate([jnp.zeros((16, 2 * LANES), F32), flipped], axis=1)
    padded = jnp.concatenate([padded, jnp.zeros((16, width + LANES - padded.shape[1]), F32)], axis=1)
    moved = pltpu.roll(padded, width + LANES - 127 - shift, 1)[:, :width]
    for part in range(2):
        spread = jnp.broadcast_to(moved[part : part + 1], (LANES, width))
        skewed = pltpu.roll(spread, 0, 1, stride=1, stride_axis=0)
        for t in range(blocks):
            first = LANES * (blocks - 1 - t)
            taps_ref[t * LANES : (t + 1) * LANES, part * LANES : (part + 1) * LANES] = skewed[
                :, first : first + LANES
            ].astype(BF)


def compress_kernel(window_ref, raw_ref, near_ref, far_ref, taps_ref, out_ref, natural, held, made, sems):
    half = out_ref.shape[0]
    span, rows, _ = near_ref.shape
    tail = held.shape[0] - span
    offset = window_ref[0] // LANES
    sub_index = lax.axis_index("sa")

    @pl.when(sub_index == 0)
    def _():
        copy_all(sems, (raw_ref.at[:, :, pl.ds(pl.multiple_of(offset * LANES, LANES), span * LANES)], natural))
        retile(natural, held, 0, span)

    @pl.when(sub_index == 1)
    def _():
        part = natural.at[:, :, pl.ds(0, tail * LANES)]
        copy_all(sems, (raw_ref.at[:, :, pl.ds(0, tail * LANES)], part), (near_ref, held.at[pl.ds(0, span)]))
        retile(natural, held, span, tail)

    @pl.when(sub_index == 2)
    def _():
        copy_all(sems, (near_ref, held.at[pl.ds(0, span)]))

    @pl.when(sub_index == 3)
    def _():
        part = natural.at[:, :, pl.ds(0, half * LANES)]
        copy_all(sems, (far_ref, part), (near_ref.at[pl.ds(0, tail)], held.at[pl.ds(half, tail)]))
        retile(natural, held, 0, half)

    base = jnp.where(sub_index == 1, span - half + offset, jnp.where(sub_index == 3, offset, 0))
    tap_tiles = taps_ref.shape[0] // LANES
    even = lax.rem(lax.broadcasted_iota(jnp.int32, (1, 8, LANES), 1), 2) == 0
    group = 8
    copies = []
    for step in range(half // group):
        into = pl.ds(group * step, group)
        blocks = [
            held[pl.ds(base + group * step + t, group)].reshape(group * rows, LANES) for t in range(tap_tiles)
        ]
        product = jnp.dot(jnp.concatenate(blocks, axis=1), taps_ref[...], preferred_element_type=F32)
        straight = product[:, :LANES].reshape(-1, 8, LANES)
        crossed = product[:, LANES:].reshape(-1, 8, LANES)
        total = straight + jnp.where(even, pltpu.roll(crossed, 7, 1), -pltpu.roll(crossed, 1, 1))
        made[into] = total.astype(BF).reshape(group, rows, LANES)
        copies.append(pltpu.make_async_copy(made.at[into], out_ref.at[into], sems.at[step]))
        copies[-1].start()
    for copy in copies:
        copy.wait()


def azimuth_taps_kernel(rows_ref, out_ref, scratch):
    size = out_ref.shape[0] // 2
    row = jnp.sum(rows_ref[...].astype(F32), axis=0).astype(BF)
    row = jnp.concatenate([row, jnp.zeros((14, row.shape[1]), BF)], axis=0)
    flipped = reversed_lanes(row)
    moved = pltpu.roll(flipped, row.shape[1] - (size - 1), 1)
    parts = []
    for part in range(2):
        spread = jnp.broadcast_to(moved[part : part + 1], (size, row.shape[1]))
        parts.append(pltpu.roll(spread, 0, 1, stride=1, stride_axis=0)[:, :size])
    columns = size // LANES
    for part, pair in enumerate(((parts[0], -parts[1]), (parts[1], parts[0]))):
        for target in range(2):
            for column in range(columns):
                scratch[target * columns + column, pl.ds(part, size, stride=2), :] = pair[target][
                    :, column * LANES : (column + 1) * LANES
                ]
    for column in range(2 * columns):
        out_ref[:, column * LANES : (column + 1) * LANES] = scratch[column].astype(BF)


def azimuth_kernel(lines_ref, taps_ref, out_ref, made, sems):
    sources, tiles, rows, _ = lines_ref.shape
    pulses = out_ref.shape[2]
    copies = []
    for tile in range(tiles):
        lines = lines_ref[:, tile].reshape(sources * rows, LANES)
        focused = lax.dot_general(
            lines, taps_ref[...], (((0,), (0,)), ((), ())), preferred_element_type=F32
        )
        into = pl.ds(tile * LANES, LANES)
        made[into, 0, :] = focused[:, :pulses]
        made[into, 1, :] = focused[:, pulses:]
        copies.append(pltpu.make_async_copy(made.at[into], out_ref.at[into], sems.at[tile]))
        copies[-1].start()
    for copy in copies:
        copy.wait()


def toeplitz(diagonal_taps, size):
    span_size = 2 * size - 1
    reversed_taps = diagonal_taps[..., ::-1]
    shifted = jnp.concatenate(
        [reversed_taps[..., size - 1 :], reversed_taps[..., : size - 1]], axis=-1
    )
    reps = (1,) * (shifted.ndim - 1) + (size,)
    tiled_flat = jnp.tile(shifted, reps)[..., : size * (span_size - 1)]
    return tiled_flat.reshape(shifted.shape[:-1] + (size, span_size - 1))[..., :size]


def tap_blocks(tap_values, size):
    block_total = tap_values.shape[1] // size + 1
    padded_taps = jnp.pad(tap_values, ((0, 0), (size, 2 * size)))
    matrices = []
    for offset_block in range(block_total):
        first_tap = offset_block * size + 1
        parts = toeplitz(padded_taps[:, first_tap : first_tap + 2 * size - 1], size)
        real_part = parts[0]
        imag_part = parts[1]
        matrices.append(
            jnp.stack([jnp.stack([real_part, -imag_part]), jnp.stack([imag_part, real_part])])
        )
    return jnp.stack(matrices)


def correlate(blocked, matrices, output_count):
    summed = jnp.zeros((blocked.shape[0], 2, output_count, blocked.shape[3]), F32)
    for offset_block in range(matrices.shape[0]):
        piece_rows = blocked[:, :, offset_block : offset_block + output_count, :]
        summed = summed + jnp.einsum(
            "rcib,cdbn->rdin", piece_rows, matrices[offset_block], preferred_element_type=F32
        )
    return summed


def focus_long(range_lines, reference_row):
    block_size = L // 2
    bin_count, _, total_pulses = range_lines.shape
    block_count = total_pulses // block_size
    blocked = range_lines.reshape(bin_count, 2, block_count, block_size)
    blocked = jnp.pad(blocked, ((0, 0), (0, 0), (1, 1), (0, 0)))
    focused = correlate(blocked, tap_blocks(reference_row, block_size), block_count)
    return focused.reshape(1, bin_count, 2, total_pulses)


def call(kernel, outs, specs, scratch=(), vmem=40):
    space = {"s": pltpu.SMEM, "v": pltpu.VMEM, "a": pl.ANY}
    blocks = [pl.BlockSpec(memory_space=space[kind]) for kind in specs]
    return pl.pallas_call(
        kernel,
        out_shape=outs,
        in_specs=blocks[: -len(outs)],
        out_specs=tuple(blocks[-len(outs) :]),
        scratch_shapes=list(scratch),
        compiler_params=pltpu.CompilerParams(vmem_limit_bytes=vmem * 2**20),
        cost_estimate=pl.CostEstimate(flops=1000, bytes_accessed=1000, transcendentals=0),
    )


def on_device(raw_echo, chirp_replica, azimuth_refs, migration_index, window_start):
    pulses = raw_echo.shape[0]
    segment_devices = lax.axis_size("sa")
    pulse_devices = lax.axis_size("pa")
    tap_count = chirp_replica.shape[1]
    kept_width = R // segment_devices
    bin_count = kept_width // pulse_devices
    total_pulses = pulses * pulse_devices
    half = kept_width // LANES
    tap_tiles = tap_count // LANES + 2
    span = half + tap_tiles - 1

    rows = 2 * pulses
    tail = 16 + tap_tiles - 1
    token = jax.ShapeDtypeStruct((1,), jnp.int32)
    shape = jax.ShapeDtypeStruct
    dma = pltpu.SemaphoreType.DMA

    far, turn = call(far_kernel, (shape((pulses, 2, half * LANES), BF), token), "aas", [dma((1,))], 60)(raw_echo)
    far = lax.ppermute(far, "sa", [(1, 3)])
    near, turn = call(
        near_kernel,
        (shape((span, rows, LANES), BF), token),
        "ssaas",
        [pltpu.VMEM((pulses, 2, span * LANES), BF), pltpu.VMEM((span, rows, LANES), BF), dma((1,))],
        60,
    )(turn, window_start, raw_echo)
    near = lax.ppermute(near, "sa", [(0, 1), (1, 2), (2, 3)])
    own_rows, turn = call(rows_kernel, (shape((pulse_devices, 2, L), BF), token), "ssvvs")(
        turn, migration_index, azimuth_refs
    )
    rows_in = lax.all_to_all(own_rows, "pa", split_axis=0, concat_axis=0, tiled=True)
    (taps,) = call(range_taps_kernel, (shape((tap_tiles * LANES, 2 * LANES), BF),), "ssvv")(
        turn, window_start, chirp_replica
    )
    (compressed,) = call(
        compress_kernel,
        (shape((half, rows, LANES), BF),),
        "saaava",
        [
            pltpu.VMEM((pulses, 2, span * LANES), BF),
            pltpu.VMEM((span + tail, rows, LANES), BF),
            pltpu.VMEM((half, rows, LANES), BF),
            dma((half // 8,)),
        ],
        60,
    )(window_start, raw_echo, near, far, taps)

    if bin_count % LANES or total_pulses != L // 2:
        kept = compressed.reshape(half, pulses, 2, LANES).transpose(0, 3, 2, 1)
        outgoing = kept.reshape(pulse_devices, bin_count, 2, pulses)
        turned = lax.all_to_all(outgoing, "pa", split_axis=0, concat_axis=3, tiled=True)
        reference_row = jnp.sum(rows_in.astype(F32), axis=0).astype(BF)
        return focus_long(turned[0], reference_row)

    width = 2 * total_pulses
    (azimuth_taps,) = call(
        azimuth_taps_kernel, (shape((width, width), BF),), "vv", [pltpu.VMEM((width // LANES, width, LANES), F32)]
    )(rows_in)
    outgoing = compressed.reshape(pulse_devices, bin_count // LANES, rows, LANES)
    lines = lax.all_to_all(outgoing, "pa", split_axis=0, concat_axis=0, tiled=True)
    (focused,) = call(
        azimuth_kernel,
        (shape((bin_count, 2, total_pulses), F32),),
        "vva",
        [pltpu.VMEM((bin_count, 2, total_pulses), F32), dma((bin_count // LANES,))],
    )(lines, azimuth_taps)
    return focused[None]


def solution(mesh):
    placed = (P("pa", None, "sa"), P(), P("pa", None, None), P(), P())
    return jax.shard_map(
        on_device, mesh=mesh, in_specs=placed, out_specs=P("sa", "pa", None, None), check_vma=False
    )
```

```python
import jax
import jax.numpy as jnp
from jax import lax
from jax.experimental import pallas as pl
from jax.experimental.pallas import tpu as pltpu
from jax.sharding import PartitionSpec as P

R = 16384
L = 512
LANES = 128
BF = jnp.bfloat16
F32 = jnp.float32


def reversed_lanes(row):
    row_id = lax.broadcasted_iota(jnp.int32, (LANES, LANES), 0)
    col_id = lax.broadcasted_iota(jnp.int32, (LANES, LANES), 1)
    flip = (row_id + col_id == LANES - 1).astype(BF)
    tiles = row.shape[1] // LANES
    pieces = [row[:, t * LANES : (t + 1) * LANES] for t in reversed(range(tiles))]
    return jnp.concatenate([jnp.dot(piece, flip, preferred_element_type=F32) for piece in pieces], axis=1)


def retile(source, target, first, tiles):
    shape = target.shape[1:]
    for t in range(tiles):
        target[first + t] = source[:, :, t * LANES : (t + 1) * LANES].reshape(shape)


def copy_all(sems, *pairs):
    copies = [pltpu.make_async_copy(*pair, sems.at[at]) for at, pair in enumerate(pairs)]
    for copy in copies:
        copy.start()
    for copy in copies:
        copy.wait()


def far_kernel(raw_ref, far_ref, turn_ref, held, in_sems, out_sems):
    turn_ref[0] = 0
    pulses, _, width = far_ref.shape
    pieces = in_sems.shape[0]
    each = pulses // pieces

    @pl.when(lax.axis_index("sa") == 1)
    def _():
        moves = []
        for at in range(pieces):
            own = pl.ds(at * each, each)
            source = raw_ref.at[own, :, pl.ds(raw_ref.shape[2] - width, width)]
            moves.append(
                (
                    pltpu.make_async_copy(source, held.at[own], in_sems.at[at]),
                    pltpu.make_async_copy(held.at[own], far_ref.at[own], out_sems.at[at]),
                )
            )
        for inward, _ in moves:
            inward.start()
        for inward, outward in moves:
            inward.wait()
            outward.start()
        for _, outward in moves:
            outward.wait()


def near_kernel(turn_in_ref, window_ref, raw_ref, near_ref, turn_ref, natural, held, in_sems, out_sems):
    turn_ref[0] = turn_in_ref[0]
    span = near_ref.shape[0]
    tiles = raw_ref.shape[2] // LANES
    sub_index = lax.axis_index("sa")
    offset = window_ref[0] // LANES
    first = jnp.where(sub_index == 0, tiles - span, jnp.where(sub_index == 1, offset, 0))
    pieces = in_sems.shape[0]
    cuts = [span * at // pieces for at in range(pieces + 1)]

    @pl.when(sub_index < 3)
    def _():
        moves = []
        for at in range(pieces):
            count = cuts[at + 1] - cuts[at]
            start = pl.multiple_of((first + cuts[at]) * LANES, LANES)
            part = natural.at[:, :, pl.ds(cuts[at] * LANES, count * LANES)]
            own = pl.ds(cuts[at], count)
            moves.append(
                (
                    pltpu.make_async_copy(raw_ref.at[:, :, pl.ds(start, count * LANES)], part, in_sems.at[at]),
                    pltpu.make_async_copy(held.at[own], near_ref.at[own], out_sems.at[at]),
                    (part, held, cuts[at], count),
                )
            )
        for inward, _, _ in moves:
            inward.start()
        for inward, outward, order in moves:
            inward.wait()
            retile(*order)
            outward.start()
        for _, outward, _ in moves:
            outward.wait()


def prep_kernel(turn_in_ref, window_ref, index_ref, chirp_ref, refs_ref, taps_ref, rows_ref, turn_ref):
    turn_ref[0] = turn_in_ref[0]
    taps = chirp_ref.shape[1]
    blocks = taps_ref.shape[0] // LANES
    width = blocks * LANES
    shift = lax.rem(window_ref[0], LANES)
    chirp = jnp.concatenate([chirp_ref[...], jnp.zeros((14, taps), BF)], axis=0)
    flipped = reversed_lanes(chirp)
    padded = jnp.concatenate([jnp.zeros((16, 2 * LANES), F32), flipped], axis=1)
    padded = jnp.concatenate([padded, jnp.zeros((16, width + LANES - padded.shape[1]), F32)], axis=1)
    moved = pltpu.roll(padded, width + LANES - 127 - shift, 1)[:, :width]
    for part in range(2):
        spread = jnp.broadcast_to(moved[part : part + 1], (LANES, width))
        skewed = pltpu.roll(spread, 0, 1, stride=1, stride_axis=0)
        for t in range(blocks):
            first = LANES * (blocks - 1 - t)
            taps_ref[t * LANES : (t + 1) * LANES, part * LANES : (part + 1) * LANES] = skewed[
                :, first : first + LANES
            ].astype(BF)
    own = refs_ref.shape[0]
    sub_index = lax.axis_index("sa")
    first_row = lax.axis_index("pa") * own

    def fill(target, carry):
        local = index_ref[sub_index, target] - first_row
        held = jnp.logical_and(local >= 0, local < own)
        row = refs_ref[jnp.clip(local, 0, own - 1)].astype(F32)
        row = jnp.where(held, row, jnp.zeros_like(row))
        pieces = [row[part : part + 1, t * LANES : (t + 1) * LANES] for part in range(2) for t in range(L // LANES)]
        rows_ref[target] = jnp.concatenate(pieces + [jnp.zeros((8, LANES), F32)], axis=0).astype(BF)
        return carry

    lax.fori_loop(0, rows_ref.shape[0], fill, 0)


def arrange_kernel(turn_in_ref, window_ref, raw_ref, far_ref, out_ref, natural, sems):
    span = natural.shape[2] // LANES
    tail = out_ref.shape[0] - span
    half = far_ref.shape[2] // LANES
    offset = window_ref[0] // LANES + turn_in_ref[0]
    sub_index = lax.axis_index("sa")

    @pl.when(sub_index == 0)
    def _():
        copy_all(sems, (raw_ref.at[:, :, pl.ds(pl.multiple_of(offset * LANES, LANES), span * LANES)], natural))
        retile(natural, out_ref, 0, span)

    @pl.when(sub_index == 1)
    def _():
        part = natural.at[:, :, pl.ds(0, tail * LANES)]
        copy_all(sems, (raw_ref.at[:, :, pl.ds(0, tail * LANES)], part))
        retile(natural, out_ref, span, tail)

    @pl.when(sub_index == 3)
    def _():
        part = natural.at[:, :, pl.ds(0, half * LANES)]
        copy_all(sems, (far_ref, part))
        retile(natural, out_ref, 0, half)


def compress_kernel(window_ref, arranged_ref, near_ref, taps_ref, rows_ref, out_ref, held, made, sems):
    span, rows, _ = near_ref.shape
    targets, _, _ = out_ref.shape
    tail = held.shape[0] - span
    group = 8
    tap_tiles = taps_ref.shape[0] // LANES
    half = span - tap_tiles + 1
    per_target = half // targets
    offset = window_ref[0] // LANES
    sub_index = lax.axis_index("sa")

    def both(at, count):
        return arranged_ref.at[pl.ds(at, count)], held.at[pl.ds(at, count)]

    @pl.when(sub_index == 0)
    def _():
        copy_all(sems, both(0, span))

    @pl.when(sub_index == 1)
    def _():
        copy_all(sems, both(span, tail), (near_ref, held.at[pl.ds(0, span)]))

    @pl.when(sub_index == 2)
    def _():
        copy_all(sems, (near_ref, held.at[pl.ds(0, span)]))

    @pl.when(sub_index == 3)
    def _():
        copy_all(sems, both(0, half), (near_ref.at[pl.ds(0, tail)], held.at[pl.ds(half, tail)]))

    base = jnp.where(sub_index == 1, span - half + offset, jnp.where(sub_index == 3, offset, 0))
    even = lax.rem(lax.broadcasted_iota(jnp.int32, (1, 8, LANES), 1), 2) == 0
    if out_ref.shape[1] > per_target * rows:
        made[:, per_target * rows :] = rows_ref[...]
    copies = []
    for step in range(half // group):
        blocks = [
            held[pl.ds(base + group * step + t, group)].reshape(group * rows, LANES) for t in range(tap_tiles)
        ]
        product = jnp.dot(jnp.concatenate(blocks, axis=1), taps_ref[...], preferred_element_type=F32)
        straight = product[:, :LANES].reshape(-1, 8, LANES)
        crossed = product[:, LANES:].reshape(-1, 8, LANES)
        total = straight + jnp.where(even, pltpu.roll(crossed, 7, 1), -pltpu.roll(crossed, 1, 1))
        count = group // per_target
        into = pl.ds(step * count, count)
        made[into, : per_target * rows] = total.astype(BF).reshape(count, per_target * rows, LANES)
        copies.append(pltpu.make_async_copy(made.at[into], out_ref.at[into], sems.at[step]))
        copies[-1].start()
    for copy in copies:
        copy.wait()


def azimuth_kernel(lines_ref, out_ref, columns_held, taps, made, sems):
    bins, _, pulses = out_ref.shape
    tiles = bins // LANES
    sources = lines_ref.shape[0]
    rows = (lines_ref.shape[1] - 16) // tiles
    picked = jnp.sum(lines_ref[:, tiles * rows :].astype(F32), axis=0)
    pieces = L // LANES
    row = [
        jnp.concatenate([picked[part * pieces + t : part * pieces + t + 1] for t in range(pieces)], axis=1)
        for part in range(2)
    ]
    row = jnp.concatenate(row + [jnp.zeros((14, L), F32)], axis=0).astype(BF)
    moved = pltpu.roll(reversed_lanes(row), L - (pulses - 1), 1)
    parts = []
    for part in range(2):
        spread = jnp.broadcast_to(moved[part : part + 1], (pulses, L))
        parts.append(pltpu.roll(spread, 0, 1, stride=1, stride_axis=0)[:, :pulses])
    columns = pulses // LANES
    for part, pair in enumerate(((parts[0], -parts[1]), (parts[1], parts[0]))):
        for target in range(2):
            for column in range(columns):
                columns_held[target * columns + column, pl.ds(part, pulses, stride=2), :] = pair[target][
                    :, column * LANES : (column + 1) * LANES
                ]
    for column in range(2 * columns):
        taps[:, column * LANES : (column + 1) * LANES] = columns_held[column].astype(BF)
    copies = []
    for tile in range(tiles):
        lines = lines_ref[:, tile * rows : (tile + 1) * rows].reshape(sources * rows, LANES)
        focused = lax.dot_general(lines, taps[...], (((0,), (0,)), ((), ())), preferred_element_type=F32)
        into = pl.ds(tile * LANES, LANES)
        made[into, 0, :] = focused[:, :pulses]
        made[into, 1, :] = focused[:, pulses:]
        copies.append(pltpu.make_async_copy(made.at[into], out_ref.at[into], sems.at[tile]))
        copies[-1].start()
    for copy in copies:
        copy.wait()


def toeplitz(diagonal_taps, size):
    span_size = 2 * size - 1
    reversed_taps = diagonal_taps[..., ::-1]
    shifted = jnp.concatenate(
        [reversed_taps[..., size - 1 :], reversed_taps[..., : size - 1]], axis=-1
    )
    reps = (1,) * (shifted.ndim - 1) + (size,)
    tiled_flat = jnp.tile(shifted, reps)[..., : size * (span_size - 1)]
    return tiled_flat.reshape(shifted.shape[:-1] + (size, span_size - 1))[..., :size]


def tap_blocks(tap_values, size):
    block_total = tap_values.shape[1] // size + 1
    padded_taps = jnp.pad(tap_values, ((0, 0), (size, 2 * size)))
    matrices = []
    for offset_block in range(block_total):
        first_tap = offset_block * size + 1
        parts = toeplitz(padded_taps[:, first_tap : first_tap + 2 * size - 1], size)
        real_part = parts[0]
        imag_part = parts[1]
        matrices.append(
            jnp.stack([jnp.stack([real_part, -imag_part]), jnp.stack([imag_part, real_part])])
        )
    return jnp.stack(matrices)


def correlate(blocked, matrices, output_count):
    summed = jnp.zeros((blocked.shape[0], 2, output_count, blocked.shape[3]), F32)
    for offset_block in range(matrices.shape[0]):
        piece_rows = blocked[:, :, offset_block : offset_block + output_count, :]
        summed = summed + jnp.einsum(
            "rcib,cdbn->rdin", piece_rows, matrices[offset_block], preferred_element_type=F32
        )
    return summed


def focus_long(range_lines, reference_row):
    block_size = L // 2
    bin_count, _, total_pulses = range_lines.shape
    block_count = total_pulses // block_size
    blocked = range_lines.reshape(bin_count, 2, block_count, block_size)
    blocked = jnp.pad(blocked, ((0, 0), (0, 0), (1, 1), (0, 0)))
    focused = correlate(blocked, tap_blocks(reference_row, block_size), block_count)
    return focused.reshape(1, bin_count, 2, total_pulses)


def call(kernel, outs, specs, scratch=(), vmem=24, flops=1000):
    space = {"s": pltpu.SMEM, "v": pltpu.VMEM, "a": pl.ANY}
    blocks = [pl.BlockSpec(memory_space=space[kind]) for kind in specs]
    return pl.pallas_call(
        kernel,
        out_shape=outs,
        in_specs=blocks[: -len(outs)],
        out_specs=tuple(blocks[-len(outs) :]),
        scratch_shapes=list(scratch),
        compiler_params=pltpu.CompilerParams(vmem_limit_bytes=vmem * 2**20),
        cost_estimate=pl.CostEstimate(flops=flops, bytes_accessed=1000, transcendentals=0),
    )


def on_device(raw_echo, chirp_replica, azimuth_refs, migration_index, window_start):
    pulses = raw_echo.shape[0]
    segment_devices = lax.axis_size("sa")
    pulse_devices = lax.axis_size("pa")
    tap_count = chirp_replica.shape[1]
    kept_width = R // segment_devices
    bin_count = kept_width // pulse_devices
    total_pulses = pulses * pulse_devices
    half = kept_width // LANES
    tap_tiles = tap_count // LANES + 2
    span = half + tap_tiles - 1

    rows = 2 * pulses
    tail = 16 + tap_tiles - 1
    token = jax.ShapeDtypeStruct((1,), jnp.int32)
    shape = jax.ShapeDtypeStruct
    dma = pltpu.SemaphoreType.DMA

    short = bin_count % LANES == 0 and total_pulses == L // 2
    natural = pltpu.VMEM((pulses, 2, span * LANES), BF)
    far, turn = call(
        far_kernel,
        (shape((pulses, 2, half * LANES), BF), token),
        "aas",
        [pltpu.VMEM((pulses, 2, half * LANES), BF), dma((8,)), dma((8,))],
        60,
    )(raw_echo)
    far = lax.ppermute(far, "sa", [(1, 3)])
    near, turn = call(
        near_kernel,
        (shape((span, rows, LANES), BF), token),
        "ssaas",
        [natural, pltpu.VMEM((span, rows, LANES), BF), dma((4,)), dma((4,))],
        60,
    )(turn, window_start, raw_echo)
    near = lax.ppermute(near, "sa", [(0, 1), (1, 2), (2, 3)])
    taps, own_rows, turn = call(
        prep_kernel,
        (shape((tap_tiles * LANES, 2 * LANES), BF), shape((pulse_devices, 16, LANES), BF), token),
        "sssvvvvs",
    )(turn, window_start, migration_index, chirp_replica, azimuth_refs)
    (arranged,) = call(
        arrange_kernel, (shape((span + tail, rows, LANES), BF),), "ssaav", [natural, dma((1,))], flops=10**10
    )(turn, window_start, raw_echo, far)

    targets, extra = (pulse_devices, 16) if short else (half // 8, 0)
    made = (targets, half // targets * rows + extra, LANES)
    (compressed,) = call(
        compress_kernel,
        (shape(made, BF),),
        "saavva",
        [pltpu.VMEM((span + tail, rows, LANES), BF), pltpu.VMEM(made, BF), dma((half // 8,))],
    )(window_start, arranged, near, taps, own_rows)

    if not short:
        kept = compressed.reshape(half, pulses, 2, LANES).transpose(0, 3, 2, 1)
        outgoing = kept.reshape(pulse_devices, bin_count, 2, pulses)
        turned = lax.all_to_all(outgoing, "pa", split_axis=0, concat_axis=3, tiled=True)
        rows_in = lax.all_to_all(own_rows, "pa", split_axis=0, concat_axis=0, tiled=True)
        reference_row = jnp.sum(rows_in[:, :8].astype(F32), axis=0).astype(BF).reshape(2, L)
        return focus_long(turned[0], reference_row)

    lines = lax.all_to_all(compressed, "pa", split_axis=0, concat_axis=0, tiled=True)
    width = 2 * total_pulses
    (focused,) = call(
        azimuth_kernel,
        (shape((bin_count, 2, total_pulses), F32),),
        "va",
        [
            pltpu.VMEM((width // LANES, width, LANES), F32),
            pltpu.VMEM((width, width), BF),
            pltpu.VMEM((bin_count, 2, total_pulses), F32),
            dma((bin_count // LANES,)),
        ],
    )(lines)
    return focused[None]


def solution(mesh):
    placed = (P("pa", None, "sa"), P(), P("pa", None, None), P(), P())
    return jax.shard_map(
        on_device, mesh=mesh, in_specs=placed, out_specs=P("sa", "pa", None, None), check_vma=False
    )
```

```python
import jax
import jax.numpy as jnp
from jax import lax
from jax.experimental import pallas as pl
from jax.experimental.pallas import tpu as pltpu
from jax.sharding import PartitionSpec as P

R = 16384
L = 512
LANES = 128
BF = jnp.bfloat16
F32 = jnp.float32


def reversed_lanes(row):
    row_id = lax.broadcasted_iota(jnp.int32, (LANES, LANES), 0)
    col_id = lax.broadcasted_iota(jnp.int32, (LANES, LANES), 1)
    flip = (row_id + col_id == LANES - 1).astype(BF)
    tiles = row.shape[1] // LANES
    pieces = [row[:, t * LANES : (t + 1) * LANES] for t in reversed(range(tiles))]
    return jnp.concatenate([jnp.dot(piece, flip, preferred_element_type=F32) for piece in pieces], axis=1)


def retile(source, target, first, tiles):
    shape = target.shape[1:]
    for t in range(tiles):
        target[first + t] = source[:, :, t * LANES : (t + 1) * LANES].reshape(shape)


def far_kernel(raw_ref, far_ref, turn_ref, held, in_sems, out_sems):
    turn_ref[0] = 0
    pulses, _, width = far_ref.shape
    pieces = in_sems.shape[0]
    each = pulses // pieces

    @pl.when(lax.axis_index("sa") == 1)
    def _():
        moves = []
        for at in range(pieces):
            own = pl.ds(at * each, each)
            source = raw_ref.at[own, :, pl.ds(raw_ref.shape[2] - width, width)]
            moves.append(
                (
                    pltpu.make_async_copy(source, held.at[own], in_sems.at[at]),
                    pltpu.make_async_copy(held.at[own], far_ref.at[own], out_sems.at[at]),
                )
            )
        for inward, _ in moves:
            inward.start()
        for inward, outward in moves:
            inward.wait()
            outward.start()
        for _, outward in moves:
            outward.wait()


def near_kernel(turn_in_ref, window_ref, raw_ref, near_ref, turn_ref, natural, held, in_sems, out_sems):
    turn_ref[0] = turn_in_ref[0]
    span = near_ref.shape[0]
    tiles = raw_ref.shape[2] // LANES
    sub_index = lax.axis_index("sa")
    offset = window_ref[0] // LANES
    first = jnp.where(sub_index == 0, tiles - span, jnp.where(sub_index == 1, offset, 0))
    pieces = in_sems.shape[0]
    cuts = [span * at // pieces for at in range(pieces + 1)]

    @pl.when(sub_index < 3)
    def _():
        moves = []
        for at in range(pieces):
            count = cuts[at + 1] - cuts[at]
            start = pl.multiple_of((first + cuts[at]) * LANES, LANES)
            part = natural.at[:, :, pl.ds(cuts[at] * LANES, count * LANES)]
            own = pl.ds(cuts[at], count)
            moves.append(
                (
                    pltpu.make_async_copy(raw_ref.at[:, :, pl.ds(start, count * LANES)], part, in_sems.at[at]),
                    pltpu.make_async_copy(held.at[own], near_ref.at[own], out_sems.at[at]),
                    (part, held, cuts[at], count),
                )
            )
        for inward, _, _ in moves:
            inward.start()
        for inward, outward, order in moves:
            inward.wait()
            retile(*order)
            outward.start()
        for _, outward, _ in moves:
            outward.wait()


def prep_kernel(turn_in_ref, window_ref, index_ref, chirp_ref, refs_ref, taps_ref, rows_ref, turn_ref):
    turn_ref[0] = turn_in_ref[0]
    taps = chirp_ref.shape[1]
    blocks = taps_ref.shape[0] // LANES
    width = blocks * LANES
    shift = lax.rem(window_ref[0], LANES)
    chirp = jnp.concatenate([chirp_ref[...], jnp.zeros((14, taps), BF)], axis=0)
    flipped = reversed_lanes(chirp)
    padded = jnp.concatenate([jnp.zeros((16, 2 * LANES), F32), flipped], axis=1)
    padded = jnp.concatenate([padded, jnp.zeros((16, width + LANES - padded.shape[1]), F32)], axis=1)
    moved = pltpu.roll(padded, width + LANES - 127 - shift, 1)[:, :width]
    for part in range(2):
        spread = jnp.broadcast_to(moved[part : part + 1], (LANES, width))
        skewed = pltpu.roll(spread, 0, 1, stride=1, stride_axis=0)
        for t in range(blocks):
            first = LANES * (blocks - 1 - t)
            taps_ref[t * LANES : (t + 1) * LANES, part * LANES : (part + 1) * LANES] = skewed[
                :, first : first + LANES
            ].astype(BF)
    own = refs_ref.shape[0]
    sub_index = lax.axis_index("sa")
    first_row = lax.axis_index("pa") * own

    def fill(target, carry):
        local = index_ref[sub_index, target] - first_row
        held = jnp.logical_and(local >= 0, local < own)
        row = refs_ref[jnp.clip(local, 0, own - 1)].astype(F32)
        row = jnp.where(held, row, jnp.zeros_like(row))
        pieces = [row[part : part + 1, t * LANES : (t + 1) * LANES] for part in range(2) for t in range(L // LANES)]
        rows_ref[target] = jnp.concatenate(pieces + [jnp.zeros((8, LANES), F32)], axis=0).astype(BF)
        return carry

    lax.fori_loop(0, rows_ref.shape[0], fill, 0)


def arrange_kernel(turn_in_ref, window_ref, raw_ref, far_ref, out_ref, ahead_ref):
    span = out_ref.shape[0]
    ahead = ahead_ref.shape[0]
    tail = 16 + ahead
    half = far_ref.shape[2] // LANES
    offset = window_ref[0] // LANES + turn_in_ref[0]
    sub_index = lax.axis_index("sa")

    start = pl.multiple_of(offset * LANES, LANES)

    @pl.when(sub_index == 0)
    def _():
        retile(raw_ref.at[:, :, pl.ds(start, span * LANES)], out_ref, 0, span)

    @pl.when(sub_index == 1)
    def _():
        retile(raw_ref, out_ref, 0, tail)

    @pl.when(sub_index == 3)
    def _():
        retile(far_ref.at[:, :, pl.ds(start, ahead * LANES)], ahead_ref, 0, ahead)
        retile(far_ref, out_ref, 0, half)


def compress_kernel(window_ref, arranged_ref, near_ref, ahead_ref, taps_ref, rows_ref, out_ref, held):
    half, rows, _ = near_ref.shape
    targets, _, _ = out_ref.shape
    span = arranged_ref.shape[0]
    tail = held.shape[0] - half
    group = 8
    tap_tiles = taps_ref.shape[0] // LANES
    per_target = half // targets
    sub_index = lax.axis_index("sa")

    @pl.when(sub_index == 0)
    def _():
        held[:span] = arranged_ref[...]

    @pl.when(sub_index == 1)
    def _():
        held[:half] = near_ref[...]
        held[half:] = arranged_ref[:tail]

    @pl.when(sub_index == 2)
    def _():
        held[:half] = near_ref[...]
        held[half:span] = ahead_ref[...]

    @pl.when(sub_index == 3)
    def _():
        held[:half] = arranged_ref[:half]
        held[half:] = near_ref[:tail]

    base = jnp.where(lax.rem(sub_index, 2) == 1, window_ref[0] // LANES, 0)
    even = lax.rem(lax.broadcasted_iota(jnp.int32, (1, 8, LANES), 1), 2) == 0
    if out_ref.shape[1] > per_target * rows:
        out_ref[:, per_target * rows :] = rows_ref[...]
    for step in range(half // group):
        blocks = [
            held[pl.ds(base + group * step + t, group)].reshape(group * rows, LANES) for t in range(tap_tiles)
        ]
        product = jnp.dot(jnp.concatenate(blocks, axis=1), taps_ref[...], preferred_element_type=F32)
        straight = product[:, :LANES].reshape(-1, 8, LANES)
        crossed = product[:, LANES:].reshape(-1, 8, LANES)
        total = straight + jnp.where(even, pltpu.roll(crossed, 7, 1), -pltpu.roll(crossed, 1, 1))
        count = group // per_target
        out_ref[pl.ds(step * count, count), : per_target * rows] = total.astype(BF).reshape(
            count, per_target * rows, LANES
        )


def azimuth_kernel(lines_ref, out_ref, columns_held, taps, made, sems):
    bins, _, pulses = out_ref.shape
    tiles = bins // LANES
    sources = lines_ref.shape[0]
    rows = (lines_ref.shape[1] - 16) // tiles
    picked = jnp.sum(lines_ref[:, tiles * rows :].astype(F32), axis=0)
    pieces = L // LANES
    row = [
        jnp.concatenate([picked[part * pieces + t : part * pieces + t + 1] for t in range(pieces)], axis=1)
        for part in range(2)
    ]
    row = jnp.concatenate(row + [jnp.zeros((14, L), F32)], axis=0).astype(BF)
    moved = pltpu.roll(reversed_lanes(row), L - (pulses - 1), 1)
    parts = []
    for part in range(2):
        spread = jnp.broadcast_to(moved[part : part + 1], (pulses, L))
        parts.append(pltpu.roll(spread, 0, 1, stride=1, stride_axis=0)[:, :pulses])
    columns = pulses // LANES
    for part, pair in enumerate(((parts[0], -parts[1]), (parts[1], parts[0]))):
        for target in range(2):
            for column in range(columns):
                columns_held[target * columns + column, pl.ds(part, pulses, stride=2), :] = pair[target][
                    :, column * LANES : (column + 1) * LANES
                ]
    for column in range(2 * columns):
        taps[:, column * LANES : (column + 1) * LANES] = columns_held[column].astype(BF)
    copies = []
    for tile in range(tiles):
        lines = lines_ref[:, tile * rows : (tile + 1) * rows].reshape(sources * rows, LANES)
        focused = lax.dot_general(lines, taps[...], (((0,), (0,)), ((), ())), preferred_element_type=F32)
        into = pl.ds(tile * LANES, LANES)
        made[into, 0, :] = focused[:, :pulses]
        made[into, 1, :] = focused[:, pulses:]
        copies.append(pltpu.make_async_copy(made.at[into], out_ref.at[into], sems.at[tile]))
        copies[-1].start()
    for copy in copies:
        copy.wait()


def toeplitz(diagonal_taps, size):
    span_size = 2 * size - 1
    reversed_taps = diagonal_taps[..., ::-1]
    shifted = jnp.concatenate(
        [reversed_taps[..., size - 1 :], reversed_taps[..., : size - 1]], axis=-1
    )
    reps = (1,) * (shifted.ndim - 1) + (size,)
    tiled_flat = jnp.tile(shifted, reps)[..., : size * (span_size - 1)]
    return tiled_flat.reshape(shifted.shape[:-1] + (size, span_size - 1))[..., :size]


def tap_blocks(tap_values, size):
    block_total = tap_values.shape[1] // size + 1
    padded_taps = jnp.pad(tap_values, ((0, 0), (size, 2 * size)))
    matrices = []
    for offset_block in range(block_total):
        first_tap = offset_block * size + 1
        parts = toeplitz(padded_taps[:, first_tap : first_tap + 2 * size - 1], size)
        real_part = parts[0]
        imag_part = parts[1]
        matrices.append(
            jnp.stack([jnp.stack([real_part, -imag_part]), jnp.stack([imag_part, real_part])])
        )
    return jnp.stack(matrices)


def correlate(blocked, matrices, output_count):
    summed = jnp.zeros((blocked.shape[0], 2, output_count, blocked.shape[3]), F32)
    for offset_block in range(matrices.shape[0]):
        piece_rows = blocked[:, :, offset_block : offset_block + output_count, :]
        summed = summed + jnp.einsum(
            "rcib,cdbn->rdin", piece_rows, matrices[offset_block], preferred_element_type=F32
        )
    return summed


def focus_long(range_lines, reference_row):
    block_size = L // 2
    bin_count, _, total_pulses = range_lines.shape
    block_count = total_pulses // block_size
    blocked = range_lines.reshape(bin_count, 2, block_count, block_size)
    blocked = jnp.pad(blocked, ((0, 0), (0, 0), (1, 1), (0, 0)))
    focused = correlate(blocked, tap_blocks(reference_row, block_size), block_count)
    return focused.reshape(1, bin_count, 2, total_pulses)


def call(kernel, outs, specs, scratch=(), vmem=24, flops=1000):
    space = {"s": pltpu.SMEM, "v": pltpu.VMEM, "a": pl.ANY}
    blocks = [pl.BlockSpec(memory_space=space[kind]) for kind in specs]
    return pl.pallas_call(
        kernel,
        out_shape=outs,
        in_specs=blocks[: -len(outs)],
        out_specs=tuple(blocks[-len(outs) :]),
        scratch_shapes=list(scratch),
        compiler_params=pltpu.CompilerParams(vmem_limit_bytes=vmem * 2**20),
        cost_estimate=pl.CostEstimate(flops=flops, bytes_accessed=1000, transcendentals=0),
    )


def on_device(raw_echo, chirp_replica, azimuth_refs, migration_index, window_start):
    pulses = raw_echo.shape[0]
    segment_devices = lax.axis_size("sa")
    pulse_devices = lax.axis_size("pa")
    tap_count = chirp_replica.shape[1]
    kept_width = R // segment_devices
    bin_count = kept_width // pulse_devices
    total_pulses = pulses * pulse_devices
    half = kept_width // LANES
    tap_tiles = tap_count // LANES + 2
    span = half + tap_tiles - 1

    rows = 2 * pulses
    token = jax.ShapeDtypeStruct((1,), jnp.int32)
    shape = jax.ShapeDtypeStruct
    dma = pltpu.SemaphoreType.DMA

    short = bin_count % LANES == 0 and total_pulses == L // 2
    far, turn = call(
        far_kernel,
        (shape((pulses, 2, half * LANES), BF), token),
        "aas",
        [pltpu.VMEM((pulses, 2, half * LANES), BF), dma((8,)), dma((8,))],
        60,
    )(raw_echo)
    far = lax.ppermute(far, "sa", [(1, 3)])
    near, turn = call(
        near_kernel,
        (shape((half, rows, LANES), BF), token),
        "ssaas",
        [pltpu.VMEM((pulses, 2, half * LANES), BF), pltpu.VMEM((half, rows, LANES), BF), dma((4,)), dma((4,))],
        60,
    )(turn, window_start, raw_echo)
    near = lax.ppermute(near, "sa", [(0, 1), (1, 2), (2, 3)])
    taps, own_rows, turn = call(
        prep_kernel,
        (shape((tap_tiles * LANES, 2 * LANES), BF), shape((pulse_devices, 16, LANES), BF), token),
        "sssvvvvs",
    )(turn, window_start, migration_index, chirp_replica, azimuth_refs)
    arranged, ahead = call(
        arrange_kernel,
        (shape((span, rows, LANES), BF), shape((span - half, rows, LANES), BF)),
        "ssvvvv",
        flops=10**10,
    )(turn, window_start, raw_echo, far)
    ahead = lax.ppermute(ahead, "sa", [(3, 2)])

    targets, extra = (pulse_devices, 16) if short else (half // 8, 0)
    made = (targets, half // targets * rows + extra, LANES)
    (compressed,) = call(
        compress_kernel,
        (shape(made, BF),),
        "svvvvvv",
        [pltpu.VMEM((span + 16, rows, LANES), BF)],
    )(window_start, arranged, near, ahead, taps, own_rows)

    if not short:
        kept = compressed.reshape(half, pulses, 2, LANES).transpose(0, 3, 2, 1)
        outgoing = kept.reshape(pulse_devices, bin_count, 2, pulses)
        turned = lax.all_to_all(outgoing, "pa", split_axis=0, concat_axis=3, tiled=True)
        rows_in = lax.all_to_all(own_rows, "pa", split_axis=0, concat_axis=0, tiled=True)
        reference_row = jnp.sum(rows_in[:, :8].astype(F32), axis=0).astype(BF).reshape(2, L)
        return focus_long(turned[0], reference_row)

    lines = lax.all_to_all(compressed, "pa", split_axis=0, concat_axis=0, tiled=True)
    width = 2 * total_pulses
    (focused,) = call(
        azimuth_kernel,
        (shape((bin_count, 2, total_pulses), F32),),
        "va",
        [
            pltpu.VMEM((width // LANES, width, LANES), F32),
            pltpu.VMEM((width, width), BF),
            pltpu.VMEM((bin_count, 2, total_pulses), F32),
            dma((bin_count // LANES,)),
        ],
    )(lines)
    return focused[None]


def solution(mesh):
    placed = (P("pa", None, "sa"), P(), P("pa", None, None), P(), P())
    return jax.shard_map(
        on_device, mesh=mesh, in_specs=placed, out_specs=P("sa", "pa", None, None), check_vma=False
    )
```

```python
import jax
import jax.numpy as jnp
from jax import lax
from jax.experimental import pallas as pl
from jax.experimental.pallas import tpu as pltpu
from jax.sharding import PartitionSpec as P

R = 16384
L = 512
LANES = 128
BF = jnp.bfloat16
F32 = jnp.float32


def reversed_lanes(row):
    row_id = lax.broadcasted_iota(jnp.int32, (LANES, LANES), 0)
    col_id = lax.broadcasted_iota(jnp.int32, (LANES, LANES), 1)
    flip = (row_id + col_id == LANES - 1).astype(BF)
    tiles = row.shape[1] // LANES
    pieces = [row[:, t * LANES : (t + 1) * LANES] for t in reversed(range(tiles))]
    return jnp.concatenate([jnp.dot(piece, flip, preferred_element_type=F32) for piece in pieces], axis=1)


def retile(source, target, first, tiles):
    shape = target.shape[1:]
    for t in range(tiles):
        target[first + t] = source[:, :, t * LANES : (t + 1) * LANES].reshape(shape)


def far_kernel(raw_ref, far_ref, turn_ref):
    turn_ref[...] = jnp.zeros_like(turn_ref)
    width = far_ref.shape[2]

    @pl.when(lax.axis_index("sa") == 1)
    def _():
        far_ref[...] = raw_ref[:, :, raw_ref.shape[2] - width :]


def near_kernel(turn_in_ref, window_ref, raw_ref, near_ref, turn_ref):
    turn_ref[...] = turn_in_ref[...]
    span = near_ref.shape[0]
    tiles = raw_ref.shape[2] // LANES
    sub_index = lax.axis_index("sa")
    offset = window_ref[0] // LANES
    first = jnp.where(sub_index == 0, tiles - span, jnp.where(sub_index == 1, offset, 0))

    @pl.when(sub_index < 3)
    def _():
        start = pl.multiple_of(first * LANES, LANES)
        retile(raw_ref.at[:, :, pl.ds(start, span * LANES)], near_ref, 0, span)


def rows_kernel(turn_in_ref, index_ref, refs_ref, rows_ref, turn_ref):
    turn_ref[...] = turn_in_ref[...]
    own = refs_ref.shape[0]
    groups, targets = index_ref.shape
    first_row = lax.axis_index("pa") * own
    mine = lax.broadcasted_iota(jnp.int32, (groups, targets), 0) == lax.axis_index("sa")
    wanted = jnp.sum(jnp.where(mine, index_ref[...], 0), axis=0, keepdims=True)
    row_id = lax.broadcasted_iota(jnp.int32, (own, targets), 0) + first_row
    picks = (row_id == jnp.broadcast_to(wanted, (own, targets))).astype(F32)
    for part in range(2):
        rows_ref[:, part, :] = lax.dot_general(
            picks, refs_ref[:, part, :].astype(F32), (((0,), (0,)), ((), ())), preferred_element_type=F32
        ).astype(BF)


def range_taps_kernel(turn_in_ref, window_ref, chirp_ref, taps_ref, turn_ref):
    turn_ref[...] = turn_in_ref[...]
    taps = chirp_ref.shape[1]
    blocks = taps_ref.shape[0] // LANES
    width = blocks * LANES
    shift = lax.rem(window_ref[0], LANES)
    chirp = jnp.concatenate([chirp_ref[...], jnp.zeros((14, taps), BF)], axis=0)
    flipped = reversed_lanes(chirp)
    padded = jnp.concatenate([jnp.zeros((16, 2 * LANES), F32), flipped], axis=1)
    padded = jnp.concatenate([padded, jnp.zeros((16, width + LANES - padded.shape[1]), F32)], axis=1)
    moved = pltpu.roll(padded, width + LANES - 127 - shift, 1)[:, :width]
    for part in range(2):
        spread = jnp.broadcast_to(moved[part : part + 1], (LANES, width))
        skewed = pltpu.roll(spread, 0, 1, stride=1, stride_axis=0)
        for t in range(blocks):
            first = LANES * (blocks - 1 - t)
            taps_ref[t * LANES : (t + 1) * LANES, part * LANES : (part + 1) * LANES] = skewed[
                :, first : first + LANES
            ].astype(BF)


def arrange_kernel(turn_in_ref, window_ref, raw_ref, far_ref, out_ref, ahead_ref):
    span = out_ref.shape[0]
    ahead = ahead_ref.shape[0]
    tail = 16 + ahead
    half = far_ref.shape[2] // LANES
    offset = window_ref[0] // LANES
    sub_index = lax.axis_index("sa")

    start = pl.multiple_of(offset * LANES, LANES)

    @pl.when(sub_index == 0)
    def _():
        retile(raw_ref.at[:, :, pl.ds(start, span * LANES)], out_ref, 0, span)

    @pl.when(sub_index == 1)
    def _():
        retile(raw_ref, out_ref, 0, tail)

    @pl.when(sub_index == 3)
    def _():
        retile(far_ref.at[:, :, pl.ds(start, ahead * LANES)], ahead_ref, 0, ahead)
        retile(far_ref, out_ref, 0, half)


def compress_kernel(window_ref, arranged_ref, near_ref, ahead_ref, taps_ref, out_ref, held):
    half, rows, _ = near_ref.shape
    targets, _, _ = out_ref.shape
    span = arranged_ref.shape[0]
    tail = held.shape[0] - half
    group = 8
    tap_tiles = taps_ref.shape[0] // LANES
    per_target = half // targets
    sub_index = lax.axis_index("sa")

    @pl.when(sub_index == 0)
    def _():
        held[:span] = arranged_ref[...]

    @pl.when(sub_index == 1)
    def _():
        held[:half] = near_ref[...]
        held[half:] = arranged_ref[:tail]

    @pl.when(sub_index == 2)
    def _():
        held[:half] = near_ref[...]
        held[half:span] = ahead_ref[...]

    @pl.when(sub_index == 3)
    def _():
        held[:half] = arranged_ref[:half]
        held[half:] = near_ref[:tail]

    base = jnp.where(lax.rem(sub_index, 2) == 1, window_ref[0] // LANES, 0)
    even = lax.rem(lax.broadcasted_iota(jnp.int32, (1, 8, LANES), 1), 2) == 0
    for step in range(half // group):
        blocks = [
            held[pl.ds(base + group * step + t, group)].reshape(group * rows, LANES) for t in range(tap_tiles)
        ]
        product = jnp.dot(jnp.concatenate(blocks, axis=1), taps_ref[...], preferred_element_type=F32)
        straight = product[:, :LANES].reshape(-1, 8, LANES)
        crossed = product[:, LANES:].reshape(-1, 8, LANES)
        total = straight + jnp.where(even, pltpu.roll(crossed, 7, 1), -pltpu.roll(crossed, 1, 1))
        count = group // per_target
        out_ref[pl.ds(step * count, count)] = total.astype(BF).reshape(count, per_target * rows, LANES)


def azimuth_taps_kernel(rows_ref, taps_ref, columns_held):
    pulses = taps_ref.shape[0] // 2
    row = jnp.sum(rows_ref[...].astype(F32), axis=0)
    row = jnp.concatenate([row, jnp.zeros((14, L), F32)], axis=0).astype(BF)
    moved = pltpu.roll(reversed_lanes(row), L - (pulses - 1), 1)
    parts = []
    for part in range(2):
        spread = jnp.broadcast_to(moved[part : part + 1], (pulses, L))
        parts.append(pltpu.roll(spread, 0, 1, stride=1, stride_axis=0)[:, :pulses])
    columns = pulses // LANES
    for part, pair in enumerate(((parts[0], -parts[1]), (parts[1], parts[0]))):
        for target in range(2):
            for column in range(columns):
                columns_held[target * columns + column, pl.ds(part, pulses, stride=2), :] = pair[target][
                    :, column * LANES : (column + 1) * LANES
                ]
    for column in range(2 * columns):
        taps_ref[:, column * LANES : (column + 1) * LANES] = columns_held[column].astype(BF)


def azimuth_kernel(lines_ref, taps_ref, out_ref, made, sems):
    bins, _, pulses = out_ref.shape
    tiles = bins // LANES
    sources = lines_ref.shape[0]
    rows = lines_ref.shape[1] // tiles
    copies = []
    for tile in range(tiles):
        lines = lines_ref[:, tile * rows : (tile + 1) * rows].reshape(sources * rows, LANES)
        focused = lax.dot_general(lines, taps_ref[...], (((0,), (0,)), ((), ())), preferred_element_type=F32)
        into = pl.ds(tile * LANES, LANES)
        made[into, 0, :] = focused[:, :pulses]
        made[into, 1, :] = focused[:, pulses:]
        copies.append(pltpu.make_async_copy(made.at[into], out_ref.at[into], sems.at[tile]))
        copies[-1].start()
    for copy in copies:
        copy.wait()


def toeplitz(diagonal_taps, size):
    span_size = 2 * size - 1
    reversed_taps = diagonal_taps[..., ::-1]
    shifted = jnp.concatenate(
        [reversed_taps[..., size - 1 :], reversed_taps[..., : size - 1]], axis=-1
    )
    reps = (1,) * (shifted.ndim - 1) + (size,)
    tiled_flat = jnp.tile(shifted, reps)[..., : size * (span_size - 1)]
    return tiled_flat.reshape(shifted.shape[:-1] + (size, span_size - 1))[..., :size]


def tap_blocks(tap_values, size):
    block_total = tap_values.shape[1] // size + 1
    padded_taps = jnp.pad(tap_values, ((0, 0), (size, 2 * size)))
    matrices = []
    for offset_block in range(block_total):
        first_tap = offset_block * size + 1
        parts = toeplitz(padded_taps[:, first_tap : first_tap + 2 * size - 1], size)
        real_part = parts[0]
        imag_part = parts[1]
        matrices.append(
            jnp.stack([jnp.stack([real_part, -imag_part]), jnp.stack([imag_part, real_part])])
        )
    return jnp.stack(matrices)


def correlate(blocked, matrices, output_count):
    summed = jnp.zeros((blocked.shape[0], 2, output_count, blocked.shape[3]), F32)
    for offset_block in range(matrices.shape[0]):
        piece_rows = blocked[:, :, offset_block : offset_block + output_count, :]
        summed = summed + jnp.einsum(
            "rcib,cdbn->rdin", piece_rows, matrices[offset_block], preferred_element_type=F32
        )
    return summed


def focus_long(range_lines, reference_row):
    block_size = L // 2
    bin_count, _, total_pulses = range_lines.shape
    block_count = total_pulses // block_size
    blocked = range_lines.reshape(bin_count, 2, block_count, block_size)
    blocked = jnp.pad(blocked, ((0, 0), (0, 0), (1, 1), (0, 0)))
    focused = correlate(blocked, tap_blocks(reference_row, block_size), block_count)
    return focused.reshape(1, bin_count, 2, total_pulses)


def call(kernel, outs, specs, scratch=(), vmem=24, flops=1000):
    space = {"s": pltpu.SMEM, "v": pltpu.VMEM, "a": pl.ANY}
    blocks = [pl.BlockSpec(memory_space=space[kind]) for kind in specs]
    return pl.pallas_call(
        kernel,
        out_shape=outs,
        in_specs=blocks[: -len(outs)],
        out_specs=tuple(blocks[-len(outs) :]),
        scratch_shapes=list(scratch),
        compiler_params=pltpu.CompilerParams(vmem_limit_bytes=vmem * 2**20),
        cost_estimate=pl.CostEstimate(flops=flops, bytes_accessed=1000, transcendentals=0),
    )


def on_device(raw_echo, chirp_replica, azimuth_refs, migration_index, window_start):
    pulses = raw_echo.shape[0]
    segment_devices = lax.axis_size("sa")
    pulse_devices = lax.axis_size("pa")
    tap_count = chirp_replica.shape[1]
    kept_width = R // segment_devices
    bin_count = kept_width // pulse_devices
    total_pulses = pulses * pulse_devices
    half = kept_width // LANES
    tap_tiles = tap_count // LANES + 2
    span = half + tap_tiles - 1

    rows = 2 * pulses
    shape = jax.ShapeDtypeStruct
    token = shape((8, LANES), F32)
    short = bin_count % LANES == 0 and total_pulses == L // 2

    far, turn = call(far_kernel, (shape((pulses, 2, half * LANES), BF), token), "vvv")(raw_echo)
    far = lax.ppermute(far, "sa", [(1, 3)])
    near, turn = call(near_kernel, (shape((half, rows, LANES), BF), token), "vsvvv")(turn, window_start, raw_echo)
    near = lax.ppermute(near, "sa", [(0, 1), (1, 2), (2, 3)])
    own_rows, turn = call(rows_kernel, (shape((pulse_devices, 2, L), BF), token), "vvvvv")(
        turn, migration_index, azimuth_refs
    )
    rows_in = lax.all_to_all(own_rows, "pa", split_axis=0, concat_axis=0, tiled=True)
    taps, turn = call(range_taps_kernel, (shape((tap_tiles * LANES, 2 * LANES), BF), token), "vsvvv")(
        turn, window_start, chirp_replica
    )
    arranged, ahead = call(
        arrange_kernel,
        (shape((span, rows, LANES), BF), shape((span - half, rows, LANES), BF)),
        "vsvvvv",
        flops=10**10,
    )(turn, window_start, raw_echo, far)
    ahead = lax.ppermute(ahead, "sa", [(3, 2)])

    targets = pulse_devices if short else half // 8
    (compressed,) = call(
        compress_kernel,
        (shape((targets, half // targets * rows, LANES), BF),),
        "svvvvv",
        [pltpu.VMEM((span + 16, rows, LANES), BF)],
    )(window_start, arranged, near, ahead, taps)

    if not short:
        kept = compressed.reshape(half, pulses, 2, LANES).transpose(0, 3, 2, 1)
        outgoing = kept.reshape(pulse_devices, bin_count, 2, pulses)
        turned = lax.all_to_all(outgoing, "pa", split_axis=0, concat_axis=3, tiled=True)
        reference_row = jnp.sum(rows_in.astype(F32), axis=0).astype(BF)
        return focus_long(turned[0], reference_row)

    lines = lax.all_to_all(compressed, "pa", split_axis=0, concat_axis=0, tiled=True)
    width = 2 * total_pulses
    (azimuth_taps,) = call(
        azimuth_taps_kernel, (shape((width, width), BF),), "vv", [pltpu.VMEM((width // LANES, width, LANES), F32)]
    )(rows_in)
    (focused,) = call(
        azimuth_kernel,
        (shape((bin_count, 2, total_pulses), F32),),
        "vva",
        [pltpu.VMEM((bin_count, 2, total_pulses), F32), pltpu.SemaphoreType.DMA((bin_count // LANES,))],
    )(lines, azimuth_taps)
    return focused[None]


def solution(mesh):
    placed = (P("pa", None, "sa"), P(), P("pa", None, None), P(), P())
    return jax.shard_map(
        on_device, mesh=mesh, in_specs=placed, out_specs=P("sa", "pa", None, None), check_vma=False
    )
```

```python
import jax
import jax.numpy as jnp
from jax import lax
from jax.experimental import pallas as pl
from jax.experimental.pallas import tpu as pltpu
from jax.sharding import PartitionSpec as P

R = 16384
L = 512
LANES = 128
BF = jnp.bfloat16
F32 = jnp.float32


def reversed_lanes(row):
    row_id = lax.broadcasted_iota(jnp.int32, (LANES, LANES), 0)
    col_id = lax.broadcasted_iota(jnp.int32, (LANES, LANES), 1)
    flip = (row_id + col_id == LANES - 1).astype(BF)
    tiles = row.shape[1] // LANES
    pieces = [row[:, t * LANES : (t + 1) * LANES] for t in reversed(range(tiles))]
    return jnp.concatenate([jnp.dot(piece, flip, preferred_element_type=F32) for piece in pieces], axis=1)


def retile(source, target, first, tiles):
    shape = target.shape[1:]
    for t in range(tiles):
        target[first + t] = source[:, :, t * LANES : (t + 1) * LANES].reshape(shape)


def far_kernel(raw_ref, far_ref, turn_ref):
    turn_ref[...] = jnp.zeros_like(turn_ref)
    width = far_ref.shape[2]

    @pl.when(lax.axis_index("sa") == 1)
    def _():
        far_ref[...] = raw_ref[:, :, raw_ref.shape[2] - width :]


def near_kernel(turn_in_ref, window_ref, raw_ref, near_ref, turn_ref):
    turn_ref[...] = turn_in_ref[...]
    span = near_ref.shape[0]
    tiles = raw_ref.shape[2] // LANES
    sub_index = lax.axis_index("sa")
    offset = window_ref[0] // LANES
    first = jnp.where(sub_index == 0, tiles - span, jnp.where(sub_index == 1, offset, 0))

    @pl.when(sub_index < 3)
    def _():
        start = pl.multiple_of(first * LANES, LANES)
        retile(raw_ref.at[:, :, pl.ds(start, span * LANES)], near_ref, 0, span)


def prep_kernel(turn_in_ref, window_ref, index_ref, chirp_ref, refs_ref, taps_ref, rows_ref, turn_ref):
    turn_ref[...] = turn_in_ref[...]
    taps = chirp_ref.shape[1]
    blocks = taps_ref.shape[0] // LANES
    width = blocks * LANES
    shift = lax.rem(window_ref[0], LANES)
    chirp = jnp.concatenate([chirp_ref[...], jnp.zeros((14, taps), BF)], axis=0)
    flipped = reversed_lanes(chirp)
    padded = jnp.concatenate([jnp.zeros((16, 2 * LANES), F32), flipped], axis=1)
    padded = jnp.concatenate([padded, jnp.zeros((16, width + LANES - padded.shape[1]), F32)], axis=1)
    moved = pltpu.roll(padded, width + LANES - 127 - shift, 1)[:, :width]
    for part in range(2):
        spread = jnp.broadcast_to(moved[part : part + 1], (LANES, width))
        skewed = pltpu.roll(spread, 0, 1, stride=1, stride_axis=0)
        for t in range(blocks):
            first = LANES * (blocks - 1 - t)
            taps_ref[t * LANES : (t + 1) * LANES, part * LANES : (part + 1) * LANES] = skewed[
                :, first : first + LANES
            ].astype(BF)
    own = refs_ref.shape[0]
    groups, targets = index_ref.shape
    first_row = lax.axis_index("pa") * own
    mine = lax.broadcasted_iota(jnp.int32, (groups, targets), 0) == lax.axis_index("sa")
    wanted = jnp.sum(jnp.where(mine, index_ref[...], 0), axis=0, keepdims=True)
    row_id = lax.broadcasted_iota(jnp.int32, (own, targets), 0) + first_row
    picks = (row_id == jnp.broadcast_to(wanted, (own, targets))).astype(F32)
    pieces = []
    for part in range(2):
        picked = lax.dot_general(
            picks, refs_ref[:, part, :].astype(F32), (((0,), (0,)), ((), ())), preferred_element_type=F32
        )
        pieces += [picked[:, t * LANES : (t + 1) * LANES] for t in range(L // LANES)]
    pieces += [jnp.zeros((targets, LANES), F32)] * (rows_ref.shape[1] - len(pieces))
    rows_ref[...] = jnp.stack(pieces, axis=1).astype(BF)


def arrange_kernel(turn_in_ref, window_ref, raw_ref, far_ref, out_ref, ahead_ref):
    span = out_ref.shape[0]
    ahead = ahead_ref.shape[0]
    tail = 16 + ahead
    half = far_ref.shape[2] // LANES
    offset = window_ref[0] // LANES
    sub_index = lax.axis_index("sa")

    start = pl.multiple_of(offset * LANES, LANES)

    @pl.when(sub_index == 0)
    def _():
        retile(raw_ref.at[:, :, pl.ds(start, span * LANES)], out_ref, 0, span)

    @pl.when(sub_index == 1)
    def _():
        retile(raw_ref, out_ref, 0, tail)

    @pl.when(sub_index == 3)
    def _():
        retile(far_ref.at[:, :, pl.ds(start, ahead * LANES)], ahead_ref, 0, ahead)
        retile(far_ref, out_ref, 0, half)


def compress_kernel(window_ref, arranged_ref, near_ref, ahead_ref, taps_ref, rows_ref, out_ref, held):
    half, rows, _ = near_ref.shape
    targets, _, _ = out_ref.shape
    span = arranged_ref.shape[0]
    tail = held.shape[0] - half
    group = 8
    tap_tiles = taps_ref.shape[0] // LANES
    per_target = half // targets
    sub_index = lax.axis_index("sa")

    @pl.when(sub_index == 0)
    def _():
        held[:span] = arranged_ref[...]

    @pl.when(sub_index == 1)
    def _():
        held[:half] = near_ref[...]
        held[half:] = arranged_ref[:tail]

    @pl.when(sub_index == 2)
    def _():
        held[:half] = near_ref[...]
        held[half:span] = ahead_ref[...]

    @pl.when(sub_index == 3)
    def _():
        held[:half] = arranged_ref[:half]
        held[half:] = near_ref[:tail]

    base = jnp.where(lax.rem(sub_index, 2) == 1, window_ref[0] // LANES, 0)
    even = lax.rem(lax.broadcasted_iota(jnp.int32, (1, 8, LANES), 1), 2) == 0
    if out_ref.shape[1] > per_target * rows:
        out_ref[:, per_target * rows :] = rows_ref[...]
    for step in range(half // group):
        blocks = [
            held[pl.ds(base + group * step + t, group)].reshape(group * rows, LANES) for t in range(tap_tiles)
        ]
        product = jnp.dot(jnp.concatenate(blocks, axis=1), taps_ref[...], preferred_element_type=F32)
        straight = product[:, :LANES].reshape(-1, 8, LANES)
        crossed = product[:, LANES:].reshape(-1, 8, LANES)
        total = straight + jnp.where(even, pltpu.roll(crossed, 7, 1), -pltpu.roll(crossed, 1, 1))
        count = group // per_target
        out_ref[pl.ds(step * count, count), : per_target * rows] = total.astype(BF).reshape(
            count, per_target * rows, LANES
        )


def azimuth_kernel(lines_ref, out_ref, columns_held, taps, made, sems):
    bins, _, pulses = out_ref.shape
    tiles = bins // LANES
    sources = lines_ref.shape[0]
    rows = (lines_ref.shape[1] - 16) // tiles
    picked = jnp.sum(lines_ref[:, tiles * rows :].astype(F32), axis=0)
    pieces = L // LANES
    row = [
        jnp.concatenate([picked[part * pieces + t : part * pieces + t + 1] for t in range(pieces)], axis=1)
        for part in range(2)
    ]
    row = jnp.concatenate(row + [jnp.zeros((14, L), F32)], axis=0).astype(BF)
    moved = pltpu.roll(reversed_lanes(row), L - (pulses - 1), 1)
    parts = []
    for part in range(2):
        spread = jnp.broadcast_to(moved[part : part + 1], (pulses, L))
        parts.append(pltpu.roll(spread, 0, 1, stride=1, stride_axis=0)[:, :pulses])
    columns = pulses // LANES
    for part, pair in enumerate(((parts[0], -parts[1]), (parts[1], parts[0]))):
        for target in range(2):
            for column in range(columns):
                columns_held[target * columns + column, pl.ds(part, pulses, stride=2), :] = pair[target][
                    :, column * LANES : (column + 1) * LANES
                ]
    for column in range(2 * columns):
        taps[:, column * LANES : (column + 1) * LANES] = columns_held[column].astype(BF)
    copies = []
    for tile in range(tiles):
        lines = lines_ref[:, tile * rows : (tile + 1) * rows].reshape(sources * rows, LANES)
        focused = lax.dot_general(lines, taps[...], (((0,), (0,)), ((), ())), preferred_element_type=F32)
        into = pl.ds(tile * LANES, LANES)
        made[into, 0, :] = focused[:, :pulses]
        made[into, 1, :] = focused[:, pulses:]
        copies.append(pltpu.make_async_copy(made.at[into], out_ref.at[into], sems.at[tile]))
        copies[-1].start()
    for copy in copies:
        copy.wait()


def toeplitz(diagonal_taps, size):
    span_size = 2 * size - 1
    reversed_taps = diagonal_taps[..., ::-1]
    shifted = jnp.concatenate(
        [reversed_taps[..., size - 1 :], reversed_taps[..., : size - 1]], axis=-1
    )
    reps = (1,) * (shifted.ndim - 1) + (size,)
    tiled_flat = jnp.tile(shifted, reps)[..., : size * (span_size - 1)]
    return tiled_flat.reshape(shifted.shape[:-1] + (size, span_size - 1))[..., :size]


def tap_blocks(tap_values, size):
    block_total = tap_values.shape[1] // size + 1
    padded_taps = jnp.pad(tap_values, ((0, 0), (size, 2 * size)))
    matrices = []
    for offset_block in range(block_total):
        first_tap = offset_block * size + 1
        parts = toeplitz(padded_taps[:, first_tap : first_tap + 2 * size - 1], size)
        real_part = parts[0]
        imag_part = parts[1]
        matrices.append(
            jnp.stack([jnp.stack([real_part, -imag_part]), jnp.stack([imag_part, real_part])])
        )
    return jnp.stack(matrices)


def correlate(blocked, matrices, output_count):
    summed = jnp.zeros((blocked.shape[0], 2, output_count, blocked.shape[3]), F32)
    for offset_block in range(matrices.shape[0]):
        piece_rows = blocked[:, :, offset_block : offset_block + output_count, :]
        summed = summed + jnp.einsum(
            "rcib,cdbn->rdin", piece_rows, matrices[offset_block], preferred_element_type=F32
        )
    return summed


def focus_long(range_lines, reference_row):
    block_size = L // 2
    bin_count, _, total_pulses = range_lines.shape
    block_count = total_pulses // block_size
    blocked = range_lines.reshape(bin_count, 2, block_count, block_size)
    blocked = jnp.pad(blocked, ((0, 0), (0, 0), (1, 1), (0, 0)))
    focused = correlate(blocked, tap_blocks(reference_row, block_size), block_count)
    return focused.reshape(1, bin_count, 2, total_pulses)


def call(kernel, outs, specs, scratch=(), vmem=24, flops=1000):
    space = {"s": pltpu.SMEM, "v": pltpu.VMEM, "a": pl.ANY}
    blocks = [pl.BlockSpec(memory_space=space[kind]) for kind in specs]
    return pl.pallas_call(
        kernel,
        out_shape=outs,
        in_specs=blocks[: -len(outs)],
        out_specs=tuple(blocks[-len(outs) :]),
        scratch_shapes=list(scratch),
        compiler_params=pltpu.CompilerParams(vmem_limit_bytes=vmem * 2**20),
        cost_estimate=pl.CostEstimate(flops=flops, bytes_accessed=1000, transcendentals=0),
    )


def on_device(raw_echo, chirp_replica, azimuth_refs, migration_index, window_start):
    pulses = raw_echo.shape[0]
    segment_devices = lax.axis_size("sa")
    pulse_devices = lax.axis_size("pa")
    tap_count = chirp_replica.shape[1]
    kept_width = R // segment_devices
    bin_count = kept_width // pulse_devices
    total_pulses = pulses * pulse_devices
    half = kept_width // LANES
    tap_tiles = tap_count // LANES + 2
    span = half + tap_tiles - 1

    rows = 2 * pulses
    shape = jax.ShapeDtypeStruct
    token = shape((8, LANES), F32)
    short = bin_count % LANES == 0 and total_pulses == L // 2

    far, turn = call(far_kernel, (shape((pulses, 2, half * LANES), BF), token), "vvv")(raw_echo)
    far = lax.ppermute(far, "sa", [(1, 3)])
    near, turn = call(near_kernel, (shape((half, rows, LANES), BF), token), "vsvvv")(turn, window_start, raw_echo)
    near = lax.ppermute(near, "sa", [(0, 1), (1, 2), (2, 3)])
    taps, own_rows, turn = call(
        prep_kernel,
        (shape((tap_tiles * LANES, 2 * LANES), BF), shape((pulse_devices, 16, LANES), BF), token),
        "vsvvvvvv",
    )(turn, window_start, migration_index, chirp_replica, azimuth_refs)
    arranged, ahead = call(
        arrange_kernel,
        (shape((span, rows, LANES), BF), shape((span - half, rows, LANES), BF)),
        "vsvvvv",
        flops=10**10,
    )(turn, window_start, raw_echo, far)
    ahead = lax.ppermute(ahead, "sa", [(3, 2)])

    targets, extra = (pulse_devices, 16) if short else (half // 8, 0)
    (compressed,) = call(
        compress_kernel,
        (shape((targets, half // targets * rows + extra, LANES), BF),),
        "svvvvvv",
        [pltpu.VMEM((span + 16, rows, LANES), BF)],
    )(window_start, arranged, near, ahead, taps, own_rows)

    if not short:
        kept = compressed.reshape(half, pulses, 2, LANES).transpose(0, 3, 2, 1)
        outgoing = kept.reshape(pulse_devices, bin_count, 2, pulses)
        turned = lax.all_to_all(outgoing, "pa", split_axis=0, concat_axis=3, tiled=True)
        rows_in = lax.all_to_all(own_rows, "pa", split_axis=0, concat_axis=0, tiled=True)
        reference_row = jnp.sum(rows_in[:, :8].astype(F32), axis=0).astype(BF).reshape(2, L)
        return focus_long(turned[0], reference_row)

    lines = lax.all_to_all(compressed, "pa", split_axis=0, concat_axis=0, tiled=True)
    width = 2 * total_pulses
    (focused,) = call(
        azimuth_kernel,
        (shape((bin_count, 2, total_pulses), F32),),
        "va",
        [
            pltpu.VMEM((width // LANES, width, LANES), F32),
            pltpu.VMEM((width, width), BF),
            pltpu.VMEM((bin_count, 2, total_pulses), F32),
            pltpu.SemaphoreType.DMA((bin_count // LANES,)),
        ],
    )(lines)
    return focused[None]


def solution(mesh):
    placed = (P("pa", None, "sa"), P(), P("pa", None, None), P(), P())
    return jax.shard_map(
        on_device, mesh=mesh, in_specs=placed, out_specs=P("sa", "pa", None, None), check_vma=False
    )
```

```python
import functools

import jax
import jax.numpy as jnp
from jax import lax
from jax.experimental import pallas as pl
from jax.experimental.pallas import tpu as pltpu
from jax.sharding import PartitionSpec as P

R = 16384
L = 512
LANES = 128
BF = jnp.bfloat16
F32 = jnp.float32


def reversed_lanes(row):
    row_id = lax.broadcasted_iota(jnp.int32, (LANES, LANES), 0)
    col_id = lax.broadcasted_iota(jnp.int32, (LANES, LANES), 1)
    flip = (row_id + col_id == LANES - 1).astype(BF)
    tiles = row.shape[1] // LANES
    pieces = [row[:, t * LANES : (t + 1) * LANES] for t in reversed(range(tiles))]
    return jnp.concatenate([jnp.dot(piece, flip, preferred_element_type=F32) for piece in pieces], axis=1)


def retile(source, target, first, tiles):
    shape = target.shape[1:]
    for t in range(tiles):
        target[first + t] = source[:, :, t * LANES : (t + 1) * LANES].reshape(shape)


def far_kernel(part, turn_in_ref, raw_ref, far_ref, turn_ref):
    turn_ref[...] = turn_in_ref[...]
    pulses, _, width = far_ref.shape

    @pl.when(lax.axis_index("sa") == 1)
    def _():
        far_ref[...] = raw_ref[part * pulses : (part + 1) * pulses, :, raw_ref.shape[2] - width :]


def near_kernel(part, turn_in_ref, window_ref, raw_ref, near_ref, turn_ref):
    turn_ref[...] = turn_in_ref[...]
    span = near_ref.shape[0]
    pulses = near_ref.shape[1] // 2
    own = pl.ds(part * pulses, pulses)
    tiles = raw_ref.shape[2] // LANES
    sub_index = lax.axis_index("sa")
    offset = window_ref[0] // LANES
    first = jnp.where(sub_index == 0, tiles - span, jnp.where(sub_index == 1, offset, 0))

    @pl.when(sub_index < 3)
    def _():
        start = pl.multiple_of(first * LANES, LANES)
        retile(raw_ref.at[own, :, pl.ds(start, span * LANES)], near_ref, 0, span)


def prep_kernel(turn_in_ref, window_ref, index_ref, chirp_ref, refs_ref, taps_ref, rows_ref, turn_ref):
    turn_ref[...] = turn_in_ref[...]
    taps = chirp_ref.shape[1]
    blocks = taps_ref.shape[0] // LANES
    width = blocks * LANES
    shift = lax.rem(window_ref[0], LANES)
    chirp = jnp.concatenate([chirp_ref[...], jnp.zeros((14, taps), BF)], axis=0)
    flipped = reversed_lanes(chirp)
    padded = jnp.concatenate([jnp.zeros((16, 2 * LANES), F32), flipped], axis=1)
    padded = jnp.concatenate([padded, jnp.zeros((16, width + LANES - padded.shape[1]), F32)], axis=1)
    moved = pltpu.roll(padded, width + LANES - 127 - shift, 1)[:, :width]
    for part in range(2):
        spread = jnp.broadcast_to(moved[part : part + 1], (LANES, width))
        skewed = pltpu.roll(spread, 0, 1, stride=1, stride_axis=0)
        for t in range(blocks):
            first = LANES * (blocks - 1 - t)
            taps_ref[t * LANES : (t + 1) * LANES, part * LANES : (part + 1) * LANES] = skewed[
                :, first : first + LANES
            ].astype(BF)
    own = refs_ref.shape[0]
    groups, targets = index_ref.shape
    first_row = lax.axis_index("pa") * own
    mine = lax.broadcasted_iota(jnp.int32, (groups, targets), 0) == lax.axis_index("sa")
    wanted = jnp.sum(jnp.where(mine, index_ref[...], 0), axis=0, keepdims=True)
    row_id = lax.broadcasted_iota(jnp.int32, (own, targets), 0) + first_row
    picks = (row_id == jnp.broadcast_to(wanted, (own, targets))).astype(F32)
    pieces = []
    for part in range(2):
        picked = lax.dot_general(
            picks, refs_ref[:, part, :].astype(F32), (((0,), (0,)), ((), ())), preferred_element_type=F32
        )
        pieces += [picked[:, t * LANES : (t + 1) * LANES] for t in range(L // LANES)]
    pieces += [jnp.zeros((targets, LANES), F32)] * (rows_ref.shape[1] - len(pieces))
    rows_ref[...] = jnp.stack(pieces, axis=1).astype(BF)


def arrange_kernel(part, turn_in_ref, window_ref, raw_ref, far_ref, out_ref, turn_ref):
    turn_ref[...] = turn_in_ref[...]
    span = out_ref.shape[0]
    half = far_ref.shape[2] // LANES
    pulses = far_ref.shape[0]
    own = pl.ds(part * pulses, pulses)
    sub_index = lax.axis_index("sa")

    @pl.when(sub_index == 0)
    def _():
        start = pl.multiple_of(window_ref[0] // LANES * LANES, LANES)
        retile(raw_ref.at[own, :, pl.ds(start, span * LANES)], out_ref, 0, span)

    @pl.when(sub_index == 1)
    def _():
        retile(raw_ref.at[own], out_ref, 0, span - half + 16)

    @pl.when(sub_index == 3)
    def _():
        retile(far_ref, out_ref, 0, half)


def compress_kernel(turn_in_ref, window_ref, arranged_ref, near_ref, taps_ref, rows_ref, out_ref, turn_ref, held):
    turn_ref[...] = turn_in_ref[...]
    span, rows, _ = near_ref.shape
    targets, _, _ = out_ref.shape
    tail = held.shape[0] - span
    tap_tiles = taps_ref.shape[0] // LANES
    half = span - tap_tiles + 1
    group = 16
    per_target = half // targets
    sub_index = lax.axis_index("sa")
    offset = window_ref[0] // LANES

    @pl.when(sub_index == 0)
    def _():
        held[:span] = arranged_ref[...]

    @pl.when(sub_index == 1)
    def _():
        held[:span] = near_ref[...]
        held[span:] = arranged_ref[:tail]

    @pl.when(sub_index == 2)
    def _():
        held[:span] = near_ref[...]

    @pl.when(sub_index == 3)
    def _():
        held[:half] = arranged_ref[:half]
        held[half : half + tail] = near_ref[:tail]

    base = jnp.where(sub_index == 1, span - half + offset, jnp.where(sub_index == 3, offset, 0))
    even = lax.rem(lax.broadcasted_iota(jnp.int32, (1, 8, LANES), 1), 2) == 0
    if out_ref.shape[1] > per_target * rows:
        out_ref[:, per_target * rows :] = rows_ref[...]
    for step in range(half // group):
        blocks = [
            held[pl.ds(base + group * step + t, group)].reshape(group * rows, LANES) for t in range(tap_tiles)
        ]
        product = jnp.dot(jnp.concatenate(blocks, axis=1), taps_ref[...], preferred_element_type=F32)
        straight = product[:, :LANES].reshape(-1, 8, LANES)
        crossed = product[:, LANES:].reshape(-1, 8, LANES)
        total = straight + jnp.where(even, pltpu.roll(crossed, 7, 1), -pltpu.roll(crossed, 1, 1))
        count = group // per_target
        out_ref[pl.ds(step * count, count), : per_target * rows] = total.astype(BF).reshape(
            count, per_target * rows, LANES
        )


def azimuth_taps(row, scratch, size):
    row = jnp.concatenate([row, jnp.zeros((14, row.shape[1]), BF)], axis=0)
    flipped = reversed_lanes(row)
    moved = pltpu.roll(flipped, row.shape[1] - (size - 1), 1)
    parts = []
    for part in range(2):
        spread = jnp.broadcast_to(moved[part : part + 1], (size, row.shape[1]))
        parts.append(pltpu.roll(spread, 0, 1, stride=1, stride_axis=0)[:, :size])
    columns = size // LANES
    for part, pair in enumerate(((parts[0], -parts[1]), (parts[1], parts[0]))):
        for target in range(2):
            for column in range(columns):
                scratch[target * columns + column, pl.ds(part, size, stride=2), :] = pair[target][
                    :, column * LANES : (column + 1) * LANES
                ]


def azimuth_product(lines_ref, tile, rows, taps):
    sources = lines_ref.shape[0]
    lines = lines_ref[:, tile * rows : (tile + 1) * rows].reshape(sources * rows, LANES)
    return lax.dot_general(lines, taps, (((0,), (0,)), ((), ())), preferred_element_type=F32)


def azimuth_first_kernel(lines_ref, later_ref, sum_ref, scratch, taps):
    size = scratch.shape[1] // 2
    sources = lines_ref.shape[0]
    tiles = sum_ref.shape[0] // LANES
    rows = (lines_ref.shape[1] - 16) // tiles
    picked = jnp.sum(lines_ref[:, tiles * rows :].astype(F32), axis=0)
    columns = L // LANES
    row = jnp.concatenate(
        [
            jnp.concatenate([picked[part * columns + t : part * columns + t + 1] for t in range(columns)], axis=1)
            for part in range(2)
        ],
        axis=0,
    ).astype(BF)
    azimuth_taps(row, scratch, size)
    for column in range(scratch.shape[0]):
        lanes = slice(column * LANES, (column + 1) * LANES)
        for source in range(sources):
            into = slice(source * rows, (source + 1) * rows)
            start = source * 2 * rows
            taps[into, lanes] = scratch[column, start : start + rows].astype(BF)
            later_ref[into, lanes] = scratch[column, start + rows : start + 2 * rows].astype(BF)
    for tile in range(tiles):
        sum_ref[tile * LANES : (tile + 1) * LANES] = azimuth_product(lines_ref, tile, rows, taps[...])


def azimuth_last_kernel(lines_ref, taps_ref, sum_ref, out_ref, made, sems):
    bins, _, pulses = out_ref.shape
    tiles = bins // LANES
    rows = lines_ref.shape[1] // tiles
    copies = []
    for tile in range(tiles):
        into = pl.ds(tile * LANES, LANES)
        focused = sum_ref[into] + azimuth_product(lines_ref, tile, rows, taps_ref[...])
        made[into, 0, :] = focused[:, :pulses]
        made[into, 1, :] = focused[:, pulses:]
        copies.append(pltpu.make_async_copy(made.at[into], out_ref.at[into], sems.at[tile]))
        copies[-1].start()
    for copy in copies:
        copy.wait()


def toeplitz(diagonal_taps, size):
    span_size = 2 * size - 1
    reversed_taps = diagonal_taps[..., ::-1]
    shifted = jnp.concatenate(
        [reversed_taps[..., size - 1 :], reversed_taps[..., : size - 1]], axis=-1
    )
    reps = (1,) * (shifted.ndim - 1) + (size,)
    tiled_flat = jnp.tile(shifted, reps)[..., : size * (span_size - 1)]
    return tiled_flat.reshape(shifted.shape[:-1] + (size, span_size - 1))[..., :size]


def tap_blocks(tap_values, size):
    block_total = tap_values.shape[1] // size + 1
    padded_taps = jnp.pad(tap_values, ((0, 0), (size, 2 * size)))
    matrices = []
    for offset_block in range(block_total):
        first_tap = offset_block * size + 1
        parts = toeplitz(padded_taps[:, first_tap : first_tap + 2 * size - 1], size)
        real_part = parts[0]
        imag_part = parts[1]
        matrices.append(
            jnp.stack([jnp.stack([real_part, -imag_part]), jnp.stack([imag_part, real_part])])
        )
    return jnp.stack(matrices)


def correlate(blocked, matrices, output_count):
    summed = jnp.zeros((blocked.shape[0], 2, output_count, blocked.shape[3]), F32)
    for offset_block in range(matrices.shape[0]):
        piece_rows = blocked[:, :, offset_block : offset_block + output_count, :]
        summed = summed + jnp.einsum(
            "rcib,cdbn->rdin", piece_rows, matrices[offset_block], preferred_element_type=F32
        )
    return summed


def focus_long(range_lines, reference_row):
    block_size = L // 2
    bin_count, _, total_pulses = range_lines.shape
    block_count = total_pulses // block_size
    blocked = range_lines.reshape(bin_count, 2, block_count, block_size)
    blocked = jnp.pad(blocked, ((0, 0), (0, 0), (1, 1), (0, 0)))
    focused = correlate(blocked, tap_blocks(reference_row, block_size), block_count)
    return focused.reshape(1, bin_count, 2, total_pulses)


def call(kernel, outs, specs, scratch=(), vmem=24, flops=1000):
    space = {"s": pltpu.SMEM, "v": pltpu.VMEM, "a": pl.ANY}
    blocks = [pl.BlockSpec(memory_space=space[kind]) for kind in specs]
    return pl.pallas_call(
        kernel,
        out_shape=outs,
        in_specs=blocks[: -len(outs)],
        out_specs=tuple(blocks[-len(outs) :]),
        scratch_shapes=list(scratch),
        compiler_params=pltpu.CompilerParams(vmem_limit_bytes=vmem * 2**20),
        cost_estimate=pl.CostEstimate(flops=flops, bytes_accessed=1000, transcendentals=0),
    )


def on_device(raw_echo, chirp_replica, azimuth_refs, migration_index, window_start):
    pulses = raw_echo.shape[0]
    segment_devices = lax.axis_size("sa")
    pulse_devices = lax.axis_size("pa")
    tap_count = chirp_replica.shape[1]
    kept_width = R // segment_devices
    bin_count = kept_width // pulse_devices
    total_pulses = pulses * pulse_devices
    half = kept_width // LANES
    tap_tiles = tap_count // LANES + 2
    span = half + tap_tiles - 1

    rows = 2 * pulses
    shape = jax.ShapeDtypeStruct
    token = shape((8, LANES), F32)
    short = bin_count % LANES == 0 and total_pulses == L // 2

    parts = 2
    pulses_each = pulses // parts
    rows_each = 2 * pulses_each
    turn = jnp.zeros(token.shape, token.dtype)

    def send(part, turn):
        far, turn = call(
            functools.partial(far_kernel, part), (shape((pulses_each, 2, half * LANES), BF), token), "vvvv"
        )(turn, raw_echo)
        far = lax.ppermute(far, "sa", [(1, 3)])
        near, turn = call(
            functools.partial(near_kernel, part), (shape((span, rows_each, LANES), BF), token), "vsvvv"
        )(turn, window_start, raw_echo)
        return far, lax.ppermute(near, "sa", [(0, 1), (1, 2), (2, 3)]), turn

    def arrange(part, turn, far):
        return call(
            functools.partial(arrange_kernel, part),
            (shape((span, rows_each, LANES), BF), token),
            "vsvvvv",
            flops=1000 if part else 10**10,
        )(turn, window_start, raw_echo, far)

    targets = pulse_devices if short else half // 16

    def compress(part, turn, arranged, near):
        extra = 16 if short and part == 0 else 0
        return call(
            compress_kernel,
            (shape((targets, half // targets * rows_each + extra, LANES), BF), token),
            "vsvvvvvv" if extra else "vsvvvavv",
            [pltpu.VMEM((span + 16 + tap_tiles - 1, rows_each, LANES), BF)],
            flops=10**12 if part else 1000,
        )(turn, window_start, arranged, near, taps, own_rows)

    far, near, turn = send(0, turn)
    taps, own_rows, turn = call(
        prep_kernel,
        (shape((tap_tiles * LANES, 2 * LANES), BF), shape((pulse_devices, 16, LANES), BF), token),
        "vsvvvvvv",
    )(turn, window_start, migration_index, chirp_replica, azimuth_refs)
    arranged, turn = arrange(0, turn, far)
    far, near_later, turn = send(1, turn)
    first, turn = compress(0, turn, arranged, near)
    arranged, turn = arrange(1, turn, far)
    second, turn = compress(1, turn, arranged, near_later)
    squeezed = [first, second]

    if not short:
        kept = jnp.stack(squeezed).reshape(parts, half, pulses_each, 2, LANES).transpose(1, 4, 3, 0, 2)
        outgoing = kept.reshape(pulse_devices, bin_count, 2, pulses)
        turned = lax.all_to_all(outgoing, "pa", split_axis=0, concat_axis=3, tiled=True)
        rows_in = lax.all_to_all(own_rows, "pa", split_axis=0, concat_axis=0, tiled=True)
        reference_row = jnp.sum(rows_in[:, :8].astype(F32), axis=0).astype(BF).reshape(2, L)
        return focus_long(turned[0], reference_row)

    lines = [lax.all_to_all(part, "pa", split_axis=0, concat_axis=0, tiled=True) for part in squeezed]
    width = 2 * total_pulses
    later_taps, first_sum = call(
        azimuth_first_kernel,
        (shape((width // 2, width), BF), shape((bin_count, width), F32)),
        "vvv",
        [pltpu.VMEM((width // LANES, width, LANES), F32), pltpu.VMEM((width // 2, width), BF)],
    )(lines[0])
    (focused,) = call(
        azimuth_last_kernel,
        (shape((bin_count, 2, total_pulses), F32),),
        "vvva",
        [pltpu.VMEM((bin_count, 2, total_pulses), F32), pltpu.SemaphoreType.DMA((bin_count // LANES,))],
    )(lines[1], later_taps, first_sum)
    return focused[None]


def solution(mesh):
    placed = (P("pa", None, "sa"), P(), P("pa", None, None), P(), P())
    return jax.shard_map(
        on_device, mesh=mesh, in_specs=placed, out_specs=P("sa", "pa", None, None), check_vma=False
    )
```

```python
import jax
import jax.numpy as jnp
from jax import lax
from jax.experimental import pallas as pl
from jax.experimental.pallas import tpu as pltpu
from jax.sharding import PartitionSpec as P

R = 16384
L = 512
LANES = 128
BF = jnp.bfloat16
F32 = jnp.float32


def reversed_lanes(row):
    row_id = lax.broadcasted_iota(jnp.int32, (LANES, LANES), 0)
    col_id = lax.broadcasted_iota(jnp.int32, (LANES, LANES), 1)
    flip = (row_id + col_id == LANES - 1).astype(BF)
    tiles = row.shape[1] // LANES
    pieces = [row[:, t * LANES : (t + 1) * LANES] for t in reversed(range(tiles))]
    return jnp.concatenate([jnp.dot(piece, flip, preferred_element_type=F32) for piece in pieces], axis=1)


def retile(source, target, first, tiles):
    shape = target.shape[1:]
    for t in range(tiles):
        target[first + t] = source[:, :, t * LANES : (t + 1) * LANES].reshape(shape)


def far_kernel(raw_ref, far_ref, turn_ref, sems):
    turn_ref[...] = jnp.zeros_like(turn_ref)
    pulses, _, width = far_ref.shape
    pieces = sems.shape[0]
    each = pulses // pieces

    @pl.when(lax.axis_index("sa") == 1)
    def _():
        copies = []
        for at in range(pieces):
            own = pl.ds(at * each, each)
            source = raw_ref.at[own, :, pl.ds(raw_ref.shape[2] - width, width)]
            copies.append(pltpu.make_async_copy(source, far_ref.at[own], sems.at[at]))
            copies[-1].start()
        for copy in copies:
            copy.wait()


def near_kernel(turn_in_ref, window_ref, raw_ref, near_ref, edge_ref, turn_ref):
    turn_ref[...] = turn_in_ref[...]
    span = near_ref.shape[0]
    half = edge_ref.shape[0]
    tiles = raw_ref.shape[2] // LANES
    sub_index = lax.axis_index("sa")

    @pl.when(sub_index == 0)
    def _():
        retile(raw_ref.at[:, :, pl.ds((tiles - half) * LANES, half * LANES)], edge_ref, 0, half)

    @pl.when(sub_index == 1)
    def _():
        start = pl.multiple_of(window_ref[0] // LANES * LANES, LANES)
        retile(raw_ref.at[:, :, pl.ds(start, span * LANES)], near_ref, 0, span)

    @pl.when(sub_index == 2)
    def _():
        retile(raw_ref, edge_ref, 0, span - half + 16)


def prep_kernel(turn_in_ref, window_ref, index_ref, chirp_ref, refs_ref, taps_ref, rows_ref, turn_ref):
    turn_ref[...] = turn_in_ref[...]
    taps = chirp_ref.shape[1]
    blocks = taps_ref.shape[0] // LANES
    width = blocks * LANES
    shift = lax.rem(window_ref[0], LANES)
    chirp = jnp.concatenate([chirp_ref[...], jnp.zeros((14, taps), BF)], axis=0)
    flipped = reversed_lanes(chirp)
    padded = jnp.concatenate([jnp.zeros((16, 2 * LANES), F32), flipped], axis=1)
    padded = jnp.concatenate([padded, jnp.zeros((16, width + LANES - padded.shape[1]), F32)], axis=1)
    moved = pltpu.roll(padded, width + LANES - 127 - shift, 1)[:, :width]
    for part in range(2):
        spread = jnp.broadcast_to(moved[part : part + 1], (LANES, width))
        skewed = pltpu.roll(spread, 0, 1, stride=1, stride_axis=0)
        for t in range(blocks):
            first = LANES * (blocks - 1 - t)
            taps_ref[t * LANES : (t + 1) * LANES, part * LANES : (part + 1) * LANES] = skewed[
                :, first : first + LANES
            ].astype(BF)
    own = refs_ref.shape[0]
    groups, targets = index_ref.shape
    first_row = lax.axis_index("pa") * own
    mine = lax.broadcasted_iota(jnp.int32, (groups, targets), 0) == lax.axis_index("sa")
    wanted = jnp.sum(jnp.where(mine, index_ref[...], 0), axis=0, keepdims=True)
    row_id = lax.broadcasted_iota(jnp.int32, (own, targets), 0) + first_row
    picks = (row_id == jnp.broadcast_to(wanted, (own, targets))).astype(F32)
    pieces = []
    for part in range(2):
        picked = lax.dot_general(
            picks, refs_ref[:, part, :].astype(F32), (((0,), (0,)), ((), ())), preferred_element_type=F32
        )
        pieces += [picked[:, t * LANES : (t + 1) * LANES] for t in range(L // LANES)]
    pieces += [jnp.zeros((targets, LANES), F32)] * (rows_ref.shape[1] - len(pieces))
    rows_ref[...] = jnp.stack(pieces, axis=1).astype(BF)


def compress(held, base, taps_ref, rows_ref, out_ref):
    rows = held.shape[1]
    targets = out_ref.shape[0]
    tap_tiles = taps_ref.shape[0] // LANES
    group = 8
    per_target = max(1, (out_ref.shape[1] - rows_ref.shape[1]) // rows)
    even = lax.rem(lax.broadcasted_iota(jnp.int32, (1, 8, LANES), 1), 2) == 0
    for step in range(targets * per_target // group):
        blocks = [
            held[pl.ds(base + group * step + t, group)].reshape(group * rows, LANES) for t in range(tap_tiles)
        ]
        product = jnp.dot(jnp.concatenate(blocks, axis=1), taps_ref[...], preferred_element_type=F32)
        straight = product[:, :LANES].reshape(-1, 8, LANES)
        crossed = product[:, LANES:].reshape(-1, 8, LANES)
        total = straight + jnp.where(even, pltpu.roll(crossed, 7, 1), -pltpu.roll(crossed, 1, 1))
        count = group // per_target
        out_ref[pl.ds(step * count, count), : per_target * rows] = total.astype(BF).reshape(
            count, per_target * rows, LANES
        )
    out_ref[:, per_target * rows :] = rows_ref[...]


def early_kernel(turn_in_ref, window_ref, raw_ref, far_ref, edge_ref, taps_ref, rows_ref, out_ref, turn_ref, held):
    turn_ref[...] = turn_in_ref[...]
    half = edge_ref.shape[0]
    tail = held.shape[0] - half
    span = tail - 16 + half
    sub_index = lax.axis_index("sa")
    offset = window_ref[0] // LANES

    @pl.when(sub_index == 0)
    def _():
        start = pl.multiple_of(offset * LANES, LANES)
        retile(raw_ref.at[:, :, pl.ds(start, span * LANES)], held, 0, span)

    @pl.when(sub_index == 1)
    def _():
        held[:half] = edge_ref[...]
        retile(raw_ref, held, half, tail)

    @pl.when(sub_index == 3)
    def _():
        retile(far_ref, held, 0, half)
        held[half:] = edge_ref[:tail]

    @pl.when(sub_index != 2)
    def _():
        compress(held, jnp.where(sub_index == 0, 0, offset), taps_ref, rows_ref, out_ref)


def late_kernel(near_ref, taps_ref, rows_ref, early_ref, out_ref):
    sub_index = lax.axis_index("sa")

    @pl.when(sub_index != 2)
    def _():
        out_ref[...] = early_ref[...]

    @pl.when(sub_index == 2)
    def _():
        compress(near_ref, 0, taps_ref, rows_ref, out_ref)


def azimuth_kernel(lines_ref, out_ref, columns_held, taps, made, sems):
    bins, _, pulses = out_ref.shape
    tiles = bins // LANES
    sources = lines_ref.shape[0]
    rows = (lines_ref.shape[1] - 16) // tiles
    picked = jnp.sum(lines_ref[:, tiles * rows :].astype(F32), axis=0)
    pieces = L // LANES
    row = [
        jnp.concatenate([picked[part * pieces + t : part * pieces + t + 1] for t in range(pieces)], axis=1)
        for part in range(2)
    ]
    row = jnp.concatenate(row + [jnp.zeros((14, L), F32)], axis=0).astype(BF)
    moved = pltpu.roll(reversed_lanes(row), L - (pulses - 1), 1)
    parts = []
    for part in range(2):
        spread = jnp.broadcast_to(moved[part : part + 1], (pulses, L))
        parts.append(pltpu.roll(spread, 0, 1, stride=1, stride_axis=0)[:, :pulses])
    columns = pulses // LANES
    for part, pair in enumerate(((parts[0], -parts[1]), (parts[1], parts[0]))):
        for target in range(2):
            for column in range(columns):
                columns_held[target * columns + column, pl.ds(part, pulses, stride=2), :] = pair[target][
                    :, column * LANES : (column + 1) * LANES
                ]
    for column in range(2 * columns):
        taps[:, column * LANES : (column + 1) * LANES] = columns_held[column].astype(BF)
    copies = []
    for tile in range(tiles):
        lines = lines_ref[:, tile * rows : (tile + 1) * rows].reshape(sources * rows, LANES)
        focused = lax.dot_general(lines, taps[...], (((0,), (0,)), ((), ())), preferred_element_type=F32)
        into = pl.ds(tile * LANES, LANES)
        made[into, 0, :] = focused[:, :pulses]
        made[into, 1, :] = focused[:, pulses:]
        copies.append(pltpu.make_async_copy(made.at[into], out_ref.at[into], sems.at[tile]))
        copies[-1].start()
    for copy in copies:
        copy.wait()


def toeplitz(diagonal_taps, size):
    span_size = 2 * size - 1
    reversed_taps = diagonal_taps[..., ::-1]
    shifted = jnp.concatenate(
        [reversed_taps[..., size - 1 :], reversed_taps[..., : size - 1]], axis=-1
    )
    reps = (1,) * (shifted.ndim - 1) + (size,)
    tiled_flat = jnp.tile(shifted, reps)[..., : size * (span_size - 1)]
    return tiled_flat.reshape(shifted.shape[:-1] + (size, span_size - 1))[..., :size]


def tap_blocks(tap_values, size):
    block_total = tap_values.shape[1] // size + 1
    padded_taps = jnp.pad(tap_values, ((0, 0), (size, 2 * size)))
    matrices = []
    for offset_block in range(block_total):
        first_tap = offset_block * size + 1
        parts = toeplitz(padded_taps[:, first_tap : first_tap + 2 * size - 1], size)
        real_part = parts[0]
        imag_part = parts[1]
        matrices.append(
            jnp.stack([jnp.stack([real_part, -imag_part]), jnp.stack([imag_part, real_part])])
        )
    return jnp.stack(matrices)


def correlate(blocked, matrices, output_count):
    summed = jnp.zeros((blocked.shape[0], 2, output_count, blocked.shape[3]), F32)
    for offset_block in range(matrices.shape[0]):
        piece_rows = blocked[:, :, offset_block : offset_block + output_count, :]
        summed = summed + jnp.einsum(
            "rcib,cdbn->rdin", piece_rows, matrices[offset_block], preferred_element_type=F32
        )
    return summed


def focus_long(range_lines, reference_row):
    block_size = L // 2
    bin_count, _, total_pulses = range_lines.shape
    block_count = total_pulses // block_size
    blocked = range_lines.reshape(bin_count, 2, block_count, block_size)
    blocked = jnp.pad(blocked, ((0, 0), (0, 0), (1, 1), (0, 0)))
    focused = correlate(blocked, tap_blocks(reference_row, block_size), block_count)
    return focused.reshape(1, bin_count, 2, total_pulses)


def call(kernel, outs, specs, scratch=(), vmem=24, flops=1000):
    space = {"s": pltpu.SMEM, "v": pltpu.VMEM, "a": pl.ANY}
    blocks = [pl.BlockSpec(memory_space=space[kind]) for kind in specs]
    return pl.pallas_call(
        kernel,
        out_shape=outs,
        in_specs=blocks[: -len(outs)],
        out_specs=tuple(blocks[-len(outs) :]),
        scratch_shapes=list(scratch),
        compiler_params=pltpu.CompilerParams(vmem_limit_bytes=int(vmem * 2**20)),
        cost_estimate=pl.CostEstimate(flops=flops, bytes_accessed=1000, transcendentals=0),
    )


def on_device(raw_echo, chirp_replica, azimuth_refs, migration_index, window_start):
    pulses = raw_echo.shape[0]
    segment_devices = lax.axis_size("sa")
    pulse_devices = lax.axis_size("pa")
    tap_count = chirp_replica.shape[1]
    kept_width = R // segment_devices
    bin_count = kept_width // pulse_devices
    total_pulses = pulses * pulse_devices
    half = kept_width // LANES
    tap_tiles = tap_count // LANES + 2
    span = half + tap_tiles - 1

    rows = 2 * pulses
    shape = jax.ShapeDtypeStruct
    token = shape((8, LANES), F32)
    short = bin_count % LANES == 0 and total_pulses == L // 2

    far, turn = call(
        far_kernel,
        (shape((pulses, 2, half * LANES), BF), token),
        "avv",
        [pltpu.SemaphoreType.DMA((8,))],
        53,
    )(raw_echo)
    far = lax.ppermute(far, "sa", [(1, 3)])
    near, edge, turn = call(
        near_kernel, (shape((span, rows, LANES), BF), shape((half, rows, LANES), BF), token), "vsvvvv"
    )(turn, window_start, raw_echo)
    near = lax.ppermute(near, "sa", [(1, 2)])
    edge = lax.ppermute(edge, "sa", [(0, 1), (2, 3)])
    targets = pulse_devices if short else half // 8
    taps, own_rows, turn = call(
        prep_kernel,
        (shape((tap_tiles * LANES, 2 * LANES), BF), shape((pulse_devices, 16, LANES), BF), token),
        "vsvvvvvv",
    )(turn, window_start, migration_index, chirp_replica, azimuth_refs)
    extra = own_rows if short else jnp.zeros((targets, 16, LANES), BF)
    made = shape((targets, half // targets * rows + 16, LANES), BF)
    early, turn = call(
        early_kernel,
        (made, token),
        "vsvvvvvvv",
        [pltpu.VMEM((span + 16, rows, LANES), BF)],
        flops=10**10,
    )(turn, window_start, raw_echo, far, edge, taps, extra)
    (compressed,) = call(late_kernel, (made,), "vvvvv")(near, taps, extra, early)

    if not short:
        kept = compressed[:, :-16].reshape(half, pulses, 2, LANES).transpose(0, 3, 2, 1)
        outgoing = kept.reshape(pulse_devices, bin_count, 2, pulses)
        turned = lax.all_to_all(outgoing, "pa", split_axis=0, concat_axis=3, tiled=True)
        rows_in = lax.all_to_all(own_rows, "pa", split_axis=0, concat_axis=0, tiled=True)
        reference_row = jnp.sum(rows_in[:, :8].astype(F32), axis=0).astype(BF).reshape(2, L)
        return focus_long(turned[0], reference_row)

    lines = lax.all_to_all(compressed, "pa", split_axis=0, concat_axis=0, tiled=True)
    width = 2 * total_pulses
    (focused,) = call(
        azimuth_kernel,
        (shape((bin_count, 2, total_pulses), F32),),
        "va",
        [
            pltpu.VMEM((width // LANES, width, LANES), F32),
            pltpu.VMEM((width, width), BF),
            pltpu.VMEM((bin_count, 2, total_pulses), F32),
            pltpu.SemaphoreType.DMA((bin_count // LANES,)),
        ],
    )(lines)
    return focused[None]


def solution(mesh):
    placed = (P("pa", None, "sa"), P(), P("pa", None, None), P(), P())
    return jax.shard_map(
        on_device, mesh=mesh, in_specs=placed, out_specs=P("sa", "pa", None, None), check_vma=False
    )
```

```python
import jax
import jax.numpy as jnp
from jax import lax
from jax.experimental import pallas as pl
from jax.experimental.pallas import tpu as pltpu
from jax.sharding import PartitionSpec as P

R = 16384
L = 512
LANES = 128
BF = jnp.bfloat16
F32 = jnp.float32


def reversed_lanes(row):
    row_id = lax.broadcasted_iota(jnp.int32, (LANES, LANES), 0)
    col_id = lax.broadcasted_iota(jnp.int32, (LANES, LANES), 1)
    flip = (row_id + col_id == LANES - 1).astype(BF)
    tiles = row.shape[1] // LANES
    pieces = [row[:, t * LANES : (t + 1) * LANES] for t in reversed(range(tiles))]
    return jnp.concatenate([jnp.dot(piece, flip, preferred_element_type=F32) for piece in pieces], axis=1)


def retile(source, target, first, tiles):
    shape = target.shape[1:]
    for t in range(tiles):
        target[first + t] = source[:, :, t * LANES : (t + 1) * LANES].reshape(shape)


def far_kernel(raw_ref, far_ref, turn_ref, natural, sems):
    turn_ref[...] = jnp.zeros_like(turn_ref)
    half, rows, _ = far_ref.shape
    pieces = sems.shape[0]
    each = rows // 2 // pieces
    width = half * LANES

    @pl.when(lax.axis_index("sa") == 1)
    def _():
        copies = []
        for at in range(pieces):
            own = pl.ds(at * each, each)
            source = raw_ref.at[own, :, pl.ds(raw_ref.shape[2] - width, width)]
            copies.append(pltpu.make_async_copy(source, natural.at[own], sems.at[at]))
            copies[-1].start()
        for at, copy in enumerate(copies):
            copy.wait()
            own = pl.ds(at * each, each)
            retile(natural.at[own], far_ref.at[:, pl.ds(at * each * 2, each * 2)], 0, half)


def edge_kernel(turn_in_ref, raw_ref, edge_ref, turn_ref):
    turn_ref[...] = turn_in_ref[...]
    half = edge_ref.shape[0]
    tiles = raw_ref.shape[2] // LANES
    sub_index = lax.axis_index("sa")

    @pl.when(sub_index == 0)
    def _():
        retile(raw_ref.at[:, :, pl.ds((tiles - half) * LANES, half * LANES)], edge_ref, 0, half)

    @pl.when(sub_index == 2)
    def _():
        retile(raw_ref, edge_ref, 0, half)


def prep_kernel(turn_in_ref, window_ref, index_ref, chirp_ref, refs_ref, taps_ref, rows_ref, turn_ref):
    turn_ref[...] = turn_in_ref[...]
    taps = chirp_ref.shape[1]
    blocks = taps_ref.shape[0] // LANES
    width = blocks * LANES
    shift = lax.rem(window_ref[0], LANES)
    chirp = jnp.concatenate([chirp_ref[...], jnp.zeros((14, taps), BF)], axis=0)
    flipped = reversed_lanes(chirp)
    padded = jnp.concatenate([jnp.zeros((16, 2 * LANES), F32), flipped], axis=1)
    padded = jnp.concatenate([padded, jnp.zeros((16, width + LANES - padded.shape[1]), F32)], axis=1)
    moved = pltpu.roll(padded, width + LANES - 127 - shift, 1)[:, :width]
    for part in range(2):
        spread = jnp.broadcast_to(moved[part : part + 1], (LANES, width))
        skewed = pltpu.roll(spread, 0, 1, stride=1, stride_axis=0)
        for t in range(blocks):
            first = LANES * (blocks - 1 - t)
            taps_ref[t * LANES : (t + 1) * LANES, part * LANES : (part + 1) * LANES] = skewed[
                :, first : first + LANES
            ].astype(BF)
    own = refs_ref.shape[0]
    groups, targets = index_ref.shape
    first_row = lax.axis_index("pa") * own
    mine = lax.broadcasted_iota(jnp.int32, (groups, targets), 0) == lax.axis_index("sa")
    wanted = jnp.sum(jnp.where(mine, index_ref[...], 0), axis=0, keepdims=True)
    row_id = lax.broadcasted_iota(jnp.int32, (own, targets), 0) + first_row
    picks = (row_id == jnp.broadcast_to(wanted, (own, targets))).astype(F32)
    pieces = []
    for part in range(2):
        picked = lax.dot_general(
            picks, refs_ref[:, part, :].astype(F32), (((0,), (0,)), ((), ())), preferred_element_type=F32
        )
        pieces += [picked[:, t * LANES : (t + 1) * LANES] for t in range(L // LANES)]
    pieces += [jnp.zeros((targets, LANES), F32)] * (rows_ref.shape[1] - len(pieces))
    rows_ref[...] = jnp.stack(pieces, axis=1).astype(BF)


def compress(held, base, taps_ref, out_ref):
    rows = held.shape[1]
    targets = out_ref.shape[0]
    tap_tiles = taps_ref.shape[0] // LANES
    group = 8
    per_target = out_ref.shape[1] // rows
    even = lax.rem(lax.broadcasted_iota(jnp.int32, (1, 8, LANES), 1), 2) == 0
    for step in range(targets * per_target // group):
        blocks = [
            held[pl.ds(base + group * step + t, group)].reshape(group * rows, LANES) for t in range(tap_tiles)
        ]
        product = jnp.dot(jnp.concatenate(blocks, axis=1), taps_ref[...], preferred_element_type=F32)
        straight = product[:, :LANES].reshape(-1, 8, LANES)
        crossed = product[:, LANES:].reshape(-1, 8, LANES)
        total = straight + jnp.where(even, pltpu.roll(crossed, 7, 1), -pltpu.roll(crossed, 1, 1))
        count = group // per_target
        out_ref[pl.ds(step * count, count), : per_target * rows] = total.astype(BF).reshape(
            count, per_target * rows, LANES
        )


def ahead_kernel(turn_in_ref, window_ref, raw_ref, taps_ref, out_ref, turn_ref, held):
    turn_ref[...] = turn_in_ref[...]
    span = held.shape[0]

    @pl.when(lax.axis_index("sa") == 1)
    def _():
        start = pl.multiple_of(window_ref[0] // LANES * LANES, LANES)
        retile(raw_ref.at[:, :, pl.ds(start, span * LANES)], held, 0, span)
        compress(held, 0, taps_ref, out_ref)


def early_kernel(turn_in_ref, window_ref, raw_ref, far_ref, edge_ref, taps_ref, rows_ref, out_ref, turn_ref, held):
    turn_ref[...] = turn_in_ref[...]
    half = edge_ref.shape[0]
    tail = held.shape[0] - half
    span = tail - 16 + half
    sub_index = lax.axis_index("sa")
    offset = window_ref[0] // LANES

    @pl.when(sub_index == 0)
    def _():
        start = pl.multiple_of(offset * LANES, LANES)
        retile(raw_ref.at[:, :, pl.ds(start, span * LANES)], held, 0, span)

    @pl.when(sub_index == 1)
    def _():
        held[:half] = edge_ref[...]
        retile(raw_ref, held, half, tail)

    @pl.when(sub_index == 3)
    def _():
        held[:half] = far_ref[...]
        held[half:] = edge_ref[:tail]

    @pl.when(sub_index != 2)
    def _():
        compress(held, jnp.where(sub_index == 0, 0, offset), taps_ref, out_ref)
        out_ref[:, out_ref.shape[1] - rows_ref.shape[1] :] = rows_ref[...]


def late_kernel(near_ref, rows_ref, early_ref, out_ref):
    bins = near_ref.shape[1]
    sub_index = lax.axis_index("sa")

    @pl.when(sub_index != 2)
    def _():
        out_ref[...] = early_ref[...]

    @pl.when(sub_index == 2)
    def _():
        out_ref[:, :bins] = near_ref[...]
        out_ref[:, bins:] = rows_ref[...]


def azimuth_kernel(lines_ref, out_ref, columns_held, taps, made, sems):
    bins, _, pulses = out_ref.shape
    tiles = bins // LANES
    sources = lines_ref.shape[0]
    rows = (lines_ref.shape[1] - 16) // tiles
    picked = jnp.sum(lines_ref[:, tiles * rows :].astype(F32), axis=0)
    pieces = L // LANES
    row = [
        jnp.concatenate([picked[part * pieces + t : part * pieces + t + 1] for t in range(pieces)], axis=1)
        for part in range(2)
    ]
    row = jnp.concatenate(row + [jnp.zeros((14, L), F32)], axis=0).astype(BF)
    moved = pltpu.roll(reversed_lanes(row), L - (pulses - 1), 1)
    parts = []
    for part in range(2):
        spread = jnp.broadcast_to(moved[part : part + 1], (pulses, L))
        parts.append(pltpu.roll(spread, 0, 1, stride=1, stride_axis=0)[:, :pulses])
    columns = pulses // LANES
    for part, pair in enumerate(((parts[0], -parts[1]), (parts[1], parts[0]))):
        for target in range(2):
            for column in range(columns):
                columns_held[target * columns + column, pl.ds(part, pulses, stride=2), :] = pair[target][
                    :, column * LANES : (column + 1) * LANES
                ]
    for column in range(2 * columns):
        taps[:, column * LANES : (column + 1) * LANES] = columns_held[column].astype(BF)
    copies = []
    for tile in range(tiles):
        lines = lines_ref[:, tile * rows : (tile + 1) * rows].reshape(sources * rows, LANES)
        focused = lax.dot_general(lines, taps[...], (((0,), (0,)), ((), ())), preferred_element_type=F32)
        into = pl.ds(tile * LANES, LANES)
        made[into, 0, :] = focused[:, :pulses]
        made[into, 1, :] = focused[:, pulses:]
        copies.append(pltpu.make_async_copy(made.at[into], out_ref.at[into], sems.at[tile]))
        copies[-1].start()
    for copy in copies:
        copy.wait()


def toeplitz(diagonal_taps, size):
    span_size = 2 * size - 1
    reversed_taps = diagonal_taps[..., ::-1]
    shifted = jnp.concatenate(
        [reversed_taps[..., size - 1 :], reversed_taps[..., : size - 1]], axis=-1
    )
    reps = (1,) * (shifted.ndim - 1) + (size,)
    tiled_flat = jnp.tile(shifted, reps)[..., : size * (span_size - 1)]
    return tiled_flat.reshape(shifted.shape[:-1] + (size, span_size - 1))[..., :size]


def tap_blocks(tap_values, size):
    block_total = tap_values.shape[1] // size + 1
    padded_taps = jnp.pad(tap_values, ((0, 0), (size, 2 * size)))
    matrices = []
    for offset_block in range(block_total):
        first_tap = offset_block * size + 1
        parts = toeplitz(padded_taps[:, first_tap : first_tap + 2 * size - 1], size)
        real_part = parts[0]
        imag_part = parts[1]
        matrices.append(
            jnp.stack([jnp.stack([real_part, -imag_part]), jnp.stack([imag_part, real_part])])
        )
    return jnp.stack(matrices)


def correlate(blocked, matrices, output_count):
    summed = jnp.zeros((blocked.shape[0], 2, output_count, blocked.shape[3]), F32)
    for offset_block in range(matrices.shape[0]):
        piece_rows = blocked[:, :, offset_block : offset_block + output_count, :]
        summed = summed + jnp.einsum(
            "rcib,cdbn->rdin", piece_rows, matrices[offset_block], preferred_element_type=F32
        )
    return summed


def focus_long(range_lines, reference_row):
    block_size = L // 2
    bin_count, _, total_pulses = range_lines.shape
    block_count = total_pulses // block_size
    blocked = range_lines.reshape(bin_count, 2, block_count, block_size)
    blocked = jnp.pad(blocked, ((0, 0), (0, 0), (1, 1), (0, 0)))
    focused = correlate(blocked, tap_blocks(reference_row, block_size), block_count)
    return focused.reshape(1, bin_count, 2, total_pulses)


def call(kernel, outs, specs, scratch=(), vmem=24, flops=1000):
    space = {"s": pltpu.SMEM, "v": pltpu.VMEM, "a": pl.ANY}
    blocks = [pl.BlockSpec(memory_space=space[kind]) for kind in specs]
    return pl.pallas_call(
        kernel,
        out_shape=outs,
        in_specs=blocks[: -len(outs)],
        out_specs=tuple(blocks[-len(outs) :]),
        scratch_shapes=list(scratch),
        compiler_params=pltpu.CompilerParams(vmem_limit_bytes=int(vmem * 2**20)),
        cost_estimate=pl.CostEstimate(flops=flops, bytes_accessed=1000, transcendentals=0),
    )


def on_device(raw_echo, chirp_replica, azimuth_refs, migration_index, window_start):
    pulses = raw_echo.shape[0]
    segment_devices = lax.axis_size("sa")
    pulse_devices = lax.axis_size("pa")
    tap_count = chirp_replica.shape[1]
    kept_width = R // segment_devices
    bin_count = kept_width // pulse_devices
    total_pulses = pulses * pulse_devices
    half = kept_width // LANES
    tap_tiles = tap_count // LANES + 2
    span = half + tap_tiles - 1

    rows = 2 * pulses
    shape = jax.ShapeDtypeStruct
    token = shape((8, LANES), F32)
    short = bin_count % LANES == 0 and total_pulses == L // 2

    targets = pulse_devices if short else half // 8
    slot = half // targets * rows

    far, turn = call(
        far_kernel,
        (shape((half, rows, LANES), BF), token),
        "avv",
        [pltpu.VMEM((pulses, 2, half * LANES), BF), pltpu.SemaphoreType.DMA((4,))],
        53,
    )(raw_echo)
    far = lax.ppermute(far, "sa", [(1, 3)])
    edge, turn = call(edge_kernel, (shape((half, rows, LANES), BF), token), "vvvv")(turn, raw_echo)
    edge = lax.ppermute(edge, "sa", [(0, 1), (2, 3)])
    taps, own_rows, turn = call(
        prep_kernel,
        (shape((tap_tiles * LANES, 2 * LANES), BF), shape((pulse_devices, 16, LANES), BF), token),
        "vsvvvvvv",
    )(turn, window_start, migration_index, chirp_replica, azimuth_refs)
    near, turn = call(
        ahead_kernel,
        (shape((targets, slot, LANES), BF), token),
        "vsvvvv",
        [pltpu.VMEM((span, rows, LANES), BF)],
    )(turn, window_start, raw_echo, taps)
    near = lax.ppermute(near, "sa", [(1, 2)])
    extra = own_rows if short else jnp.zeros((targets, 16, LANES), BF)
    made = shape((targets, slot + 16, LANES), BF)
    early, turn = call(
        early_kernel,
        (made, token),
        "vsvvvvvvv",
        [pltpu.VMEM((span + 16, rows, LANES), BF)],
        flops=10**10,
    )(turn, window_start, raw_echo, far, edge, taps, extra)
    (compressed,) = call(late_kernel, (made,), "vvvv")(near, extra, early)

    if not short:
        kept = compressed[:, :-16].reshape(half, pulses, 2, LANES).transpose(0, 3, 2, 1)
        outgoing = kept.reshape(pulse_devices, bin_count, 2, pulses)
        turned = lax.all_to_all(outgoing, "pa", split_axis=0, concat_axis=3, tiled=True)
        rows_in = lax.all_to_all(own_rows, "pa", split_axis=0, concat_axis=0, tiled=True)
        reference_row = jnp.sum(rows_in[:, :8].astype(F32), axis=0).astype(BF).reshape(2, L)
        return focus_long(turned[0], reference_row)

    lines = lax.all_to_all(compressed, "pa", split_axis=0, concat_axis=0, tiled=True)
    width = 2 * total_pulses
    (focused,) = call(
        azimuth_kernel,
        (shape((bin_count, 2, total_pulses), F32),),
        "va",
        [
            pltpu.VMEM((width // LANES, width, LANES), F32),
            pltpu.VMEM((width, width), BF),
            pltpu.VMEM((bin_count, 2, total_pulses), F32),
            pltpu.SemaphoreType.DMA((bin_count // LANES,)),
        ],
    )(lines)
    return focused[None]


def solution(mesh):
    placed = (P("pa", None, "sa"), P(), P("pa", None, None), P(), P())
    return jax.shard_map(
        on_device, mesh=mesh, in_specs=placed, out_specs=P("sa", "pa", None, None), check_vma=False
    )
```

```python
import jax
import jax.numpy as jnp
from jax import lax
from jax.experimental import pallas as pl
from jax.experimental.pallas import tpu as pltpu
from jax.sharding import PartitionSpec as P

R = 16384
L = 512
LANES = 128
BF = jnp.bfloat16
F32 = jnp.float32


def reversed_lanes(row):
    row_id = lax.broadcasted_iota(jnp.int32, (LANES, LANES), 0)
    col_id = lax.broadcasted_iota(jnp.int32, (LANES, LANES), 1)
    flip = (row_id + col_id == LANES - 1).astype(BF)
    tiles = row.shape[1] // LANES
    pieces = [row[:, t * LANES : (t + 1) * LANES] for t in reversed(range(tiles))]
    return jnp.concatenate([jnp.dot(piece, flip, preferred_element_type=F32) for piece in pieces], axis=1)


def retile(source, target, first, tiles):
    shape = target.shape[1:]
    for t in range(tiles):
        target[first + t] = source[:, :, t * LANES : (t + 1) * LANES].reshape(shape)


def far_kernel(raw_ref, far_ref, turn_ref, natural, sems):
    turn_ref[...] = jnp.zeros_like(turn_ref)
    half, rows, _ = far_ref.shape
    pieces = sems.shape[0]
    each = rows // 2 // pieces
    width = half * LANES

    @pl.when(lax.axis_index("sa") == 1)
    def _():
        copies = []
        for at in range(pieces):
            own = pl.ds(at * each, each)
            source = raw_ref.at[own, :, pl.ds(raw_ref.shape[2] - width, width)]
            copies.append(pltpu.make_async_copy(source, natural.at[own], sems.at[at]))
            copies[-1].start()
        for at, copy in enumerate(copies):
            copy.wait()
            own = pl.ds(at * each, each)
            retile(natural.at[own], far_ref.at[:, pl.ds(at * each * 2, each * 2)], 0, half)


def edge_kernel(turn_in_ref, raw_ref, edge_ref, turn_ref):
    turn_ref[...] = turn_in_ref[...]
    half = edge_ref.shape[0]
    tiles = raw_ref.shape[2] // LANES
    sub_index = lax.axis_index("sa")

    @pl.when(sub_index == 0)
    def _():
        retile(raw_ref.at[:, :, pl.ds((tiles - half) * LANES, half * LANES)], edge_ref, 0, half)

    @pl.when(sub_index == 2)
    def _():
        retile(raw_ref, edge_ref, 0, half)


def prep_kernel(turn_in_ref, window_ref, index_ref, chirp_ref, refs_ref, taps_ref, rows_ref, turn_ref):
    turn_ref[...] = turn_in_ref[...]
    taps = chirp_ref.shape[1]
    blocks = taps_ref.shape[0] // LANES
    width = blocks * LANES
    shift = lax.rem(window_ref[0], LANES)
    chirp = jnp.concatenate([chirp_ref[...], jnp.zeros((14, taps), BF)], axis=0)
    flipped = reversed_lanes(chirp)
    padded = jnp.concatenate([jnp.zeros((16, 2 * LANES), F32), flipped], axis=1)
    padded = jnp.concatenate([padded, jnp.zeros((16, width + LANES - padded.shape[1]), F32)], axis=1)
    moved = pltpu.roll(padded, width + LANES - 127 - shift, 1)[:, :width]
    for part in range(2):
        spread = jnp.broadcast_to(moved[part : part + 1], (LANES, width))
        skewed = pltpu.roll(spread, 0, 1, stride=1, stride_axis=0)
        for t in range(blocks):
            first = LANES * (blocks - 1 - t)
            taps_ref[t * LANES : (t + 1) * LANES, part * LANES : (part + 1) * LANES] = skewed[
                :, first : first + LANES
            ].astype(BF)
    own = refs_ref.shape[0]
    groups, targets = index_ref.shape
    first_row = lax.axis_index("pa") * own
    mine = lax.broadcasted_iota(jnp.int32, (groups, targets), 0) == lax.axis_index("sa")
    wanted = jnp.sum(jnp.where(mine, index_ref[...], 0), axis=0, keepdims=True)
    row_id = lax.broadcasted_iota(jnp.int32, (own, targets), 0) + first_row
    picks = (row_id == jnp.broadcast_to(wanted, (own, targets))).astype(F32)
    pieces = []
    for part in range(2):
        picked = lax.dot_general(
            picks, refs_ref[:, part, :].astype(F32), (((0,), (0,)), ((), ())), preferred_element_type=F32
        )
        pieces += [picked[:, t * LANES : (t + 1) * LANES] for t in range(L // LANES)]
    pieces += [jnp.zeros((targets, LANES), F32)] * (rows_ref.shape[1] - len(pieces))
    rows_ref[...] = jnp.stack(pieces, axis=1).astype(BF)


def compress(held, base, taps_ref, out_ref):
    rows = held.shape[1]
    targets = out_ref.shape[0]
    tap_tiles = taps_ref.shape[0] // LANES
    group = 8
    per_target = out_ref.shape[1] // rows
    even = lax.rem(lax.broadcasted_iota(jnp.int32, (1, 8, LANES), 1), 2) == 0
    for step in range(targets * per_target // group):
        blocks = [
            held[pl.ds(base + group * step + t, group)].reshape(group * rows, LANES) for t in range(tap_tiles)
        ]
        product = jnp.dot(jnp.concatenate(blocks, axis=1), taps_ref[...], preferred_element_type=F32)
        straight = product[:, :LANES].reshape(-1, 8, LANES)
        crossed = product[:, LANES:].reshape(-1, 8, LANES)
        total = straight + jnp.where(even, pltpu.roll(crossed, 7, 1), -pltpu.roll(crossed, 1, 1))
        count = group // per_target
        out_ref[pl.ds(step * count, count), : per_target * rows] = total.astype(BF).reshape(
            count, per_target * rows, LANES
        )


def ahead_kernel(turn_in_ref, window_ref, raw_ref, taps_ref, out_ref, turn_ref, held):
    turn_ref[...] = turn_in_ref[...]
    span = held.shape[0]

    @pl.when(lax.axis_index("sa") == 1)
    def _():
        start = pl.multiple_of(window_ref[0] // LANES * LANES, LANES)
        retile(raw_ref.at[:, :, pl.ds(start, span * LANES)], held, 0, span)
        compress(held, 0, taps_ref, out_ref)


def gate_kernel(turn_in_ref, _, turn_ref):
    turn_ref[...] = turn_in_ref[...]


def early_kernel(turn_in_ref, window_ref, raw_ref, far_ref, edge_ref, taps_ref, out_ref, held):
    half = edge_ref.shape[0]
    tail = held.shape[0] - half
    span = tail - 16 + half
    sub_index = lax.axis_index("sa")
    offset = window_ref[0] // LANES

    @pl.when(sub_index == 0)
    def _():
        start = pl.multiple_of(offset * LANES, LANES)
        retile(raw_ref.at[:, :, pl.ds(start, span * LANES)], held, 0, span)

    @pl.when(sub_index == 1)
    def _():
        held[:half] = edge_ref[...]
        retile(raw_ref, held, half, tail)

    @pl.when(sub_index == 3)
    def _():
        held[:half] = far_ref[...]
        held[half:] = edge_ref[:tail]

    @pl.when(sub_index != 2)
    def _():
        compress(held, jnp.where(sub_index == 0, 0, offset), taps_ref, out_ref)


def late_kernel(near_ref, early_ref, out_ref, turn_ref):
    turn_ref[...] = jnp.zeros_like(turn_ref)
    sub_index = lax.axis_index("sa")

    @pl.when(sub_index != 2)
    def _():
        out_ref[...] = early_ref[...]

    @pl.when(sub_index == 2)
    def _():
        out_ref[...] = near_ref[...]


def azimuth_taps_kernel(turn_in_ref, rows_ref, taps_ref, columns_held):
    pulses = taps_ref.shape[0] // 2
    picked = rows_ref[0].astype(F32)
    pieces = L // LANES
    row = [
        jnp.concatenate([picked[part * pieces + t : part * pieces + t + 1] for t in range(pieces)], axis=1)
        for part in range(2)
    ]
    row = jnp.concatenate(row + [jnp.zeros((14, L), F32)], axis=0).astype(BF)
    moved = pltpu.roll(reversed_lanes(row), L - (pulses - 1), 1)
    parts = []
    for part in range(2):
        spread = jnp.broadcast_to(moved[part : part + 1], (pulses, L))
        parts.append(pltpu.roll(spread, 0, 1, stride=1, stride_axis=0)[:, :pulses])
    columns = pulses // LANES
    for part, pair in enumerate(((parts[0], -parts[1]), (parts[1], parts[0]))):
        for target in range(2):
            for column in range(columns):
                columns_held[target * columns + column, pl.ds(part, pulses, stride=2), :] = pair[target][
                    :, column * LANES : (column + 1) * LANES
                ]
    for column in range(2 * columns):
        taps_ref[:, column * LANES : (column + 1) * LANES] = columns_held[column].astype(BF)


def azimuth_kernel(lines_ref, taps_ref, out_ref, made, sems):
    bins, _, pulses = out_ref.shape
    tiles = bins // LANES
    sources = lines_ref.shape[0]
    rows = lines_ref.shape[1] // tiles
    copies = []
    for tile in range(tiles):
        lines = lines_ref[:, tile * rows : (tile + 1) * rows].reshape(sources * rows, LANES)
        focused = lax.dot_general(lines, taps_ref[...], (((0,), (0,)), ((), ())), preferred_element_type=F32)
        into = pl.ds(tile * LANES, LANES)
        made[into, 0, :] = focused[:, :pulses]
        made[into, 1, :] = focused[:, pulses:]
        copies.append(pltpu.make_async_copy(made.at[into], out_ref.at[into], sems.at[tile]))
        copies[-1].start()
    for copy in copies:
        copy.wait()


def toeplitz(diagonal_taps, size):
    span_size = 2 * size - 1
    reversed_taps = diagonal_taps[..., ::-1]
    shifted = jnp.concatenate(
        [reversed_taps[..., size - 1 :], reversed_taps[..., : size - 1]], axis=-1
    )
    reps = (1,) * (shifted.ndim - 1) + (size,)
    tiled_flat = jnp.tile(shifted, reps)[..., : size * (span_size - 1)]
    return tiled_flat.reshape(shifted.shape[:-1] + (size, span_size - 1))[..., :size]


def tap_blocks(tap_values, size):
    block_total = tap_values.shape[1] // size + 1
    padded_taps = jnp.pad(tap_values, ((0, 0), (size, 2 * size)))
    matrices = []
    for offset_block in range(block_total):
        first_tap = offset_block * size + 1
        parts = toeplitz(padded_taps[:, first_tap : first_tap + 2 * size - 1], size)
        real_part = parts[0]
        imag_part = parts[1]
        matrices.append(
            jnp.stack([jnp.stack([real_part, -imag_part]), jnp.stack([imag_part, real_part])])
        )
    return jnp.stack(matrices)


def correlate(blocked, matrices, output_count):
    summed = jnp.zeros((blocked.shape[0], 2, output_count, blocked.shape[3]), F32)
    for offset_block in range(matrices.shape[0]):
        piece_rows = blocked[:, :, offset_block : offset_block + output_count, :]
        summed = summed + jnp.einsum(
            "rcib,cdbn->rdin", piece_rows, matrices[offset_block], preferred_element_type=F32
        )
    return summed


def focus_long(range_lines, reference_row):
    block_size = L // 2
    bin_count, _, total_pulses = range_lines.shape
    block_count = total_pulses // block_size
    blocked = range_lines.reshape(bin_count, 2, block_count, block_size)
    blocked = jnp.pad(blocked, ((0, 0), (0, 0), (1, 1), (0, 0)))
    focused = correlate(blocked, tap_blocks(reference_row, block_size), block_count)
    return focused.reshape(1, bin_count, 2, total_pulses)


def call(kernel, outs, specs, scratch=(), vmem=24, flops=1000):
    space = {"s": pltpu.SMEM, "v": pltpu.VMEM, "a": pl.ANY}
    blocks = [pl.BlockSpec(memory_space=space[kind]) for kind in specs]
    return pl.pallas_call(
        kernel,
        out_shape=outs,
        in_specs=blocks[: -len(outs)],
        out_specs=tuple(blocks[-len(outs) :]),
        scratch_shapes=list(scratch),
        compiler_params=pltpu.CompilerParams(vmem_limit_bytes=int(vmem * 2**20)),
        cost_estimate=pl.CostEstimate(flops=flops, bytes_accessed=1000, transcendentals=0),
    )


def on_device(raw_echo, chirp_replica, azimuth_refs, migration_index, window_start):
    pulses = raw_echo.shape[0]
    segment_devices = lax.axis_size("sa")
    pulse_devices = lax.axis_size("pa")
    tap_count = chirp_replica.shape[1]
    kept_width = R // segment_devices
    bin_count = kept_width // pulse_devices
    total_pulses = pulses * pulse_devices
    half = kept_width // LANES
    tap_tiles = tap_count // LANES + 2
    span = half + tap_tiles - 1

    rows = 2 * pulses
    shape = jax.ShapeDtypeStruct
    token = shape((8, LANES), F32)
    short = bin_count % LANES == 0 and total_pulses == L // 2

    targets = pulse_devices if short else half // 8
    made = shape((targets, half // targets * rows, LANES), BF)

    far, turn = call(
        far_kernel,
        (shape((half, rows, LANES), BF), token),
        "avv",
        [pltpu.VMEM((pulses, 2, half * LANES), BF), pltpu.SemaphoreType.DMA((4,))],
        53,
    )(raw_echo)
    far = lax.ppermute(far, "sa", [(1, 3)])
    edge, turn = call(edge_kernel, (shape((half, rows, LANES), BF), token), "vvvv")(turn, raw_echo)
    edge = lax.ppermute(edge, "sa", [(0, 1), (2, 3)])
    taps, own_rows, turn = call(
        prep_kernel,
        (shape((tap_tiles * LANES, 2 * LANES), BF), shape((pulse_devices, 16, LANES), BF), token),
        "vsvvvvvv",
    )(turn, window_start, migration_index, chirp_replica, azimuth_refs)
    row_in = lax.psum_scatter(own_rows, "pa", scatter_dimension=0, tiled=True)
    near, turn = call(ahead_kernel, (made, token), "vsvvvv", [pltpu.VMEM((span, rows, LANES), BF)])(
        turn, window_start, raw_echo, taps
    )
    near = lax.ppermute(near, "sa", [(1, 2)])
    (turn,) = call(gate_kernel, (token,), "vav", flops=10**10)(turn, far)
    (early,) = call(
        early_kernel, (made,), "vsvvvvv", [pltpu.VMEM((span + 16, rows, LANES), BF)], flops=10**10
    )(turn, window_start, raw_echo, far, edge, taps)
    compressed, turn = call(late_kernel, (made, token), "vvvv")(near, early)

    if not short:
        kept = compressed.reshape(half, pulses, 2, LANES).transpose(0, 3, 2, 1)
        outgoing = kept.reshape(pulse_devices, bin_count, 2, pulses)
        turned = lax.all_to_all(outgoing, "pa", split_axis=0, concat_axis=3, tiled=True)
        return focus_long(turned[0], row_in[0, :8].reshape(2, L))

    lines = lax.all_to_all(compressed, "pa", split_axis=0, concat_axis=0, tiled=True)
    width = 2 * total_pulses
    (azimuth_taps,) = call(
        azimuth_taps_kernel, (shape((width, width), BF),), "vvv", [pltpu.VMEM((width // LANES, width, LANES), F32)]
    )(turn, row_in)
    (focused,) = call(
        azimuth_kernel,
        (shape((bin_count, 2, total_pulses), F32),),
        "vva",
        [pltpu.VMEM((bin_count, 2, total_pulses), F32), pltpu.SemaphoreType.DMA((bin_count // LANES,))],
    )(lines, azimuth_taps)
    return focused[None]


def solution(mesh):
    placed = (P("pa", None, "sa"), P(), P("pa", None, None), P(), P())
    return jax.shard_map(
        on_device, mesh=mesh, in_specs=placed, out_specs=P("sa", "pa", None, None), check_vma=False
    )
```

```python
import jax
import jax.numpy as jnp
from jax import lax
from jax.experimental import pallas as pl
from jax.experimental.pallas import tpu as pltpu
from jax.sharding import PartitionSpec as P

R = 16384
L = 512
LANES = 128
BF = jnp.bfloat16
F32 = jnp.float32


def reversed_lanes(row):
    row_id = lax.broadcasted_iota(jnp.int32, (LANES, LANES), 0)
    col_id = lax.broadcasted_iota(jnp.int32, (LANES, LANES), 1)
    flip = (row_id + col_id == LANES - 1).astype(BF)
    tiles = row.shape[1] // LANES
    pieces = [row[:, t * LANES : (t + 1) * LANES] for t in reversed(range(tiles))]
    return jnp.concatenate([jnp.dot(piece, flip, preferred_element_type=F32) for piece in pieces], axis=1)


def retile(source, target, first, tiles):
    shape = target.shape[1:]
    for t in range(tiles):
        target[first + t] = source[:, :, t * LANES : (t + 1) * LANES].reshape(shape)


def far_kernel(raw_ref, far_ref, turn_ref, natural, sems):
    turn_ref[...] = jnp.zeros_like(turn_ref)
    half, rows, _ = far_ref.shape
    pieces = sems.shape[0]
    each = rows // 2 // pieces
    width = half * LANES

    @pl.when(lax.axis_index("sa") == 1)
    def _():
        copies = []
        for at in range(pieces):
            own = pl.ds(at * each, each)
            source = raw_ref.at[own, :, pl.ds(raw_ref.shape[2] - width, width)]
            copies.append(pltpu.make_async_copy(source, natural.at[own], sems.at[at]))
            copies[-1].start()
        for at, copy in enumerate(copies):
            copy.wait()
            own = pl.ds(at * each, each)
            retile(natural.at[own], far_ref.at[:, pl.ds(at * each * 2, each * 2)], 0, half)


def edge_kernel(turn_in_ref, raw_ref, edge_ref, turn_ref):
    turn_ref[...] = turn_in_ref[...]
    half = edge_ref.shape[0]
    tiles = raw_ref.shape[2] // LANES
    sub_index = lax.axis_index("sa")

    @pl.when(sub_index == 0)
    def _():
        retile(raw_ref.at[:, :, pl.ds((tiles - half) * LANES, half * LANES)], edge_ref, 0, half)

    @pl.when(sub_index == 2)
    def _():
        retile(raw_ref, edge_ref, 0, half)


def prep_kernel(turn_in_ref, window_ref, index_ref, chirp_ref, refs_ref, taps_ref, rows_ref, turn_ref):
    turn_ref[...] = turn_in_ref[...]
    taps = chirp_ref.shape[1]
    blocks = taps_ref.shape[0] // LANES
    width = blocks * LANES
    shift = lax.rem(window_ref[0], LANES)
    chirp = jnp.concatenate([chirp_ref[...], jnp.zeros((14, taps), BF)], axis=0)
    flipped = reversed_lanes(chirp)
    padded = jnp.concatenate([jnp.zeros((16, 2 * LANES), F32), flipped], axis=1)
    padded = jnp.concatenate([padded, jnp.zeros((16, width + LANES - padded.shape[1]), F32)], axis=1)
    moved = pltpu.roll(padded, width + LANES - 127 - shift, 1)[:, :width]
    for part in range(2):
        spread = jnp.broadcast_to(moved[part : part + 1], (LANES, width))
        skewed = pltpu.roll(spread, 0, 1, stride=1, stride_axis=0)
        for t in range(blocks):
            first = LANES * (blocks - 1 - t)
            taps_ref[t * LANES : (t + 1) * LANES, part * LANES : (part + 1) * LANES] = skewed[
                :, first : first + LANES
            ].astype(BF)
    own = refs_ref.shape[0]
    groups, targets = index_ref.shape
    first_row = lax.axis_index("pa") * own
    mine = lax.broadcasted_iota(jnp.int32, (groups, targets), 0) == lax.axis_index("sa")
    wanted = jnp.sum(jnp.where(mine, index_ref[...], 0), axis=0, keepdims=True)
    row_id = lax.broadcasted_iota(jnp.int32, (own, targets), 0) + first_row
    picks = (row_id == jnp.broadcast_to(wanted, (own, targets))).astype(F32)
    pieces = []
    for part in range(2):
        picked = lax.dot_general(
            picks, refs_ref[:, part, :].astype(F32), (((0,), (0,)), ((), ())), preferred_element_type=F32
        )
        pieces += [picked[:, t * LANES : (t + 1) * LANES] for t in range(L // LANES)]
    pieces += [jnp.zeros((targets, LANES), F32)] * (rows_ref.shape[1] - len(pieces))
    rows_ref[...] = jnp.stack(pieces, axis=1).astype(BF)


def compress(held, base, taps_ref, out_ref):
    rows = held.shape[1]
    targets = out_ref.shape[0]
    tap_tiles = taps_ref.shape[0] // LANES
    group = 8
    per_target = out_ref.shape[1] // rows
    even = lax.rem(lax.broadcasted_iota(jnp.int32, (1, 8, LANES), 1), 2) == 0
    for step in range(targets * per_target // group):
        blocks = [
            held[pl.ds(base + group * step + t, group)].reshape(group * rows, LANES) for t in range(tap_tiles)
        ]
        product = jnp.dot(jnp.concatenate(blocks, axis=1), taps_ref[...], preferred_element_type=F32)
        straight = product[:, :LANES].reshape(-1, 8, LANES)
        crossed = product[:, LANES:].reshape(-1, 8, LANES)
        total = straight + jnp.where(even, pltpu.roll(crossed, 7, 1), -pltpu.roll(crossed, 1, 1))
        count = group // per_target
        out_ref[pl.ds(step * count, count), : per_target * rows] = total.astype(BF).reshape(
            count, per_target * rows, LANES
        )


def ahead_kernel(turn_in_ref, window_ref, raw_ref, taps_ref, out_ref, turn_ref, held):
    turn_ref[...] = turn_in_ref[...]
    span = held.shape[0]

    @pl.when(lax.axis_index("sa") == 1)
    def _():
        start = pl.multiple_of(window_ref[0] // LANES * LANES, LANES)
        retile(raw_ref.at[:, :, pl.ds(start, span * LANES)], held, 0, span)
        compress(held, 0, taps_ref, out_ref)


def early_kernel(turn_in_ref, window_ref, raw_ref, far_ref, edge_ref, taps_ref, rows_ref, out_ref, held):
    half = edge_ref.shape[0]
    tail = held.shape[0] - half
    span = tail - 16 + half
    sub_index = lax.axis_index("sa")
    offset = window_ref[0] // LANES

    @pl.when(sub_index == 0)
    def _():
        start = pl.multiple_of(offset * LANES, LANES)
        retile(raw_ref.at[:, :, pl.ds(start, span * LANES)], held, 0, span)

    @pl.when(sub_index == 1)
    def _():
        held[:half] = edge_ref[...]
        retile(raw_ref, held, half, tail)

    @pl.when(sub_index == 3)
    def _():
        held[:half] = far_ref[...]
        held[half:] = edge_ref[:tail]

    @pl.when(sub_index != 2)
    def _():
        compress(held, jnp.where(sub_index == 0, 0, offset), taps_ref, out_ref)
        out_ref[:, out_ref.shape[1] - rows_ref.shape[1] :] = rows_ref[...]


def late_kernel(near_ref, rows_ref, early_ref, out_ref):
    bins = near_ref.shape[1]
    sub_index = lax.axis_index("sa")

    @pl.when(sub_index != 2)
    def _():
        out_ref[...] = early_ref[...]

    @pl.when(sub_index == 2)
    def _():
        out_ref[:, :bins] = near_ref[...]
        out_ref[:, bins:] = rows_ref[...]


def azimuth_kernel(lines_ref, out_ref, columns_held, taps, made, sems):
    pulses = taps.shape[0] // 2
    columns = pulses // LANES
    tiles = sems.shape[0]
    each = out_ref.shape[0] // tiles
    sources = lines_ref.shape[0]
    rows = (lines_ref.shape[1] - 16) // tiles
    picked = jnp.sum(lines_ref[:, tiles * rows :].astype(F32), axis=0)
    pieces = L // LANES
    row = [
        jnp.concatenate([picked[part * pieces + t : part * pieces + t + 1] for t in range(pieces)], axis=1)
        for part in range(2)
    ]
    row = jnp.concatenate(row + [jnp.zeros((14, L), F32)], axis=0).astype(BF)
    moved = pltpu.roll(reversed_lanes(row), L - (pulses - 1), 1)
    parts = []
    for part in range(2):
        spread = jnp.broadcast_to(moved[part : part + 1], (pulses, L))
        parts.append(pltpu.roll(spread, 0, 1, stride=1, stride_axis=0)[:, :pulses])
    for part, pair in enumerate(((parts[0], -parts[1]), (parts[1], parts[0]))):
        for target in range(2):
            for column in range(columns):
                columns_held[target * columns + column, pl.ds(part, pulses, stride=2), :] = pair[target][
                    :, column * LANES : (column + 1) * LANES
                ]
    for column in range(2 * columns):
        taps[:, column * LANES : (column + 1) * LANES] = columns_held[column].astype(BF)
    copies = []
    for tile in range(tiles):
        lines = lines_ref[:, tile * rows : (tile + 1) * rows].reshape(sources * rows, LANES)
        focused = lax.dot_general(lines, taps[...], (((0,), (0,)), ((), ())), preferred_element_type=F32)
        into = pl.ds(tile * each, each)
        for part in range(2):
            for column in range(columns):
                lane = part * pulses + column * LANES
                made[pl.ds(tile * each + 2 * column + part, LANES, stride=2 * columns), :] = focused[
                    :, lane : lane + LANES
                ]
        copies.append(pltpu.make_async_copy(made.at[into], out_ref.at[into], sems.at[tile]))
        copies[-1].start()
    for copy in copies:
        copy.wait()


def toeplitz(diagonal_taps, size):
    span_size = 2 * size - 1
    reversed_taps = diagonal_taps[..., ::-1]
    shifted = jnp.concatenate(
        [reversed_taps[..., size - 1 :], reversed_taps[..., : size - 1]], axis=-1
    )
    reps = (1,) * (shifted.ndim - 1) + (size,)
    tiled_flat = jnp.tile(shifted, reps)[..., : size * (span_size - 1)]
    return tiled_flat.reshape(shifted.shape[:-1] + (size, span_size - 1))[..., :size]


def tap_blocks(tap_values, size):
    block_total = tap_values.shape[1] // size + 1
    padded_taps = jnp.pad(tap_values, ((0, 0), (size, 2 * size)))
    matrices = []
    for offset_block in range(block_total):
        first_tap = offset_block * size + 1
        parts = toeplitz(padded_taps[:, first_tap : first_tap + 2 * size - 1], size)
        real_part = parts[0]
        imag_part = parts[1]
        matrices.append(
            jnp.stack([jnp.stack([real_part, -imag_part]), jnp.stack([imag_part, real_part])])
        )
    return jnp.stack(matrices)


def correlate(blocked, matrices, output_count):
    summed = jnp.zeros((blocked.shape[0], 2, output_count, blocked.shape[3]), F32)
    for offset_block in range(matrices.shape[0]):
        piece_rows = blocked[:, :, offset_block : offset_block + output_count, :]
        summed = summed + jnp.einsum(
            "rcib,cdbn->rdin", piece_rows, matrices[offset_block], preferred_element_type=F32
        )
    return summed


def focus_long(range_lines, reference_row):
    block_size = L // 2
    bin_count, _, total_pulses = range_lines.shape
    block_count = total_pulses // block_size
    blocked = range_lines.reshape(bin_count, 2, block_count, block_size)
    blocked = jnp.pad(blocked, ((0, 0), (0, 0), (1, 1), (0, 0)))
    focused = correlate(blocked, tap_blocks(reference_row, block_size), block_count)
    return focused.reshape(1, bin_count, 2, total_pulses)


def call(kernel, outs, specs, scratch=(), vmem=24, flops=1000):
    space = {"s": pltpu.SMEM, "v": pltpu.VMEM, "a": pl.ANY}
    blocks = [pl.BlockSpec(memory_space=space[kind]) for kind in specs]
    return pl.pallas_call(
        kernel,
        out_shape=outs,
        in_specs=blocks[: -len(outs)],
        out_specs=tuple(blocks[-len(outs) :]),
        scratch_shapes=list(scratch),
        compiler_params=pltpu.CompilerParams(vmem_limit_bytes=int(vmem * 2**20)),
        cost_estimate=pl.CostEstimate(flops=flops, bytes_accessed=1000, transcendentals=0),
    )


def on_device(raw_echo, chirp_replica, azimuth_refs, migration_index, window_start):
    pulses = raw_echo.shape[0]
    segment_devices = lax.axis_size("sa")
    pulse_devices = lax.axis_size("pa")
    tap_count = chirp_replica.shape[1]
    kept_width = R // segment_devices
    bin_count = kept_width // pulse_devices
    total_pulses = pulses * pulse_devices
    half = kept_width // LANES
    tap_tiles = tap_count // LANES + 2
    span = half + tap_tiles - 1

    rows = 2 * pulses
    shape = jax.ShapeDtypeStruct
    token = shape((8, LANES), F32)
    short = bin_count % LANES == 0 and total_pulses == L // 2

    targets = pulse_devices if short else half // 8
    slot = half // targets * rows

    far, turn = call(
        far_kernel,
        (shape((half, rows, LANES), BF), token),
        "avv",
        [pltpu.VMEM((pulses, 2, half * LANES), BF), pltpu.SemaphoreType.DMA((4,))],
        53,
    )(raw_echo)
    far = lax.ppermute(far, "sa", [(1, 3)])
    edge, turn = call(edge_kernel, (shape((half, rows, LANES), BF), token), "vvvv")(turn, raw_echo)
    edge = lax.ppermute(edge, "sa", [(0, 1), (2, 3)])
    taps, own_rows, turn = call(
        prep_kernel,
        (shape((tap_tiles * LANES, 2 * LANES), BF), shape((pulse_devices, 16, LANES), BF), token),
        "vsvvvvvv",
    )(turn, window_start, migration_index, chirp_replica, azimuth_refs)
    near, turn = call(
        ahead_kernel,
        (shape((targets, slot, LANES), BF), token),
        "vsvvvv",
        [pltpu.VMEM((span, rows, LANES), BF)],
    )(turn, window_start, raw_echo, taps)
    near = lax.ppermute(near, "sa", [(1, 2)])
    extra = own_rows if short else jnp.zeros((targets, 16, LANES), BF)
    made = shape((targets, slot + 16, LANES), BF)
    (early,) = call(
        early_kernel,
        (made,),
        "vsvvvvvv",
        [pltpu.VMEM((span + 16, rows, LANES), BF)],
        flops=10**10,
    )(turn, window_start, raw_echo, far, edge, taps, extra)
    (compressed,) = call(late_kernel, (made,), "vvvv")(near, extra, early)

    if not short:
        kept = compressed[:, :-16].reshape(half, pulses, 2, LANES).transpose(0, 3, 2, 1)
        outgoing = kept.reshape(pulse_devices, bin_count, 2, pulses)
        turned = lax.all_to_all(outgoing, "pa", split_axis=0, concat_axis=3, tiled=True)
        rows_in = lax.all_to_all(own_rows, "pa", split_axis=0, concat_axis=0, tiled=True)
        reference_row = jnp.sum(rows_in[:, :8].astype(F32), axis=0).astype(BF).reshape(2, L)
        return focus_long(turned[0], reference_row)

    lines = lax.all_to_all(compressed, "pa", split_axis=0, concat_axis=0, tiled=True)
    width = 2 * total_pulses
    (focused,) = call(
        azimuth_kernel,
        (shape((bin_count * width // LANES, LANES), F32),),
        "va",
        [
            pltpu.VMEM((width // LANES, width, LANES), F32),
            pltpu.VMEM((width, width), BF),
            pltpu.VMEM((bin_count * width // LANES, LANES), F32),
            pltpu.SemaphoreType.DMA((bin_count // LANES,)),
        ],
    )(lines)
    focused = focused.reshape(1, bin_count, total_pulses // LANES, 2, LANES).swapaxes(2, 3)
    return focused.reshape(1, bin_count, 2, total_pulses)


def solution(mesh):
    placed = (P("pa", None, "sa"), P(), P("pa", None, None), P(), P())
    return jax.shard_map(
        on_device, mesh=mesh, in_specs=placed, out_specs=P("sa", "pa", None, None), check_vma=False
    )
```

```python
import jax
import jax.numpy as jnp
from jax import lax
from jax.experimental import pallas as pl
from jax.experimental.pallas import tpu as pltpu
from jax.sharding import PartitionSpec as P

R = 16384
L = 512
LANES = 128
EXTRA = 8
BF = jnp.bfloat16
F32 = jnp.float32


def reversed_lanes(row):
    row_id = lax.broadcasted_iota(jnp.int32, (LANES, LANES), 0)
    col_id = lax.broadcasted_iota(jnp.int32, (LANES, LANES), 1)
    flip = (row_id + col_id == LANES - 1).astype(BF)
    tiles = row.shape[1] // LANES
    pieces = [row[:, t * LANES : (t + 1) * LANES] for t in reversed(range(tiles))]
    return jnp.concatenate([jnp.dot(piece, flip, preferred_element_type=F32) for piece in pieces], axis=1)


def retile(source, target, first, tiles):
    shape = target.shape[1:]
    for t in range(tiles):
        target[first + t] = source[:, :, t * LANES : (t + 1) * LANES].reshape(shape)


def tail_kernel(raw_ref, tail_ref, turn_ref, natural, sems):
    turn_ref[...] = jnp.zeros_like(turn_ref)
    half, rows, _ = tail_ref.shape
    pieces = sems.shape[0]
    each = rows // 2 // pieces
    width = half * LANES

    @pl.when(lax.axis_index("sa") < 2)
    def _():
        copies = []
        for at in range(pieces):
            own = pl.ds(at * each, each)
            source = raw_ref.at[own, :, pl.ds(raw_ref.shape[2] - width, width)]
            copies.append(pltpu.make_async_copy(source, natural.at[own], sems.at[at]))
            copies[-1].start()
        for at, copy in enumerate(copies):
            copy.wait()
            own = pl.ds(at * each, each)
            retile(natural.at[own], tail_ref.at[:, pl.ds(at * each * 2, each * 2)], 0, half)


def head_kernel(turn_in_ref, raw_ref, head_ref, turn_ref):
    turn_ref[...] = turn_in_ref[...]

    @pl.when(lax.axis_index("sa") == 2)
    def _():
        retile(raw_ref, head_ref, 0, head_ref.shape[0])


def prep_kernel(turn_in_ref, window_ref, index_ref, chirp_ref, refs_ref, taps_ref, rows_ref, turn_ref):
    turn_ref[...] = turn_in_ref[...]
    taps = chirp_ref.shape[1]
    blocks = taps_ref.shape[0] // LANES
    width = blocks * LANES
    shift = lax.rem(window_ref[0], LANES)
    chirp = jnp.concatenate([chirp_ref[...], jnp.zeros((14, taps), BF)], axis=0)
    flipped = reversed_lanes(chirp)
    padded = jnp.concatenate([jnp.zeros((16, 2 * LANES), F32), flipped], axis=1)
    padded = jnp.concatenate([padded, jnp.zeros((16, width + LANES - padded.shape[1]), F32)], axis=1)
    moved = pltpu.roll(padded, width + LANES - 127 - shift, 1)[:, :width]
    for part in range(2):
        spread = jnp.broadcast_to(moved[part : part + 1], (LANES, width))
        skewed = pltpu.roll(spread, 0, 1, stride=1, stride_axis=0)
        for t in range(blocks):
            first = LANES * (blocks - 1 - t)
            taps_ref[t * LANES : (t + 1) * LANES, part * LANES : (part + 1) * LANES] = skewed[
                :, first : first + LANES
            ].astype(BF)
    own = refs_ref.shape[0]
    groups, targets = index_ref.shape
    first_row = lax.axis_index("pa") * own
    mine = lax.broadcasted_iota(jnp.int32, (groups, targets), 0) == lax.axis_index("sa")
    wanted = jnp.sum(jnp.where(mine, index_ref[...], 0), axis=0, keepdims=True)
    row_id = lax.broadcasted_iota(jnp.int32, (own, targets), 0) + first_row
    picks = (row_id == jnp.broadcast_to(wanted, (own, targets))).astype(F32)
    pieces = []
    for part in range(2):
        picked = lax.dot_general(
            picks, refs_ref[:, part, :].astype(F32), (((0,), (0,)), ((), ())), preferred_element_type=F32
        )
        pieces += [picked[:, t * LANES : (t + 1) * LANES] for t in range(L // LANES)]
    pieces += [jnp.zeros((targets, LANES), F32)] * (rows_ref.shape[1] - len(pieces))
    rows_ref[...] = jnp.stack(pieces, axis=1).astype(BF)


def compress(held, base, taps_ref, out_ref):
    rows = held.shape[1]
    targets = out_ref.shape[0]
    tap_tiles = taps_ref.shape[0] // LANES
    group = 8
    per_target = out_ref.shape[1] // rows
    even = lax.rem(lax.broadcasted_iota(jnp.int32, (1, 8, LANES), 1), 2) == 0
    for step in range(targets * per_target // group):
        blocks = [
            held[pl.ds(base + group * step + t, group)].reshape(group * rows, LANES) for t in range(tap_tiles)
        ]
        product = jnp.dot(jnp.concatenate(blocks, axis=1), taps_ref[...], preferred_element_type=F32)
        straight = product[:, :LANES].reshape(-1, 8, LANES)
        crossed = product[:, LANES:].reshape(-1, 8, LANES)
        total = straight + jnp.where(even, pltpu.roll(crossed, 7, 1), -pltpu.roll(crossed, 1, 1))
        count = group // per_target
        out_ref[pl.ds(step * count, count), : per_target * rows] = total.astype(BF).reshape(
            count, per_target * rows, LANES
        )


def ahead_kernel(turn_in_ref, window_ref, raw_ref, taps_ref, out_ref, turn_ref, held):
    turn_ref[...] = turn_in_ref[...]
    span = held.shape[0]

    @pl.when(lax.axis_index("sa") == 1)
    def _():
        start = pl.multiple_of(window_ref[0] // LANES * LANES, LANES)
        retile(raw_ref.at[:, :, pl.ds(start, span * LANES)], held, 0, span)
        compress(held, 0, taps_ref, out_ref)


def early_kernel(turn_in_ref, window_ref, raw_ref, tail_ref, head_ref, taps_ref, rows_ref, out_ref, held):
    half = tail_ref.shape[0]
    more = head_ref.shape[0]
    span = half + more - 16
    sub_index = lax.axis_index("sa")
    offset = window_ref[0] // LANES

    @pl.when(sub_index == 0)
    def _():
        start = pl.multiple_of(offset * LANES, LANES)
        retile(raw_ref.at[:, :, pl.ds(start, span * LANES)], held, 0, span)

    @pl.when(sub_index == 1)
    def _():
        held[:half] = tail_ref[...]
        retile(raw_ref, held, half, more)

    @pl.when(sub_index == 3)
    def _():
        held[:half] = tail_ref[...]
        held[half:] = head_ref[...]

    @pl.when(sub_index != 2)
    def _():
        compress(held, jnp.where(sub_index == 0, 0, offset), taps_ref, out_ref)
        out_ref[:, out_ref.shape[1] - rows_ref.shape[1] :] = rows_ref[...]


def late_kernel(near_ref, rows_ref, early_ref, out_ref):
    bins = near_ref.shape[1]
    sub_index = lax.axis_index("sa")

    @pl.when(sub_index != 2)
    def _():
        out_ref[...] = early_ref[...]

    @pl.when(sub_index == 2)
    def _():
        out_ref[:, :bins] = near_ref[...]
        out_ref[:, bins:] = rows_ref[...]


def azimuth_kernel(lines_ref, out_ref, columns_held, taps, made, sems):
    pulses = taps.shape[0] // 2
    columns = pulses // LANES
    tiles = sems.shape[0]
    each = out_ref.shape[0] // tiles
    sources = lines_ref.shape[0]
    rows = (lines_ref.shape[1] - EXTRA) // tiles
    picked = jnp.sum(lines_ref[:, tiles * rows :].astype(F32), axis=0)
    pieces = L // LANES
    row = [
        jnp.concatenate([picked[part * pieces + t : part * pieces + t + 1] for t in range(pieces)], axis=1)
        for part in range(2)
    ]
    row = jnp.concatenate(row + [jnp.zeros((14, L), F32)], axis=0).astype(BF)
    moved = pltpu.roll(reversed_lanes(row), L - (pulses - 1), 1)
    parts = []
    for part in range(2):
        spread = jnp.broadcast_to(moved[part : part + 1], (pulses, L))
        parts.append(pltpu.roll(spread, 0, 1, stride=1, stride_axis=0)[:, :pulses])
    for part, pair in enumerate(((parts[0], -parts[1]), (parts[1], parts[0]))):
        for target in range(2):
            for column in range(columns):
                columns_held[target * columns + column, pl.ds(part, pulses, stride=2), :] = pair[target][
                    :, column * LANES : (column + 1) * LANES
                ]
    for column in range(2 * columns):
        taps[:, column * LANES : (column + 1) * LANES] = columns_held[column].astype(BF)
    copies = []
    for tile in range(tiles):
        lines = lines_ref[:, tile * rows : (tile + 1) * rows].reshape(sources * rows, LANES)
        focused = lax.dot_general(lines, taps[...], (((0,), (0,)), ((), ())), preferred_element_type=F32)
        into = pl.ds(tile * each, each)
        for part in range(2):
            for column in range(columns):
                lane = part * pulses + column * LANES
                made[pl.ds(tile * each + 2 * column + part, LANES, stride=2 * columns), :] = focused[
                    :, lane : lane + LANES
                ]
        copies.append(pltpu.make_async_copy(made.at[into], out_ref.at[into], sems.at[tile]))
        copies[-1].start()
    for copy in copies:
        copy.wait()


def toeplitz(diagonal_taps, size):
    span_size = 2 * size - 1
    reversed_taps = diagonal_taps[..., ::-1]
    shifted = jnp.concatenate(
        [reversed_taps[..., size - 1 :], reversed_taps[..., : size - 1]], axis=-1
    )
    reps = (1,) * (shifted.ndim - 1) + (size,)
    tiled_flat = jnp.tile(shifted, reps)[..., : size * (span_size - 1)]
    return tiled_flat.reshape(shifted.shape[:-1] + (size, span_size - 1))[..., :size]


def tap_blocks(tap_values, size):
    block_total = tap_values.shape[1] // size + 1
    padded_taps = jnp.pad(tap_values, ((0, 0), (size, 2 * size)))
    matrices = []
    for offset_block in range(block_total):
        first_tap = offset_block * size + 1
        parts = toeplitz(padded_taps[:, first_tap : first_tap + 2 * size - 1], size)
        real_part = parts[0]
        imag_part = parts[1]
        matrices.append(
            jnp.stack([jnp.stack([real_part, -imag_part]), jnp.stack([imag_part, real_part])])
        )
    return jnp.stack(matrices)


def correlate(blocked, matrices, output_count):
    summed = jnp.zeros((blocked.shape[0], 2, output_count, blocked.shape[3]), F32)
    for offset_block in range(matrices.shape[0]):
        piece_rows = blocked[:, :, offset_block : offset_block + output_count, :]
        summed = summed + jnp.einsum(
            "rcib,cdbn->rdin", piece_rows, matrices[offset_block], preferred_element_type=F32
        )
    return summed


def focus_long(range_lines, reference_row):
    block_size = L // 2
    bin_count, _, total_pulses = range_lines.shape
    block_count = total_pulses // block_size
    blocked = range_lines.reshape(bin_count, 2, block_count, block_size)
    blocked = jnp.pad(blocked, ((0, 0), (0, 0), (1, 1), (0, 0)))
    focused = correlate(blocked, tap_blocks(reference_row, block_size), block_count)
    return focused.reshape(1, bin_count, 2, total_pulses)


def call(kernel, outs, specs, scratch=(), vmem=24, flops=1000):
    space = {"s": pltpu.SMEM, "v": pltpu.VMEM, "a": pl.ANY}
    blocks = [pl.BlockSpec(memory_space=space[kind]) for kind in specs]
    return pl.pallas_call(
        kernel,
        out_shape=outs,
        in_specs=blocks[: -len(outs)],
        out_specs=tuple(blocks[-len(outs) :]),
        scratch_shapes=list(scratch),
        compiler_params=pltpu.CompilerParams(vmem_limit_bytes=int(vmem * 2**20)),
        cost_estimate=pl.CostEstimate(flops=flops, bytes_accessed=1000, transcendentals=0),
    )


def on_device(raw_echo, chirp_replica, azimuth_refs, migration_index, window_start):
    pulses = raw_echo.shape[0]
    segment_devices = lax.axis_size("sa")
    pulse_devices = lax.axis_size("pa")
    tap_count = chirp_replica.shape[1]
    kept_width = R // segment_devices
    bin_count = kept_width // pulse_devices
    total_pulses = pulses * pulse_devices
    half = kept_width // LANES
    tap_tiles = tap_count // LANES + 2
    span = half + tap_tiles - 1

    rows = 2 * pulses
    shape = jax.ShapeDtypeStruct
    token = shape((8, LANES), F32)
    short = bin_count % LANES == 0 and total_pulses == L // 2

    targets = pulse_devices if short else half // 8
    slot = half // targets * rows

    tail, turn = call(
        tail_kernel,
        (shape((half, rows, LANES), BF), token),
        "avv",
        [pltpu.VMEM((pulses, 2, half * LANES), BF), pltpu.SemaphoreType.DMA((4,))],
        53,
    )(raw_echo)
    tail = lax.ppermute(tail, "sa", [(0, 1), (1, 3)])
    head, turn = call(head_kernel, (shape((span - half + 16, rows, LANES), BF), token), "vvvv")(turn, raw_echo)
    head = lax.ppermute(head, "sa", [(2, 3)])
    taps, own_rows, turn = call(
        prep_kernel,
        (shape((tap_tiles * LANES, 2 * LANES), BF), shape((pulse_devices, EXTRA, LANES), BF), token),
        "vsvvvvvv",
    )(turn, window_start, migration_index, chirp_replica, azimuth_refs)
    near, turn = call(
        ahead_kernel,
        (shape((targets, slot, LANES), BF), token),
        "vsvvvv",
        [pltpu.VMEM((span, rows, LANES), BF)],
    )(turn, window_start, raw_echo, taps)
    near = lax.ppermute(near, "sa", [(1, 2)])
    extra = own_rows if short else jnp.zeros((targets, EXTRA, LANES), BF)
    made = shape((targets, slot + EXTRA, LANES), BF)
    (early,) = call(
        early_kernel,
        (made,),
        "vsvvvvvv",
        [pltpu.VMEM((span + 16, rows, LANES), BF)],
        flops=10**10,
    )(turn, window_start, raw_echo, tail, head, taps, extra)
    (compressed,) = call(late_kernel, (made,), "vvvv")(near, extra, early)

    if not short:
        kept = compressed[:, :-EXTRA].reshape(half, pulses, 2, LANES).transpose(0, 3, 2, 1)
        outgoing = kept.reshape(pulse_devices, bin_count, 2, pulses)
        turned = lax.all_to_all(outgoing, "pa", split_axis=0, concat_axis=3, tiled=True)
        rows_in = lax.all_to_all(own_rows, "pa", split_axis=0, concat_axis=0, tiled=True)
        reference_row = jnp.sum(rows_in[:, :8].astype(F32), axis=0).astype(BF).reshape(2, L)
        return focus_long(turned[0], reference_row)

    lines = lax.all_to_all(compressed, "pa", split_axis=0, concat_axis=0, tiled=True)
    width = 2 * total_pulses
    (focused,) = call(
        azimuth_kernel,
        (shape((bin_count * width // LANES, LANES), F32),),
        "va",
        [
            pltpu.VMEM((width // LANES, width, LANES), F32),
            pltpu.VMEM((width, width), BF),
            pltpu.VMEM((bin_count * width // LANES, LANES), F32),
            pltpu.SemaphoreType.DMA((bin_count // LANES,)),
        ],
    )(lines)
    focused = focused.reshape(1, bin_count, total_pulses // LANES, 2, LANES).swapaxes(2, 3)
    return focused.reshape(1, bin_count, 2, total_pulses)


def solution(mesh):
    placed = (P("pa", None, "sa"), P(), P("pa", None, None), P(), P())
    return jax.shard_map(
        on_device, mesh=mesh, in_specs=placed, out_specs=P("sa", "pa", None, None), check_vma=False
    )
```

```python
import jax
import jax.numpy as jnp
from jax import lax
from jax.experimental import pallas as pl
from jax.experimental.pallas import tpu as pltpu
from jax.sharding import PartitionSpec as P

R = 16384
L = 512
LANES = 128
EXTRA = 8
BF = jnp.bfloat16
F32 = jnp.float32


def reversed_lanes(row):
    row_id = lax.broadcasted_iota(jnp.int32, (LANES, LANES), 0)
    col_id = lax.broadcasted_iota(jnp.int32, (LANES, LANES), 1)
    flip = (row_id + col_id == LANES - 1).astype(BF)
    tiles = row.shape[1] // LANES
    pieces = [row[:, t * LANES : (t + 1) * LANES] for t in reversed(range(tiles))]
    return jnp.concatenate([jnp.dot(piece, flip, preferred_element_type=F32) for piece in pieces], axis=1)


def retile(source, target, first, tiles):
    shape = target.shape[1:]
    for t in range(tiles):
        target[first + t] = source[:, :, t * LANES : (t + 1) * LANES].reshape(shape)


def tail_kernel(raw_ref, tail_ref, turn_ref, natural, sems):
    turn_ref[...] = jnp.zeros_like(turn_ref)
    half, rows, _ = tail_ref.shape
    pieces = sems.shape[0]
    each = rows // 2 // pieces
    width = half * LANES

    @pl.when(lax.axis_index("sa") < 2)
    def _():
        copies = []
        for at in range(pieces):
            own = pl.ds(at * each, each)
            source = raw_ref.at[own, :, pl.ds(raw_ref.shape[2] - width, width)]
            copies.append(pltpu.make_async_copy(source, natural.at[own], sems.at[at]))
            copies[-1].start()
        for at, copy in enumerate(copies):
            copy.wait()
            own = pl.ds(at * each, each)
            retile(natural.at[own], tail_ref.at[:, pl.ds(at * each * 2, each * 2)], 0, half)


def head_kernel(turn_in_ref, raw_ref, head_ref, turn_ref):
    turn_ref[...] = turn_in_ref[...]

    @pl.when(lax.axis_index("sa") == 2)
    def _():
        retile(raw_ref, head_ref, 0, head_ref.shape[0])


def prep_kernel(turn_in_ref, window_ref, index_ref, chirp_ref, refs_ref, taps_ref, rows_ref, turn_ref):
    turn_ref[...] = turn_in_ref[...]
    taps = chirp_ref.shape[1]
    blocks = taps_ref.shape[0] // LANES
    width = blocks * LANES
    shift = lax.rem(window_ref[0], LANES)
    chirp = jnp.concatenate([chirp_ref[...], jnp.zeros((14, taps), BF)], axis=0)
    flipped = reversed_lanes(chirp)
    padded = jnp.concatenate([jnp.zeros((16, 2 * LANES), F32), flipped], axis=1)
    padded = jnp.concatenate([padded, jnp.zeros((16, width + LANES - padded.shape[1]), F32)], axis=1)
    moved = pltpu.roll(padded, width + LANES - 127 - shift, 1)[:, :width]
    for part in range(2):
        spread = jnp.broadcast_to(moved[part : part + 1], (LANES, width))
        skewed = pltpu.roll(spread, 0, 1, stride=1, stride_axis=0)
        for t in range(blocks):
            first = LANES * (blocks - 1 - t)
            taps_ref[t * LANES : (t + 1) * LANES, part * LANES : (part + 1) * LANES] = skewed[
                :, first : first + LANES
            ].astype(BF)
    own = refs_ref.shape[0]
    groups, targets = index_ref.shape
    first_row = lax.axis_index("pa") * own
    mine = lax.broadcasted_iota(jnp.int32, (groups, targets), 0) == lax.axis_index("sa")
    wanted = jnp.sum(jnp.where(mine, index_ref[...], 0), axis=0, keepdims=True)
    row_id = lax.broadcasted_iota(jnp.int32, (own, targets), 0) + first_row
    picks = (row_id == jnp.broadcast_to(wanted, (own, targets))).astype(F32)
    pieces = []
    for part in range(2):
        picked = lax.dot_general(
            picks, refs_ref[:, part, :].astype(F32), (((0,), (0,)), ((), ())), preferred_element_type=F32
        )
        pieces += [picked[:, t * LANES : (t + 1) * LANES] for t in range(L // LANES)]
    pieces += [jnp.zeros((targets, LANES), F32)] * (rows_ref.shape[1] - len(pieces))
    rows_ref[...] = jnp.stack(pieces, axis=1).astype(BF)


def compress(held, base, taps_ref, out_ref):
    rows = held.shape[1]
    targets = out_ref.shape[0]
    tap_tiles = taps_ref.shape[0] // LANES
    group = 8
    per_target = out_ref.shape[1] // rows
    even = lax.rem(lax.broadcasted_iota(jnp.int32, (1, 8, LANES), 1), 2) == 0
    for step in range(targets * per_target // group):
        blocks = [
            held[pl.ds(base + group * step + t, group)].reshape(group * rows, LANES) for t in range(tap_tiles)
        ]
        product = jnp.dot(jnp.concatenate(blocks, axis=1), taps_ref[...], preferred_element_type=F32)
        straight = product[:, :LANES].reshape(-1, 8, LANES)
        crossed = product[:, LANES:].reshape(-1, 8, LANES)
        total = straight + jnp.where(even, pltpu.roll(crossed, 7, 1), -pltpu.roll(crossed, 1, 1))
        count = group // per_target
        out_ref[pl.ds(step * count, count), : per_target * rows] = total.astype(BF).reshape(
            count, per_target * rows, LANES
        )


def ahead_kernel(turn_in_ref, window_ref, raw_ref, taps_ref, out_ref, turn_ref, held):
    turn_ref[...] = turn_in_ref[...]
    span = held.shape[0]

    @pl.when(lax.axis_index("sa") == 1)
    def _():
        start = pl.multiple_of(window_ref[0] // LANES * LANES, LANES)
        retile(raw_ref.at[:, :, pl.ds(start, span * LANES)], held, 0, span)
        compress(held, 0, taps_ref, out_ref)


def early_kernel(turn_in_ref, window_ref, raw_ref, tail_ref, head_ref, taps_ref, rows_ref, out_ref, held):
    half = tail_ref.shape[0]
    more = head_ref.shape[0]
    span = half + more - 16
    sub_index = lax.axis_index("sa")
    offset = window_ref[0] // LANES

    @pl.when(sub_index == 0)
    def _():
        start = pl.multiple_of(offset * LANES, LANES)
        retile(raw_ref.at[:, :, pl.ds(start, span * LANES)], held, 0, span)

    @pl.when(sub_index == 1)
    def _():
        held[:half] = tail_ref[...]
        retile(raw_ref, held, half, more)

    @pl.when(sub_index == 3)
    def _():
        held[:half] = tail_ref[...]
        held[half:] = head_ref[...]

    @pl.when(sub_index != 2)
    def _():
        compress(held, jnp.where(sub_index == 0, 0, offset), taps_ref, out_ref)
        out_ref[:, out_ref.shape[1] - rows_ref.shape[1] :] = rows_ref[...]


def late_kernel(near_ref, rows_ref, early_ref, out_ref):
    bins = near_ref.shape[1]
    sub_index = lax.axis_index("sa")

    @pl.when(sub_index != 2)
    def _():
        out_ref[...] = early_ref[...]

    @pl.when(sub_index == 2)
    def _():
        out_ref[:, :bins] = near_ref[...]
        out_ref[:, bins:] = rows_ref[...]


def azimuth_kernel(lines_ref, out_ref, columns_held, taps, made, sems):
    pulses = taps.shape[0] // 2
    columns = pulses // LANES
    pieces_out = sems.shape[0]
    each = out_ref.shape[0] // pieces_out
    tiles = out_ref.shape[0] // (2 * columns * LANES)
    sources = lines_ref.shape[0]
    rows = (lines_ref.shape[1] - EXTRA) // tiles
    picked = jnp.sum(lines_ref[:, tiles * rows :].astype(F32), axis=0)
    pieces = L // LANES
    row = [
        jnp.concatenate([picked[part * pieces + t : part * pieces + t + 1] for t in range(pieces)], axis=1)
        for part in range(2)
    ]
    row = jnp.concatenate(row + [jnp.zeros((14, L), F32)], axis=0).astype(BF)
    moved = pltpu.roll(reversed_lanes(row), L - (pulses - 1), 1)
    parts = []
    for part in range(2):
        spread = jnp.broadcast_to(moved[part : part + 1], (pulses, L))
        parts.append(pltpu.roll(spread, 0, 1, stride=1, stride_axis=0)[:, :pulses])
    for part, pair in enumerate(((parts[0], -parts[1]), (parts[1], parts[0]))):
        for target in range(2):
            for column in range(columns):
                columns_held[target * columns + column, pl.ds(part, pulses, stride=2), :] = pair[target][
                    :, column * LANES : (column + 1) * LANES
                ]
    for column in range(2 * columns):
        taps[:, column * LANES : (column + 1) * LANES] = columns_held[column].astype(BF)
    lines = [
        lines_ref[:, tile * rows : (tile + 1) * rows].reshape(sources * rows, LANES) for tile in range(tiles)
    ]
    focused = lax.dot_general(
        jnp.concatenate(lines, axis=1), taps[...], (((0,), (0,)), ((), ())), preferred_element_type=F32
    )
    copies = []
    bins = each // (2 * columns)
    for piece in range(pieces_out):
        into = pl.ds(piece * each, each)
        for part in range(2):
            for column in range(columns):
                lane = part * pulses + column * LANES
                made[pl.ds(piece * each + 2 * column + part, bins, stride=2 * columns), :] = focused[
                    piece * bins : (piece + 1) * bins, lane : lane + LANES
                ]
        copies.append(pltpu.make_async_copy(made.at[into], out_ref.at[into], sems.at[piece]))
        copies[-1].start()
    for copy in copies:
        copy.wait()


def toeplitz(diagonal_taps, size):
    span_size = 2 * size - 1
    reversed_taps = diagonal_taps[..., ::-1]
    shifted = jnp.concatenate(
        [reversed_taps[..., size - 1 :], reversed_taps[..., : size - 1]], axis=-1
    )
    reps = (1,) * (shifted.ndim - 1) + (size,)
    tiled_flat = jnp.tile(shifted, reps)[..., : size * (span_size - 1)]
    return tiled_flat.reshape(shifted.shape[:-1] + (size, span_size - 1))[..., :size]


def tap_blocks(tap_values, size):
    block_total = tap_values.shape[1] // size + 1
    padded_taps = jnp.pad(tap_values, ((0, 0), (size, 2 * size)))
    matrices = []
    for offset_block in range(block_total):
        first_tap = offset_block * size + 1
        parts = toeplitz(padded_taps[:, first_tap : first_tap + 2 * size - 1], size)
        real_part = parts[0]
        imag_part = parts[1]
        matrices.append(
            jnp.stack([jnp.stack([real_part, -imag_part]), jnp.stack([imag_part, real_part])])
        )
    return jnp.stack(matrices)


def correlate(blocked, matrices, output_count):
    summed = jnp.zeros((blocked.shape[0], 2, output_count, blocked.shape[3]), F32)
    for offset_block in range(matrices.shape[0]):
        piece_rows = blocked[:, :, offset_block : offset_block + output_count, :]
        summed = summed + jnp.einsum(
            "rcib,cdbn->rdin", piece_rows, matrices[offset_block], preferred_element_type=F32
        )
    return summed


def focus_long(range_lines, reference_row):
    block_size = L // 2
    bin_count, _, total_pulses = range_lines.shape
    block_count = total_pulses // block_size
    blocked = range_lines.reshape(bin_count, 2, block_count, block_size)
    blocked = jnp.pad(blocked, ((0, 0), (0, 0), (1, 1), (0, 0)))
    focused = correlate(blocked, tap_blocks(reference_row, block_size), block_count)
    return focused.reshape(1, bin_count, 2, total_pulses)


def call(kernel, outs, specs, scratch=(), vmem=24, flops=1000):
    space = {"s": pltpu.SMEM, "v": pltpu.VMEM, "a": pl.ANY}
    blocks = [pl.BlockSpec(memory_space=space[kind]) for kind in specs]
    return pl.pallas_call(
        kernel,
        out_shape=outs,
        in_specs=blocks[: -len(outs)],
        out_specs=tuple(blocks[-len(outs) :]),
        scratch_shapes=list(scratch),
        compiler_params=pltpu.CompilerParams(vmem_limit_bytes=int(vmem * 2**20)),
        cost_estimate=pl.CostEstimate(flops=flops, bytes_accessed=1000, transcendentals=0),
    )


def on_device(raw_echo, chirp_replica, azimuth_refs, migration_index, window_start):
    pulses = raw_echo.shape[0]
    segment_devices = lax.axis_size("sa")
    pulse_devices = lax.axis_size("pa")
    tap_count = chirp_replica.shape[1]
    kept_width = R // segment_devices
    bin_count = kept_width // pulse_devices
    total_pulses = pulses * pulse_devices
    half = kept_width // LANES
    tap_tiles = tap_count // LANES + 2
    span = half + tap_tiles - 1

    rows = 2 * pulses
    shape = jax.ShapeDtypeStruct
    token = shape((8, LANES), F32)
    short = bin_count % LANES == 0 and total_pulses == L // 2

    targets = pulse_devices if short else half // 8
    slot = half // targets * rows

    tail, turn = call(
        tail_kernel,
        (shape((half, rows, LANES), BF), token),
        "avv",
        [pltpu.VMEM((pulses, 2, half * LANES), BF), pltpu.SemaphoreType.DMA((4,))],
        53,
    )(raw_echo)
    tail = lax.ppermute(tail, "sa", [(0, 1), (1, 3)])
    head, turn = call(head_kernel, (shape((span - half + 16, rows, LANES), BF), token), "vvvv")(turn, raw_echo)
    head = lax.ppermute(head, "sa", [(2, 3)])
    taps, own_rows, turn = call(
        prep_kernel,
        (shape((tap_tiles * LANES, 2 * LANES), BF), shape((pulse_devices, EXTRA, LANES), BF), token),
        "vsvvvvvv",
    )(turn, window_start, migration_index, chirp_replica, azimuth_refs)
    near, turn = call(
        ahead_kernel,
        (shape((targets, slot, LANES), BF), token),
        "vsvvvv",
        [pltpu.VMEM((span, rows, LANES), BF)],
    )(turn, window_start, raw_echo, taps)
    near = lax.ppermute(near, "sa", [(1, 2)])
    extra = own_rows if short else jnp.zeros((targets, EXTRA, LANES), BF)
    made = shape((targets, slot + EXTRA, LANES), BF)
    (early,) = call(
        early_kernel,
        (made,),
        "vsvvvvvv",
        [pltpu.VMEM((span + 16, rows, LANES), BF)],
        flops=10**10,
    )(turn, window_start, raw_echo, tail, head, taps, extra)
    (compressed,) = call(late_kernel, (made,), "vvvv")(near, extra, early)

    if not short:
        kept = compressed[:, :-EXTRA].reshape(half, pulses, 2, LANES).transpose(0, 3, 2, 1)
        outgoing = kept.reshape(pulse_devices, bin_count, 2, pulses)
        turned = lax.all_to_all(outgoing, "pa", split_axis=0, concat_axis=3, tiled=True)
        rows_in = lax.all_to_all(own_rows, "pa", split_axis=0, concat_axis=0, tiled=True)
        reference_row = jnp.sum(rows_in[:, :8].astype(F32), axis=0).astype(BF).reshape(2, L)
        return focus_long(turned[0], reference_row)

    lines = lax.all_to_all(compressed, "pa", split_axis=0, concat_axis=0, tiled=True)
    width = 2 * total_pulses
    (focused,) = call(
        azimuth_kernel,
        (shape((bin_count * width // LANES, LANES), F32),),
        "va",
        [
            pltpu.VMEM((width // LANES, width, LANES), F32),
            pltpu.VMEM((width, width), BF),
            pltpu.VMEM((bin_count * width // LANES, LANES), F32),
            pltpu.SemaphoreType.DMA((2 * bin_count // LANES,)),
        ],
    )(lines)
    focused = focused.reshape(1, bin_count, total_pulses // LANES, 2, LANES).swapaxes(2, 3)
    return focused.reshape(1, bin_count, 2, total_pulses)


def solution(mesh):
    placed = (P("pa", None, "sa"), P(), P("pa", None, None), P(), P())
    return jax.shard_map(
        on_device, mesh=mesh, in_specs=placed, out_specs=P("sa", "pa", None, None), check_vma=False
    )
```

```python
import jax
import jax.numpy as jnp
from jax import lax
from jax.experimental import pallas as pl
from jax.experimental.pallas import tpu as pltpu
from jax.sharding import PartitionSpec as P

R = 16384
L = 512
LANES = 128
EXTRA = 8
BF = jnp.bfloat16
F32 = jnp.float32


def reversed_lanes(row):
    row_id = lax.broadcasted_iota(jnp.int32, (LANES, LANES), 0)
    col_id = lax.broadcasted_iota(jnp.int32, (LANES, LANES), 1)
    flip = (row_id + col_id == LANES - 1).astype(BF)
    tiles = row.shape[1] // LANES
    pieces = [row[:, t * LANES : (t + 1) * LANES] for t in reversed(range(tiles))]
    return jnp.concatenate([jnp.dot(piece, flip, preferred_element_type=F32) for piece in pieces], axis=1)


def retile(source, target, first, tiles):
    shape = target.shape[1:]
    for t in range(tiles):
        target[first + t] = source[:, :, t * LANES : (t + 1) * LANES].reshape(shape)


def tail_kernel(raw_ref, tail_ref, turn_ref, natural, sems):
    turn_ref[...] = jnp.zeros_like(turn_ref)
    half, rows, _ = tail_ref.shape
    pieces = sems.shape[0]
    each = rows // 2 // pieces
    width = half * LANES

    @pl.when(lax.axis_index("sa") < 2)
    def _():
        copies = []
        for at in range(pieces):
            own = pl.ds(at * each, each)
            source = raw_ref.at[own, :, pl.ds(raw_ref.shape[2] - width, width)]
            copies.append(pltpu.make_async_copy(source, natural.at[own], sems.at[at]))
            copies[-1].start()
        for at, copy in enumerate(copies):
            copy.wait()
            own = pl.ds(at * each, each)
            retile(natural.at[own], tail_ref.at[:, pl.ds(at * each * 2, each * 2)], 0, half)


def head_kernel(turn_in_ref, raw_ref, head_ref, turn_ref):
    turn_ref[...] = turn_in_ref[...]

    @pl.when(lax.axis_index("sa") == 2)
    def _():
        retile(raw_ref, head_ref, 0, head_ref.shape[0])


def prep_kernel(turn_in_ref, window_ref, index_ref, chirp_ref, refs_ref, taps_ref, rows_ref, turn_ref):
    turn_ref[...] = turn_in_ref[...]
    taps = chirp_ref.shape[1]
    blocks = taps_ref.shape[0] // LANES
    width = blocks * LANES
    shift = lax.rem(window_ref[0], LANES)
    chirp = jnp.concatenate([chirp_ref[...], jnp.zeros((14, taps), BF)], axis=0)
    flipped = reversed_lanes(chirp)
    padded = jnp.concatenate([jnp.zeros((16, 2 * LANES), F32), flipped], axis=1)
    padded = jnp.concatenate([padded, jnp.zeros((16, width + LANES - padded.shape[1]), F32)], axis=1)
    moved = pltpu.roll(padded, width + LANES - 127 - shift, 1)[:, :width]
    for part in range(2):
        spread = jnp.broadcast_to(moved[part : part + 1], (LANES, width))
        skewed = pltpu.roll(spread, 0, 1, stride=1, stride_axis=0)
        for t in range(blocks):
            first = LANES * (blocks - 1 - t)
            taps_ref[t * LANES : (t + 1) * LANES, part * LANES : (part + 1) * LANES] = skewed[
                :, first : first + LANES
            ].astype(BF)
    own = refs_ref.shape[0]
    groups, targets = index_ref.shape
    first_row = lax.axis_index("pa") * own
    mine = lax.broadcasted_iota(jnp.int32, (groups, targets), 0) == lax.axis_index("sa")
    wanted = jnp.sum(jnp.where(mine, index_ref[...], 0), axis=0, keepdims=True)
    row_id = lax.broadcasted_iota(jnp.int32, (own, targets), 0) + first_row
    picks = (row_id == jnp.broadcast_to(wanted, (own, targets))).astype(F32)
    pieces = []
    for part in range(2):
        picked = lax.dot_general(
            picks, refs_ref[:, part, :].astype(F32), (((0,), (0,)), ((), ())), preferred_element_type=F32
        )
        picked = reversed_lanes(picked.astype(BF))
        pieces += [picked[:, t * LANES : (t + 1) * LANES] for t in range(L // LANES)]
    pieces += [jnp.zeros((targets, LANES), F32)] * (rows_ref.shape[1] - len(pieces))
    rows_ref[...] = jnp.stack(pieces, axis=1).astype(BF)


def compress(held, base, taps_ref, out_ref):
    rows = held.shape[1]
    targets = out_ref.shape[0]
    tap_tiles = taps_ref.shape[0] // LANES
    group = 8
    per_target = out_ref.shape[1] // rows
    even = lax.rem(lax.broadcasted_iota(jnp.int32, (1, 8, LANES), 1), 2) == 0
    for step in range(targets * per_target // group):
        blocks = [
            held[pl.ds(base + group * step + t, group)].reshape(group * rows, LANES) for t in range(tap_tiles)
        ]
        product = jnp.dot(jnp.concatenate(blocks, axis=1), taps_ref[...], preferred_element_type=F32)
        straight = product[:, :LANES].reshape(-1, 8, LANES)
        crossed = product[:, LANES:].reshape(-1, 8, LANES)
        total = straight + jnp.where(even, pltpu.roll(crossed, 7, 1), -pltpu.roll(crossed, 1, 1))
        count = group // per_target
        out_ref[pl.ds(step * count, count), : per_target * rows] = total.astype(BF).reshape(
            count, per_target * rows, LANES
        )


def ahead_kernel(turn_in_ref, window_ref, raw_ref, taps_ref, out_ref, turn_ref, held):
    turn_ref[...] = turn_in_ref[...]
    span = held.shape[0]

    @pl.when(lax.axis_index("sa") == 1)
    def _():
        start = pl.multiple_of(window_ref[0] // LANES * LANES, LANES)
        retile(raw_ref.at[:, :, pl.ds(start, span * LANES)], held, 0, span)
        compress(held, 0, taps_ref, out_ref)


def early_kernel(turn_in_ref, window_ref, raw_ref, tail_ref, head_ref, taps_ref, rows_ref, out_ref, held):
    half = tail_ref.shape[0]
    more = head_ref.shape[0]
    span = half + more - 16
    sub_index = lax.axis_index("sa")
    offset = window_ref[0] // LANES

    @pl.when(sub_index == 0)
    def _():
        start = pl.multiple_of(offset * LANES, LANES)
        retile(raw_ref.at[:, :, pl.ds(start, span * LANES)], held, 0, span)

    @pl.when(sub_index == 1)
    def _():
        held[:half] = tail_ref[...]
        retile(raw_ref, held, half, more)

    @pl.when(sub_index == 3)
    def _():
        held[:half] = tail_ref[...]
        held[half:] = head_ref[...]

    @pl.when(sub_index != 2)
    def _():
        compress(held, jnp.where(sub_index == 0, 0, offset), taps_ref, out_ref)
        out_ref[:, out_ref.shape[1] - rows_ref.shape[1] :] = rows_ref[...]


def late_kernel(near_ref, rows_ref, early_ref, out_ref):
    bins = near_ref.shape[1]
    sub_index = lax.axis_index("sa")

    @pl.when(sub_index != 2)
    def _():
        out_ref[...] = early_ref[...]

    @pl.when(sub_index == 2)
    def _():
        out_ref[:, :bins] = near_ref[...]
        out_ref[:, bins:] = rows_ref[...]


def azimuth_kernel(lines_ref, out_ref, columns_held, taps, made, sems):
    pulses = taps.shape[0] // 2
    columns = pulses // LANES
    tiles = sems.shape[0]
    each = out_ref.shape[0] // tiles
    sources = lines_ref.shape[0]
    rows = (lines_ref.shape[1] - EXTRA) // tiles
    picked = jnp.sum(lines_ref[:, tiles * rows :].astype(F32), axis=0)
    pieces = L // LANES
    row = jnp.concatenate(
        [
            jnp.concatenate([picked[part * pieces + t : part * pieces + t + 1] for t in range(pieces)], axis=1)
            for part in range(2)
        ],
        axis=0,
    )
    moved = pltpu.roll(jnp.concatenate([row] * 4, axis=0), L - (pulses - 1), 1)
    skewed = [
        pltpu.roll(jnp.broadcast_to(moved[part : part + 1], (LANES, L)), 0, 1, stride=1, stride_axis=0)
        for part in range(2)
    ]
    for apart in range(1 - columns, columns):
        at = apart % pieces * LANES
        straight, crossed = (skewed[part][:, at : at + LANES] for part in range(2))
        for target, pair in enumerate(((straight, crossed), (-crossed, straight))):
            slot = (apart + columns - 1) * 2 + target
            for part in range(2):
                columns_held[slot, pl.ds(part, LANES, stride=2), :] = pair[part]
            block = columns_held[slot].astype(BF)
            for column in range(columns):
                line = column - apart
                if 0 <= line < columns:
                    lane = target * pulses + column * LANES
                    taps[2 * line * LANES : 2 * (line + 1) * LANES, lane : lane + LANES] = block
    copies = []
    for tile in range(tiles):
        lines = lines_ref[:, tile * rows : (tile + 1) * rows].reshape(sources * rows, LANES)
        focused = lax.dot_general(lines, taps[...], (((0,), (0,)), ((), ())), preferred_element_type=F32)
        into = pl.ds(tile * each, each)
        for part in range(2):
            for column in range(columns):
                lane = part * pulses + column * LANES
                made[pl.ds(tile * each + 2 * column + part, LANES, stride=2 * columns), :] = focused[
                    :, lane : lane + LANES
                ]
        copies.append(pltpu.make_async_copy(made.at[into], out_ref.at[into], sems.at[tile]))
        copies[-1].start()
    for copy in copies:
        copy.wait()


def toeplitz(diagonal_taps, size):
    span_size = 2 * size - 1
    reversed_taps = diagonal_taps[..., ::-1]
    shifted = jnp.concatenate(
        [reversed_taps[..., size - 1 :], reversed_taps[..., : size - 1]], axis=-1
    )
    reps = (1,) * (shifted.ndim - 1) + (size,)
    tiled_flat = jnp.tile(shifted, reps)[..., : size * (span_size - 1)]
    return tiled_flat.reshape(shifted.shape[:-1] + (size, span_size - 1))[..., :size]


def tap_blocks(tap_values, size):
    block_total = tap_values.shape[1] // size + 1
    padded_taps = jnp.pad(tap_values, ((0, 0), (size, 2 * size)))
    matrices = []
    for offset_block in range(block_total):
        first_tap = offset_block * size + 1
        parts = toeplitz(padded_taps[:, first_tap : first_tap + 2 * size - 1], size)
        real_part = parts[0]
        imag_part = parts[1]
        matrices.append(
            jnp.stack([jnp.stack([real_part, -imag_part]), jnp.stack([imag_part, real_part])])
        )
    return jnp.stack(matrices)


def correlate(blocked, matrices, output_count):
    summed = jnp.zeros((blocked.shape[0], 2, output_count, blocked.shape[3]), F32)
    for offset_block in range(matrices.shape[0]):
        piece_rows = blocked[:, :, offset_block : offset_block + output_count, :]
        summed = summed + jnp.einsum(
            "rcib,cdbn->rdin", piece_rows, matrices[offset_block], preferred_element_type=F32
        )
    return summed


def focus_long(range_lines, reference_row):
    block_size = L // 2
    bin_count, _, total_pulses = range_lines.shape
    block_count = total_pulses // block_size
    blocked = range_lines.reshape(bin_count, 2, block_count, block_size)
    blocked = jnp.pad(blocked, ((0, 0), (0, 0), (1, 1), (0, 0)))
    focused = correlate(blocked, tap_blocks(reference_row, block_size), block_count)
    return focused.reshape(1, bin_count, 2, total_pulses)


def call(kernel, outs, specs, scratch=(), vmem=24, flops=1000):
    space = {"s": pltpu.SMEM, "v": pltpu.VMEM, "a": pl.ANY}
    blocks = [pl.BlockSpec(memory_space=space[kind]) for kind in specs]
    return pl.pallas_call(
        kernel,
        out_shape=outs,
        in_specs=blocks[: -len(outs)],
        out_specs=tuple(blocks[-len(outs) :]),
        scratch_shapes=list(scratch),
        compiler_params=pltpu.CompilerParams(vmem_limit_bytes=int(vmem * 2**20)),
        cost_estimate=pl.CostEstimate(flops=flops, bytes_accessed=1000, transcendentals=0),
    )


def on_device(raw_echo, chirp_replica, azimuth_refs, migration_index, window_start):
    pulses = raw_echo.shape[0]
    segment_devices = lax.axis_size("sa")
    pulse_devices = lax.axis_size("pa")
    tap_count = chirp_replica.shape[1]
    kept_width = R // segment_devices
    bin_count = kept_width // pulse_devices
    total_pulses = pulses * pulse_devices
    half = kept_width // LANES
    tap_tiles = tap_count // LANES + 2
    span = half + tap_tiles - 1

    rows = 2 * pulses
    shape = jax.ShapeDtypeStruct
    token = shape((8, LANES), F32)
    short = bin_count % LANES == 0 and total_pulses == L // 2

    targets = pulse_devices if short else half // 8
    slot = half // targets * rows

    tail, turn = call(
        tail_kernel,
        (shape((half, rows, LANES), BF), token),
        "avv",
        [pltpu.VMEM((pulses, 2, half * LANES), BF), pltpu.SemaphoreType.DMA((4,))],
        53,
    )(raw_echo)
    tail = lax.ppermute(tail, "sa", [(0, 1), (1, 3)])
    head, turn = call(head_kernel, (shape((span - half + 16, rows, LANES), BF), token), "vvvv")(turn, raw_echo)
    head = lax.ppermute(head, "sa", [(2, 3)])
    taps, own_rows, turn = call(
        prep_kernel,
        (shape((tap_tiles * LANES, 2 * LANES), BF), shape((pulse_devices, EXTRA, LANES), BF), token),
        "vsvvvvvv",
    )(turn, window_start, migration_index, chirp_replica, azimuth_refs)
    near, turn = call(
        ahead_kernel,
        (shape((targets, slot, LANES), BF), token),
        "vsvvvv",
        [pltpu.VMEM((span, rows, LANES), BF)],
    )(turn, window_start, raw_echo, taps)
    near = lax.ppermute(near, "sa", [(1, 2)])
    extra = own_rows if short else jnp.zeros((targets, EXTRA, LANES), BF)
    made = shape((targets, slot + EXTRA, LANES), BF)
    (early,) = call(
        early_kernel,
        (made,),
        "vsvvvvvv",
        [pltpu.VMEM((span + 16, rows, LANES), BF)],
        flops=10**10,
    )(turn, window_start, raw_echo, tail, head, taps, extra)
    (compressed,) = call(late_kernel, (made,), "vvvv")(near, extra, early)

    if not short:
        kept = compressed[:, :-EXTRA].reshape(half, pulses, 2, LANES).transpose(0, 3, 2, 1)
        outgoing = kept.reshape(pulse_devices, bin_count, 2, pulses)
        turned = lax.all_to_all(outgoing, "pa", split_axis=0, concat_axis=3, tiled=True)
        rows_in = lax.all_to_all(own_rows, "pa", split_axis=0, concat_axis=0, tiled=True)
        reference_row = jnp.sum(rows_in[:, :8].astype(F32), axis=0).astype(BF).reshape(2, L)
        return focus_long(turned[0], reference_row[:, ::-1])

    lines = lax.all_to_all(compressed, "pa", split_axis=0, concat_axis=0, tiled=True)
    width = 2 * total_pulses
    (focused,) = call(
        azimuth_kernel,
        (shape((bin_count * width // LANES, LANES), F32),),
        "va",
        [
            pltpu.VMEM((width // LANES * 2 - 2, 2 * LANES, LANES), F32),
            pltpu.VMEM((width, width), BF),
            pltpu.VMEM((bin_count * width // LANES, LANES), F32),
            pltpu.SemaphoreType.DMA((bin_count // LANES,)),
        ],
    )(lines)
    focused = focused.reshape(1, bin_count, total_pulses // LANES, 2, LANES).swapaxes(2, 3)
    return focused.reshape(1, bin_count, 2, total_pulses)


def solution(mesh):
    placed = (P("pa", None, "sa"), P(), P("pa", None, None), P(), P())
    return jax.shard_map(
        on_device, mesh=mesh, in_specs=placed, out_specs=P("sa", "pa", None, None), check_vma=False
    )
```

```python
import jax
import jax.numpy as jnp
from jax import lax
from jax.experimental import pallas as pl
from jax.experimental.pallas import tpu as pltpu
from jax.sharding import PartitionSpec as P

R = 16384
L = 512
LANES = 128
EXTRA = 8
BF = jnp.bfloat16
F32 = jnp.float32


def reversed_lanes(row):
    row_id = lax.broadcasted_iota(jnp.int32, (LANES, LANES), 0)
    col_id = lax.broadcasted_iota(jnp.int32, (LANES, LANES), 1)
    flip = (row_id + col_id == LANES - 1).astype(BF)
    tiles = row.shape[1] // LANES
    pieces = [row[:, t * LANES : (t + 1) * LANES] for t in reversed(range(tiles))]
    return jnp.concatenate([jnp.dot(piece, flip, preferred_element_type=F32) for piece in pieces], axis=1)


def retile(source, target, first, tiles):
    shape = target.shape[1:]
    for t in range(tiles):
        target[first + t] = source[:, :, t * LANES : (t + 1) * LANES].reshape(shape)


def tail_first_kernel(raw_ref, tail_ref, turn_ref, natural, sems):
    turn_ref[...] = jnp.zeros_like(turn_ref)
    half, rows, _ = tail_ref.shape
    pieces = sems.shape[0]
    each = rows // 2 // pieces
    width = half * LANES

    @pl.when(lax.axis_index("sa") < 2)
    def _():
        copies = []
        for at in range(pieces):
            own = pl.ds(at * each, each)
            source = raw_ref.at[own, :, pl.ds(raw_ref.shape[2] - width, width)]
            copies.append(pltpu.make_async_copy(source, natural.at[own], sems.at[at]))
            copies[-1].start()
        for at, copy in enumerate(copies):
            copy.wait()
            own = pl.ds(at * each, each)
            retile(natural.at[own], tail_ref.at[:, pl.ds(at * each * 2, each * 2)], 0, half)


def tail_second_kernel(turn_in_ref, raw_ref, tail_ref, head_ref, turn_ref):
    turn_ref[...] = turn_in_ref[...]
    half, rows, _ = tail_ref.shape
    pulses = rows // 2
    sub_index = lax.axis_index("sa")

    @pl.when(sub_index < 2)
    def _():
        own = pl.ds(raw_ref.shape[0] - pulses, pulses)
        width = half * LANES
        retile(raw_ref.at[own, :, pl.ds(raw_ref.shape[2] - width, width)], tail_ref, 0, half)

    @pl.when(sub_index == 2)
    def _():
        retile(raw_ref, head_ref, 0, head_ref.shape[0])


def prep_kernel(turn_in_ref, window_ref, index_ref, chirp_ref, refs_ref, taps_ref, rows_ref, turn_ref):
    turn_ref[...] = turn_in_ref[...]
    taps = chirp_ref.shape[1]
    blocks = taps_ref.shape[0] // LANES
    width = blocks * LANES
    shift = lax.rem(window_ref[0], LANES)
    chirp = jnp.concatenate([chirp_ref[...], jnp.zeros((14, taps), BF)], axis=0)
    flipped = reversed_lanes(chirp)
    padded = jnp.concatenate([jnp.zeros((16, 2 * LANES), F32), flipped], axis=1)
    padded = jnp.concatenate([padded, jnp.zeros((16, width + LANES - padded.shape[1]), F32)], axis=1)
    moved = pltpu.roll(padded, width + LANES - 127 - shift, 1)[:, :width]
    for part in range(2):
        spread = jnp.broadcast_to(moved[part : part + 1], (LANES, width))
        skewed = pltpu.roll(spread, 0, 1, stride=1, stride_axis=0)
        for t in range(blocks):
            first = LANES * (blocks - 1 - t)
            taps_ref[t * LANES : (t + 1) * LANES, part * LANES : (part + 1) * LANES] = skewed[
                :, first : first + LANES
            ].astype(BF)
    own = refs_ref.shape[0]
    groups, targets = index_ref.shape
    first_row = lax.axis_index("pa") * own
    mine = lax.broadcasted_iota(jnp.int32, (groups, targets), 0) == lax.axis_index("sa")
    wanted = jnp.sum(jnp.where(mine, index_ref[...], 0), axis=0, keepdims=True)
    row_id = lax.broadcasted_iota(jnp.int32, (own, targets), 0) + first_row
    picks = (row_id == jnp.broadcast_to(wanted, (own, targets))).astype(F32)
    pieces = []
    for part in range(2):
        picked = lax.dot_general(
            picks, refs_ref[:, part, :].astype(F32), (((0,), (0,)), ((), ())), preferred_element_type=F32
        )
        picked = reversed_lanes(picked.astype(BF))
        pieces += [picked[:, t * LANES : (t + 1) * LANES] for t in range(L // LANES)]
    pieces += [jnp.zeros((targets, LANES), F32)] * (rows_ref.shape[1] - len(pieces))
    rows_ref[...] = jnp.stack(pieces, axis=1).astype(BF)


def compress(held, base, taps_ref, out_ref, first_row, tile_rows):
    rows = held.shape[1]
    tap_tiles = taps_ref.shape[0] // LANES
    group = 8 if rows > 32 else 512 // rows
    per_target = out_ref.shape[1] // tile_rows
    even = lax.rem(lax.broadcasted_iota(jnp.int32, (1, 8, LANES), 1), 2) == 0
    for step in range(out_ref.shape[0] * per_target // group):
        blocks = [
            held[pl.ds(base + group * step + t, group)].reshape(group * rows, LANES) for t in range(tap_tiles)
        ]
        product = jnp.dot(jnp.concatenate(blocks, axis=1), taps_ref[...], preferred_element_type=F32)
        straight = product[:, :LANES].reshape(-1, 8, LANES)
        crossed = product[:, LANES:].reshape(-1, 8, LANES)
        total = straight + jnp.where(even, pltpu.roll(crossed, 7, 1), -pltpu.roll(crossed, 1, 1))
        count = group // per_target
        total = total.astype(BF).reshape(count, per_target, rows, LANES)
        for tile in range(per_target):
            at = tile * tile_rows + first_row
            out_ref[pl.ds(step * count, count), at : at + rows] = total[:, tile]


def ahead_kernel(turn_in_ref, window_ref, raw_ref, taps_ref, out_ref, turn_ref, held):
    turn_ref[...] = turn_in_ref[...]
    span = held.shape[0]

    @pl.when(lax.axis_index("sa") == 1)
    def _():
        start = pl.multiple_of(window_ref[0] // LANES * LANES, LANES)
        retile(raw_ref.at[:, :, pl.ds(start, span * LANES)], held, 0, span)
        compress(held, 0, taps_ref, out_ref, 0, held.shape[1])


def gate_kernel(turn_in_ref, _, turn_ref):
    turn_ref[...] = turn_in_ref[...]


def fill_window(first_pulse, offset, raw_ref, tail_ref, head_ref, held):
    half, rows, _ = tail_ref.shape
    more = head_ref.shape[0]
    span = half + more - 16
    sub_index = lax.axis_index("sa")
    pulses = pl.ds(first_pulse, rows // 2)

    @pl.when(sub_index == 0)
    def _():
        start = pl.multiple_of(offset * LANES, LANES)
        retile(raw_ref.at[pulses, :, pl.ds(start, span * LANES)], held, 0, span)

    @pl.when(sub_index == 1)
    def _():
        held[:half] = tail_ref[...]
        retile(raw_ref.at[pulses], held, half, more)

    @pl.when(sub_index == 3)
    def _():
        held[:half] = tail_ref[...]
        held[half:] = head_ref[:, 2 * first_pulse : 2 * first_pulse + rows]

    return jnp.where(sub_index == 0, 0, offset)


def first_kernel(turn_in_ref, window_ref, raw_ref, tail_ref, head_ref, taps_ref, out_ref, held):
    @pl.when(lax.axis_index("sa") != 2)
    def _():
        base = fill_window(0, window_ref[0] // LANES, raw_ref, tail_ref, head_ref, held)
        compress(held, base, taps_ref, out_ref, 0, held.shape[1])


def second_kernel(window_ref, raw_ref, tail_ref, head_ref, taps_ref, rows_ref, first_ref, out_ref, held):
    rows = held.shape[1]
    tile_rows = head_ref.shape[1]
    before = tile_rows - rows
    bins = out_ref.shape[1] - rows_ref.shape[1]

    @pl.when(lax.axis_index("sa") != 2)
    def _():
        base = fill_window(before // 2, window_ref[0] // LANES, raw_ref, tail_ref, head_ref, held)
        for tile in range(bins // tile_rows):
            out_ref[:, tile * tile_rows : tile * tile_rows + before] = first_ref[:, tile * before : (tile + 1) * before]
        out_ref[:, bins:] = rows_ref[...]
        compress(held, base, taps_ref, out_ref.at[:, pl.ds(0, bins)], before, tile_rows)


def late_kernel(near_ref, rows_ref, early_ref, out_ref):
    bins = near_ref.shape[1]
    sub_index = lax.axis_index("sa")

    @pl.when(sub_index != 2)
    def _():
        out_ref[...] = early_ref[...]

    @pl.when(sub_index == 2)
    def _():
        out_ref[:, :bins] = near_ref[...]
        out_ref[:, bins:] = rows_ref[...]


def azimuth_kernel(lines_ref, out_ref, columns_held, taps, made, sems):
    pulses = taps.shape[0] // 2
    columns = pulses // LANES
    tiles = sems.shape[0]
    each = out_ref.shape[0] // tiles
    sources = lines_ref.shape[0]
    rows = (lines_ref.shape[1] - EXTRA) // tiles
    picked = jnp.sum(lines_ref[:, tiles * rows :].astype(F32), axis=0)
    pieces = L // LANES
    row = jnp.concatenate(
        [
            jnp.concatenate([picked[part * pieces + t : part * pieces + t + 1] for t in range(pieces)], axis=1)
            for part in range(2)
        ],
        axis=0,
    )
    moved = pltpu.roll(jnp.concatenate([row] * 4, axis=0), L - (pulses - 1), 1)
    skewed = [
        pltpu.roll(jnp.broadcast_to(moved[part : part + 1], (LANES, L)), 0, 1, stride=1, stride_axis=0)
        for part in range(2)
    ]
    for apart in range(1 - columns, columns):
        at = apart % pieces * LANES
        straight, crossed = (skewed[part][:, at : at + LANES] for part in range(2))
        for target, pair in enumerate(((straight, crossed), (-crossed, straight))):
            slot = (apart + columns - 1) * 2 + target
            for part in range(2):
                columns_held[slot, pl.ds(part, LANES, stride=2), :] = pair[part]
            block = columns_held[slot].astype(BF)
            for column in range(columns):
                line = column - apart
                if 0 <= line < columns:
                    lane = target * pulses + column * LANES
                    taps[2 * line * LANES : 2 * (line + 1) * LANES, lane : lane + LANES] = block
    copies = []
    for tile in range(tiles):
        lines = lines_ref[:, tile * rows : (tile + 1) * rows].reshape(sources * rows, LANES)
        focused = lax.dot_general(lines, taps[...], (((0,), (0,)), ((), ())), preferred_element_type=F32)
        into = pl.ds(tile * each, each)
        for part in range(2):
            for column in range(columns):
                lane = part * pulses + column * LANES
                made[pl.ds(tile * each + 2 * column + part, LANES, stride=2 * columns), :] = focused[
                    :, lane : lane + LANES
                ]
        copies.append(pltpu.make_async_copy(made.at[into], out_ref.at[into], sems.at[tile]))
        copies[-1].start()
    for copy in copies:
        copy.wait()


def toeplitz(diagonal_taps, size):
    span_size = 2 * size - 1
    reversed_taps = diagonal_taps[..., ::-1]
    shifted = jnp.concatenate(
        [reversed_taps[..., size - 1 :], reversed_taps[..., : size - 1]], axis=-1
    )
    reps = (1,) * (shifted.ndim - 1) + (size,)
    tiled_flat = jnp.tile(shifted, reps)[..., : size * (span_size - 1)]
    return tiled_flat.reshape(shifted.shape[:-1] + (size, span_size - 1))[..., :size]


def tap_blocks(tap_values, size):
    block_total = tap_values.shape[1] // size + 1
    padded_taps = jnp.pad(tap_values, ((0, 0), (size, 2 * size)))
    matrices = []
    for offset_block in range(block_total):
        first_tap = offset_block * size + 1
        parts = toeplitz(padded_taps[:, first_tap : first_tap + 2 * size - 1], size)
        real_part = parts[0]
        imag_part = parts[1]
        matrices.append(
            jnp.stack([jnp.stack([real_part, -imag_part]), jnp.stack([imag_part, real_part])])
        )
    return jnp.stack(matrices)


def correlate(blocked, matrices, output_count):
    summed = jnp.zeros((blocked.shape[0], 2, output_count, blocked.shape[3]), F32)
    for offset_block in range(matrices.shape[0]):
        piece_rows = blocked[:, :, offset_block : offset_block + output_count, :]
        summed = summed + jnp.einsum(
            "rcib,cdbn->rdin", piece_rows, matrices[offset_block], preferred_element_type=F32
        )
    return summed


def focus_long(range_lines, reference_row):
    block_size = L // 2
    bin_count, _, total_pulses = range_lines.shape
    block_count = total_pulses // block_size
    blocked = range_lines.reshape(bin_count, 2, block_count, block_size)
    blocked = jnp.pad(blocked, ((0, 0), (0, 0), (1, 1), (0, 0)))
    focused = correlate(blocked, tap_blocks(reference_row, block_size), block_count)
    return focused.reshape(1, bin_count, 2, total_pulses)


def call(kernel, outs, specs, scratch=(), vmem=24, flops=1000):
    space = {"s": pltpu.SMEM, "v": pltpu.VMEM, "a": pl.ANY}
    blocks = [pl.BlockSpec(memory_space=space[kind]) for kind in specs]
    return pl.pallas_call(
        kernel,
        out_shape=outs,
        in_specs=blocks[: -len(outs)],
        out_specs=tuple(blocks[-len(outs) :]),
        scratch_shapes=list(scratch),
        compiler_params=pltpu.CompilerParams(vmem_limit_bytes=int(vmem * 2**20)),
        cost_estimate=pl.CostEstimate(flops=flops, bytes_accessed=1000, transcendentals=0),
    )


def on_device(raw_echo, chirp_replica, azimuth_refs, migration_index, window_start):
    pulses = raw_echo.shape[0]
    segment_devices = lax.axis_size("sa")
    pulse_devices = lax.axis_size("pa")
    tap_count = chirp_replica.shape[1]
    kept_width = R // segment_devices
    bin_count = kept_width // pulse_devices
    total_pulses = pulses * pulse_devices
    half = kept_width // LANES
    tap_tiles = tap_count // LANES + 2
    span = half + tap_tiles - 1

    rows = 2 * pulses
    shape = jax.ShapeDtypeStruct
    token = shape((8, LANES), F32)
    short = bin_count % LANES == 0 and total_pulses == L // 2

    targets = pulse_devices if short else half // 8
    slot = half // targets * rows

    to_next = [(0, 1), (1, 3)]
    first_rows = rows // 4 * 3
    tail, turn = call(
        tail_first_kernel,
        (shape((half, first_rows, LANES), BF), token),
        "avv",
        [pltpu.VMEM((first_rows // 2, 2, half * LANES), BF), pltpu.SemaphoreType.DMA((3,))],
        53,
    )(raw_echo)
    tail_first = lax.ppermute(tail, "sa", to_next)
    tail, head, turn = call(
        tail_second_kernel,
        (shape((half, rows - first_rows, LANES), BF), shape((span - half + 16, rows, LANES), BF), token),
        "vvvvv",
    )(turn, raw_echo)
    tail_second = lax.ppermute(tail, "sa", to_next)
    head = lax.ppermute(head, "sa", [(2, 3)])
    taps, own_rows, turn = call(
        prep_kernel,
        (shape((tap_tiles * LANES, 2 * LANES), BF), shape((pulse_devices, EXTRA, LANES), BF), token),
        "vsvvvvvv",
    )(turn, window_start, migration_index, chirp_replica, azimuth_refs)
    near, turn = call(
        ahead_kernel,
        (shape((targets, slot, LANES), BF), token),
        "vsvvvv",
        [pltpu.VMEM((span, rows, LANES), BF)],
    )(turn, window_start, raw_echo, taps)
    near = lax.ppermute(near, "sa", [(1, 2)])
    extra = own_rows if short else jnp.zeros((targets, EXTRA, LANES), BF)
    made = shape((targets, slot + EXTRA, LANES), BF)
    (turn,) = call(gate_kernel, (token,), "vav", flops=10**10)(turn, tail_first)
    (first,) = call(
        first_kernel,
        (shape((targets, slot // rows * first_rows, LANES), BF),),
        "vsvvvvv",
        [pltpu.VMEM((span + 16, first_rows, LANES), BF)],
        flops=10**10,
    )(turn, window_start, raw_echo, tail_first, head, taps)
    (early,) = call(
        second_kernel,
        (made,),
        "svvvvvvv",
        [pltpu.VMEM((span + 16, rows - first_rows, LANES), BF)],
        flops=10**10,
    )(window_start, raw_echo, tail_second, head, taps, extra, first)
    (compressed,) = call(late_kernel, (made,), "vvvv")(near, extra, early)

    if not short:
        kept = compressed[:, :-EXTRA].reshape(half, pulses, 2, LANES).transpose(0, 3, 2, 1)
        outgoing = kept.reshape(pulse_devices, bin_count, 2, pulses)
        turned = lax.all_to_all(outgoing, "pa", split_axis=0, concat_axis=3, tiled=True)
        rows_in = lax.all_to_all(own_rows, "pa", split_axis=0, concat_axis=0, tiled=True)
        reference_row = jnp.sum(rows_in[:, :8].astype(F32), axis=0).astype(BF).reshape(2, L)
        return focus_long(turned[0], reference_row[:, ::-1])

    lines = lax.all_to_all(compressed, "pa", split_axis=0, concat_axis=0, tiled=True)
    width = 2 * total_pulses
    (focused,) = call(
        azimuth_kernel,
        (shape((bin_count * width // LANES, LANES), F32),),
        "va",
        [
            pltpu.VMEM((width // LANES * 2 - 2, 2 * LANES, LANES), F32),
            pltpu.VMEM((width, width), BF),
            pltpu.VMEM((bin_count * width // LANES, LANES), F32),
            pltpu.SemaphoreType.DMA((bin_count // LANES,)),
        ],
    )(lines)
    focused = focused.reshape(1, bin_count, total_pulses // LANES, 2, LANES).swapaxes(2, 3)
    return focused.reshape(1, bin_count, 2, total_pulses)


def solution(mesh):
    placed = (P("pa", None, "sa"), P(), P("pa", None, None), P(), P())
    return jax.shard_map(
        on_device, mesh=mesh, in_specs=placed, out_specs=P("sa", "pa", None, None), check_vma=False
    )
```

```python
import jax
import jax.numpy as jnp
from jax import lax
from jax.experimental import pallas as pl
from jax.experimental.pallas import tpu as pltpu
from jax.sharding import PartitionSpec as P

R = 16384
L = 512
LANES = 128
EXTRA = 8
BF = jnp.bfloat16
F32 = jnp.float32


def reversed_lanes(row):
    row_id = lax.broadcasted_iota(jnp.int32, (LANES, LANES), 0)
    col_id = lax.broadcasted_iota(jnp.int32, (LANES, LANES), 1)
    flip = (row_id + col_id == LANES - 1).astype(BF)
    tiles = row.shape[1] // LANES
    pieces = [row[:, t * LANES : (t + 1) * LANES] for t in reversed(range(tiles))]
    return jnp.concatenate([jnp.dot(piece, flip, preferred_element_type=F32) for piece in pieces], axis=1)


def retile(source, target, first, tiles):
    shape = target.shape[1:]
    for t in range(tiles):
        target[first + t] = source[:, :, t * LANES : (t + 1) * LANES].reshape(shape)


def tail_first_kernel(raw_ref, tail_ref, turn_ref, natural, sems):
    turn_ref[...] = jnp.zeros_like(turn_ref)
    half, rows, _ = tail_ref.shape
    pieces = sems.shape[0]
    each = rows // 2 // pieces
    width = half * LANES

    @pl.when(lax.axis_index("sa") < 2)
    def _():
        copies = []
        for at in range(pieces):
            own = pl.ds(at * each, each)
            source = raw_ref.at[own, :, pl.ds(raw_ref.shape[2] - width, width)]
            copies.append(pltpu.make_async_copy(source, natural.at[own], sems.at[at]))
            copies[-1].start()
        for at, copy in enumerate(copies):
            copy.wait()
            own = pl.ds(at * each, each)
            retile(natural.at[own], tail_ref.at[:, pl.ds(at * each * 2, each * 2)], 0, half)


def tail_second_kernel(turn_in_ref, raw_ref, tail_ref, turn_ref):
    turn_ref[...] = turn_in_ref[...]
    half, rows, _ = tail_ref.shape
    pulses = rows // 2

    @pl.when(lax.axis_index("sa") < 2)
    def _():
        own = pl.ds(raw_ref.shape[0] - pulses, pulses)
        width = half * LANES
        retile(raw_ref.at[own, :, pl.ds(raw_ref.shape[2] - width, width)], tail_ref, 0, half)


def range_taps_kernel(turn_in_ref, window_ref, chirp_ref, taps_ref, turn_ref):
    turn_ref[...] = turn_in_ref[...]
    taps = chirp_ref.shape[1]
    blocks = taps_ref.shape[0] // LANES
    width = blocks * LANES
    shift = lax.rem(window_ref[0], LANES)
    chirp = jnp.concatenate([chirp_ref[...], jnp.zeros((14, taps), BF)], axis=0)
    flipped = reversed_lanes(chirp)
    padded = jnp.concatenate([jnp.zeros((16, 2 * LANES), F32), flipped], axis=1)
    padded = jnp.concatenate([padded, jnp.zeros((16, width + LANES - padded.shape[1]), F32)], axis=1)
    moved = pltpu.roll(padded, width + LANES - 127 - shift, 1)[:, :width]
    for part in range(2):
        spread = jnp.broadcast_to(moved[part : part + 1], (LANES, width))
        skewed = pltpu.roll(spread, 0, 1, stride=1, stride_axis=0)
        for t in range(blocks):
            first = LANES * (blocks - 1 - t)
            taps_ref[t * LANES : (t + 1) * LANES, part * LANES : (part + 1) * LANES] = skewed[
                :, first : first + LANES
            ].astype(BF)


def rows_kernel(turn_in_ref, index_ref, refs_ref, rows_ref, turn_ref):
    turn_ref[...] = turn_in_ref[...]
    own = refs_ref.shape[0]
    groups, targets = index_ref.shape
    first_row = lax.axis_index("pa") * own
    mine = lax.broadcasted_iota(jnp.int32, (groups, targets), 0) == lax.axis_index("sa")
    wanted = jnp.sum(jnp.where(mine, index_ref[...], 0), axis=0, keepdims=True)
    row_id = lax.broadcasted_iota(jnp.int32, (own, targets), 0) + first_row
    picks = (row_id == jnp.broadcast_to(wanted, (own, targets))).astype(F32)
    pieces = []
    for part in range(2):
        picked = lax.dot_general(
            picks, refs_ref[:, part, :].astype(F32), (((0,), (0,)), ((), ())), preferred_element_type=F32
        )
        picked = reversed_lanes(picked.astype(BF))
        pieces += [picked[:, t * LANES : (t + 1) * LANES] for t in range(L // LANES)]
    pieces += [jnp.zeros((targets, LANES), F32)] * (rows_ref.shape[1] - len(pieces))
    rows_ref[...] = jnp.stack(pieces, axis=1).astype(BF)


def compress(held, base, taps_ref, out_ref, first_row, tile_rows):
    rows = held.shape[1]
    tap_tiles = taps_ref.shape[0] // LANES
    group = 8 if rows > 32 else 512 // rows
    per_target = out_ref.shape[1] // tile_rows
    even = lax.rem(lax.broadcasted_iota(jnp.int32, (1, 8, LANES), 1), 2) == 0
    for step in range(out_ref.shape[0] * per_target // group):
        blocks = [
            held[pl.ds(base + group * step + t, group)].reshape(group * rows, LANES) for t in range(tap_tiles)
        ]
        product = jnp.dot(jnp.concatenate(blocks, axis=1), taps_ref[...], preferred_element_type=F32)
        straight = product[:, :LANES].reshape(-1, 8, LANES)
        crossed = product[:, LANES:].reshape(-1, 8, LANES)
        total = straight + jnp.where(even, pltpu.roll(crossed, 7, 1), -pltpu.roll(crossed, 1, 1))
        count = group // per_target
        total = total.astype(BF).reshape(count, per_target, rows, LANES)
        for tile in range(per_target):
            at = tile * tile_rows + first_row
            out_ref[pl.ds(step * count, count), at : at + rows] = total[:, tile]


def ahead_kernel(turn_in_ref, window_ref, raw_ref, taps_ref, out_ref, turn_ref, held):
    turn_ref[...] = turn_in_ref[...]
    span = held.shape[0]

    @pl.when(lax.axis_index("sa") == 1)
    def _():
        start = pl.multiple_of(window_ref[0] // LANES * LANES, LANES)
        retile(raw_ref.at[:, :, pl.ds(start, span * LANES)], held, 0, span)
        compress(held, 0, taps_ref, out_ref, 0, held.shape[1])

    @pl.when(lax.axis_index("sa") == 2)
    def _():
        rows = held.shape[1]
        per_target = out_ref.shape[1] // rows
        for t in range(out_ref.shape[0] * per_target):
            tile = raw_ref[:, :, t * LANES : (t + 1) * LANES].reshape(rows, LANES)
            out_ref[t // per_target, t % per_target * rows : (t % per_target + 1) * rows] = tile


def gate_kernel(turn_in_ref, _, turn_ref):
    turn_ref[...] = turn_in_ref[...]


def fill_own(first_pulse, offset, raw_ref, tail_ref, held):
    half, rows, _ = tail_ref.shape
    more = held.shape[0] - half
    span = half + more - 16
    sub_index = lax.axis_index("sa")
    pulses = pl.ds(first_pulse, rows // 2)

    @pl.when(sub_index == 0)
    def _():
        start = pl.multiple_of(offset * LANES, LANES)
        retile(raw_ref.at[pulses, :, pl.ds(start, span * LANES)], held, 0, span)

    @pl.when(sub_index == 1)
    def _():
        held[:half] = tail_ref[...]
        retile(raw_ref.at[pulses], held, half, more)


def fill_far(first_pulse, tail_ref, near_ref, held):
    half, rows, _ = tail_ref.shape
    tile_rows = near_ref.shape[1] * near_ref.shape[0] // half
    per_target = near_ref.shape[1] // tile_rows
    held[:half] = tail_ref[...]
    for t in range(held.shape[0] - half):
        at = t % per_target * tile_rows + 2 * first_pulse
        held[half + t] = near_ref[t // per_target, at : at + rows]


def first_own_kernel(turn_in_ref, window_ref, raw_ref, tail_ref, taps_ref, out_ref, turn_ref, held):
    turn_ref[...] = turn_in_ref[...]
    sub_index = lax.axis_index("sa")
    offset = window_ref[0] // LANES

    @pl.when(sub_index < 2)
    def _():
        fill_own(0, offset, raw_ref, tail_ref, held)
        compress(held, jnp.where(sub_index == 0, 0, offset), taps_ref, out_ref, 0, held.shape[1])


def first_far_kernel(turn_in_ref, window_ref, tail_ref, near_ref, taps_ref, own_ref, out_ref, turn_ref, held):
    turn_ref[...] = turn_in_ref[...]
    sub_index = lax.axis_index("sa")

    @pl.when(sub_index < 2)
    def _():
        out_ref[...] = own_ref[...]

    @pl.when(sub_index == 3)
    def _():
        fill_far(0, tail_ref, near_ref, held)
        compress(held, window_ref[0] // LANES, taps_ref, out_ref, 0, held.shape[1])


def second_kernel(
    turn_in_ref, window_ref, raw_ref, tail_ref, near_ref, taps_ref, rows_ref, first_ref, out_ref, held
):
    rows = held.shape[1]
    bins = near_ref.shape[1]
    tile_rows = 2 * raw_ref.shape[0]
    before = tile_rows - rows
    sub_index = lax.axis_index("sa")
    offset = window_ref[0] // LANES
    out_ref[:, bins:] = rows_ref[...]

    @pl.when(sub_index == 2)
    def _():
        out_ref[:, :bins] = near_ref[...]

    @pl.when(sub_index < 2)
    def _():
        fill_own(before // 2, offset, raw_ref, tail_ref, held)

    @pl.when(sub_index == 3)
    def _():
        fill_far(before // 2, tail_ref, near_ref, held)

    @pl.when(sub_index != 2)
    def _():
        for tile in range(bins // tile_rows):
            out_ref[:, tile * tile_rows : tile * tile_rows + before] = first_ref[:, tile * before : (tile + 1) * before]
        base = jnp.where(sub_index == 0, 0, offset)
        compress(held, base, taps_ref, out_ref.at[:, pl.ds(0, bins)], before, tile_rows)


def azimuth_kernel(lines_ref, out_ref, columns_held, taps, made, sems):
    pulses = taps.shape[0] // 2
    columns = pulses // LANES
    tiles = sems.shape[0]
    each = out_ref.shape[0] // tiles
    sources = lines_ref.shape[0]
    rows = (lines_ref.shape[1] - EXTRA) // tiles
    picked = jnp.sum(lines_ref[:, tiles * rows :].astype(F32), axis=0)
    pieces = L // LANES
    row = jnp.concatenate(
        [
            jnp.concatenate([picked[part * pieces + t : part * pieces + t + 1] for t in range(pieces)], axis=1)
            for part in range(2)
        ],
        axis=0,
    )
    moved = pltpu.roll(jnp.concatenate([row] * 4, axis=0), L - (pulses - 1), 1)
    skewed = [
        pltpu.roll(jnp.broadcast_to(moved[part : part + 1], (LANES, L)), 0, 1, stride=1, stride_axis=0)
        for part in range(2)
    ]
    for apart in range(1 - columns, columns):
        at = apart % pieces * LANES
        straight, crossed = (skewed[part][:, at : at + LANES] for part in range(2))
        for target, pair in enumerate(((straight, crossed), (-crossed, straight))):
            slot = (apart + columns - 1) * 2 + target
            for part in range(2):
                columns_held[slot, pl.ds(part, LANES, stride=2), :] = pair[part]
            block = columns_held[slot].astype(BF)
            for column in range(columns):
                line = column - apart
                if 0 <= line < columns:
                    lane = target * pulses + column * LANES
                    taps[2 * line * LANES : 2 * (line + 1) * LANES, lane : lane + LANES] = block
    copies = []
    for tile in range(tiles):
        lines = lines_ref[:, tile * rows : (tile + 1) * rows].reshape(sources * rows, LANES)
        focused = lax.dot_general(lines, taps[...], (((0,), (0,)), ((), ())), preferred_element_type=F32)
        into = pl.ds(tile * each, each)
        for part in range(2):
            for column in range(columns):
                lane = part * pulses + column * LANES
                made[pl.ds(tile * each + 2 * column + part, LANES, stride=2 * columns), :] = focused[
                    :, lane : lane + LANES
                ]
        copies.append(pltpu.make_async_copy(made.at[into], out_ref.at[into], sems.at[tile]))
        copies[-1].start()
    for copy in copies:
        copy.wait()


def toeplitz(diagonal_taps, size):
    span_size = 2 * size - 1
    reversed_taps = diagonal_taps[..., ::-1]
    shifted = jnp.concatenate(
        [reversed_taps[..., size - 1 :], reversed_taps[..., : size - 1]], axis=-1
    )
    reps = (1,) * (shifted.ndim - 1) + (size,)
    tiled_flat = jnp.tile(shifted, reps)[..., : size * (span_size - 1)]
    return tiled_flat.reshape(shifted.shape[:-1] + (size, span_size - 1))[..., :size]


def tap_blocks(tap_values, size):
    block_total = tap_values.shape[1] // size + 1
    padded_taps = jnp.pad(tap_values, ((0, 0), (size, 2 * size)))
    matrices = []
    for offset_block in range(block_total):
        first_tap = offset_block * size + 1
        parts = toeplitz(padded_taps[:, first_tap : first_tap + 2 * size - 1], size)
        real_part = parts[0]
        imag_part = parts[1]
        matrices.append(
            jnp.stack([jnp.stack([real_part, -imag_part]), jnp.stack([imag_part, real_part])])
        )
    return jnp.stack(matrices)


def correlate(blocked, matrices, output_count):
    summed = jnp.zeros((blocked.shape[0], 2, output_count, blocked.shape[3]), F32)
    for offset_block in range(matrices.shape[0]):
        piece_rows = blocked[:, :, offset_block : offset_block + output_count, :]
        summed = summed + jnp.einsum(
            "rcib,cdbn->rdin", piece_rows, matrices[offset_block], preferred_element_type=F32
        )
    return summed


def focus_long(range_lines, reference_row):
    block_size = L // 2
    bin_count, _, total_pulses = range_lines.shape
    block_count = total_pulses // block_size
    blocked = range_lines.reshape(bin_count, 2, block_count, block_size)
    blocked = jnp.pad(blocked, ((0, 0), (0, 0), (1, 1), (0, 0)))
    focused = correlate(blocked, tap_blocks(reference_row, block_size), block_count)
    return focused.reshape(1, bin_count, 2, total_pulses)


def call(kernel, outs, specs, scratch=(), vmem=24, flops=1000):
    space = {"s": pltpu.SMEM, "v": pltpu.VMEM, "a": pl.ANY}
    blocks = [pl.BlockSpec(memory_space=space[kind]) for kind in specs]
    return pl.pallas_call(
        kernel,
        out_shape=outs,
        in_specs=blocks[: -len(outs)],
        out_specs=tuple(blocks[-len(outs) :]),
        scratch_shapes=list(scratch),
        compiler_params=pltpu.CompilerParams(vmem_limit_bytes=int(vmem * 2**20)),
        cost_estimate=pl.CostEstimate(flops=flops, bytes_accessed=1000, transcendentals=0),
    )


def on_device(raw_echo, chirp_replica, azimuth_refs, migration_index, window_start):
    pulses = raw_echo.shape[0]
    segment_devices = lax.axis_size("sa")
    pulse_devices = lax.axis_size("pa")
    tap_count = chirp_replica.shape[1]
    kept_width = R // segment_devices
    bin_count = kept_width // pulse_devices
    total_pulses = pulses * pulse_devices
    half = kept_width // LANES
    tap_tiles = tap_count // LANES + 2
    span = half + tap_tiles - 1

    rows = 2 * pulses
    shape = jax.ShapeDtypeStruct
    token = shape((8, LANES), F32)
    short = bin_count % LANES == 0 and total_pulses == L // 2

    targets = pulse_devices if short else half // 8
    slot = half // targets * rows

    to_next = [(0, 1), (1, 3)]
    first_rows = rows // 4 * 3
    tail, turn = call(
        tail_first_kernel,
        (shape((half, first_rows, LANES), BF), token),
        "avv",
        [pltpu.VMEM((first_rows // 2, 2, half * LANES), BF), pltpu.SemaphoreType.DMA((3,))],
        53,
    )(raw_echo)
    tail_first = lax.ppermute(tail, "sa", to_next)
    tail, turn = call(
        tail_second_kernel, (shape((half, rows - first_rows, LANES), BF), token), "vvvv"
    )(turn, raw_echo)
    tail_second = lax.ppermute(tail, "sa", to_next)
    taps, turn = call(range_taps_kernel, (shape((tap_tiles * LANES, 2 * LANES), BF), token), "vsvvv")(
        turn, window_start, chirp_replica
    )
    near, turn = call(
        ahead_kernel, (shape((targets, slot, LANES), BF), token), "vsvvvv", [pltpu.VMEM((span, rows, LANES), BF)]
    )(turn, window_start, raw_echo, taps)
    near = lax.ppermute(near, "sa", [(1, 2), (2, 3)])
    (turn,) = call(gate_kernel, (token,), "vav", flops=10**10)(turn, tail_first)
    own_rows, turn = call(rows_kernel, (shape((pulse_devices, EXTRA, LANES), BF), token), "vvvvv")(
        turn, migration_index, azimuth_refs
    )
    extra = own_rows if short else jnp.zeros((targets, EXTRA, LANES), BF)
    made = shape((targets, slot + EXTRA, LANES), BF)
    first_shape = shape((targets, slot // rows * first_rows, LANES), BF)
    first_held = pltpu.VMEM((span + 16, first_rows, LANES), BF)
    first, turn = call(first_own_kernel, (first_shape, token), "vsvvvvv", [first_held], flops=10**10)(
        turn, window_start, raw_echo, tail_first, taps
    )
    first, turn = call(first_far_kernel, (first_shape, token), "vsvvvvvv", [first_held], flops=10**10)(
        turn, window_start, tail_first, near, taps, first
    )
    (compressed,) = call(
        second_kernel,
        (made,),
        "vsvvvvvvv",
        [pltpu.VMEM((span + 16, rows - first_rows, LANES), BF)],
        flops=10**10,
    )(turn, window_start, raw_echo, tail_second, near, taps, extra, first)

    if not short:
        kept = compressed[:, :-EXTRA].reshape(half, pulses, 2, LANES).transpose(0, 3, 2, 1)
        outgoing = kept.reshape(pulse_devices, bin_count, 2, pulses)
        turned = lax.all_to_all(outgoing, "pa", split_axis=0, concat_axis=3, tiled=True)
        rows_in = lax.all_to_all(own_rows, "pa", split_axis=0, concat_axis=0, tiled=True)
        reference_row = jnp.sum(rows_in[:, :8].astype(F32), axis=0).astype(BF).reshape(2, L)
        return focus_long(turned[0], reference_row[:, ::-1])

    lines = lax.all_to_all(compressed, "pa", split_axis=0, concat_axis=0, tiled=True)
    width = 2 * total_pulses
    (focused,) = call(
        azimuth_kernel,
        (shape((bin_count * width // LANES, LANES), F32),),
        "va",
        [
            pltpu.VMEM((width // LANES * 2 - 2, 2 * LANES, LANES), F32),
            pltpu.VMEM((width, width), BF),
            pltpu.VMEM((bin_count * width // LANES, LANES), F32),
            pltpu.SemaphoreType.DMA((bin_count // LANES,)),
        ],
    )(lines)
    focused = focused.reshape(1, bin_count, total_pulses // LANES, 2, LANES).swapaxes(2, 3)
    return focused.reshape(1, bin_count, 2, total_pulses)


def solution(mesh):
    placed = (P("pa", None, "sa"), P(), P("pa", None, None), P(), P())
    return jax.shard_map(
        on_device, mesh=mesh, in_specs=placed, out_specs=P("sa", "pa", None, None), check_vma=False
    )
```

```python
import jax
import jax.numpy as jnp
from jax import lax
from jax.experimental import pallas as pl
from jax.experimental.pallas import tpu as pltpu
from jax.sharding import PartitionSpec as P

R = 16384
L = 512
LANES = 128
EXTRA = 8
BF = jnp.bfloat16
F32 = jnp.float32


def reversed_lanes(row):
    row_id = lax.broadcasted_iota(jnp.int32, (LANES, LANES), 0)
    col_id = lax.broadcasted_iota(jnp.int32, (LANES, LANES), 1)
    flip = (row_id + col_id == LANES - 1).astype(BF)
    tiles = row.shape[1] // LANES
    pieces = [row[:, t * LANES : (t + 1) * LANES] for t in reversed(range(tiles))]
    return jnp.concatenate([jnp.dot(piece, flip, preferred_element_type=F32) for piece in pieces], axis=1)


def retile(source, target, first, tiles):
    shape = target.shape[1:]
    for t in range(tiles):
        target[first + t] = source[:, :, t * LANES : (t + 1) * LANES].reshape(shape)


def tail_first_kernel(raw_ref, tail_ref, turn_ref, natural, sems):
    turn_ref[...] = jnp.zeros_like(turn_ref)
    half, rows, _ = tail_ref.shape
    pieces = sems.shape[0]
    each = rows // 2 // pieces
    width = half * LANES

    @pl.when(lax.axis_index("sa") == 1)
    def _():
        copies = []
        for at in range(pieces):
            own = pl.ds(at * each, each)
            source = raw_ref.at[own, :, pl.ds(raw_ref.shape[2] - width, width)]
            copies.append(pltpu.make_async_copy(source, natural.at[own], sems.at[at]))
            copies[-1].start()
        for at, copy in enumerate(copies):
            copy.wait()
            own = pl.ds(at * each, each)
            retile(natural.at[own], tail_ref.at[:, pl.ds(at * each * 2, each * 2)], 0, half)


def tail_second_kernel(turn_in_ref, raw_ref, tail_ref, turn_ref):
    turn_ref[...] = turn_in_ref[...]
    half, rows, _ = tail_ref.shape
    pulses = rows // 2

    @pl.when(lax.axis_index("sa") == 1)
    def _():
        own = pl.ds(raw_ref.shape[0] - pulses, pulses)
        width = half * LANES
        retile(raw_ref.at[own, :, pl.ds(raw_ref.shape[2] - width, width)], tail_ref, 0, half)


def prep_kernel(turn_in_ref, window_ref, index_ref, chirp_ref, refs_ref, taps_ref, rows_ref, turn_ref):
    turn_ref[...] = turn_in_ref[...]
    taps = chirp_ref.shape[1]
    blocks = taps_ref.shape[0] // LANES
    width = blocks * LANES
    shift = lax.rem(window_ref[0], LANES)
    chirp = jnp.concatenate([chirp_ref[...], jnp.zeros((14, taps), BF)], axis=0)
    flipped = reversed_lanes(chirp)
    padded = jnp.concatenate([jnp.zeros((16, 2 * LANES), F32), flipped], axis=1)
    padded = jnp.concatenate([padded, jnp.zeros((16, width + LANES - padded.shape[1]), F32)], axis=1)
    moved = pltpu.roll(padded, width + LANES - 127 - shift, 1)[:, :width]
    for part in range(2):
        spread = jnp.broadcast_to(moved[part : part + 1], (LANES, width))
        skewed = pltpu.roll(spread, 0, 1, stride=1, stride_axis=0)
        for t in range(blocks):
            first = LANES * (blocks - 1 - t)
            taps_ref[t * LANES : (t + 1) * LANES, part * LANES : (part + 1) * LANES] = skewed[
                :, first : first + LANES
            ].astype(BF)
    own = refs_ref.shape[0]
    groups, targets = index_ref.shape
    first_row = lax.axis_index("pa") * own
    mine = lax.broadcasted_iota(jnp.int32, (groups, targets), 0) == lax.axis_index("sa")
    wanted = jnp.sum(jnp.where(mine, index_ref[...], 0), axis=0, keepdims=True)
    row_id = lax.broadcasted_iota(jnp.int32, (own, targets), 0) + first_row
    picks = (row_id == jnp.broadcast_to(wanted, (own, targets))).astype(F32)
    pieces = []
    for part in range(2):
        picked = lax.dot_general(
            picks, refs_ref[:, part, :].astype(F32), (((0,), (0,)), ((), ())), preferred_element_type=F32
        )
        picked = reversed_lanes(picked.astype(BF))
        pieces += [picked[:, t * LANES : (t + 1) * LANES] for t in range(L // LANES)]
    pieces += [jnp.zeros((targets, LANES), F32)] * (rows_ref.shape[1] - len(pieces))
    rows_ref[...] = jnp.stack(pieces, axis=1).astype(BF)


def compress(held, base, taps_ref, out_ref, first_row, tile_rows):
    rows = held.shape[1]
    tap_tiles = taps_ref.shape[0] // LANES
    group = 8 if rows > 32 else 512 // rows
    per_target = out_ref.shape[1] // tile_rows
    even = lax.rem(lax.broadcasted_iota(jnp.int32, (1, 8, LANES), 1), 2) == 0
    for step in range(out_ref.shape[0] * per_target // group):
        blocks = [
            held[pl.ds(base + group * step + t, group)].reshape(group * rows, LANES) for t in range(tap_tiles)
        ]
        product = jnp.dot(jnp.concatenate(blocks, axis=1), taps_ref[...], preferred_element_type=F32)
        straight = product[:, :LANES].reshape(-1, 8, LANES)
        crossed = product[:, LANES:].reshape(-1, 8, LANES)
        total = straight + jnp.where(even, pltpu.roll(crossed, 7, 1), -pltpu.roll(crossed, 1, 1))
        count = group // per_target
        total = total.astype(BF).reshape(count, per_target, rows, LANES)
        for tile in range(per_target):
            at = tile * tile_rows + first_row
            out_ref[pl.ds(step * count, count), at : at + rows] = total[:, tile]


def own_kernel(turn_in_ref, window_ref, raw_ref, taps_ref, out_ref, turn_ref, held):
    turn_ref[...] = turn_in_ref[...]
    span = held.shape[0]

    @pl.when(lax.axis_index("sa") == 0)
    def _():
        start = pl.multiple_of(window_ref[0] // LANES * LANES, LANES)
        retile(raw_ref.at[:, :, pl.ds(start, span * LANES)], held, 0, span)
        compress(held, 0, taps_ref, out_ref, 0, held.shape[1])


def hand_tiles(raw_ref, first, out_ref):
    rows = 2 * raw_ref.shape[0]
    per_target = out_ref.shape[1] // rows
    for t in range(out_ref.shape[0] * per_target):
        start = (first + t) * LANES
        at = t % per_target * rows
        out_ref[t // per_target, at : at + rows] = raw_ref[:, :, start : start + LANES].reshape(rows, LANES)


def ahead_kernel(turn_in_ref, window_ref, raw_ref, taps_ref, out_ref, turn_ref, held):
    turn_ref[...] = turn_in_ref[...]
    span = held.shape[0]
    tiles = raw_ref.shape[2] // LANES
    count = out_ref.shape[0] * out_ref.shape[1] // held.shape[1]
    sub_index = lax.axis_index("sa")

    @pl.when(sub_index == 0)
    def _():
        hand_tiles(raw_ref, tiles - count, out_ref)

    @pl.when(sub_index == 1)
    def _():
        start = pl.multiple_of(window_ref[0] // LANES * LANES, LANES)
        retile(raw_ref.at[:, :, pl.ds(start, span * LANES)], held, 0, span)
        compress(held, 0, taps_ref, out_ref, 0, held.shape[1])

    @pl.when(sub_index == 2)
    def _():
        hand_tiles(raw_ref, 0, out_ref)


def gate_kernel(turn_in_ref, _, turn_ref):
    turn_ref[...] = turn_in_ref[...]


def take_tiles(near_ref, tile_rows, first_row, held, into, count):
    rows = held.shape[1]
    per_target = near_ref.shape[1] // tile_rows
    for t in range(count):
        at = t % per_target * tile_rows + first_row
        held[into + t] = near_ref[t // per_target, at : at + rows]


def middle_kernel(
    turn_in_ref, window_ref, raw_ref, tail_ref, near_ref, own_ref, taps_ref, rows_ref, out_ref, turn_ref, held, far_held
):
    turn_ref[...] = turn_in_ref[...]
    half = tail_ref.shape[0]
    more = held.shape[0] - half
    bins = near_ref.shape[1]
    tile_rows = held.shape[1]
    sub_index = lax.axis_index("sa")
    offset = window_ref[0] // LANES
    made = out_ref.at[:, pl.ds(0, bins)]
    out_ref[:, bins:] = rows_ref[...]

    @pl.when(sub_index == 0)
    def _():
        made[...] = own_ref[...]

    @pl.when(sub_index == 1)
    def _():
        take_tiles(near_ref, tile_rows, 0, held, 0, half)
        retile(raw_ref, held, half, more)
        compress(held, offset, taps_ref, made, 0, tile_rows)

    @pl.when(sub_index == 2)
    def _():
        made[...] = near_ref[...]

    @pl.when(sub_index == 3)
    def _():
        far_held[:half] = tail_ref[...]
        take_tiles(near_ref, tile_rows, 0, far_held, half, more)
        compress(far_held, offset, taps_ref, made, 0, tile_rows)


def last_kernel(turn_in_ref, window_ref, tail_ref, near_ref, taps_ref, middle_ref, out_ref, held):
    half, rows, _ = tail_ref.shape
    bins = near_ref.shape[1]
    tile_rows = bins * near_ref.shape[0] // half
    out_ref[...] = middle_ref[...]

    @pl.when(lax.axis_index("sa") == 3)
    def _():
        held[:half] = tail_ref[...]
        take_tiles(near_ref, tile_rows, tile_rows - rows, held, half, held.shape[0] - half)
        made = out_ref.at[:, pl.ds(0, bins)]
        compress(held, window_ref[0] // LANES, taps_ref, made, tile_rows - rows, tile_rows)


def azimuth_kernel(lines_ref, out_ref, columns_held, taps, made, sems):
    pulses = taps.shape[0] // 2
    columns = pulses // LANES
    tiles = sems.shape[0]
    each = out_ref.shape[0] // tiles
    sources = lines_ref.shape[0]
    rows = (lines_ref.shape[1] - EXTRA) // tiles
    picked = jnp.sum(lines_ref[:, tiles * rows :].astype(F32), axis=0)
    pieces = L // LANES
    row = jnp.concatenate(
        [
            jnp.concatenate([picked[part * pieces + t : part * pieces + t + 1] for t in range(pieces)], axis=1)
            for part in range(2)
        ],
        axis=0,
    )
    moved = pltpu.roll(jnp.concatenate([row] * 4, axis=0), L - (pulses - 1), 1)
    skewed = [
        pltpu.roll(jnp.broadcast_to(moved[part : part + 1], (LANES, L)), 0, 1, stride=1, stride_axis=0)
        for part in range(2)
    ]
    for apart in range(1 - columns, columns):
        at = apart % pieces * LANES
        straight, crossed = (skewed[part][:, at : at + LANES] for part in range(2))
        for target, pair in enumerate(((straight, crossed), (-crossed, straight))):
            slot = (apart + columns - 1) * 2 + target
            for part in range(2):
                columns_held[slot, pl.ds(part, LANES, stride=2), :] = pair[part]
            block = columns_held[slot].astype(BF)
            for column in range(columns):
                line = column - apart
                if 0 <= line < columns:
                    lane = target * pulses + column * LANES
                    taps[2 * line * LANES : 2 * (line + 1) * LANES, lane : lane + LANES] = block
    copies = []
    for tile in range(tiles):
        lines = lines_ref[:, tile * rows : (tile + 1) * rows].reshape(sources * rows, LANES)
        focused = lax.dot_general(lines, taps[...], (((0,), (0,)), ((), ())), preferred_element_type=F32)
        into = pl.ds(tile * each, each)
        for part in range(2):
            for column in range(columns):
                lane = part * pulses + column * LANES
                made[pl.ds(tile * each + 2 * column + part, LANES, stride=2 * columns), :] = focused[
                    :, lane : lane + LANES
                ]
        copies.append(pltpu.make_async_copy(made.at[into], out_ref.at[into], sems.at[tile]))
        copies[-1].start()
    for copy in copies:
        copy.wait()


def toeplitz(diagonal_taps, size):
    span_size = 2 * size - 1
    reversed_taps = diagonal_taps[..., ::-1]
    shifted = jnp.concatenate(
        [reversed_taps[..., size - 1 :], reversed_taps[..., : size - 1]], axis=-1
    )
    reps = (1,) * (shifted.ndim - 1) + (size,)
    tiled_flat = jnp.tile(shifted, reps)[..., : size * (span_size - 1)]
    return tiled_flat.reshape(shifted.shape[:-1] + (size, span_size - 1))[..., :size]


def tap_blocks(tap_values, size):
    block_total = tap_values.shape[1] // size + 1
    padded_taps = jnp.pad(tap_values, ((0, 0), (size, 2 * size)))
    matrices = []
    for offset_block in range(block_total):
        first_tap = offset_block * size + 1
        parts = toeplitz(padded_taps[:, first_tap : first_tap + 2 * size - 1], size)
        real_part = parts[0]
        imag_part = parts[1]
        matrices.append(
            jnp.stack([jnp.stack([real_part, -imag_part]), jnp.stack([imag_part, real_part])])
        )
    return jnp.stack(matrices)


def correlate(blocked, matrices, output_count):
    summed = jnp.zeros((blocked.shape[0], 2, output_count, blocked.shape[3]), F32)
    for offset_block in range(matrices.shape[0]):
        piece_rows = blocked[:, :, offset_block : offset_block + output_count, :]
        summed = summed + jnp.einsum(
            "rcib,cdbn->rdin", piece_rows, matrices[offset_block], preferred_element_type=F32
        )
    return summed


def focus_long(range_lines, reference_row):
    block_size = L // 2
    bin_count, _, total_pulses = range_lines.shape
    block_count = total_pulses // block_size
    blocked = range_lines.reshape(bin_count, 2, block_count, block_size)
    blocked = jnp.pad(blocked, ((0, 0), (0, 0), (1, 1), (0, 0)))
    focused = correlate(blocked, tap_blocks(reference_row, block_size), block_count)
    return focused.reshape(1, bin_count, 2, total_pulses)


def call(kernel, outs, specs, scratch=(), vmem=24, flops=1000):
    space = {"s": pltpu.SMEM, "v": pltpu.VMEM, "a": pl.ANY}
    blocks = [pl.BlockSpec(memory_space=space[kind]) for kind in specs]
    return pl.pallas_call(
        kernel,
        out_shape=outs,
        in_specs=blocks[: -len(outs)],
        out_specs=tuple(blocks[-len(outs) :]),
        scratch_shapes=list(scratch),
        compiler_params=pltpu.CompilerParams(vmem_limit_bytes=int(vmem * 2**20)),
        cost_estimate=pl.CostEstimate(flops=flops, bytes_accessed=1000, transcendentals=0),
    )


def on_device(raw_echo, chirp_replica, azimuth_refs, migration_index, window_start):
    pulses = raw_echo.shape[0]
    segment_devices = lax.axis_size("sa")
    pulse_devices = lax.axis_size("pa")
    tap_count = chirp_replica.shape[1]
    kept_width = R // segment_devices
    bin_count = kept_width // pulse_devices
    total_pulses = pulses * pulse_devices
    half = kept_width // LANES
    tap_tiles = tap_count // LANES + 2
    span = half + tap_tiles - 1

    rows = 2 * pulses
    shape = jax.ShapeDtypeStruct
    token = shape((8, LANES), F32)
    short = bin_count % LANES == 0 and total_pulses == L // 2

    targets = pulse_devices if short else half // 8
    slot = half // targets * rows

    first_rows = rows // 4 * 3
    part = shape((targets, slot, LANES), BF)
    tail, turn = call(
        tail_first_kernel,
        (shape((half, first_rows, LANES), BF), token),
        "avv",
        [pltpu.VMEM((first_rows // 2, 2, half * LANES), BF), pltpu.SemaphoreType.DMA((3,))],
        53,
    )(raw_echo)
    tail_first = lax.ppermute(tail, "sa", [(1, 3)])
    taps, own_rows, turn = call(
        prep_kernel,
        (shape((tap_tiles * LANES, 2 * LANES), BF), shape((pulse_devices, EXTRA, LANES), BF), token),
        "vsvvvvvv",
    )(turn, window_start, migration_index, chirp_replica, azimuth_refs)
    window_held = [pltpu.VMEM((span, rows, LANES), BF)]
    own, turn = call(own_kernel, (part, token), "vsvvvv", window_held)(turn, window_start, raw_echo, taps)
    near, turn = call(ahead_kernel, (part, token), "vsvvvv", window_held)(turn, window_start, raw_echo, taps)
    near = lax.ppermute(near, "sa", [(0, 1), (1, 2), (2, 3)])
    (turn,) = call(gate_kernel, (token,), "vav", flops=10**10)(turn, tail_first)
    tail, turn = call(
        tail_second_kernel, (shape((half, rows - first_rows, LANES), BF), token), "vvvv"
    )(turn, raw_echo)
    tail_second = lax.ppermute(tail, "sa", [(1, 3)])
    extra = own_rows if short else jnp.zeros((targets, EXTRA, LANES), BF)
    made = shape((targets, slot + EXTRA, LANES), BF)
    wide = span + 16
    middle, turn = call(
        middle_kernel,
        (made, token),
        "vsvvvvvvvv",
        [pltpu.VMEM((wide, rows, LANES), BF), pltpu.VMEM((wide, first_rows, LANES), BF)],
        flops=10**10,
    )(turn, window_start, raw_echo, tail_first, near, own, taps, extra)
    (compressed,) = call(
        last_kernel, (made,), "vsvvvvv", [pltpu.VMEM((wide, rows - first_rows, LANES), BF)], flops=10**10
    )(turn, window_start, tail_second, near, taps, middle)

    if not short:
        kept = compressed[:, :-EXTRA].reshape(half, pulses, 2, LANES).transpose(0, 3, 2, 1)
        outgoing = kept.reshape(pulse_devices, bin_count, 2, pulses)
        turned = lax.all_to_all(outgoing, "pa", split_axis=0, concat_axis=3, tiled=True)
        rows_in = lax.all_to_all(own_rows, "pa", split_axis=0, concat_axis=0, tiled=True)
        reference_row = jnp.sum(rows_in[:, :8].astype(F32), axis=0).astype(BF).reshape(2, L)
        return focus_long(turned[0], reference_row[:, ::-1])

    lines = lax.all_to_all(compressed, "pa", split_axis=0, concat_axis=0, tiled=True)
    width = 2 * total_pulses
    (focused,) = call(
        azimuth_kernel,
        (shape((bin_count * width // LANES, LANES), F32),),
        "va",
        [
            pltpu.VMEM((width // LANES * 2 - 2, 2 * LANES, LANES), F32),
            pltpu.VMEM((width, width), BF),
            pltpu.VMEM((bin_count * width // LANES, LANES), F32),
            pltpu.SemaphoreType.DMA((bin_count // LANES,)),
        ],
    )(lines)
    focused = focused.reshape(1, bin_count, total_pulses // LANES, 2, LANES).swapaxes(2, 3)
    return focused.reshape(1, bin_count, 2, total_pulses)


def solution(mesh):
    placed = (P("pa", None, "sa"), P(), P("pa", None, None), P(), P())
    return jax.shard_map(
        on_device, mesh=mesh, in_specs=placed, out_specs=P("sa", "pa", None, None), check_vma=False
    )
```

```python
import jax
import jax.numpy as jnp
from jax import lax
from jax.experimental import pallas as pl
from jax.experimental.pallas import tpu as pltpu
from jax.sharding import PartitionSpec as P

R = 16384
L = 512
LANES = 128
EXTRA = 8
BF = jnp.bfloat16
F32 = jnp.float32


def reversed_lanes(row):
    row_id = lax.broadcasted_iota(jnp.int32, (LANES, LANES), 0)
    col_id = lax.broadcasted_iota(jnp.int32, (LANES, LANES), 1)
    flip = (row_id + col_id == LANES - 1).astype(BF)
    tiles = row.shape[1] // LANES
    pieces = [row[:, t * LANES : (t + 1) * LANES] for t in reversed(range(tiles))]
    return jnp.concatenate([jnp.dot(piece, flip, preferred_element_type=F32) for piece in pieces], axis=1)


def retile(source, target, first, tiles):
    shape = target.shape[1:]
    for t in range(tiles):
        target[first + t] = source[:, :, t * LANES : (t + 1) * LANES].reshape(shape)


def tail_kernel(raw_ref, tail_ref, turn_ref, natural, sems):
    turn_ref[...] = jnp.zeros_like(turn_ref)
    half, rows, _ = tail_ref.shape
    pieces = sems.shape[0]
    each = rows // 2 // pieces
    width = half * LANES

    @pl.when(lax.axis_index("sa") < 2)
    def _():
        copies = []
        for at in range(pieces):
            own = pl.ds(at * each, each)
            source = raw_ref.at[own, :, pl.ds(raw_ref.shape[2] - width, width)]
            copies.append(pltpu.make_async_copy(source, natural.at[own], sems.at[at]))
            copies[-1].start()
        for at, copy in enumerate(copies):
            copy.wait()
            own = pl.ds(at * each, each)
            retile(natural.at[own], tail_ref.at[:, pl.ds(at * each * 2, each * 2)], 0, half)


def head_kernel(turn_in_ref, raw_ref, head_ref, turn_ref):
    turn_ref[...] = turn_in_ref[...]

    @pl.when(lax.axis_index("sa") == 2)
    def _():
        retile(raw_ref, head_ref, 0, head_ref.shape[0])


def prep_kernel(turn_in_ref, window_ref, index_ref, chirp_ref, refs_ref, taps_ref, rows_ref, turn_ref):
    turn_ref[...] = turn_in_ref[...]
    taps = chirp_ref.shape[1]
    blocks = taps_ref.shape[0] // LANES
    width = blocks * LANES
    shift = lax.rem(window_ref[0], LANES)
    chirp = jnp.concatenate([chirp_ref[...], jnp.zeros((14, taps), BF)], axis=0)
    flipped = reversed_lanes(chirp)
    padded = jnp.concatenate([jnp.zeros((16, 2 * LANES), F32), flipped], axis=1)
    padded = jnp.concatenate([padded, jnp.zeros((16, width + LANES - padded.shape[1]), F32)], axis=1)
    moved = pltpu.roll(padded, width + LANES - 127 - shift, 1)[:, :width]
    for part in range(2):
        spread = jnp.broadcast_to(moved[part : part + 1], (LANES, width))
        skewed = pltpu.roll(spread, 0, 1, stride=1, stride_axis=0)
        for t in range(blocks):
            first = LANES * (blocks - 1 - t)
            taps_ref[t * LANES : (t + 1) * LANES, part * LANES : (part + 1) * LANES] = skewed[
                :, first : first + LANES
            ].astype(BF)
    own = refs_ref.shape[0]
    groups, targets = index_ref.shape
    first_row = lax.axis_index("pa") * own
    mine = lax.broadcasted_iota(jnp.int32, (groups, targets), 0) == lax.axis_index("sa")
    wanted = jnp.sum(jnp.where(mine, index_ref[...], 0), axis=0, keepdims=True)
    row_id = lax.broadcasted_iota(jnp.int32, (own, targets), 0) + first_row
    picks = (row_id == jnp.broadcast_to(wanted, (own, targets))).astype(F32)
    pieces = []
    for part in range(2):
        picked = lax.dot_general(
            picks, refs_ref[:, part, :].astype(F32), (((0,), (0,)), ((), ())), preferred_element_type=F32
        )
        picked = reversed_lanes(picked.astype(BF))
        pieces += [picked[:, t * LANES : (t + 1) * LANES] for t in range(L // LANES)]
    pieces += [jnp.zeros((targets, LANES), F32)] * (rows_ref.shape[1] - len(pieces))
    rows_ref[...] = jnp.stack(pieces, axis=1).astype(BF)


def compress(held, base, taps_ref, out_ref):
    rows = held.shape[1]
    targets = out_ref.shape[0]
    tap_tiles = taps_ref.shape[0] // LANES
    group = 8
    per_target = out_ref.shape[1] // rows
    even = lax.rem(lax.broadcasted_iota(jnp.int32, (1, 8, LANES), 1), 2) == 0
    for step in range(targets * per_target // group):
        blocks = [
            held[pl.ds(base + group * step + t, group)].reshape(group * rows, LANES) for t in range(tap_tiles)
        ]
        product = jnp.dot(jnp.concatenate(blocks, axis=1), taps_ref[...], preferred_element_type=F32)
        straight = product[:, :LANES].reshape(-1, 8, LANES)
        crossed = product[:, LANES:].reshape(-1, 8, LANES)
        total = straight + jnp.where(even, pltpu.roll(crossed, 7, 1), -pltpu.roll(crossed, 1, 1))
        count = group // per_target
        out_ref[pl.ds(step * count, count), : per_target * rows] = total.astype(BF).reshape(
            count, per_target * rows, LANES
        )


def ahead_kernel(turn_in_ref, window_ref, raw_ref, taps_ref, out_ref, turn_ref, held):
    turn_ref[...] = turn_in_ref[...]
    span = held.shape[0]

    @pl.when(lax.axis_index("sa") == 1)
    def _():
        start = pl.multiple_of(window_ref[0] // LANES * LANES, LANES)
        retile(raw_ref.at[:, :, pl.ds(start, span * LANES)], held, 0, span)
        compress(held, 0, taps_ref, out_ref)


def early_kernel(turn_in_ref, window_ref, raw_ref, tail_ref, head_ref, taps_ref, rows_ref, out_ref, held):
    half = tail_ref.shape[0]
    more = head_ref.shape[0]
    span = half + more - 16
    sub_index = lax.axis_index("sa")
    offset = window_ref[0] // LANES

    @pl.when(sub_index == 0)
    def _():
        start = pl.multiple_of(offset * LANES, LANES)
        retile(raw_ref.at[:, :, pl.ds(start, span * LANES)], held, 0, span)

    @pl.when(sub_index == 1)
    def _():
        held[:half] = tail_ref[...]
        retile(raw_ref, held, half, more)

    @pl.when(sub_index == 3)
    def _():
        held[:half] = tail_ref[...]
        held[half:] = head_ref[...]

    @pl.when(sub_index != 2)
    def _():
        compress(held, jnp.where(sub_index == 0, 0, offset), taps_ref, out_ref)
        out_ref[:, out_ref.shape[1] - rows_ref.shape[1] :] = rows_ref[...]


def late_kernel(near_ref, rows_ref, early_ref, out_ref):
    bins = near_ref.shape[1]
    sub_index = lax.axis_index("sa")

    @pl.when(sub_index != 2)
    def _():
        out_ref[...] = early_ref[...]

    @pl.when(sub_index == 2)
    def _():
        out_ref[:, :bins] = near_ref[...]
        out_ref[:, bins:] = rows_ref[...]


def azimuth_kernel(lines_ref, out_ref, columns_held, taps, made, sems):
    pulses = taps.shape[0] // 2
    columns = pulses // LANES
    tiles = sems.shape[0]
    each = out_ref.shape[0] // tiles
    sources = lines_ref.shape[0]
    rows = (lines_ref.shape[1] - EXTRA) // tiles
    picked = jnp.sum(lines_ref[:, tiles * rows :].astype(F32), axis=0)
    pieces = L // LANES
    row = jnp.concatenate(
        [
            jnp.concatenate([picked[part * pieces + t : part * pieces + t + 1] for t in range(pieces)], axis=1)
            for part in range(2)
        ],
        axis=0,
    )
    moved = pltpu.roll(jnp.concatenate([row] * 4, axis=0), L - (pulses - 1), 1)
    skewed = [
        pltpu.roll(jnp.broadcast_to(moved[part : part + 1], (LANES, L)), 0, 1, stride=1, stride_axis=0)
        for part in range(2)
    ]
    for apart in range(1 - columns, columns):
        at = apart % pieces * LANES
        straight, crossed = (skewed[part][:, at : at + LANES] for part in range(2))
        for target, pair in enumerate(((straight, crossed), (-crossed, straight))):
            slot = (apart + columns - 1) * 2 + target
            for part in range(2):
                columns_held[slot, pl.ds(part, LANES, stride=2), :] = pair[part]
            block = columns_held[slot].astype(BF)
            for column in range(columns):
                line = column - apart
                if 0 <= line < columns:
                    lane = target * pulses + column * LANES
                    taps[2 * line * LANES : 2 * (line + 1) * LANES, lane : lane + LANES] = block
    copies = []
    for tile in range(tiles):
        lines = lines_ref[:, tile * rows : (tile + 1) * rows].reshape(sources * rows, LANES)
        focused = lax.dot_general(lines, taps[...], (((0,), (0,)), ((), ())), preferred_element_type=F32)
        for part in range(2):
            for column in range(columns):
                lane = part * pulses + column * LANES
                made[pl.ds(tile * each + 2 * column + part, LANES, stride=2 * columns), :] = focused[
                    :, lane : lane + LANES
                ]
        for piece in range(2):
            into = pl.ds(tile * each + piece * each // 2, each // 2)
            copies.append(pltpu.make_async_copy(made.at[into], out_ref.at[into], sems.at[tile, piece]))
            copies[-1].start(priority=piece)
    for copy in copies:
        copy.wait()


def toeplitz(diagonal_taps, size):
    span_size = 2 * size - 1
    reversed_taps = diagonal_taps[..., ::-1]
    shifted = jnp.concatenate(
        [reversed_taps[..., size - 1 :], reversed_taps[..., : size - 1]], axis=-1
    )
    reps = (1,) * (shifted.ndim - 1) + (size,)
    tiled_flat = jnp.tile(shifted, reps)[..., : size * (span_size - 1)]
    return tiled_flat.reshape(shifted.shape[:-1] + (size, span_size - 1))[..., :size]


def tap_blocks(tap_values, size):
    block_total = tap_values.shape[1] // size + 1
    padded_taps = jnp.pad(tap_values, ((0, 0), (size, 2 * size)))
    matrices = []
    for offset_block in range(block_total):
        first_tap = offset_block * size + 1
        parts = toeplitz(padded_taps[:, first_tap : first_tap + 2 * size - 1], size)
        real_part = parts[0]
        imag_part = parts[1]
        matrices.append(
            jnp.stack([jnp.stack([real_part, -imag_part]), jnp.stack([imag_part, real_part])])
        )
    return jnp.stack(matrices)


def correlate(blocked, matrices, output_count):
    summed = jnp.zeros((blocked.shape[0], 2, output_count, blocked.shape[3]), F32)
    for offset_block in range(matrices.shape[0]):
        piece_rows = blocked[:, :, offset_block : offset_block + output_count, :]
        summed = summed + jnp.einsum(
            "rcib,cdbn->rdin", piece_rows, matrices[offset_block], preferred_element_type=F32
        )
    return summed


def focus_long(range_lines, reference_row):
    block_size = L // 2
    bin_count, _, total_pulses = range_lines.shape
    block_count = total_pulses // block_size
    blocked = range_lines.reshape(bin_count, 2, block_count, block_size)
    blocked = jnp.pad(blocked, ((0, 0), (0, 0), (1, 1), (0, 0)))
    focused = correlate(blocked, tap_blocks(reference_row, block_size), block_count)
    return focused.reshape(1, bin_count, 2, total_pulses)


def call(kernel, outs, specs, scratch=(), vmem=24, flops=1000):
    space = {"s": pltpu.SMEM, "v": pltpu.VMEM, "a": pl.ANY}
    blocks = [pl.BlockSpec(memory_space=space[kind]) for kind in specs]
    return pl.pallas_call(
        kernel,
        out_shape=outs,
        in_specs=blocks[: -len(outs)],
        out_specs=tuple(blocks[-len(outs) :]),
        scratch_shapes=list(scratch),
        compiler_params=pltpu.CompilerParams(vmem_limit_bytes=int(vmem * 2**20)),
        cost_estimate=pl.CostEstimate(flops=flops, bytes_accessed=1000, transcendentals=0),
    )


def on_device(raw_echo, chirp_replica, azimuth_refs, migration_index, window_start):
    pulses = raw_echo.shape[0]
    segment_devices = lax.axis_size("sa")
    pulse_devices = lax.axis_size("pa")
    tap_count = chirp_replica.shape[1]
    kept_width = R // segment_devices
    bin_count = kept_width // pulse_devices
    total_pulses = pulses * pulse_devices
    half = kept_width // LANES
    tap_tiles = tap_count // LANES + 2
    span = half + tap_tiles - 1

    rows = 2 * pulses
    shape = jax.ShapeDtypeStruct
    token = shape((8, LANES), F32)
    short = bin_count % LANES == 0 and total_pulses == L // 2

    targets = pulse_devices if short else half // 8
    slot = half // targets * rows

    tail, turn = call(
        tail_kernel,
        (shape((half, rows, LANES), BF), token),
        "avv",
        [pltpu.VMEM((pulses, 2, half * LANES), BF), pltpu.SemaphoreType.DMA((4,))],
        53,
    )(raw_echo)
    tail = lax.ppermute(tail, "sa", [(0, 1), (1, 3)])
    head, turn = call(head_kernel, (shape((span - half + 16, rows, LANES), BF), token), "vvvv")(turn, raw_echo)
    head = lax.ppermute(head, "sa", [(2, 3)])
    taps, own_rows, turn = call(
        prep_kernel,
        (shape((tap_tiles * LANES, 2 * LANES), BF), shape((pulse_devices, EXTRA, LANES), BF), token),
        "vsvvvvvv",
    )(turn, window_start, migration_index, chirp_replica, azimuth_refs)
    near, turn = call(
        ahead_kernel,
        (shape((targets, slot, LANES), BF), token),
        "vsvvvv",
        [pltpu.VMEM((span, rows, LANES), BF)],
    )(turn, window_start, raw_echo, taps)
    near = lax.ppermute(near, "sa", [(1, 2)])
    extra = own_rows if short else jnp.zeros((targets, EXTRA, LANES), BF)
    made = shape((targets, slot + EXTRA, LANES), BF)
    (early,) = call(
        early_kernel,
        (made,),
        "vsvvvvvv",
        [pltpu.VMEM((span + 16, rows, LANES), BF)],
        flops=10**10,
    )(turn, window_start, raw_echo, tail, head, taps, extra)
    (compressed,) = call(late_kernel, (made,), "vvvv")(near, extra, early)

    if not short:
        kept = compressed[:, :-EXTRA].reshape(half, pulses, 2, LANES).transpose(0, 3, 2, 1)
        outgoing = kept.reshape(pulse_devices, bin_count, 2, pulses)
        turned = lax.all_to_all(outgoing, "pa", split_axis=0, concat_axis=3, tiled=True)
        rows_in = lax.all_to_all(own_rows, "pa", split_axis=0, concat_axis=0, tiled=True)
        reference_row = jnp.sum(rows_in[:, :8].astype(F32), axis=0).astype(BF).reshape(2, L)
        return focus_long(turned[0], reference_row[:, ::-1])

    lines = lax.all_to_all(compressed, "pa", split_axis=0, concat_axis=0, tiled=True)
    width = 2 * total_pulses
    (focused,) = call(
        azimuth_kernel,
        (shape((bin_count * width // LANES, LANES), F32),),
        "va",
        [
            pltpu.VMEM((width // LANES * 2 - 2, 2 * LANES, LANES), F32),
            pltpu.VMEM((width, width), BF),
            pltpu.VMEM((bin_count * width // LANES, LANES), F32),
            pltpu.SemaphoreType.DMA((bin_count // LANES, 2)),
        ],
    )(lines)
    focused = focused.reshape(1, bin_count, total_pulses // LANES, 2, LANES).swapaxes(2, 3)
    return focused.reshape(1, bin_count, 2, total_pulses)


def solution(mesh):
    placed = (P("pa", None, "sa"), P(), P("pa", None, None), P(), P())
    return jax.shard_map(
        on_device, mesh=mesh, in_specs=placed, out_specs=P("sa", "pa", None, None), check_vma=False
    )
```

```python
import jax
import jax.numpy as jnp
from jax import lax
from jax.experimental import pallas as pl
from jax.experimental.pallas import tpu as pltpu
from jax.sharding import PartitionSpec as P

R = 16384
L = 512
LANES = 128
EXTRA = 8
BF = jnp.bfloat16
F32 = jnp.float32


def reversed_lanes(row):
    row_id = lax.broadcasted_iota(jnp.int32, (LANES, LANES), 0)
    col_id = lax.broadcasted_iota(jnp.int32, (LANES, LANES), 1)
    flip = (row_id + col_id == LANES - 1).astype(BF)
    tiles = row.shape[1] // LANES
    pieces = [row[:, t * LANES : (t + 1) * LANES] for t in reversed(range(tiles))]
    return jnp.concatenate([jnp.dot(piece, flip, preferred_element_type=F32) for piece in pieces], axis=1)


def retile(source, target, first, tiles):
    shape = target.shape[1:]
    for t in range(tiles):
        target[first + t] = source[:, :, t * LANES : (t + 1) * LANES].reshape(shape)


def tail_kernel(raw_ref, tail_ref, turn_ref, natural, sems):
    turn_ref[...] = jnp.zeros_like(turn_ref)
    half, rows, _ = tail_ref.shape
    pieces = sems.shape[0]
    each = rows // 2 // pieces
    width = half * LANES

    @pl.when(lax.axis_index("sa") < 2)
    def _():
        copies = []
        for at in range(pieces):
            own = pl.ds(at * each, each)
            source = raw_ref.at[own, :, pl.ds(raw_ref.shape[2] - width, width)]
            copies.append(pltpu.make_async_copy(source, natural.at[own], sems.at[at]))
            copies[-1].start()
        for at, copy in enumerate(copies):
            copy.wait()
            own = pl.ds(at * each, each)
            retile(natural.at[own], tail_ref.at[:, pl.ds(at * each * 2, each * 2)], 0, half)


def head_kernel(turn_in_ref, raw_ref, head_ref, turn_ref):
    turn_ref[...] = turn_in_ref[...]

    @pl.when(lax.axis_index("sa") == 2)
    def _():
        retile(raw_ref, head_ref, 0, head_ref.shape[0])


def prep_kernel(turn_in_ref, window_ref, index_ref, chirp_ref, refs_ref, taps_ref, rows_ref, turn_ref):
    turn_ref[...] = turn_in_ref[...]
    taps = chirp_ref.shape[1]
    blocks = taps_ref.shape[0] // LANES
    width = blocks * LANES
    shift = lax.rem(window_ref[0], LANES)
    chirp = jnp.concatenate([chirp_ref[...], jnp.zeros((14, taps), BF)], axis=0)
    flipped = reversed_lanes(chirp)
    padded = jnp.concatenate([jnp.zeros((16, 2 * LANES), F32), flipped], axis=1)
    padded = jnp.concatenate([padded, jnp.zeros((16, width + LANES - padded.shape[1]), F32)], axis=1)
    moved = pltpu.roll(padded, width + LANES - 127 - shift, 1)[:, :width]
    for part in range(2):
        spread = jnp.broadcast_to(moved[part : part + 1], (LANES, width))
        skewed = pltpu.roll(spread, 0, 1, stride=1, stride_axis=0)
        for t in range(blocks):
            first = LANES * (blocks - 1 - t)
            taps_ref[t * LANES : (t + 1) * LANES, part * LANES : (part + 1) * LANES] = skewed[
                :, first : first + LANES
            ].astype(BF)
    own = refs_ref.shape[0]
    groups, targets = index_ref.shape
    first_row = lax.axis_index("pa") * own
    mine = lax.broadcasted_iota(jnp.int32, (groups, targets), 0) == lax.axis_index("sa")
    wanted = jnp.sum(jnp.where(mine, index_ref[...], 0), axis=0, keepdims=True)
    row_id = lax.broadcasted_iota(jnp.int32, (own, targets), 0) + first_row
    picks = (row_id == jnp.broadcast_to(wanted, (own, targets))).astype(F32)
    pieces = []
    for part in range(2):
        picked = lax.dot_general(
            picks, refs_ref[:, part, :].astype(F32), (((0,), (0,)), ((), ())), preferred_element_type=F32
        )
        picked = reversed_lanes(picked.astype(BF))
        pieces += [picked[:, t * LANES : (t + 1) * LANES] for t in range(L // LANES)]
    pieces += [jnp.zeros((targets, LANES), F32)] * (rows_ref.shape[1] - len(pieces))
    rows_ref[...] = jnp.stack(pieces, axis=1).astype(BF)


def compress(held, base, taps_ref, out_ref):
    rows = held.shape[1]
    targets = out_ref.shape[0]
    tap_tiles = taps_ref.shape[0] // LANES
    group = 16
    per_target = out_ref.shape[1] // rows
    even = lax.rem(lax.broadcasted_iota(jnp.int32, (1, 8, LANES), 1), 2) == 0
    for step in range(targets * per_target // group):
        blocks = [
            held[pl.ds(base + group * step + t, group)].reshape(group * rows, LANES) for t in range(tap_tiles)
        ]
        product = jnp.dot(jnp.concatenate(blocks, axis=1), taps_ref[...], preferred_element_type=F32)
        straight = product[:, :LANES].reshape(-1, 8, LANES)
        crossed = product[:, LANES:].reshape(-1, 8, LANES)
        total = straight + jnp.where(even, pltpu.roll(crossed, 7, 1), -pltpu.roll(crossed, 1, 1))
        count = group // per_target
        out_ref[pl.ds(step * count, count), : per_target * rows] = total.astype(BF).reshape(
            count, per_target * rows, LANES
        )


def ahead_kernel(turn_in_ref, window_ref, raw_ref, taps_ref, out_ref, turn_ref, held):
    turn_ref[...] = turn_in_ref[...]
    span = held.shape[0]

    @pl.when(lax.axis_index("sa") == 1)
    def _():
        start = pl.multiple_of(window_ref[0] // LANES * LANES, LANES)
        retile(raw_ref.at[:, :, pl.ds(start, span * LANES)], held, 0, span)
        compress(held, 0, taps_ref, out_ref)


def early_kernel(turn_in_ref, window_ref, raw_ref, tail_ref, head_ref, taps_ref, rows_ref, out_ref, held):
    half = tail_ref.shape[0]
    more = head_ref.shape[0]
    span = half + more - 16
    sub_index = lax.axis_index("sa")
    offset = window_ref[0] // LANES

    @pl.when(sub_index == 0)
    def _():
        start = pl.multiple_of(offset * LANES, LANES)
        retile(raw_ref.at[:, :, pl.ds(start, span * LANES)], held, 0, span)

    @pl.when(sub_index == 1)
    def _():
        held[:half] = tail_ref[...]
        retile(raw_ref, held, half, more)

    @pl.when(sub_index == 3)
    def _():
        held[:half] = tail_ref[...]
        held[half:] = head_ref[...]

    @pl.when(sub_index != 2)
    def _():
        compress(held, jnp.where(sub_index == 0, 0, offset), taps_ref, out_ref)
        out_ref[:, out_ref.shape[1] - rows_ref.shape[1] :] = rows_ref[...]


def late_kernel(near_ref, rows_ref, early_ref, out_ref):
    bins = near_ref.shape[1]
    sub_index = lax.axis_index("sa")

    @pl.when(sub_index != 2)
    def _():
        out_ref[...] = early_ref[...]

    @pl.when(sub_index == 2)
    def _():
        out_ref[:, :bins] = near_ref[...]
        out_ref[:, bins:] = rows_ref[...]


def azimuth_kernel(lines_ref, out_ref, columns_held, taps, made, sems):
    pulses = taps.shape[0] // 2
    columns = pulses // LANES
    tiles = sems.shape[0]
    each = out_ref.shape[0] // tiles
    sources = lines_ref.shape[0]
    rows = (lines_ref.shape[1] - EXTRA) // tiles
    picked = jnp.sum(lines_ref[:, tiles * rows :].astype(F32), axis=0)
    pieces = L // LANES
    row = jnp.concatenate(
        [
            jnp.concatenate([picked[part * pieces + t : part * pieces + t + 1] for t in range(pieces)], axis=1)
            for part in range(2)
        ],
        axis=0,
    )
    moved = pltpu.roll(jnp.concatenate([row] * 4, axis=0), L - (pulses - 1), 1)
    skewed = [
        pltpu.roll(jnp.broadcast_to(moved[part : part + 1], (LANES, L)), 0, 1, stride=1, stride_axis=0)
        for part in range(2)
    ]
    for apart in range(1 - columns, columns):
        at = apart % pieces * LANES
        straight, crossed = (skewed[part][:, at : at + LANES] for part in range(2))
        for target, pair in enumerate(((straight, crossed), (-crossed, straight))):
            slot = (apart + columns - 1) * 2 + target
            for part in range(2):
                columns_held[slot, pl.ds(part, LANES, stride=2), :] = pair[part]
            block = columns_held[slot].astype(BF)
            for column in range(columns):
                line = column - apart
                if 0 <= line < columns:
                    lane = target * pulses + column * LANES
                    taps[2 * line * LANES : 2 * (line + 1) * LANES, lane : lane + LANES] = block
    copies = []
    for tile in range(tiles):
        lines = lines_ref[:, tile * rows : (tile + 1) * rows].reshape(sources * rows, LANES)
        focused = lax.dot_general(lines, taps[...], (((0,), (0,)), ((), ())), preferred_element_type=F32)
        into = pl.ds(tile * each, each)
        for part in range(2):
            for column in range(columns):
                lane = part * pulses + column * LANES
                made[pl.ds(tile * each + 2 * column + part, LANES, stride=2 * columns), :] = focused[
                    :, lane : lane + LANES
                ]
        copies.append(pltpu.make_async_copy(made.at[into], out_ref.at[into], sems.at[tile]))
        copies[-1].start()
    for copy in copies:
        copy.wait()


def toeplitz(diagonal_taps, size):
    span_size = 2 * size - 1
    reversed_taps = diagonal_taps[..., ::-1]
    shifted = jnp.concatenate(
        [reversed_taps[..., size - 1 :], reversed_taps[..., : size - 1]], axis=-1
    )
    reps = (1,) * (shifted.ndim - 1) + (size,)
    tiled_flat = jnp.tile(shifted, reps)[..., : size * (span_size - 1)]
    return tiled_flat.reshape(shifted.shape[:-1] + (size, span_size - 1))[..., :size]


def tap_blocks(tap_values, size):
    block_total = tap_values.shape[1] // size + 1
    padded_taps = jnp.pad(tap_values, ((0, 0), (size, 2 * size)))
    matrices = []
    for offset_block in range(block_total):
        first_tap = offset_block * size + 1
        parts = toeplitz(padded_taps[:, first_tap : first_tap + 2 * size - 1], size)
        real_part = parts[0]
        imag_part = parts[1]
        matrices.append(
            jnp.stack([jnp.stack([real_part, -imag_part]), jnp.stack([imag_part, real_part])])
        )
    return jnp.stack(matrices)


def correlate(blocked, matrices, output_count):
    summed = jnp.zeros((blocked.shape[0], 2, output_count, blocked.shape[3]), F32)
    for offset_block in range(matrices.shape[0]):
        piece_rows = blocked[:, :, offset_block : offset_block + output_count, :]
        summed = summed + jnp.einsum(
            "rcib,cdbn->rdin", piece_rows, matrices[offset_block], preferred_element_type=F32
        )
    return summed


def focus_long(range_lines, reference_row):
    block_size = L // 2
    bin_count, _, total_pulses = range_lines.shape
    block_count = total_pulses // block_size
    blocked = range_lines.reshape(bin_count, 2, block_count, block_size)
    blocked = jnp.pad(blocked, ((0, 0), (0, 0), (1, 1), (0, 0)))
    focused = correlate(blocked, tap_blocks(reference_row, block_size), block_count)
    return focused.reshape(1, bin_count, 2, total_pulses)


def call(kernel, outs, specs, scratch=(), vmem=24, flops=1000):
    space = {"s": pltpu.SMEM, "v": pltpu.VMEM, "a": pl.ANY}
    blocks = [pl.BlockSpec(memory_space=space[kind]) for kind in specs]
    return pl.pallas_call(
        kernel,
        out_shape=outs,
        in_specs=blocks[: -len(outs)],
        out_specs=tuple(blocks[-len(outs) :]),
        scratch_shapes=list(scratch),
        compiler_params=pltpu.CompilerParams(vmem_limit_bytes=int(vmem * 2**20)),
        cost_estimate=pl.CostEstimate(flops=flops, bytes_accessed=1000, transcendentals=0),
    )


def on_device(raw_echo, chirp_replica, azimuth_refs, migration_index, window_start):
    pulses = raw_echo.shape[0]
    segment_devices = lax.axis_size("sa")
    pulse_devices = lax.axis_size("pa")
    tap_count = chirp_replica.shape[1]
    kept_width = R // segment_devices
    bin_count = kept_width // pulse_devices
    total_pulses = pulses * pulse_devices
    half = kept_width // LANES
    tap_tiles = tap_count // LANES + 2
    span = half + tap_tiles - 1

    rows = 2 * pulses
    shape = jax.ShapeDtypeStruct
    token = shape((8, LANES), F32)
    short = bin_count % LANES == 0 and total_pulses == L // 2

    targets = pulse_devices if short else half // 8
    slot = half // targets * rows

    tail, turn = call(
        tail_kernel,
        (shape((half, rows, LANES), BF), token),
        "avv",
        [pltpu.VMEM((pulses, 2, half * LANES), BF), pltpu.SemaphoreType.DMA((4,))],
        53,
    )(raw_echo)
    tail = lax.ppermute(tail, "sa", [(0, 1), (1, 3)])
    head, turn = call(head_kernel, (shape((span - half + 16, rows, LANES), BF), token), "vvvv")(turn, raw_echo)
    head = lax.ppermute(head, "sa", [(2, 3)])
    taps, own_rows, turn = call(
        prep_kernel,
        (shape((tap_tiles * LANES, 2 * LANES), BF), shape((pulse_devices, EXTRA, LANES), BF), token),
        "vsvvvvvv",
    )(turn, window_start, migration_index, chirp_replica, azimuth_refs)
    near, turn = call(
        ahead_kernel,
        (shape((targets, slot, LANES), BF), token),
        "vsvvvv",
        [pltpu.VMEM((span, rows, LANES), BF)],
    )(turn, window_start, raw_echo, taps)
    near = lax.ppermute(near, "sa", [(1, 2)])
    extra = own_rows if short else jnp.zeros((targets, EXTRA, LANES), BF)
    made = shape((targets, slot + EXTRA, LANES), BF)
    (early,) = call(
        early_kernel,
        (made,),
        "vsvvvvvv",
        [pltpu.VMEM((span + 16, rows, LANES), BF)],
        flops=10**10,
    )(turn, window_start, raw_echo, tail, head, taps, extra)
    (compressed,) = call(late_kernel, (made,), "vvvv")(near, extra, early)

    if not short:
        kept = compressed[:, :-EXTRA].reshape(half, pulses, 2, LANES).transpose(0, 3, 2, 1)
        outgoing = kept.reshape(pulse_devices, bin_count, 2, pulses)
        turned = lax.all_to_all(outgoing, "pa", split_axis=0, concat_axis=3, tiled=True)
        rows_in = lax.all_to_all(own_rows, "pa", split_axis=0, concat_axis=0, tiled=True)
        reference_row = jnp.sum(rows_in[:, :8].astype(F32), axis=0).astype(BF).reshape(2, L)
        return focus_long(turned[0], reference_row[:, ::-1])

    lines = lax.all_to_all(compressed, "pa", split_axis=0, concat_axis=0, tiled=True)
    width = 2 * total_pulses
    (focused,) = call(
        azimuth_kernel,
        (shape((bin_count * width // LANES, LANES), F32),),
        "va",
        [
            pltpu.VMEM((width // LANES * 2 - 2, 2 * LANES, LANES), F32),
            pltpu.VMEM((width, width), BF),
            pltpu.VMEM((bin_count * width // LANES, LANES), F32),
            pltpu.SemaphoreType.DMA((bin_count // LANES,)),
        ],
    )(lines)
    focused = focused.reshape(1, bin_count, total_pulses // LANES, 2, LANES).swapaxes(2, 3)
    return focused.reshape(1, bin_count, 2, total_pulses)


def solution(mesh):
    placed = (P("pa", None, "sa"), P(), P("pa", None, None), P(), P())
    return jax.shard_map(
        on_device, mesh=mesh, in_specs=placed, out_specs=P("sa", "pa", None, None), check_vma=False
    )
```

```python
import jax
import jax.numpy as jnp
from jax import lax
from jax.experimental import pallas as pl
from jax.experimental.pallas import tpu as pltpu
from jax.sharding import PartitionSpec as P

R = 16384
L = 512
LANES = 128
EXTRA = 8
BF = jnp.bfloat16
F32 = jnp.float32


def reversed_lanes(row):
    row_id = lax.broadcasted_iota(jnp.int32, (LANES, LANES), 0)
    col_id = lax.broadcasted_iota(jnp.int32, (LANES, LANES), 1)
    flip = (row_id + col_id == LANES - 1).astype(BF)
    tiles = row.shape[1] // LANES
    pieces = [row[:, t * LANES : (t + 1) * LANES] for t in reversed(range(tiles))]
    return jnp.concatenate([jnp.dot(piece, flip, preferred_element_type=F32) for piece in pieces], axis=1)


def retile(source, target, first, tiles):
    shape = target.shape[1:]
    for t in range(tiles):
        target[first + t] = source[:, :, t * LANES : (t + 1) * LANES].reshape(shape)


def tail_kernel(raw_ref, tail_ref, turn_ref, natural, sems):
    turn_ref[...] = jnp.zeros_like(turn_ref)
    half, rows, _ = tail_ref.shape
    pieces = sems.shape[0]
    each = rows // 2 // pieces
    width = half * LANES

    @pl.when(lax.axis_index("sa") < 2)
    def _():
        copies = []
        for at in range(pieces):
            own = pl.ds(at * each, each)
            source = raw_ref.at[own, :, pl.ds(raw_ref.shape[2] - width, width)]
            copies.append(pltpu.make_async_copy(source, natural.at[own], sems.at[at]))
            copies[-1].start()
        for at, copy in enumerate(copies):
            copy.wait()
            own = pl.ds(at * each, each)
            retile(natural.at[own], tail_ref.at[:, pl.ds(at * each * 2, each * 2)], 0, half)


def head_kernel(turn_in_ref, raw_ref, head_ref, turn_ref):
    turn_ref[...] = turn_in_ref[...]

    @pl.when(lax.axis_index("sa") == 2)
    def _():
        retile(raw_ref, head_ref, 0, head_ref.shape[0])


def prep_kernel(turn_in_ref, window_ref, index_ref, chirp_ref, refs_ref, taps_ref, rows_ref, turn_ref):
    turn_ref[...] = turn_in_ref[...]
    taps = chirp_ref.shape[1]
    blocks = taps_ref.shape[0] // LANES
    width = blocks * LANES
    shift = lax.rem(window_ref[0], LANES)
    chirp = jnp.concatenate([chirp_ref[...], jnp.zeros((14, taps), BF)], axis=0)
    flipped = reversed_lanes(chirp)
    padded = jnp.concatenate([jnp.zeros((16, 2 * LANES), F32), flipped], axis=1)
    padded = jnp.concatenate([padded, jnp.zeros((16, width + LANES - padded.shape[1]), F32)], axis=1)
    moved = pltpu.roll(padded, width + LANES - 127 - shift, 1)[:, :width]
    for part in range(2):
        spread = jnp.broadcast_to(moved[part : part + 1], (LANES, width))
        skewed = pltpu.roll(spread, 0, 1, stride=1, stride_axis=0)
        for t in range(blocks):
            first = LANES * (blocks - 1 - t)
            taps_ref[t * LANES : (t + 1) * LANES, part * LANES : (part + 1) * LANES] = skewed[
                :, first : first + LANES
            ].astype(BF)
    own = refs_ref.shape[0]
    groups, targets = index_ref.shape
    first_row = lax.axis_index("pa") * own
    mine = lax.broadcasted_iota(jnp.int32, (groups, targets), 0) == lax.axis_index("sa")
    wanted = jnp.sum(jnp.where(mine, index_ref[...], 0), axis=0, keepdims=True)
    row_id = lax.broadcasted_iota(jnp.int32, (own, targets), 0) + first_row
    picks = (row_id == jnp.broadcast_to(wanted, (own, targets))).astype(F32)
    pieces = []
    for part in range(2):
        picked = lax.dot_general(
            picks, refs_ref[:, part, :].astype(F32), (((0,), (0,)), ((), ())), preferred_element_type=F32
        )
        picked = reversed_lanes(picked.astype(BF))
        picked = pltpu.roll(picked, L // 2 + 1, 1)
        pieces += [picked[:, t * LANES : (t + 1) * LANES] for t in range(L // LANES)]
    pieces += [jnp.zeros((targets, LANES), F32)] * (rows_ref.shape[1] - len(pieces))
    rows_ref[...] = jnp.stack(pieces, axis=1).astype(BF)


def compress(held, base, taps_ref, out_ref):
    rows = held.shape[1]
    targets = out_ref.shape[0]
    tap_tiles = taps_ref.shape[0] // LANES
    group = 8
    per_target = out_ref.shape[1] // rows
    even = lax.rem(lax.broadcasted_iota(jnp.int32, (1, 8, LANES), 1), 2) == 0
    for step in range(targets * per_target // group):
        blocks = [
            held[pl.ds(base + group * step + t, group)].reshape(group * rows, LANES) for t in range(tap_tiles)
        ]
        product = jnp.dot(jnp.concatenate(blocks, axis=1), taps_ref[...], preferred_element_type=F32)
        straight = product[:, :LANES].reshape(-1, 8, LANES)
        crossed = product[:, LANES:].reshape(-1, 8, LANES)
        total = straight + jnp.where(even, pltpu.roll(crossed, 7, 1), -pltpu.roll(crossed, 1, 1))
        count = group // per_target
        out_ref[pl.ds(step * count, count), : per_target * rows] = total.astype(BF).reshape(
            count, per_target * rows, LANES
        )


def ahead_kernel(turn_in_ref, window_ref, raw_ref, taps_ref, out_ref, turn_ref, held):
    turn_ref[...] = turn_in_ref[...]
    span = held.shape[0]

    @pl.when(lax.axis_index("sa") == 1)
    def _():
        start = pl.multiple_of(window_ref[0] // LANES * LANES, LANES)
        retile(raw_ref.at[:, :, pl.ds(start, span * LANES)], held, 0, span)
        compress(held, 0, taps_ref, out_ref)


def early_kernel(turn_in_ref, window_ref, raw_ref, tail_ref, head_ref, taps_ref, rows_ref, out_ref, held):
    half = tail_ref.shape[0]
    more = head_ref.shape[0]
    span = half + more - 16
    sub_index = lax.axis_index("sa")
    offset = window_ref[0] // LANES

    @pl.when(sub_index == 0)
    def _():
        start = pl.multiple_of(offset * LANES, LANES)
        retile(raw_ref.at[:, :, pl.ds(start, span * LANES)], held, 0, span)

    @pl.when(sub_index == 1)
    def _():
        held[:half] = tail_ref[...]
        retile(raw_ref, held, half, more)

    @pl.when(sub_index == 3)
    def _():
        held[:half] = tail_ref[...]
        held[half:] = head_ref[...]

    @pl.when(sub_index != 2)
    def _():
        compress(held, jnp.where(sub_index == 0, 0, offset), taps_ref, out_ref)
        out_ref[:, out_ref.shape[1] - rows_ref.shape[1] :] = rows_ref[...]


def late_kernel(near_ref, rows_ref, early_ref, out_ref):
    bins = near_ref.shape[1]
    sub_index = lax.axis_index("sa")

    @pl.when(sub_index != 2)
    def _():
        out_ref[...] = early_ref[...]

    @pl.when(sub_index == 2)
    def _():
        out_ref[:, :bins] = near_ref[...]
        out_ref[:, bins:] = rows_ref[...]


def azimuth_kernel(lines_ref, out_ref, columns_held, taps, made, sems):
    pulses = taps.shape[0] // 2
    columns = pulses // LANES
    tiles = sems.shape[0]
    each = out_ref.shape[0] // tiles
    sources = lines_ref.shape[0]
    rows = (lines_ref.shape[1] - EXTRA) // tiles
    picked = jnp.sum(lines_ref[:, tiles * rows :].astype(F32), axis=0)
    pieces = L // LANES
    skewed = []
    for part in range(2):
        spread = [jnp.broadcast_to(picked[part * pieces + t][None], (LANES, LANES)) for t in range(pieces)]
        skewed.append(pltpu.roll(jnp.concatenate(spread, axis=1), 0, 1, stride=1, stride_axis=0))
    for apart in range(1 - columns, columns):
        at = apart % pieces * LANES
        straight, crossed = (skewed[part][:, at : at + LANES] for part in range(2))
        for target, pair in enumerate(((straight, crossed), (-crossed, straight))):
            slot = (apart + columns - 1) * 2 + target
            for part in range(2):
                columns_held[slot, pl.ds(part, LANES, stride=2), :] = pair[part]
            block = columns_held[slot].astype(BF)
            for column in range(columns):
                line = column - apart
                if 0 <= line < columns:
                    lane = target * pulses + column * LANES
                    taps[2 * line * LANES : 2 * (line + 1) * LANES, lane : lane + LANES] = block
    copies = []
    for tile in range(tiles):
        lines = lines_ref[:, tile * rows : (tile + 1) * rows].reshape(sources * rows, LANES)
        focused = lax.dot_general(lines, taps[...], (((0,), (0,)), ((), ())), preferred_element_type=F32)
        into = pl.ds(tile * each, each)
        for part in range(2):
            for column in range(columns):
                lane = part * pulses + column * LANES
                made[pl.ds(tile * each + 2 * column + part, LANES, stride=2 * columns), :] = focused[
                    :, lane : lane + LANES
                ]
        copies.append(pltpu.make_async_copy(made.at[into], out_ref.at[into], sems.at[tile]))
        copies[-1].start()
    for copy in copies:
        copy.wait()


def toeplitz(diagonal_taps, size):
    span_size = 2 * size - 1
    reversed_taps = diagonal_taps[..., ::-1]
    shifted = jnp.concatenate(
        [reversed_taps[..., size - 1 :], reversed_taps[..., : size - 1]], axis=-1
    )
    reps = (1,) * (shifted.ndim - 1) + (size,)
    tiled_flat = jnp.tile(shifted, reps)[..., : size * (span_size - 1)]
    return tiled_flat.reshape(shifted.shape[:-1] + (size, span_size - 1))[..., :size]


def tap_blocks(tap_values, size):
    block_total = tap_values.shape[1] // size + 1
    padded_taps = jnp.pad(tap_values, ((0, 0), (size, 2 * size)))
    matrices = []
    for offset_block in range(block_total):
        first_tap = offset_block * size + 1
        parts = toeplitz(padded_taps[:, first_tap : first_tap + 2 * size - 1], size)
        real_part = parts[0]
        imag_part = parts[1]
        matrices.append(
            jnp.stack([jnp.stack([real_part, -imag_part]), jnp.stack([imag_part, real_part])])
        )
    return jnp.stack(matrices)


def correlate(blocked, matrices, output_count):
    summed = jnp.zeros((blocked.shape[0], 2, output_count, blocked.shape[3]), F32)
    for offset_block in range(matrices.shape[0]):
        piece_rows = blocked[:, :, offset_block : offset_block + output_count, :]
        summed = summed + jnp.einsum(
            "rcib,cdbn->rdin", piece_rows, matrices[offset_block], preferred_element_type=F32
        )
    return summed


def focus_long(range_lines, reference_row):
    block_size = L // 2
    bin_count, _, total_pulses = range_lines.shape
    block_count = total_pulses // block_size
    blocked = range_lines.reshape(bin_count, 2, block_count, block_size)
    blocked = jnp.pad(blocked, ((0, 0), (0, 0), (1, 1), (0, 0)))
    focused = correlate(blocked, tap_blocks(reference_row, block_size), block_count)
    return focused.reshape(1, bin_count, 2, total_pulses)


def call(kernel, outs, specs, scratch=(), vmem=24, flops=1000):
    space = {"s": pltpu.SMEM, "v": pltpu.VMEM, "a": pl.ANY}
    blocks = [pl.BlockSpec(memory_space=space[kind]) for kind in specs]
    return pl.pallas_call(
        kernel,
        out_shape=outs,
        in_specs=blocks[: -len(outs)],
        out_specs=tuple(blocks[-len(outs) :]),
        scratch_shapes=list(scratch),
        compiler_params=pltpu.CompilerParams(vmem_limit_bytes=int(vmem * 2**20)),
        cost_estimate=pl.CostEstimate(flops=flops, bytes_accessed=1000, transcendentals=0),
    )


def on_device(raw_echo, chirp_replica, azimuth_refs, migration_index, window_start):
    pulses = raw_echo.shape[0]
    segment_devices = lax.axis_size("sa")
    pulse_devices = lax.axis_size("pa")
    tap_count = chirp_replica.shape[1]
    kept_width = R // segment_devices
    bin_count = kept_width // pulse_devices
    total_pulses = pulses * pulse_devices
    half = kept_width // LANES
    tap_tiles = tap_count // LANES + 2
    span = half + tap_tiles - 1

    rows = 2 * pulses
    shape = jax.ShapeDtypeStruct
    token = shape((8, LANES), F32)
    short = bin_count % LANES == 0 and total_pulses == L // 2

    targets = pulse_devices if short else half // 8
    slot = half // targets * rows

    tail, turn = call(
        tail_kernel,
        (shape((half, rows, LANES), BF), token),
        "avv",
        [pltpu.VMEM((pulses, 2, half * LANES), BF), pltpu.SemaphoreType.DMA((4,))],
        53,
    )(raw_echo)
    tail = lax.ppermute(tail, "sa", [(0, 1), (1, 3)])
    head, turn = call(head_kernel, (shape((span - half + 16, rows, LANES), BF), token), "vvvv")(turn, raw_echo)
    head = lax.ppermute(head, "sa", [(2, 3)])
    taps, own_rows, turn = call(
        prep_kernel,
        (shape((tap_tiles * LANES, 2 * LANES), BF), shape((pulse_devices, EXTRA, LANES), BF), token),
        "vsvvvvvv",
    )(turn, window_start, migration_index, chirp_replica, azimuth_refs)
    near, turn = call(
        ahead_kernel,
        (shape((targets, slot, LANES), BF), token),
        "vsvvvv",
        [pltpu.VMEM((span, rows, LANES), BF)],
    )(turn, window_start, raw_echo, taps)
    near = lax.ppermute(near, "sa", [(1, 2)])
    extra = own_rows if short else jnp.zeros((targets, EXTRA, LANES), BF)
    made = shape((targets, slot + EXTRA, LANES), BF)
    (early,) = call(
        early_kernel,
        (made,),
        "vsvvvvvv",
        [pltpu.VMEM((span + 16, rows, LANES), BF)],
        flops=10**10,
    )(turn, window_start, raw_echo, tail, head, taps, extra)
    (compressed,) = call(late_kernel, (made,), "vvvv")(near, extra, early)

    if not short:
        kept = compressed[:, :-EXTRA].reshape(half, pulses, 2, LANES).transpose(0, 3, 2, 1)
        outgoing = kept.reshape(pulse_devices, bin_count, 2, pulses)
        turned = lax.all_to_all(outgoing, "pa", split_axis=0, concat_axis=3, tiled=True)
        rows_in = lax.all_to_all(own_rows, "pa", split_axis=0, concat_axis=0, tiled=True)
        reference_row = jnp.sum(rows_in[:, :8].astype(F32), axis=0).astype(BF).reshape(2, L)
        reference_row = jnp.roll(reference_row, -(L // 2 + 1), axis=1)[:, ::-1]
        return focus_long(turned[0], reference_row)

    lines = lax.all_to_all(compressed, "pa", split_axis=0, concat_axis=0, tiled=True)
    width = 2 * total_pulses
    (focused,) = call(
        azimuth_kernel,
        (shape((bin_count * width // LANES, LANES), F32),),
        "va",
        [
            pltpu.VMEM((width // LANES * 2 - 2, 2 * LANES, LANES), F32),
            pltpu.VMEM((width, width), BF),
            pltpu.VMEM((bin_count * width // LANES, LANES), F32),
            pltpu.SemaphoreType.DMA((bin_count // LANES,)),
        ],
    )(lines)
    focused = focused.reshape(1, bin_count, total_pulses // LANES, 2, LANES).swapaxes(2, 3)
    return focused.reshape(1, bin_count, 2, total_pulses)


def solution(mesh):
    placed = (P("pa", None, "sa"), P(), P("pa", None, None), P(), P())
    return jax.shard_map(
        on_device, mesh=mesh, in_specs=placed, out_specs=P("sa", "pa", None, None), check_vma=False
    )
```

```python
import jax
import jax.numpy as jnp
from jax import lax
from jax.experimental import pallas as pl
from jax.experimental.pallas import tpu as pltpu
from jax.sharding import PartitionSpec as P

R = 16384
L = 512
LANES = 128
EXTRA = 16
BF = jnp.bfloat16
F32 = jnp.float32


def reversed_lanes(row):
    row_id = lax.broadcasted_iota(jnp.int32, (LANES, LANES), 0)
    col_id = lax.broadcasted_iota(jnp.int32, (LANES, LANES), 1)
    flip = (row_id + col_id == LANES - 1).astype(BF)
    tiles = row.shape[1] // LANES
    pieces = [row[:, t * LANES : (t + 1) * LANES] for t in reversed(range(tiles))]
    return jnp.concatenate([jnp.dot(piece, flip, preferred_element_type=F32) for piece in pieces], axis=1)


def retile(source, target, first, tiles):
    shape = target.shape[1:]
    for t in range(tiles):
        target[first + t] = source[:, :, t * LANES : (t + 1) * LANES].reshape(shape)


def tail_kernel(raw_ref, tail_ref, turn_ref, natural, sems):
    turn_ref[...] = jnp.zeros_like(turn_ref)
    half, rows, _ = tail_ref.shape
    pieces = sems.shape[0]
    each = rows // 2 // pieces
    width = half * LANES

    @pl.when(lax.axis_index("sa") < 2)
    def _():
        copies = []
        for at in range(pieces):
            own = pl.ds(at * each, each)
            source = raw_ref.at[own, :, pl.ds(raw_ref.shape[2] - width, width)]
            copies.append(pltpu.make_async_copy(source, natural.at[own, :, pl.ds(0, width)], sems.at[at]))
            copies[-1].start()
        for at, copy in enumerate(copies):
            copy.wait()
            own = pl.ds(at * each, each)
            retile(natural.at[own], tail_ref.at[:, pl.ds(at * each * 2, each * 2)], 0, half)


def head_kernel(turn_in_ref, raw_ref, head_ref, turn_ref):
    turn_ref[...] = turn_in_ref[...]

    @pl.when(lax.axis_index("sa") == 2)
    def _():
        retile(raw_ref, head_ref, 0, head_ref.shape[0])


def prep_kernel(turn_in_ref, window_ref, index_ref, chirp_ref, refs_ref, taps_ref, rows_ref, turn_ref):
    turn_ref[...] = turn_in_ref[...]
    taps = chirp_ref.shape[1]
    blocks = taps_ref.shape[0] // LANES
    width = blocks * LANES
    shift = lax.rem(window_ref[0], LANES)
    chirp = jnp.concatenate([chirp_ref[...], jnp.zeros((14, taps), BF)], axis=0)
    flipped = reversed_lanes(chirp)
    padded = jnp.concatenate([jnp.zeros((16, 2 * LANES), F32), flipped], axis=1)
    padded = jnp.concatenate([padded, jnp.zeros((16, width + LANES - padded.shape[1]), F32)], axis=1)
    moved = pltpu.roll(padded, width + LANES - 127 - shift, 1)[:, :width]
    for part in range(2):
        spread = jnp.broadcast_to(moved[part : part + 1], (LANES, width))
        skewed = pltpu.roll(spread, 0, 1, stride=1, stride_axis=0)
        for t in range(blocks):
            first = LANES * (blocks - 1 - t)
            taps_ref[t * LANES : (t + 1) * LANES, part * LANES : (part + 1) * LANES] = skewed[
                :, first : first + LANES
            ].astype(BF)
    own = refs_ref.shape[0]
    groups, targets = index_ref.shape
    first_row = lax.axis_index("pa") * own
    mine = lax.broadcasted_iota(jnp.int32, (groups, targets), 0) == lax.axis_index("sa")
    wanted = jnp.sum(jnp.where(mine, index_ref[...], 0), axis=0, keepdims=True)
    row_id = lax.broadcasted_iota(jnp.int32, (own, targets), 0) + first_row
    picks = (row_id == jnp.broadcast_to(wanted, (own, targets))).astype(F32)
    pieces = []
    for part in range(2):
        picked = lax.dot_general(
            picks, refs_ref[:, part, :].astype(F32), (((0,), (0,)), ((), ())), preferred_element_type=F32
        )
        picked = reversed_lanes(picked.astype(BF))
        picked = pltpu.roll(picked, L // 2 + 1, 1)
        pieces += [picked[:, t * LANES : (t + 1) * LANES] for t in range(L // LANES)]
    pieces += [jnp.zeros((targets, LANES), F32)] * (rows_ref.shape[1] - len(pieces))
    rows_ref[...] = jnp.stack(pieces, axis=1).astype(BF)


def compress(held, base, taps_ref, out_ref):
    rows = held.shape[1]
    targets = out_ref.shape[0]
    tap_tiles = taps_ref.shape[0] // LANES
    group = 8
    per_target = out_ref.shape[1] // rows
    even = lax.rem(lax.broadcasted_iota(jnp.int32, (1, 8, LANES), 1), 2) == 0
    for step in range(targets * per_target // group):
        blocks = [
            held[pl.ds(base + group * step + t, group)].reshape(group * rows, LANES) for t in range(tap_tiles)
        ]
        product = jnp.dot(jnp.concatenate(blocks, axis=1), taps_ref[...], preferred_element_type=F32)
        straight = product[:, :LANES].reshape(-1, 8, LANES)
        crossed = product[:, LANES:].reshape(-1, 8, LANES)
        total = straight + jnp.where(even, pltpu.roll(crossed, 7, 1), -pltpu.roll(crossed, 1, 1))
        count = group // per_target
        out_ref[pl.ds(step * count, count), : per_target * rows] = total.astype(BF).reshape(
            count, per_target * rows, LANES
        )


def ahead_kernel(turn_in_ref, window_ref, raw_ref, taps_ref, out_ref, turn_ref, held):
    turn_ref[...] = turn_in_ref[...]
    span = held.shape[0]

    @pl.when(lax.axis_index("sa") == 1)
    def _():
        start = pl.multiple_of(window_ref[0] // LANES * LANES, LANES)
        retile(raw_ref.at[:, :, pl.ds(start, span * LANES)], held, 0, span)
        compress(held, 0, taps_ref, out_ref)


def early_kernel(turn_in_ref, window_ref, raw_ref, tail_ref, head_ref, taps_ref, rows_ref, out_ref, held):
    half = tail_ref.shape[0]
    more = head_ref.shape[0]
    span = half + more - 16
    sub_index = lax.axis_index("sa")
    offset = window_ref[0] // LANES

    @pl.when(sub_index == 0)
    def _():
        start = pl.multiple_of(offset * LANES, LANES)
        retile(raw_ref.at[:, :, pl.ds(start, span * LANES)], held, 0, span)

    @pl.when(sub_index == 1)
    def _():
        held[:half] = tail_ref[...]
        retile(raw_ref, held, half, more)

    @pl.when(sub_index == 3)
    def _():
        held[:half] = tail_ref[...]
        held[half:] = head_ref[...]

    @pl.when(sub_index != 2)
    def _():
        compress(held, jnp.where(sub_index == 0, 0, offset), taps_ref, out_ref)
        out_ref[:, out_ref.shape[1] - rows_ref.shape[1] :] = rows_ref[...]


def late_kernel(near_ref, rows_ref, early_ref, out_ref):
    bins = near_ref.shape[1]
    sub_index = lax.axis_index("sa")

    @pl.when(sub_index != 2)
    def _():
        out_ref[...] = early_ref[...]

    @pl.when(sub_index == 2)
    def _():
        out_ref[:, :bins] = near_ref[...]
        out_ref[:, bins:] = rows_ref[...]


def azimuth_kernel(lines_ref, out_ref, columns_held, taps, made, sems):
    pulses = taps.shape[0] // 2
    columns = pulses // LANES
    tiles = sems.shape[0]
    each = out_ref.shape[0] // tiles
    sources = lines_ref.shape[0]
    rows = (lines_ref.shape[1] - EXTRA) // tiles
    picked = jnp.sum(lines_ref[:, tiles * rows :].astype(F32), axis=0)
    pieces = L // LANES
    skewed = []
    for part in range(2):
        spread = [jnp.broadcast_to(picked[part * pieces + t][None], (LANES, LANES)) for t in range(pieces)]
        skewed.append(pltpu.roll(jnp.concatenate(spread, axis=1), 0, 1, stride=1, stride_axis=0))
    for apart in range(1 - columns, columns):
        at = apart % pieces * LANES
        straight, crossed = (skewed[part][:, at : at + LANES] for part in range(2))
        for target, pair in enumerate(((straight, crossed), (-crossed, straight))):
            slot = (apart + columns - 1) * 2 + target
            for part in range(2):
                columns_held[slot, pl.ds(part, LANES, stride=2), :] = pair[part]
            block = columns_held[slot].astype(BF)
            for column in range(columns):
                line = column - apart
                if 0 <= line < columns:
                    lane = target * pulses + column * LANES
                    taps[2 * line * LANES : 2 * (line + 1) * LANES, lane : lane + LANES] = block
    copies = []
    for tile in range(tiles):
        lines = lines_ref[:, tile * rows : (tile + 1) * rows].reshape(sources * rows, LANES)
        focused = lax.dot_general(lines, taps[...], (((0,), (0,)), ((), ())), preferred_element_type=F32)
        into = pl.ds(tile * each, each)
        for part in range(2):
            for column in range(columns):
                lane = part * pulses + column * LANES
                made[pl.ds(tile * each + 2 * column + part, LANES, stride=2 * columns), :] = focused[
                    :, lane : lane + LANES
                ]
        copies.append(pltpu.make_async_copy(made.at[into], out_ref.at[into], sems.at[tile]))
        copies[-1].start()
    for copy in copies:
        copy.wait()


def toeplitz(diagonal_taps, size):
    span_size = 2 * size - 1
    reversed_taps = diagonal_taps[..., ::-1]
    shifted = jnp.concatenate(
        [reversed_taps[..., size - 1 :], reversed_taps[..., : size - 1]], axis=-1
    )
    reps = (1,) * (shifted.ndim - 1) + (size,)
    tiled_flat = jnp.tile(shifted, reps)[..., : size * (span_size - 1)]
    return tiled_flat.reshape(shifted.shape[:-1] + (size, span_size - 1))[..., :size]


def tap_blocks(tap_values, size):
    block_total = tap_values.shape[1] // size + 1
    padded_taps = jnp.pad(tap_values, ((0, 0), (size, 2 * size)))
    matrices = []
    for offset_block in range(block_total):
        first_tap = offset_block * size + 1
        parts = toeplitz(padded_taps[:, first_tap : first_tap + 2 * size - 1], size)
        real_part = parts[0]
        imag_part = parts[1]
        matrices.append(
            jnp.stack([jnp.stack([real_part, -imag_part]), jnp.stack([imag_part, real_part])])
        )
    return jnp.stack(matrices)


def correlate(blocked, matrices, output_count):
    summed = jnp.zeros((blocked.shape[0], 2, output_count, blocked.shape[3]), F32)
    for offset_block in range(matrices.shape[0]):
        piece_rows = blocked[:, :, offset_block : offset_block + output_count, :]
        summed = summed + jnp.einsum(
            "rcib,cdbn->rdin", piece_rows, matrices[offset_block], preferred_element_type=F32
        )
    return summed


def focus_long(range_lines, reference_row):
    block_size = L // 2
    bin_count, _, total_pulses = range_lines.shape
    block_count = total_pulses // block_size
    blocked = range_lines.reshape(bin_count, 2, block_count, block_size)
    blocked = jnp.pad(blocked, ((0, 0), (0, 0), (1, 1), (0, 0)))
    focused = correlate(blocked, tap_blocks(reference_row, block_size), block_count)
    return focused.reshape(1, bin_count, 2, total_pulses)


def call(kernel, outs, specs, scratch=(), vmem=24, flops=1000):
    space = {"s": pltpu.SMEM, "v": pltpu.VMEM, "a": pl.ANY}
    blocks = [pl.BlockSpec(memory_space=space[kind]) for kind in specs]
    return pl.pallas_call(
        kernel,
        out_shape=outs,
        in_specs=blocks[: -len(outs)],
        out_specs=tuple(blocks[-len(outs) :]),
        scratch_shapes=list(scratch),
        compiler_params=pltpu.CompilerParams(vmem_limit_bytes=int(vmem * 2**20)),
        cost_estimate=pl.CostEstimate(flops=flops, bytes_accessed=1000, transcendentals=0),
    )


def on_device(raw_echo, chirp_replica, azimuth_refs, migration_index, window_start):
    pulses = raw_echo.shape[0]
    segment_devices = lax.axis_size("sa")
    pulse_devices = lax.axis_size("pa")
    tap_count = chirp_replica.shape[1]
    kept_width = R // segment_devices
    bin_count = kept_width // pulse_devices
    total_pulses = pulses * pulse_devices
    half = kept_width // LANES
    tap_tiles = tap_count // LANES + 2
    span = half + tap_tiles - 1

    rows = 2 * pulses
    shape = jax.ShapeDtypeStruct
    token = shape((8, LANES), F32)
    short = bin_count % LANES == 0 and total_pulses == L // 2

    targets = pulse_devices if short else half // 8
    slot = half // targets * rows

    tail, turn = call(
        tail_kernel,
        (shape((half, rows, LANES), BF), token),
        "avv",
        [pltpu.VMEM((pulses, 2, (half + 8) * LANES), BF), pltpu.SemaphoreType.DMA((4,))],
        53,
    )(raw_echo)
    tail = lax.ppermute(tail, "sa", [(0, 1), (1, 3)])
    head, turn = call(head_kernel, (shape((span - half + 16, rows, LANES), BF), token), "vvvv")(turn, raw_echo)
    head = lax.ppermute(head, "sa", [(2, 3)])
    taps, own_rows, turn = call(
        prep_kernel,
        (shape((tap_tiles * LANES, 2 * LANES), BF), shape((pulse_devices, EXTRA, LANES), BF), token),
        "vsvvvvvv",
    )(turn, window_start, migration_index, chirp_replica, azimuth_refs)
    near, turn = call(
        ahead_kernel,
        (shape((targets, slot, LANES), BF), token),
        "vsvvvv",
        [pltpu.VMEM((span, rows, LANES), BF)],
    )(turn, window_start, raw_echo, taps)
    near = lax.ppermute(near, "sa", [(1, 2)])
    extra = own_rows if short else jnp.zeros((targets, EXTRA, LANES), BF)
    made = shape((targets, slot + EXTRA, LANES), BF)
    (early,) = call(
        early_kernel,
        (made,),
        "vsvvvvvv",
        [pltpu.VMEM((span + 16, rows, LANES), BF)],
        flops=10**10,
    )(turn, window_start, raw_echo, tail, head, taps, extra)
    (compressed,) = call(late_kernel, (made,), "vvvv")(near, extra, early)

    if not short:
        kept = compressed[:, :-EXTRA].reshape(half, pulses, 2, LANES).transpose(0, 3, 2, 1)
        outgoing = kept.reshape(pulse_devices, bin_count, 2, pulses)
        turned = lax.all_to_all(outgoing, "pa", split_axis=0, concat_axis=3, tiled=True)
        rows_in = lax.all_to_all(own_rows, "pa", split_axis=0, concat_axis=0, tiled=True)
        reference_row = jnp.sum(rows_in[:, :8].astype(F32), axis=0).astype(BF).reshape(2, L)
        reference_row = jnp.roll(reference_row, -(L // 2 + 1), axis=1)[:, ::-1]
        return focus_long(turned[0], reference_row)

    lines = lax.all_to_all(compressed, "pa", split_axis=0, concat_axis=0, tiled=True)
    width = 2 * total_pulses
    (focused,) = call(
        azimuth_kernel,
        (shape((bin_count * width // LANES, LANES), F32),),
        "va",
        [
            pltpu.VMEM((width // LANES * 2 - 1, 2 * LANES, LANES), F32),
            pltpu.VMEM((width, width), BF),
            pltpu.VMEM((bin_count * width // LANES + 8, LANES), F32),
            pltpu.SemaphoreType.DMA((bin_count // LANES,)),
        ],
    )(lines)
    focused = focused.reshape(1, bin_count, total_pulses // LANES, 2, LANES).swapaxes(2, 3)
    return focused.reshape(1, bin_count, 2, total_pulses)


def solution(mesh):
    placed = (P("pa", None, "sa"), P(), P("pa", None, None), P(), P())
    return jax.shard_map(
        on_device, mesh=mesh, in_specs=placed, out_specs=P("sa", "pa", None, None), check_vma=False
    )
```

```python
import jax
import jax.numpy as jnp
from jax import lax
from jax.experimental import pallas as pl
from jax.experimental.pallas import tpu as pltpu
from jax.sharding import PartitionSpec as P

R = 16384
L = 512
LANES = 128
EXTRA = 16
BF = jnp.bfloat16
F32 = jnp.float32


def reversed_lanes(row):
    row_id = lax.broadcasted_iota(jnp.int32, (LANES, LANES), 0)
    col_id = lax.broadcasted_iota(jnp.int32, (LANES, LANES), 1)
    flip = (row_id + col_id == LANES - 1).astype(BF)
    tiles = row.shape[1] // LANES
    pieces = [row[:, t * LANES : (t + 1) * LANES] for t in reversed(range(tiles))]
    return jnp.concatenate([jnp.dot(piece, flip, preferred_element_type=F32) for piece in pieces], axis=1)


def retile(source, target, first, tiles):
    shape = target.shape[1:]
    for t in range(tiles):
        target[first + t] = source[:, :, t * LANES : (t + 1) * LANES].reshape(shape)


def tail_kernel(raw_ref, tail_ref, turn_ref, natural, sems):
    turn_ref[...] = jnp.zeros_like(turn_ref)
    half, rows, _ = tail_ref.shape
    pieces = sems.shape[0]
    each = rows // 2 // pieces
    width = half * LANES

    @pl.when(lax.axis_index("sa") < 2)
    def _():
        copies = []
        for at in range(pieces):
            own = pl.ds(at * each, each)
            source = raw_ref.at[own, :, pl.ds(raw_ref.shape[2] - width, width)]
            copies.append(pltpu.make_async_copy(source, natural.at[own, :, pl.ds(0, width)], sems.at[at]))
            copies[-1].start()
        for at, copy in enumerate(copies):
            copy.wait()
            own = pl.ds(at * each, each)
            retile(natural.at[own], tail_ref.at[:, pl.ds(at * each * 2, each * 2)], 0, half)


def head_kernel(turn_in_ref, raw_ref, head_ref, turn_ref):
    turn_ref[...] = turn_in_ref[...]

    @pl.when(lax.axis_index("sa") == 2)
    def _():
        retile(raw_ref, head_ref, 0, head_ref.shape[0])


def prep_kernel(turn_in_ref, window_ref, index_ref, chirp_ref, refs_ref, taps_ref, rows_ref, turn_ref):
    turn_ref[...] = turn_in_ref[...]
    taps = chirp_ref.shape[1]
    blocks = taps_ref.shape[0] // LANES
    width = blocks * LANES
    shift = lax.rem(window_ref[0], LANES)
    chirp = jnp.concatenate([chirp_ref[...], jnp.zeros((14, taps), BF)], axis=0)
    flipped = reversed_lanes(chirp)
    padded = jnp.concatenate([jnp.zeros((16, 2 * LANES), F32), flipped], axis=1)
    padded = jnp.concatenate([padded, jnp.zeros((16, width + LANES - padded.shape[1]), F32)], axis=1)
    moved = pltpu.roll(padded, width + LANES - 127 - shift, 1)[:, :width]
    for part in range(2):
        spread = jnp.broadcast_to(moved[part : part + 1], (LANES, width))
        skewed = pltpu.roll(spread, 0, 1, stride=1, stride_axis=0)
        for t in range(blocks):
            first = LANES * (blocks - 1 - t)
            taps_ref[t * LANES : (t + 1) * LANES, part * LANES : (part + 1) * LANES] = skewed[
                :, first : first + LANES
            ].astype(BF)
    own = refs_ref.shape[0]
    groups, targets = index_ref.shape
    first_row = lax.axis_index("pa") * own
    mine = lax.broadcasted_iota(jnp.int32, (groups, targets), 0) == lax.axis_index("sa")
    wanted = jnp.sum(jnp.where(mine, index_ref[...], 0), axis=0, keepdims=True)
    row_id = lax.broadcasted_iota(jnp.int32, (own, targets), 0) + first_row
    picks = (row_id == jnp.broadcast_to(wanted, (own, targets))).astype(F32)
    pieces = []
    for part in range(2):
        picked = lax.dot_general(
            picks, refs_ref[:, part, :].astype(F32), (((0,), (0,)), ((), ())), preferred_element_type=F32
        )
        picked = reversed_lanes(picked.astype(BF))
        picked = pltpu.roll(picked, L // 2 + 1, 1)
        pieces += [picked[:, t * LANES : (t + 1) * LANES] for t in range(L // LANES)]
    pieces += [jnp.zeros((targets, LANES), F32)] * (rows_ref.shape[1] - len(pieces))
    rows_ref[...] = jnp.stack(pieces, axis=1).astype(BF)


def compress(held, base, taps_ref, out_ref, opening=None):
    rows = held.shape[1]
    targets = out_ref.shape[0]
    tap_tiles = taps_ref.shape[0] // LANES
    group = 8
    per_target = out_ref.shape[1] // rows
    even = lax.rem(lax.broadcasted_iota(jnp.int32, (1, 8, LANES), 1), 2) == 0
    for step in range(targets * per_target // group):
        source = held if step or opening is None else opening
        blocks = [
            source[pl.ds(base + group * step + t, group)].reshape(group * rows, LANES) for t in range(tap_tiles)
        ]
        product = jnp.dot(jnp.concatenate(blocks, axis=1), taps_ref[...], preferred_element_type=F32)
        straight = product[:, :LANES].reshape(-1, 8, LANES)
        crossed = product[:, LANES:].reshape(-1, 8, LANES)
        total = straight + jnp.where(even, pltpu.roll(crossed, 7, 1), -pltpu.roll(crossed, 1, 1))
        count = group // per_target
        out_ref[pl.ds(step * count, count), : per_target * rows] = total.astype(BF).reshape(
            count, per_target * rows, LANES
        )


def ahead_kernel(turn_in_ref, window_ref, raw_ref, taps_ref, out_ref, turn_ref, held):
    turn_ref[...] = turn_in_ref[...]
    span = held.shape[0]

    @pl.when(lax.axis_index("sa") == 1)
    def _():
        start = pl.multiple_of(window_ref[0] // LANES * LANES, LANES)
        retile(raw_ref.at[:, :, pl.ds(start, span * LANES)], held, 0, span)
        compress(held, 0, taps_ref, out_ref)


def early_kernel(turn_in_ref, window_ref, raw_ref, tail_ref, head_ref, taps_ref, rows_ref, out_ref, held):
    half = tail_ref.shape[0]
    more = head_ref.shape[0]
    span = half + more - 16
    sub_index = lax.axis_index("sa")
    offset = window_ref[0] // LANES

    @pl.when(sub_index == 0)
    def _():
        start = pl.multiple_of(offset * LANES, LANES)
        retile(raw_ref.at[:, :, pl.ds(start, span * LANES)], held, 0, span)

    @pl.when(sub_index == 1)
    def _():
        held[:half] = tail_ref[...]
        retile(raw_ref, held, half, more)

    @pl.when(sub_index < 2)
    def _():
        compress(held, jnp.where(sub_index == 0, 0, offset), taps_ref, out_ref)

    @pl.when(sub_index == 3)
    def _():
        held[:half] = tail_ref[...]
        held[half:] = head_ref[...]
        compress(held, offset, taps_ref, out_ref, tail_ref)

    @pl.when(sub_index != 2)
    def _():
        out_ref[:, out_ref.shape[1] - rows_ref.shape[1] :] = rows_ref[...]


def late_kernel(near_ref, rows_ref, early_ref, out_ref):
    bins = near_ref.shape[1]
    sub_index = lax.axis_index("sa")

    @pl.when(sub_index != 2)
    def _():
        out_ref[...] = early_ref[...]

    @pl.when(sub_index == 2)
    def _():
        out_ref[:, :bins] = near_ref[...]
        out_ref[:, bins:] = rows_ref[...]


def azimuth_kernel(lines_ref, out_ref, columns_held, taps, made, sems):
    pulses = taps.shape[0] // 2
    columns = pulses // LANES
    tiles = sems.shape[0]
    each = out_ref.shape[0] // tiles
    sources = lines_ref.shape[0]
    rows = (lines_ref.shape[1] - EXTRA) // tiles
    picked = jnp.sum(lines_ref[:, tiles * rows :].astype(F32), axis=0)
    pieces = L // LANES
    skewed = []
    for part in range(2):
        spread = [jnp.broadcast_to(picked[part * pieces + t][None], (LANES, LANES)) for t in range(pieces)]
        skewed.append(pltpu.roll(jnp.concatenate(spread, axis=1), 0, 1, stride=1, stride_axis=0))
    for apart in range(1 - columns, columns):
        at = apart % pieces * LANES
        straight, crossed = (skewed[part][:, at : at + LANES] for part in range(2))
        for target, pair in enumerate(((straight, crossed), (-crossed, straight))):
            slot = (apart + columns - 1) * 2 + target
            for part in range(2):
                columns_held[slot, pl.ds(part, LANES, stride=2), :] = pair[part]
            block = columns_held[slot].astype(BF)
            for column in range(columns):
                line = column - apart
                if 0 <= line < columns:
                    lane = target * pulses + column * LANES
                    taps[2 * line * LANES : 2 * (line + 1) * LANES, lane : lane + LANES] = block
    copies = []
    for tile in range(tiles):
        lines = lines_ref[:, tile * rows : (tile + 1) * rows].reshape(sources * rows, LANES)
        focused = lax.dot_general(lines, taps[...], (((0,), (0,)), ((), ())), preferred_element_type=F32)
        into = pl.ds(tile * each, each)
        for part in range(2):
            for column in range(columns):
                lane = part * pulses + column * LANES
                made[pl.ds(tile * each + 2 * column + part, LANES, stride=2 * columns), :] = focused[
                    :, lane : lane + LANES
                ]
        copies.append(pltpu.make_async_copy(made.at[into], out_ref.at[into], sems.at[tile]))
        copies[-1].start()
    for copy in copies:
        copy.wait()


def toeplitz(diagonal_taps, size):
    span_size = 2 * size - 1
    reversed_taps = diagonal_taps[..., ::-1]
    shifted = jnp.concatenate(
        [reversed_taps[..., size - 1 :], reversed_taps[..., : size - 1]], axis=-1
    )
    reps = (1,) * (shifted.ndim - 1) + (size,)
    tiled_flat = jnp.tile(shifted, reps)[..., : size * (span_size - 1)]
    return tiled_flat.reshape(shifted.shape[:-1] + (size, span_size - 1))[..., :size]


def tap_blocks(tap_values, size):
    block_total = tap_values.shape[1] // size + 1
    padded_taps = jnp.pad(tap_values, ((0, 0), (size, 2 * size)))
    matrices = []
    for offset_block in range(block_total):
        first_tap = offset_block * size + 1
        parts = toeplitz(padded_taps[:, first_tap : first_tap + 2 * size - 1], size)
        real_part = parts[0]
        imag_part = parts[1]
        matrices.append(
            jnp.stack([jnp.stack([real_part, -imag_part]), jnp.stack([imag_part, real_part])])
        )
    return jnp.stack(matrices)


def correlate(blocked, matrices, output_count):
    summed = jnp.zeros((blocked.shape[0], 2, output_count, blocked.shape[3]), F32)
    for offset_block in range(matrices.shape[0]):
        piece_rows = blocked[:, :, offset_block : offset_block + output_count, :]
        summed = summed + jnp.einsum(
            "rcib,cdbn->rdin", piece_rows, matrices[offset_block], preferred_element_type=F32
        )
    return summed


def focus_long(range_lines, reference_row):
    block_size = L // 2
    bin_count, _, total_pulses = range_lines.shape
    block_count = total_pulses // block_size
    blocked = range_lines.reshape(bin_count, 2, block_count, block_size)
    blocked = jnp.pad(blocked, ((0, 0), (0, 0), (1, 1), (0, 0)))
    focused = correlate(blocked, tap_blocks(reference_row, block_size), block_count)
    return focused.reshape(1, bin_count, 2, total_pulses)


def call(kernel, outs, specs, scratch=(), vmem=24, flops=1000):
    space = {"s": pltpu.SMEM, "v": pltpu.VMEM, "a": pl.ANY}
    blocks = [pl.BlockSpec(memory_space=space[kind]) for kind in specs]
    return pl.pallas_call(
        kernel,
        out_shape=outs,
        in_specs=blocks[: -len(outs)],
        out_specs=tuple(blocks[-len(outs) :]),
        scratch_shapes=list(scratch),
        compiler_params=pltpu.CompilerParams(vmem_limit_bytes=int(vmem * 2**20)),
        cost_estimate=pl.CostEstimate(flops=flops, bytes_accessed=1000, transcendentals=0),
    )


def on_device(raw_echo, chirp_replica, azimuth_refs, migration_index, window_start):
    pulses = raw_echo.shape[0]
    segment_devices = lax.axis_size("sa")
    pulse_devices = lax.axis_size("pa")
    tap_count = chirp_replica.shape[1]
    kept_width = R // segment_devices
    bin_count = kept_width // pulse_devices
    total_pulses = pulses * pulse_devices
    half = kept_width // LANES
    tap_tiles = tap_count // LANES + 2
    span = half + tap_tiles - 1

    rows = 2 * pulses
    shape = jax.ShapeDtypeStruct
    token = shape((8, LANES), F32)
    short = bin_count % LANES == 0 and total_pulses == L // 2

    targets = pulse_devices if short else half // 8
    slot = half // targets * rows

    tail, turn = call(
        tail_kernel,
        (shape((half, rows, LANES), BF), token),
        "avv",
        [pltpu.VMEM((pulses, 2, (half + 8) * LANES), BF), pltpu.SemaphoreType.DMA((4,))],
        53,
    )(raw_echo)
    tail = lax.ppermute(tail, "sa", [(0, 1), (1, 3)])
    head, turn = call(head_kernel, (shape((span - half + 16, rows, LANES), BF), token), "vvvv")(turn, raw_echo)
    head = lax.ppermute(head, "sa", [(2, 3)])
    taps, own_rows, turn = call(
        prep_kernel,
        (shape((tap_tiles * LANES, 2 * LANES), BF), shape((pulse_devices, EXTRA, LANES), BF), token),
        "vsvvvvvv",
    )(turn, window_start, migration_index, chirp_replica, azimuth_refs)
    near, turn = call(
        ahead_kernel,
        (shape((targets, slot, LANES), BF), token),
        "vsvvvv",
        [pltpu.VMEM((span, rows, LANES), BF)],
    )(turn, window_start, raw_echo, taps)
    near = lax.ppermute(near, "sa", [(1, 2)])
    extra = own_rows if short else jnp.zeros((targets, EXTRA, LANES), BF)
    made = shape((targets, slot + EXTRA, LANES), BF)
    (early,) = call(
        early_kernel,
        (made,),
        "vsvvvvvv",
        [pltpu.VMEM((span + 16, rows, LANES), BF)],
        flops=10**10,
    )(turn, window_start, raw_echo, tail, head, taps, extra)
    (compressed,) = call(late_kernel, (made,), "vvvv")(near, extra, early)

    if not short:
        kept = compressed[:, :-EXTRA].reshape(half, pulses, 2, LANES).transpose(0, 3, 2, 1)
        outgoing = kept.reshape(pulse_devices, bin_count, 2, pulses)
        turned = lax.all_to_all(outgoing, "pa", split_axis=0, concat_axis=3, tiled=True)
        rows_in = lax.all_to_all(own_rows, "pa", split_axis=0, concat_axis=0, tiled=True)
        reference_row = jnp.sum(rows_in[:, :8].astype(F32), axis=0).astype(BF).reshape(2, L)
        reference_row = jnp.roll(reference_row, -(L // 2 + 1), axis=1)[:, ::-1]
        return focus_long(turned[0], reference_row)

    lines = lax.all_to_all(compressed, "pa", split_axis=0, concat_axis=0, tiled=True)
    width = 2 * total_pulses
    (focused,) = call(
        azimuth_kernel,
        (shape((bin_count * width // LANES, LANES), F32),),
        "va",
        [
            pltpu.VMEM((width // LANES * 2 - 1, 2 * LANES, LANES), F32),
            pltpu.VMEM((width, width), BF),
            pltpu.VMEM((bin_count * width // LANES + 8, LANES), F32),
            pltpu.SemaphoreType.DMA((bin_count // LANES,)),
        ],
    )(lines)
    focused = focused.reshape(1, bin_count, total_pulses // LANES, 2, LANES).swapaxes(2, 3)
    return focused.reshape(1, bin_count, 2, total_pulses)


def solution(mesh):
    placed = (P("pa", None, "sa"), P(), P("pa", None, None), P(), P())
    return jax.shard_map(
        on_device, mesh=mesh, in_specs=placed, out_specs=P("sa", "pa", None, None), check_vma=False
    )
```

```python
import jax
import jax.numpy as jnp
from jax import lax
from jax.experimental import pallas as pl
from jax.experimental.pallas import tpu as pltpu
from jax.sharding import PartitionSpec as P

R = 16384
L = 512
LANES = 128
EXTRA = 16
BF = jnp.bfloat16
F32 = jnp.float32


def reversed_lanes(row):
    row_id = lax.broadcasted_iota(jnp.int32, (LANES, LANES), 0)
    col_id = lax.broadcasted_iota(jnp.int32, (LANES, LANES), 1)
    flip = (row_id + col_id == LANES - 1).astype(BF)
    tiles = row.shape[1] // LANES
    pieces = [row[:, t * LANES : (t + 1) * LANES] for t in reversed(range(tiles))]
    return jnp.concatenate([jnp.dot(piece, flip, preferred_element_type=F32) for piece in pieces], axis=1)


def retile(source, target, first, tiles):
    shape = target.shape[1:]
    for t in range(tiles):
        target[first + t] = source[:, :, t * LANES : (t + 1) * LANES].reshape(shape)


def tail_first_kernel(raw_ref, tail_ref, turn_ref, natural, sems):
    turn_ref[...] = jnp.zeros_like(turn_ref)
    half, rows, _ = tail_ref.shape
    pieces = sems.shape[0]
    each = rows // 2 // pieces
    width = half * LANES

    @pl.when(lax.axis_index("sa") < 2)
    def _():
        copies = []
        for at in range(pieces):
            own = pl.ds(at * each, each)
            source = raw_ref.at[own, :, pl.ds(raw_ref.shape[2] - width, width)]
            copies.append(pltpu.make_async_copy(source, natural.at[own, :, pl.ds(0, width)], sems.at[at]))
            copies[-1].start()
        for at, copy in enumerate(copies):
            copy.wait()
            own = pl.ds(at * each, each)
            retile(natural.at[own], tail_ref.at[:, pl.ds(at * each * 2, each * 2)], 0, half)


def tail_second_kernel(turn_in_ref, raw_ref, tail_ref, turn_ref):
    turn_ref[...] = turn_in_ref[...]
    half, rows, _ = tail_ref.shape
    pulses = rows // 2

    @pl.when(lax.axis_index("sa") == 1)
    def _():
        own = pl.ds(raw_ref.shape[0] - pulses, pulses)
        width = half * LANES
        retile(raw_ref.at[own, :, pl.ds(raw_ref.shape[2] - width, width)], tail_ref, 0, half)


def prep_kernel(turn_in_ref, window_ref, index_ref, chirp_ref, refs_ref, taps_ref, rows_ref, turn_ref):
    turn_ref[...] = turn_in_ref[...]
    taps = chirp_ref.shape[1]
    blocks = taps_ref.shape[0] // LANES
    width = blocks * LANES
    shift = lax.rem(window_ref[0], LANES)
    chirp = jnp.concatenate([chirp_ref[...], jnp.zeros((14, taps), BF)], axis=0)
    flipped = reversed_lanes(chirp)
    padded = jnp.concatenate([jnp.zeros((16, 2 * LANES), F32), flipped], axis=1)
    padded = jnp.concatenate([padded, jnp.zeros((16, width + LANES - padded.shape[1]), F32)], axis=1)
    moved = pltpu.roll(padded, width + LANES - 127 - shift, 1)[:, :width]
    for part in range(2):
        spread = jnp.broadcast_to(moved[part : part + 1], (LANES, width))
        skewed = pltpu.roll(spread, 0, 1, stride=1, stride_axis=0)
        for t in range(blocks):
            first = LANES * (blocks - 1 - t)
            taps_ref[t * LANES : (t + 1) * LANES, part * LANES : (part + 1) * LANES] = skewed[
                :, first : first + LANES
            ].astype(BF)
    own = refs_ref.shape[0]
    groups, targets = index_ref.shape
    first_row = lax.axis_index("pa") * own
    mine = lax.broadcasted_iota(jnp.int32, (groups, targets), 0) == lax.axis_index("sa")
    wanted = jnp.sum(jnp.where(mine, index_ref[...], 0), axis=0, keepdims=True)
    row_id = lax.broadcasted_iota(jnp.int32, (own, targets), 0) + first_row
    picks = (row_id == jnp.broadcast_to(wanted, (own, targets))).astype(F32)
    pieces = []
    for part in range(2):
        picked = lax.dot_general(
            picks, refs_ref[:, part, :].astype(F32), (((0,), (0,)), ((), ())), preferred_element_type=F32
        )
        picked = reversed_lanes(picked.astype(BF))
        picked = pltpu.roll(picked, L // 2 + 1, 1)
        pieces += [picked[:, t * LANES : (t + 1) * LANES] for t in range(L // LANES)]
    pieces += [jnp.zeros((targets, LANES), F32)] * (rows_ref.shape[1] - len(pieces))
    rows_ref[...] = jnp.stack(pieces, axis=1).astype(BF)


def compress(held, base, taps_ref, out_ref, first_row, tile_rows):
    rows = held.shape[1]
    tap_tiles = taps_ref.shape[0] // LANES
    group = 8 if rows > 32 else 512 // rows
    per_target = out_ref.shape[1] // tile_rows
    even = lax.rem(lax.broadcasted_iota(jnp.int32, (1, 8, LANES), 1), 2) == 0
    for step in range(out_ref.shape[0] * per_target // group):
        blocks = [
            held[pl.ds(base + group * step + t, group)].reshape(group * rows, LANES) for t in range(tap_tiles)
        ]
        product = jnp.dot(jnp.concatenate(blocks, axis=1), taps_ref[...], preferred_element_type=F32)
        straight = product[:, :LANES].reshape(-1, 8, LANES)
        crossed = product[:, LANES:].reshape(-1, 8, LANES)
        total = straight + jnp.where(even, pltpu.roll(crossed, 7, 1), -pltpu.roll(crossed, 1, 1))
        count = group // per_target
        total = total.astype(BF).reshape(count, per_target, rows, LANES)
        for tile in range(per_target):
            at = tile * tile_rows + first_row
            out_ref[pl.ds(step * count, count), at : at + rows] = total[:, tile]


def own_kernel(turn_in_ref, window_ref, raw_ref, taps_ref, out_ref, turn_ref, held):
    turn_ref[...] = turn_in_ref[...]
    span = held.shape[0]

    @pl.when(lax.axis_index("sa") == 0)
    def _():
        start = pl.multiple_of(window_ref[0] // LANES * LANES, LANES)
        retile(raw_ref.at[:, :, pl.ds(start, span * LANES)], held, 0, span)
        compress(held, 0, taps_ref, out_ref, 0, held.shape[1])


def hand_tiles(raw_ref, first, out_ref):
    rows = 2 * raw_ref.shape[0]
    per_target = out_ref.shape[1] // rows
    for t in range(out_ref.shape[0] * per_target):
        start = (first + t) * LANES
        at = t % per_target * rows
        out_ref[t // per_target, at : at + rows] = raw_ref[:, :, start : start + LANES].reshape(rows, LANES)


def ahead_kernel(turn_in_ref, window_ref, raw_ref, taps_ref, out_ref, turn_ref, held):
    turn_ref[...] = turn_in_ref[...]
    span = held.shape[0]
    tiles = raw_ref.shape[2] // LANES
    count = out_ref.shape[0] * out_ref.shape[1] // held.shape[1]
    sub_index = lax.axis_index("sa")

    @pl.when(sub_index == 0)
    def _():
        hand_tiles(raw_ref, tiles - count, out_ref)

    @pl.when(sub_index == 1)
    def _():
        start = pl.multiple_of(window_ref[0] // LANES * LANES, LANES)
        retile(raw_ref.at[:, :, pl.ds(start, span * LANES)], held, 0, span)
        compress(held, 0, taps_ref, out_ref, 0, held.shape[1])

    @pl.when(sub_index == 2)
    def _():
        hand_tiles(raw_ref, 0, out_ref)


def gate_kernel(turn_in_ref, _, turn_ref):
    turn_ref[...] = turn_in_ref[...]


def take_tiles(near_ref, tile_rows, first_row, held, into, count):
    rows = held.shape[1]
    per_target = near_ref.shape[1] // tile_rows
    for t in range(count):
        at = t % per_target * tile_rows + first_row
        held[into + t] = near_ref[t // per_target, at : at + rows]


def fill_next(half, raw_ref, first_pulse, held):
    rows = held.shape[1]
    pulses = pl.ds(first_pulse, rows // 2)
    retile(raw_ref.at[pulses], held, half, held.shape[0] - half)


def first_kernel(turn_in_ref, window_ref, raw_ref, tail_ref, taps_ref, out_ref, turn_ref, held):
    turn_ref[...] = turn_in_ref[...]
    half = tail_ref.shape[0]

    @pl.when(lax.axis_index("sa") == 1)
    def _():
        held[:half] = tail_ref[...]
        fill_next(half, raw_ref, 0, held)
        compress(held, window_ref[0] // LANES, taps_ref, out_ref, 0, held.shape[1])


def middle_kernel(
    turn_in_ref, window_ref, raw_ref, tail_ref, near_ref, own_ref, first_ref, taps_ref, rows_ref, out_ref, turn_ref, held, far_held
):
    turn_ref[...] = turn_in_ref[...]
    half, before, _ = tail_ref.shape
    rows = held.shape[1]
    tile_rows = before + rows
    bins = near_ref.shape[1]
    sub_index = lax.axis_index("sa")
    offset = window_ref[0] // LANES
    made = out_ref.at[:, pl.ds(0, bins)]
    out_ref[:, bins:] = rows_ref[...]

    @pl.when(sub_index == 0)
    def _():
        made[...] = own_ref[...]

    @pl.when(sub_index == 1)
    def _():
        for tile in range(bins // tile_rows):
            out_ref[:, tile * tile_rows : tile * tile_rows + before] = first_ref[:, tile * before : (tile + 1) * before]
        take_tiles(near_ref, tile_rows, before, held, 0, half)
        fill_next(half, raw_ref, before // 2, held)
        compress(held, offset, taps_ref, made, before, tile_rows)

    @pl.when(sub_index == 2)
    def _():
        made[...] = near_ref[...]

    @pl.when(sub_index == 3)
    def _():
        far_held[:half] = tail_ref[...]
        take_tiles(near_ref, tile_rows, 0, far_held, half, far_held.shape[0] - half)
        compress(far_held, offset, taps_ref, made, 0, tile_rows)


def last_kernel(turn_in_ref, window_ref, tail_ref, near_ref, taps_ref, middle_ref, out_ref, held):
    half, rows, _ = tail_ref.shape
    bins = near_ref.shape[1]
    tile_rows = bins * near_ref.shape[0] // half
    out_ref[...] = middle_ref[...]

    @pl.when(lax.axis_index("sa") == 3)
    def _():
        held[:half] = tail_ref[...]
        take_tiles(near_ref, tile_rows, tile_rows - rows, held, half, held.shape[0] - half)
        made = out_ref.at[:, pl.ds(0, bins)]
        compress(held, window_ref[0] // LANES, taps_ref, made, tile_rows - rows, tile_rows)


def azimuth_kernel(lines_ref, out_ref, columns_held, taps, made, sems):
    pulses = taps.shape[0] // 2
    columns = pulses // LANES
    tiles = sems.shape[0]
    each = out_ref.shape[0] // tiles
    sources = lines_ref.shape[0]
    rows = (lines_ref.shape[1] - EXTRA) // tiles
    picked = jnp.sum(lines_ref[:, tiles * rows :].astype(F32), axis=0)
    pieces = L // LANES
    skewed = []
    for part in range(2):
        spread = [jnp.broadcast_to(picked[part * pieces + t][None], (LANES, LANES)) for t in range(pieces)]
        skewed.append(pltpu.roll(jnp.concatenate(spread, axis=1), 0, 1, stride=1, stride_axis=0))
    for apart in range(1 - columns, columns):
        at = apart % pieces * LANES
        straight, crossed = (skewed[part][:, at : at + LANES] for part in range(2))
        for target, pair in enumerate(((straight, crossed), (-crossed, straight))):
            slot = (apart + columns - 1) * 2 + target
            for part in range(2):
                columns_held[slot, pl.ds(part, LANES, stride=2), :] = pair[part]
            block = columns_held[slot].astype(BF)
            for column in range(columns):
                line = column - apart
                if 0 <= line < columns:
                    lane = target * pulses + column * LANES
                    taps[2 * line * LANES : 2 * (line + 1) * LANES, lane : lane + LANES] = block
    copies = []
    for tile in range(tiles):
        lines = lines_ref[:, tile * rows : (tile + 1) * rows].reshape(sources * rows, LANES)
        focused = lax.dot_general(lines, taps[...], (((0,), (0,)), ((), ())), preferred_element_type=F32)
        into = pl.ds(tile * each, each)
        for part in range(2):
            for column in range(columns):
                lane = part * pulses + column * LANES
                made[pl.ds(tile * each + 2 * column + part, LANES, stride=2 * columns), :] = focused[
                    :, lane : lane + LANES
                ]
        copies.append(pltpu.make_async_copy(made.at[into], out_ref.at[into], sems.at[tile]))
        copies[-1].start()
    for copy in copies:
        copy.wait()


def toeplitz(diagonal_taps, size):
    span_size = 2 * size - 1
    reversed_taps = diagonal_taps[..., ::-1]
    shifted = jnp.concatenate(
        [reversed_taps[..., size - 1 :], reversed_taps[..., : size - 1]], axis=-1
    )
    reps = (1,) * (shifted.ndim - 1) + (size,)
    tiled_flat = jnp.tile(shifted, reps)[..., : size * (span_size - 1)]
    return tiled_flat.reshape(shifted.shape[:-1] + (size, span_size - 1))[..., :size]


def tap_blocks(tap_values, size):
    block_total = tap_values.shape[1] // size + 1
    padded_taps = jnp.pad(tap_values, ((0, 0), (size, 2 * size)))
    matrices = []
    for offset_block in range(block_total):
        first_tap = offset_block * size + 1
        parts = toeplitz(padded_taps[:, first_tap : first_tap + 2 * size - 1], size)
        real_part = parts[0]
        imag_part = parts[1]
        matrices.append(
            jnp.stack([jnp.stack([real_part, -imag_part]), jnp.stack([imag_part, real_part])])
        )
    return jnp.stack(matrices)


def correlate(blocked, matrices, output_count):
    summed = jnp.zeros((blocked.shape[0], 2, output_count, blocked.shape[3]), F32)
    for offset_block in range(matrices.shape[0]):
        piece_rows = blocked[:, :, offset_block : offset_block + output_count, :]
        summed = summed + jnp.einsum(
            "rcib,cdbn->rdin", piece_rows, matrices[offset_block], preferred_element_type=F32
        )
    return summed


def focus_long(range_lines, reference_row):
    block_size = L // 2
    bin_count, _, total_pulses = range_lines.shape
    block_count = total_pulses // block_size
    blocked = range_lines.reshape(bin_count, 2, block_count, block_size)
    blocked = jnp.pad(blocked, ((0, 0), (0, 0), (1, 1), (0, 0)))
    focused = correlate(blocked, tap_blocks(reference_row, block_size), block_count)
    return focused.reshape(1, bin_count, 2, total_pulses)


def call(kernel, outs, specs, scratch=(), vmem=24, flops=1000):
    space = {"s": pltpu.SMEM, "v": pltpu.VMEM, "a": pl.ANY}
    blocks = [pl.BlockSpec(memory_space=space[kind]) for kind in specs]
    return pl.pallas_call(
        kernel,
        out_shape=outs,
        in_specs=blocks[: -len(outs)],
        out_specs=tuple(blocks[-len(outs) :]),
        scratch_shapes=list(scratch),
        compiler_params=pltpu.CompilerParams(vmem_limit_bytes=int(vmem * 2**20)),
        cost_estimate=pl.CostEstimate(flops=flops, bytes_accessed=1000, transcendentals=0),
    )


def on_device(raw_echo, chirp_replica, azimuth_refs, migration_index, window_start):
    pulses = raw_echo.shape[0]
    segment_devices = lax.axis_size("sa")
    pulse_devices = lax.axis_size("pa")
    tap_count = chirp_replica.shape[1]
    kept_width = R // segment_devices
    bin_count = kept_width // pulse_devices
    total_pulses = pulses * pulse_devices
    half = kept_width // LANES
    tap_tiles = tap_count // LANES + 2
    span = half + tap_tiles - 1

    rows = 2 * pulses
    shape = jax.ShapeDtypeStruct
    token = shape((8, LANES), F32)
    short = bin_count % LANES == 0 and total_pulses == L // 2

    targets = pulse_devices if short else half // 8
    slot = half // targets * rows

    first_rows = rows // 4 * 3
    part = shape((targets, slot, LANES), BF)
    tail, turn = call(
        tail_first_kernel,
        (shape((half, first_rows, LANES), BF), token),
        "avv",
        [pltpu.VMEM((first_rows // 2, 2, (half + 8) * LANES), BF), pltpu.SemaphoreType.DMA((3,))],
        53,
    )(raw_echo)
    tail_first = lax.ppermute(tail, "sa", [(0, 1), (1, 3)])
    tail, turn = call(
        tail_second_kernel, (shape((half, rows - first_rows, LANES), BF), token), "vvvv"
    )(turn, raw_echo)
    tail_second = lax.ppermute(tail, "sa", [(1, 3)])
    taps, own_rows, turn = call(
        prep_kernel,
        (shape((tap_tiles * LANES, 2 * LANES), BF), shape((pulse_devices, EXTRA, LANES), BF), token),
        "vsvvvvvv",
    )(turn, window_start, migration_index, chirp_replica, azimuth_refs)
    window_held = [pltpu.VMEM((span, rows, LANES), BF)]
    own, turn = call(own_kernel, (part, token), "vsvvvv", window_held)(turn, window_start, raw_echo, taps)
    near, turn = call(ahead_kernel, (part, token), "vsvvvv", window_held)(turn, window_start, raw_echo, taps)
    near = lax.ppermute(near, "sa", [(0, 1), (1, 2), (2, 3)])
    extra = own_rows if short else jnp.zeros((targets, EXTRA, LANES), BF)
    made = shape((targets, slot + EXTRA, LANES), BF)
    wide = span + 16
    (turn,) = call(gate_kernel, (token,), "vav", flops=10**10)(turn, tail_first)
    first_held = pltpu.VMEM((wide, first_rows, LANES), BF)
    last_held = pltpu.VMEM((wide, rows - first_rows, LANES), BF)
    first, turn = call(
        first_kernel,
        (shape((targets, slot // rows * first_rows, LANES), BF), token),
        "vsvvvvv",
        [first_held],
        flops=10**10,
    )(turn, window_start, raw_echo, tail_first, taps)
    middle, turn = call(
        middle_kernel, (made, token), "vsvvvvvvvvv", [last_held, first_held], flops=10**10
    )(turn, window_start, raw_echo, tail_first, near, own, first, taps, extra)
    (compressed,) = call(last_kernel, (made,), "vsvvvvv", [last_held], flops=10**10)(
        turn, window_start, tail_second, near, taps, middle
    )

    if not short:
        kept = compressed[:, :-EXTRA].reshape(half, pulses, 2, LANES).transpose(0, 3, 2, 1)
        outgoing = kept.reshape(pulse_devices, bin_count, 2, pulses)
        turned = lax.all_to_all(outgoing, "pa", split_axis=0, concat_axis=3, tiled=True)
        rows_in = lax.all_to_all(own_rows, "pa", split_axis=0, concat_axis=0, tiled=True)
        reference_row = jnp.sum(rows_in[:, :8].astype(F32), axis=0).astype(BF).reshape(2, L)
        reference_row = jnp.roll(reference_row, -(L // 2 + 1), axis=1)[:, ::-1]
        return focus_long(turned[0], reference_row)

    lines = lax.all_to_all(compressed, "pa", split_axis=0, concat_axis=0, tiled=True)
    width = 2 * total_pulses
    (focused,) = call(
        azimuth_kernel,
        (shape((bin_count * width // LANES, LANES), F32),),
        "va",
        [
            pltpu.VMEM((width // LANES * 2 - 1, 2 * LANES, LANES), F32),
            pltpu.VMEM((width, width), BF),
            pltpu.VMEM((bin_count * width // LANES + 8, LANES), F32),
            pltpu.SemaphoreType.DMA((bin_count // LANES,)),
        ],
    )(lines)
    focused = focused.reshape(1, bin_count, total_pulses // LANES, 2, LANES).swapaxes(2, 3)
    return focused.reshape(1, bin_count, 2, total_pulses)


def solution(mesh):
    placed = (P("pa", None, "sa"), P(), P("pa", None, None), P(), P())
    return jax.shard_map(
        on_device, mesh=mesh, in_specs=placed, out_specs=P("sa", "pa", None, None), check_vma=False
    )
```

```python
import jax
import jax.numpy as jnp
from jax import lax
from jax.experimental import pallas as pl
from jax.experimental.pallas import tpu as pltpu
from jax.sharding import PartitionSpec as P

R = 16384
L = 512
LANES = 128
EXTRA = 8
BF = jnp.bfloat16
F32 = jnp.float32


def reversed_lanes(row):
    row_id = lax.broadcasted_iota(jnp.int32, (LANES, LANES), 0)
    col_id = lax.broadcasted_iota(jnp.int32, (LANES, LANES), 1)
    flip = (row_id + col_id == LANES - 1).astype(BF)
    tiles = row.shape[1] // LANES
    pieces = [row[:, t * LANES : (t + 1) * LANES] for t in reversed(range(tiles))]
    return jnp.concatenate([jnp.dot(piece, flip, preferred_element_type=F32) for piece in pieces], axis=1)


def retile(source, target, first, tiles):
    shape = target.shape[1:]
    for t in range(tiles):
        target[first + t] = source[:, :, t * LANES : (t + 1) * LANES].reshape(shape)


def tail_kernel(raw_ref, tail_ref, turn_ref, natural, sems):
    turn_ref[...] = jnp.zeros_like(turn_ref)
    half, rows, _ = tail_ref.shape
    pieces = sems.shape[0]
    each = rows // 2 // pieces
    width = half * LANES

    @pl.when(lax.axis_index("sa") < 2)
    def _():
        copies = []
        for at in range(pieces):
            own = pl.ds(at * each, each)
            source = raw_ref.at[own, :, pl.ds(raw_ref.shape[2] - width, width)]
            copies.append(pltpu.make_async_copy(source, natural.at[own, :, pl.ds(0, width)], sems.at[at]))
            copies[-1].start()
        for at, copy in enumerate(copies):
            copy.wait()
            own = pl.ds(at * each, each)
            retile(natural.at[own], tail_ref.at[:, pl.ds(at * each * 2, each * 2)], 0, half)


def head_kernel(turn_in_ref, raw_ref, head_ref, turn_ref):
    turn_ref[...] = turn_in_ref[...]

    @pl.when(lax.axis_index("sa") == 2)
    def _():
        retile(raw_ref, head_ref, 0, head_ref.shape[0])


def prep_kernel(turn_in_ref, window_ref, index_ref, chirp_ref, refs_ref, taps_ref, rows_ref, turn_ref):
    turn_ref[...] = turn_in_ref[...]
    taps = chirp_ref.shape[1]
    blocks = taps_ref.shape[0] // LANES
    width = blocks * LANES
    shift = lax.rem(window_ref[0], LANES)
    chirp = jnp.concatenate([chirp_ref[...], jnp.zeros((14, taps), BF)], axis=0)
    flipped = reversed_lanes(chirp)
    padded = jnp.concatenate([jnp.zeros((16, 2 * LANES), F32), flipped], axis=1)
    padded = jnp.concatenate([padded, jnp.zeros((16, width + LANES - padded.shape[1]), F32)], axis=1)
    moved = pltpu.roll(padded, width + LANES - 127 - shift, 1)[:, :width]
    for part in range(2):
        spread = jnp.broadcast_to(moved[part : part + 1], (LANES, width))
        skewed = pltpu.roll(spread, 0, 1, stride=1, stride_axis=0)
        for t in range(blocks):
            first = LANES * (blocks - 1 - t)
            taps_ref[t * LANES : (t + 1) * LANES, part * LANES : (part + 1) * LANES] = skewed[
                :, first : first + LANES
            ].astype(BF)
    own = refs_ref.shape[0]
    groups, targets = index_ref.shape
    first_row = lax.axis_index("pa") * own
    mine = lax.broadcasted_iota(jnp.int32, (groups, targets), 0) == lax.axis_index("sa")
    wanted = jnp.sum(jnp.where(mine, index_ref[...], 0), axis=0, keepdims=True)
    row_id = lax.broadcasted_iota(jnp.int32, (own, targets), 0) + first_row
    picks = (row_id == jnp.broadcast_to(wanted, (own, targets))).astype(F32)
    pieces = []
    for part in range(2):
        picked = lax.dot_general(
            picks, refs_ref[:, part, :].astype(F32), (((0,), (0,)), ((), ())), preferred_element_type=F32
        )
        picked = reversed_lanes(picked.astype(BF))
        picked = pltpu.roll(picked, L // 2 + 1, 1)
        pieces += [picked[:, t * LANES : (t + 1) * LANES] for t in range(L // LANES)]
    pieces += [jnp.zeros((targets, LANES), F32)] * (rows_ref.shape[1] - len(pieces))
    rows_ref[...] = jnp.stack(pieces, axis=1).astype(BF)


def compress(held, base, taps_ref, out_ref, opening=None):
    rows = held.shape[1]
    targets = out_ref.shape[0]
    tap_tiles = taps_ref.shape[0] // LANES
    group = 8
    per_target = out_ref.shape[1] // rows
    even = lax.rem(lax.broadcasted_iota(jnp.int32, (1, 8, LANES), 1), 2) == 0
    for step in range(targets * per_target // group):
        source = held if step or opening is None else opening
        blocks = [
            source[pl.ds(base + group * step + t, group)].reshape(group * rows, LANES) for t in range(tap_tiles)
        ]
        product = jnp.dot(jnp.concatenate(blocks, axis=1), taps_ref[...], preferred_element_type=F32)
        straight = product[:, :LANES].reshape(-1, 8, LANES)
        crossed = product[:, LANES:].reshape(-1, 8, LANES)
        total = straight + jnp.where(even, pltpu.roll(crossed, 7, 1), -pltpu.roll(crossed, 1, 1))
        count = group // per_target
        out_ref[pl.ds(step * count, count), : per_target * rows] = total.astype(BF).reshape(
            count, per_target * rows, LANES
        )


def ahead_kernel(turn_in_ref, window_ref, raw_ref, taps_ref, out_ref, turn_ref, held):
    turn_ref[...] = turn_in_ref[...]
    span = held.shape[0]

    @pl.when(lax.axis_index("sa") == 1)
    def _():
        start = pl.multiple_of(window_ref[0] // LANES * LANES, LANES)
        retile(raw_ref.at[:, :, pl.ds(start, span * LANES)], held, 0, span)
        compress(held, 0, taps_ref, out_ref)


def early_kernel(turn_in_ref, window_ref, raw_ref, tail_ref, head_ref, taps_ref, rows_ref, out_ref, held):
    half = tail_ref.shape[0]
    more = head_ref.shape[0]
    span = half + more - 16
    sub_index = lax.axis_index("sa")
    offset = window_ref[0] // LANES
    made = out_ref.at[:, pl.ds(EXTRA, out_ref.shape[1] - EXTRA)]

    @pl.when(sub_index == 0)
    def _():
        start = pl.multiple_of(offset * LANES, LANES)
        retile(raw_ref.at[:, :, pl.ds(start, span * LANES)], held, 0, span)

    @pl.when(sub_index == 1)
    def _():
        held[:half] = tail_ref[...]
        retile(raw_ref, held, half, more)

    @pl.when(sub_index < 2)
    def _():
        compress(held, jnp.where(sub_index == 0, 0, offset), taps_ref, made)

    @pl.when(sub_index == 3)
    def _():
        held[:half] = tail_ref[...]
        held[half:] = head_ref[...]
        compress(held, offset, taps_ref, made, tail_ref)

    @pl.when(sub_index != 2)
    def _():
        out_ref[:, :EXTRA] = rows_ref[...][:, :EXTRA]


def late_kernel(near_ref, rows_ref, early_ref, out_ref):
    sub_index = lax.axis_index("sa")

    @pl.when(sub_index != 2)
    def _():
        out_ref[...] = early_ref[...]

    @pl.when(sub_index == 2)
    def _():
        out_ref[:, EXTRA:] = near_ref[...]
        out_ref[:, :EXTRA] = rows_ref[...][:, :EXTRA]


def azimuth_kernel(lines_ref, out_ref, columns_held, taps, made, sems):
    pulses = taps.shape[0] // 2
    columns = pulses // LANES
    tiles = sems.shape[0]
    each = out_ref.shape[0] // tiles
    sources = lines_ref.shape[0]
    rows = (lines_ref.shape[1] - EXTRA) // tiles
    picked = jnp.sum(lines_ref[:, :EXTRA].astype(F32), axis=0)
    pieces = L // LANES
    skewed = []
    for part in range(2):
        spread = [jnp.broadcast_to(picked[part * pieces + t][None], (LANES, LANES)) for t in range(pieces)]
        skewed.append(pltpu.roll(jnp.concatenate(spread, axis=1), 0, 1, stride=1, stride_axis=0))
    for apart in range(1 - columns, columns):
        at = apart % pieces * LANES
        straight, crossed = (skewed[part][:, at : at + LANES] for part in range(2))
        for target, pair in enumerate(((straight, crossed), (-crossed, straight))):
            slot = (apart + columns - 1) * 2 + target
            for part in range(2):
                columns_held[slot, pl.ds(part, LANES, stride=2), :] = pair[part]
            block = columns_held[slot].astype(BF)
            for column in range(columns):
                line = column - apart
                if 0 <= line < columns:
                    lane = target * pulses + column * LANES
                    taps[2 * line * LANES : 2 * (line + 1) * LANES, lane : lane + LANES] = block
    copies = []
    for tile in range(tiles):
        lines = lines_ref[:, EXTRA + tile * rows : EXTRA + (tile + 1) * rows].reshape(sources * rows, LANES)
        focused = lax.dot_general(lines, taps[...], (((0,), (0,)), ((), ())), preferred_element_type=F32)
        into = pl.ds(tile * each, each)
        for part in range(2):
            for column in range(columns):
                lane = part * pulses + column * LANES
                made[pl.ds(tile * each + 2 * column + part, LANES, stride=2 * columns), :] = focused[
                    :, lane : lane + LANES
                ]
        copies.append(pltpu.make_async_copy(made.at[into], out_ref.at[into], sems.at[tile]))
        copies[-1].start()
    for copy in copies:
        copy.wait()


def toeplitz(diagonal_taps, size):
    span_size = 2 * size - 1
    reversed_taps = diagonal_taps[..., ::-1]
    shifted = jnp.concatenate(
        [reversed_taps[..., size - 1 :], reversed_taps[..., : size - 1]], axis=-1
    )
    reps = (1,) * (shifted.ndim - 1) + (size,)
    tiled_flat = jnp.tile(shifted, reps)[..., : size * (span_size - 1)]
    return tiled_flat.reshape(shifted.shape[:-1] + (size, span_size - 1))[..., :size]


def tap_blocks(tap_values, size):
    block_total = tap_values.shape[1] // size + 1
    padded_taps = jnp.pad(tap_values, ((0, 0), (size, 2 * size)))
    matrices = []
    for offset_block in range(block_total):
        first_tap = offset_block * size + 1
        parts = toeplitz(padded_taps[:, first_tap : first_tap + 2 * size - 1], size)
        real_part = parts[0]
        imag_part = parts[1]
        matrices.append(
            jnp.stack([jnp.stack([real_part, -imag_part]), jnp.stack([imag_part, real_part])])
        )
    return jnp.stack(matrices)


def correlate(blocked, matrices, output_count):
    summed = jnp.zeros((blocked.shape[0], 2, output_count, blocked.shape[3]), F32)
    for offset_block in range(matrices.shape[0]):
        piece_rows = blocked[:, :, offset_block : offset_block + output_count, :]
        summed = summed + jnp.einsum(
            "rcib,cdbn->rdin", piece_rows, matrices[offset_block], preferred_element_type=F32
        )
    return summed


def focus_long(range_lines, reference_row):
    block_size = L // 2
    bin_count, _, total_pulses = range_lines.shape
    block_count = total_pulses // block_size
    blocked = range_lines.reshape(bin_count, 2, block_count, block_size)
    blocked = jnp.pad(blocked, ((0, 0), (0, 0), (1, 1), (0, 0)))
    focused = correlate(blocked, tap_blocks(reference_row, block_size), block_count)
    return focused.reshape(1, bin_count, 2, total_pulses)


def call(kernel, outs, specs, scratch=(), vmem=24, flops=1000):
    space = {"s": pltpu.SMEM, "v": pltpu.VMEM, "a": pl.ANY}
    blocks = [pl.BlockSpec(memory_space=space[kind]) for kind in specs]
    return pl.pallas_call(
        kernel,
        out_shape=outs,
        in_specs=blocks[: -len(outs)],
        out_specs=tuple(blocks[-len(outs) :]),
        scratch_shapes=list(scratch),
        compiler_params=pltpu.CompilerParams(vmem_limit_bytes=int(vmem * 2**20)),
        cost_estimate=pl.CostEstimate(flops=flops, bytes_accessed=1000, transcendentals=0),
    )


def on_device(raw_echo, chirp_replica, azimuth_refs, migration_index, window_start):
    pulses = raw_echo.shape[0]
    segment_devices = lax.axis_size("sa")
    pulse_devices = lax.axis_size("pa")
    tap_count = chirp_replica.shape[1]
    kept_width = R // segment_devices
    bin_count = kept_width // pulse_devices
    total_pulses = pulses * pulse_devices
    half = kept_width // LANES
    tap_tiles = tap_count // LANES + 2
    span = half + tap_tiles - 1

    rows = 2 * pulses
    shape = jax.ShapeDtypeStruct
    token = shape((8, LANES), F32)
    short = bin_count % LANES == 0 and total_pulses == L // 2

    targets = pulse_devices if short else half // 8
    slot = half // targets * rows

    tail, turn = call(
        tail_kernel,
        (shape((half, rows, LANES), BF), token),
        "avv",
        [pltpu.VMEM((pulses, 2, (half + 8) * LANES), BF), pltpu.SemaphoreType.DMA((4,))],
        53,
    )(raw_echo)
    tail = lax.ppermute(tail, "sa", [(0, 1), (1, 3)])
    head, turn = call(head_kernel, (shape((span - half + 16, rows, LANES), BF), token), "vvvv")(turn, raw_echo)
    head = lax.ppermute(head, "sa", [(2, 3)])
    taps, own_rows, turn = call(
        prep_kernel,
        (shape((tap_tiles * LANES, 2 * LANES), BF), shape((pulse_devices, 2 * EXTRA, LANES), BF), token),
        "vsvvvvvv",
    )(turn, window_start, migration_index, chirp_replica, azimuth_refs)
    near, turn = call(
        ahead_kernel,
        (shape((targets, slot, LANES), BF), token),
        "vsvvvv",
        [pltpu.VMEM((span, rows, LANES), BF)],
    )(turn, window_start, raw_echo, taps)
    near = lax.ppermute(near, "sa", [(1, 2)])
    extra = own_rows if short else jnp.zeros((targets, 2 * EXTRA, LANES), BF)
    made = shape((targets, slot + EXTRA, LANES), BF)
    (early,) = call(
        early_kernel,
        (made,),
        "vsvvvvvv",
        [pltpu.VMEM((span + 16, rows, LANES), BF)],
        flops=10**10,
    )(turn, window_start, raw_echo, tail, head, taps, extra)
    (compressed,) = call(late_kernel, (made,), "vvvv")(near, extra, early)

    if not short:
        kept = compressed[:, EXTRA:].reshape(half, pulses, 2, LANES).transpose(0, 3, 2, 1)
        outgoing = kept.reshape(pulse_devices, bin_count, 2, pulses)
        turned = lax.all_to_all(outgoing, "pa", split_axis=0, concat_axis=3, tiled=True)
        rows_in = lax.all_to_all(own_rows, "pa", split_axis=0, concat_axis=0, tiled=True)
        reference_row = jnp.sum(rows_in[:, :8].astype(F32), axis=0).astype(BF).reshape(2, L)
        reference_row = jnp.roll(reference_row, -(L // 2 + 1), axis=1)[:, ::-1]
        return focus_long(turned[0], reference_row)

    lines = lax.all_to_all(compressed, "pa", split_axis=0, concat_axis=0, tiled=True)
    width = 2 * total_pulses
    (focused,) = call(
        azimuth_kernel,
        (shape((bin_count * width // LANES, LANES), F32),),
        "va",
        [
            pltpu.VMEM((width // LANES * 2 - 1, 2 * LANES, LANES), F32),
            pltpu.VMEM((width, width), BF),
            pltpu.VMEM((bin_count * width // LANES + 8, LANES), F32),
            pltpu.SemaphoreType.DMA((bin_count // LANES,)),
        ],
    )(lines)
    focused = focused.reshape(1, bin_count, total_pulses // LANES, 2, LANES).swapaxes(2, 3)
    return focused.reshape(1, bin_count, 2, total_pulses)


def solution(mesh):
    placed = (P("pa", None, "sa"), P(), P("pa", None, None), P(), P())
    return jax.shard_map(
        on_device, mesh=mesh, in_specs=placed, out_specs=P("sa", "pa", None, None), check_vma=False
    )
```

```python
import jax
import jax.numpy as jnp
from jax import lax
from jax.experimental import pallas as pl
from jax.experimental.pallas import tpu as pltpu
from jax.sharding import PartitionSpec as P

R = 16384
L = 512
LANES = 128
EXTRA = 8
BF = jnp.bfloat16
F32 = jnp.float32


def reversed_lanes(row):
    row_id = lax.broadcasted_iota(jnp.int32, (LANES, LANES), 0)
    col_id = lax.broadcasted_iota(jnp.int32, (LANES, LANES), 1)
    flip = (row_id + col_id == LANES - 1).astype(BF)
    tiles = row.shape[1] // LANES
    pieces = [row[:, t * LANES : (t + 1) * LANES] for t in reversed(range(tiles))]
    return jnp.concatenate([jnp.dot(piece, flip, preferred_element_type=F32) for piece in pieces], axis=1)


def retile(source, target, first, tiles):
    shape = target.shape[1:]
    for t in range(tiles):
        target[first + t] = source[:, :, t * LANES : (t + 1) * LANES].reshape(shape)


def tail_kernel(raw_ref, tail_ref, turn_ref, natural, sems):
    turn_ref[...] = jnp.zeros_like(turn_ref)
    half, rows, _ = tail_ref.shape
    pieces = sems.shape[0]
    each = rows // 2 // pieces
    width = half * LANES

    @pl.when(lax.axis_index("sa") < 2)
    def _():
        copies = []
        for at in range(pieces):
            own = pl.ds(at * each, each)
            source = raw_ref.at[own, :, pl.ds(raw_ref.shape[2] - width, width)]
            copies.append(pltpu.make_async_copy(source, natural.at[own, :, pl.ds(0, width)], sems.at[at]))
            copies[-1].start()
        for at, copy in enumerate(copies):
            copy.wait()
            own = pl.ds(at * each, each)
            retile(natural.at[own], tail_ref.at[:, pl.ds(at * each * 2, each * 2)], 0, half)


def head_kernel(turn_in_ref, raw_ref, head_ref, turn_ref):
    turn_ref[...] = turn_in_ref[...]

    @pl.when(lax.axis_index("sa") == 2)
    def _():
        retile(raw_ref, head_ref, 0, head_ref.shape[0])


def prep_kernel(turn_in_ref, window_ref, index_ref, chirp_ref, refs_ref, taps_ref, rows_ref, turn_ref):
    turn_ref[...] = turn_in_ref[...]
    taps = chirp_ref.shape[1]
    blocks = taps_ref.shape[0] // LANES
    width = blocks * LANES
    shift = lax.rem(window_ref[0], LANES)
    chirp = jnp.concatenate([chirp_ref[...], jnp.zeros((14, taps), BF)], axis=0)
    flipped = reversed_lanes(chirp)
    padded = jnp.concatenate([jnp.zeros((16, 2 * LANES), F32), flipped], axis=1)
    padded = jnp.concatenate([padded, jnp.zeros((16, width + LANES - padded.shape[1]), F32)], axis=1)
    moved = pltpu.roll(padded, width + LANES - 127 - shift, 1)[:, :width]
    for part in range(2):
        spread = jnp.broadcast_to(moved[part : part + 1], (LANES, width))
        skewed = pltpu.roll(spread, 0, 1, stride=1, stride_axis=0)
        for t in range(blocks):
            first = LANES * (blocks - 1 - t)
            taps_ref[t * LANES : (t + 1) * LANES, part * LANES : (part + 1) * LANES] = skewed[
                :, first : first + LANES
            ].astype(BF)
    own = refs_ref.shape[0]
    groups, targets = index_ref.shape
    first_row = lax.axis_index("pa") * own
    mine = lax.broadcasted_iota(jnp.int32, (groups, targets), 0) == lax.axis_index("sa")
    wanted = jnp.sum(jnp.where(mine, index_ref[...], 0), axis=0, keepdims=True)
    row_id = lax.broadcasted_iota(jnp.int32, (own, targets), 0) + first_row
    picks = (row_id == jnp.broadcast_to(wanted, (own, targets))).astype(F32)
    pieces = []
    for part in range(2):
        picked = lax.dot_general(
            picks, refs_ref[:, part, :].astype(F32), (((0,), (0,)), ((), ())), preferred_element_type=F32
        )
        picked = reversed_lanes(picked.astype(BF))
        picked = pltpu.roll(picked, L // 2 + 1, 1)
        pieces += [picked[:, t * LANES : (t + 1) * LANES] for t in range(L // LANES)]
    pieces += [jnp.zeros((targets, LANES), F32)] * (rows_ref.shape[1] - len(pieces))
    rows_ref[...] = jnp.stack(pieces, axis=1).astype(BF)


def compress(held, base, taps_ref, out_ref, opening=None):
    rows = held.shape[1]
    targets = out_ref.shape[0]
    tap_tiles = taps_ref.shape[0] // LANES
    group = 8
    per_target = out_ref.shape[1] // rows
    even = lax.rem(lax.broadcasted_iota(jnp.int32, (1, 8, LANES), 1), 2) == 0
    for step in range(targets * per_target // group):
        source = held if step or opening is None else opening
        blocks = [
            source[pl.ds(base + group * step + t, group)].reshape(group * rows, LANES) for t in range(tap_tiles)
        ]
        product = jnp.dot(jnp.concatenate(blocks, axis=1), taps_ref[...], preferred_element_type=F32)
        straight = product[:, :LANES].reshape(-1, 8, LANES)
        crossed = product[:, LANES:].reshape(-1, 8, LANES)
        total = straight + jnp.where(even, pltpu.roll(crossed, 7, 1), -pltpu.roll(crossed, 1, 1))
        count = group // per_target
        out_ref[pl.ds(step * count, count), : per_target * rows] = total.astype(BF).reshape(
            count, per_target * rows, LANES
        )


def ahead_kernel(turn_in_ref, window_ref, raw_ref, taps_ref, out_ref, turn_ref, held):
    turn_ref[...] = turn_in_ref[...]
    span = held.shape[0]

    @pl.when(lax.axis_index("sa") == 1)
    def _():
        start = pl.multiple_of(window_ref[0] // LANES * LANES, LANES)
        retile(raw_ref.at[:, :, pl.ds(start, span * LANES)], held, 0, span)
        compress(held, 0, taps_ref, out_ref)


def early_kernel(turn_in_ref, window_ref, raw_ref, tail_ref, head_ref, taps_ref, rows_ref, out_ref, held):
    half = tail_ref.shape[0]
    more = head_ref.shape[0]
    span = half + more - 16
    sub_index = lax.axis_index("sa")
    offset = window_ref[0] // LANES
    made = out_ref.at[:, pl.ds(EXTRA, out_ref.shape[1] - EXTRA)]

    @pl.when(sub_index == 0)
    def _():
        start = pl.multiple_of(offset * LANES, LANES)
        retile(raw_ref.at[:, :, pl.ds(start, span * LANES)], held, 0, span)

    @pl.when(sub_index == 1)
    def _():
        held[:half] = tail_ref[...]
        retile(raw_ref, held, half, more)

    @pl.when(sub_index < 2)
    def _():
        compress(held, jnp.where(sub_index == 0, 0, offset), taps_ref, made)

    @pl.when(sub_index == 3)
    def _():
        held[:half] = tail_ref[...]
        held[half:] = head_ref[...]
        compress(held, offset, taps_ref, made, tail_ref)

    @pl.when(sub_index != 2)
    def _():
        out_ref[:, :EXTRA] = rows_ref[...][:, :EXTRA]


def late_kernel(near_ref, rows_ref, early_ref, out_ref):
    sub_index = lax.axis_index("sa")

    @pl.when(sub_index != 2)
    def _():
        out_ref[...] = early_ref[...]

    @pl.when(sub_index == 2)
    def _():
        out_ref[:, EXTRA:] = near_ref[...]
        out_ref[:, :EXTRA] = rows_ref[...][:, :EXTRA]


def azimuth_kernel(lines_ref, out_ref, columns_held, taps, made, sems):
    pulses = taps.shape[0] // 2
    columns = pulses // LANES
    tiles = sems.shape[0]
    each = out_ref.shape[0] // tiles
    sources = lines_ref.shape[0]
    rows = (lines_ref.shape[1] - EXTRA) // tiles
    turned = [
        lines_ref[:, EXTRA + tile * rows : EXTRA + (tile + 1) * rows].reshape(sources * rows, LANES).T
        for tile in range(tiles)
    ]
    picked = jnp.sum(lines_ref[:, :EXTRA].astype(F32), axis=0)
    pieces = L // LANES
    skewed = []
    for part in range(2):
        spread = [jnp.broadcast_to(picked[part * pieces + t][None], (LANES, LANES)) for t in range(pieces)]
        skewed.append(pltpu.roll(jnp.concatenate(spread, axis=1), 0, 1, stride=1, stride_axis=0))
    for apart in range(1 - columns, columns):
        at = apart % pieces * LANES
        straight, crossed = (skewed[part][:, at : at + LANES] for part in range(2))
        for target, pair in enumerate(((straight, crossed), (-crossed, straight))):
            slot = (apart + columns - 1) * 2 + target
            for part in range(2):
                columns_held[slot, pl.ds(part, LANES, stride=2), :] = pair[part]
            block = columns_held[slot].astype(BF)
            for column in range(columns):
                line = column - apart
                if 0 <= line < columns:
                    lane = target * pulses + column * LANES
                    taps[2 * line * LANES : 2 * (line + 1) * LANES, lane : lane + LANES] = block
    copies = []
    for tile in range(tiles):
        focused = jnp.dot(turned[tile], taps[...], preferred_element_type=F32)
        into = pl.ds(tile * each, each)
        for part in range(2):
            for column in range(columns):
                lane = part * pulses + column * LANES
                made[pl.ds(tile * each + 2 * column + part, LANES, stride=2 * columns), :] = focused[
                    :, lane : lane + LANES
                ]
        copies.append(pltpu.make_async_copy(made.at[into], out_ref.at[into], sems.at[tile]))
        copies[-1].start()
    for copy in copies:
        copy.wait()


def toeplitz(diagonal_taps, size):
    span_size = 2 * size - 1
    reversed_taps = diagonal_taps[..., ::-1]
    shifted = jnp.concatenate(
        [reversed_taps[..., size - 1 :], reversed_taps[..., : size - 1]], axis=-1
    )
    reps = (1,) * (shifted.ndim - 1) + (size,)
    tiled_flat = jnp.tile(shifted, reps)[..., : size * (span_size - 1)]
    return tiled_flat.reshape(shifted.shape[:-1] + (size, span_size - 1))[..., :size]


def tap_blocks(tap_values, size):
    block_total = tap_values.shape[1] // size + 1
    padded_taps = jnp.pad(tap_values, ((0, 0), (size, 2 * size)))
    matrices = []
    for offset_block in range(block_total):
        first_tap = offset_block * size + 1
        parts = toeplitz(padded_taps[:, first_tap : first_tap + 2 * size - 1], size)
        real_part = parts[0]
        imag_part = parts[1]
        matrices.append(
            jnp.stack([jnp.stack([real_part, -imag_part]), jnp.stack([imag_part, real_part])])
        )
    return jnp.stack(matrices)


def correlate(blocked, matrices, output_count):
    summed = jnp.zeros((blocked.shape[0], 2, output_count, blocked.shape[3]), F32)
    for offset_block in range(matrices.shape[0]):
        piece_rows = blocked[:, :, offset_block : offset_block + output_count, :]
        summed = summed + jnp.einsum(
            "rcib,cdbn->rdin", piece_rows, matrices[offset_block], preferred_element_type=F32
        )
    return summed


def focus_long(range_lines, reference_row):
    block_size = L // 2
    bin_count, _, total_pulses = range_lines.shape
    block_count = total_pulses // block_size
    blocked = range_lines.reshape(bin_count, 2, block_count, block_size)
    blocked = jnp.pad(blocked, ((0, 0), (0, 0), (1, 1), (0, 0)))
    focused = correlate(blocked, tap_blocks(reference_row, block_size), block_count)
    return focused.reshape(1, bin_count, 2, total_pulses)


def call(kernel, outs, specs, scratch=(), vmem=24, flops=1000):
    space = {"s": pltpu.SMEM, "v": pltpu.VMEM, "a": pl.ANY}
    blocks = [pl.BlockSpec(memory_space=space[kind]) for kind in specs]
    return pl.pallas_call(
        kernel,
        out_shape=outs,
        in_specs=blocks[: -len(outs)],
        out_specs=tuple(blocks[-len(outs) :]),
        scratch_shapes=list(scratch),
        compiler_params=pltpu.CompilerParams(vmem_limit_bytes=int(vmem * 2**20)),
        cost_estimate=pl.CostEstimate(flops=flops, bytes_accessed=1000, transcendentals=0),
    )


def on_device(raw_echo, chirp_replica, azimuth_refs, migration_index, window_start):
    pulses = raw_echo.shape[0]
    segment_devices = lax.axis_size("sa")
    pulse_devices = lax.axis_size("pa")
    tap_count = chirp_replica.shape[1]
    kept_width = R // segment_devices
    bin_count = kept_width // pulse_devices
    total_pulses = pulses * pulse_devices
    half = kept_width // LANES
    tap_tiles = tap_count // LANES + 2
    span = half + tap_tiles - 1

    rows = 2 * pulses
    shape = jax.ShapeDtypeStruct
    token = shape((8, LANES), F32)
    short = bin_count % LANES == 0 and total_pulses == L // 2

    targets = pulse_devices if short else half // 8
    slot = half // targets * rows

    tail, turn = call(
        tail_kernel,
        (shape((half, rows, LANES), BF), token),
        "avv",
        [pltpu.VMEM((pulses, 2, (half + 8) * LANES), BF), pltpu.SemaphoreType.DMA((4,))],
        53,
    )(raw_echo)
    tail = lax.ppermute(tail, "sa", [(0, 1), (1, 3)])
    head, turn = call(head_kernel, (shape((span - half + 16, rows, LANES), BF), token), "vvvv")(turn, raw_echo)
    head = lax.ppermute(head, "sa", [(2, 3)])
    taps, own_rows, turn = call(
        prep_kernel,
        (shape((tap_tiles * LANES, 2 * LANES), BF), shape((pulse_devices, 2 * EXTRA, LANES), BF), token),
        "vsvvvvvv",
    )(turn, window_start, migration_index, chirp_replica, azimuth_refs)
    near, turn = call(
        ahead_kernel,
        (shape((targets, slot, LANES), BF), token),
        "vsvvvv",
        [pltpu.VMEM((span, rows, LANES), BF)],
    )(turn, window_start, raw_echo, taps)
    near = lax.ppermute(near, "sa", [(1, 2)])
    extra = own_rows if short else jnp.zeros((targets, 2 * EXTRA, LANES), BF)
    made = shape((targets, slot + EXTRA, LANES), BF)
    (early,) = call(
        early_kernel,
        (made,),
        "vsvvvvvv",
        [pltpu.VMEM((span + 16, rows, LANES), BF)],
        flops=10**10,
    )(turn, window_start, raw_echo, tail, head, taps, extra)
    (compressed,) = call(late_kernel, (made,), "vvvv")(near, extra, early)

    if not short:
        kept = compressed[:, EXTRA:].reshape(half, pulses, 2, LANES).transpose(0, 3, 2, 1)
        outgoing = kept.reshape(pulse_devices, bin_count, 2, pulses)
        turned = lax.all_to_all(outgoing, "pa", split_axis=0, concat_axis=3, tiled=True)
        rows_in = lax.all_to_all(own_rows, "pa", split_axis=0, concat_axis=0, tiled=True)
        reference_row = jnp.sum(rows_in[:, :8].astype(F32), axis=0).astype(BF).reshape(2, L)
        reference_row = jnp.roll(reference_row, -(L // 2 + 1), axis=1)[:, ::-1]
        return focus_long(turned[0], reference_row)

    lines = lax.all_to_all(compressed, "pa", split_axis=0, concat_axis=0, tiled=True)
    width = 2 * total_pulses
    (focused,) = call(
        azimuth_kernel,
        (shape((bin_count * width // LANES, LANES), F32),),
        "va",
        [
            pltpu.VMEM((width // LANES * 2 - 1, 2 * LANES, LANES), F32),
            pltpu.VMEM((width, width), BF),
            pltpu.VMEM((bin_count * width // LANES + 8, LANES), F32),
            pltpu.SemaphoreType.DMA((bin_count // LANES,)),
        ],
    )(lines)
    focused = focused.reshape(1, bin_count, total_pulses // LANES, 2, LANES).swapaxes(2, 3)
    return focused.reshape(1, bin_count, 2, total_pulses)


def solution(mesh):
    placed = (P("pa", None, "sa"), P(), P("pa", None, None), P(), P())
    return jax.shard_map(
        on_device, mesh=mesh, in_specs=placed, out_specs=P("sa", "pa", None, None), check_vma=False
    )
```

```python
import jax
import jax.numpy as jnp
from jax import lax
from jax.experimental import pallas as pl
from jax.experimental.pallas import tpu as pltpu
from jax.sharding import PartitionSpec as P

R = 16384
L = 512
LANES = 128
EXTRA = 8
BF = jnp.bfloat16
F32 = jnp.float32


def reversed_lanes(row):
    row_id = lax.broadcasted_iota(jnp.int32, (LANES, LANES), 0)
    col_id = lax.broadcasted_iota(jnp.int32, (LANES, LANES), 1)
    flip = (row_id + col_id == LANES - 1).astype(BF)
    tiles = row.shape[1] // LANES
    pieces = [row[:, t * LANES : (t + 1) * LANES] for t in reversed(range(tiles))]
    return jnp.concatenate([jnp.dot(piece, flip, preferred_element_type=F32) for piece in pieces], axis=1)


def retile(source, target, first, tiles):
    shape = target.shape[1:]
    for t in range(tiles):
        target[first + t] = source[:, :, t * LANES : (t + 1) * LANES].reshape(shape)


def tail_kernel(raw_ref, tail_ref, turn_ref, natural, sems):
    turn_ref[...] = jnp.zeros_like(turn_ref)
    half, rows, _ = tail_ref.shape
    pieces = sems.shape[0]
    each = rows // 2 // pieces
    width = half * LANES

    @pl.when(lax.axis_index("sa") < 2)
    def _():
        copies = []
        for at in range(pieces):
            own = pl.ds(at * each, each)
            source = raw_ref.at[own, :, pl.ds(raw_ref.shape[2] - width, width)]
            copies.append(pltpu.make_async_copy(source, natural.at[own, :, pl.ds(0, width)], sems.at[at]))
            copies[-1].start()
        for at, copy in enumerate(copies):
            copy.wait()
            own = pl.ds(at * each, each)
            retile(natural.at[own], tail_ref.at[:, pl.ds(at * each * 2, each * 2)], 0, half)


def head_kernel(turn_in_ref, raw_ref, head_ref, turn_ref):
    turn_ref[...] = turn_in_ref[...]

    @pl.when(lax.axis_index("sa") == 2)
    def _():
        retile(raw_ref, head_ref, 0, head_ref.shape[0])


def prep_kernel(turn_in_ref, window_ref, index_ref, chirp_ref, refs_ref, taps_ref, rows_ref, turn_ref):
    turn_ref[...] = turn_in_ref[...]
    taps = chirp_ref.shape[1]
    blocks = taps_ref.shape[0] // LANES
    width = blocks * LANES
    shift = lax.rem(window_ref[0], LANES)
    chirp = jnp.concatenate([chirp_ref[...], jnp.zeros((14, taps), BF)], axis=0)
    flipped = reversed_lanes(chirp)
    padded = jnp.concatenate([jnp.zeros((16, 2 * LANES), F32), flipped], axis=1)
    padded = jnp.concatenate([padded, jnp.zeros((16, width + LANES - padded.shape[1]), F32)], axis=1)
    moved = pltpu.roll(padded, width + LANES - 127 - shift, 1)[:, :width]
    for part in range(2):
        spread = jnp.broadcast_to(moved[part : part + 1], (LANES, width))
        skewed = pltpu.roll(spread, 0, 1, stride=1, stride_axis=0)
        for t in range(blocks):
            first = LANES * (blocks - 1 - t)
            taps_ref[t * LANES : (t + 1) * LANES, part * LANES : (part + 1) * LANES] = skewed[
                :, first : first + LANES
            ].astype(BF)
    own = refs_ref.shape[0]
    groups, targets = index_ref.shape
    first_row = lax.axis_index("pa") * own
    mine = lax.broadcasted_iota(jnp.int32, (groups, targets), 0) == lax.axis_index("sa")
    wanted = jnp.sum(jnp.where(mine, index_ref[...], 0), axis=0, keepdims=True)
    row_id = lax.broadcasted_iota(jnp.int32, (own, targets), 0) + first_row
    picks = (row_id == jnp.broadcast_to(wanted, (own, targets))).astype(F32)
    pieces = []
    for part in range(2):
        picked = lax.dot_general(
            picks, refs_ref[:, part, :].astype(F32), (((0,), (0,)), ((), ())), preferred_element_type=F32
        )
        picked = reversed_lanes(picked.astype(BF))
        picked = pltpu.roll(picked, L // 2 + 1, 1)
        pieces += [picked[:, t * LANES : (t + 1) * LANES] for t in range(L // LANES)]
    pieces += [jnp.zeros((targets, LANES), F32)] * (rows_ref.shape[1] - len(pieces))
    rows_ref[...] = jnp.stack(pieces, axis=1).astype(BF)


def compress(held, base, taps_ref, out_ref, opening=None):
    rows = held.shape[1]
    targets = out_ref.shape[0]
    tap_tiles = taps_ref.shape[0] // LANES
    group = 8
    per_target = out_ref.shape[1] // rows
    even = lax.rem(lax.broadcasted_iota(jnp.int32, (1, 8, LANES), 1), 2) == 0
    for step in range(targets * per_target // group):
        source = held if step or opening is None else opening
        blocks = [
            source[pl.ds(base + group * step + t, group)].reshape(group * rows, LANES) for t in range(tap_tiles)
        ]
        product = jnp.dot(jnp.concatenate(blocks, axis=1), taps_ref[...], preferred_element_type=F32)
        straight = product[:, :LANES].reshape(-1, 8, LANES)
        crossed = product[:, LANES:].reshape(-1, 8, LANES)
        total = straight + jnp.where(even, pltpu.roll(crossed, 7, 1), -pltpu.roll(crossed, 1, 1))
        count = group // per_target
        out_ref[pl.ds(step * count, count), : per_target * rows] = total.astype(BF).reshape(
            count, per_target * rows, LANES
        )


def ahead_kernel(turn_in_ref, window_ref, raw_ref, taps_ref, out_ref, turn_ref, held):
    turn_ref[...] = turn_in_ref[...]
    span = held.shape[0]

    @pl.when(lax.axis_index("sa") == 1)
    def _():
        start = pl.multiple_of(window_ref[0] // LANES * LANES, LANES)
        retile(raw_ref.at[:, :, pl.ds(start, span * LANES)], held, 0, span)
        compress(held, 0, taps_ref, out_ref)


def early_kernel(turn_in_ref, window_ref, raw_ref, tail_ref, head_ref, taps_ref, rows_ref, out_ref, held):
    half = tail_ref.shape[0]
    more = head_ref.shape[0]
    span = half + more - 16
    sub_index = lax.axis_index("sa")
    offset = window_ref[0] // LANES
    made = out_ref.at[:, pl.ds(EXTRA, out_ref.shape[1] - EXTRA)]

    @pl.when(sub_index == 0)
    def _():
        start = pl.multiple_of(offset * LANES, LANES)
        retile(raw_ref.at[:, :, pl.ds(start, span * LANES)], held, 0, span)

    @pl.when(sub_index == 1)
    def _():
        held[:half] = tail_ref[...]
        retile(raw_ref, held, half, more)

    @pl.when(sub_index < 2)
    def _():
        compress(held, jnp.where(sub_index == 0, 0, offset), taps_ref, made)

    @pl.when(sub_index == 3)
    def _():
        held[:half] = tail_ref[...]
        held[half:] = head_ref[...]
        compress(held, offset, taps_ref, made, tail_ref)

    @pl.when(sub_index != 2)
    def _():
        out_ref[:, :EXTRA] = rows_ref[...][:, :EXTRA]


def late_kernel(near_ref, rows_ref, early_ref, out_ref):
    sub_index = lax.axis_index("sa")

    @pl.when(sub_index != 2)
    def _():
        out_ref[...] = early_ref[...]

    @pl.when(sub_index == 2)
    def _():
        out_ref[:, EXTRA:] = near_ref[...]
        out_ref[:, :EXTRA] = rows_ref[...][:, :EXTRA]


def azimuth_kernel(lines_ref, out_ref, columns_held, taps, made, sems):
    pulses = taps.shape[0] // 2
    columns = pulses // LANES
    tiles = out_ref.shape[0] // (2 * columns * LANES)
    sources = lines_ref.shape[0]
    rows = (lines_ref.shape[1] - EXTRA) // tiles
    turned = [
        lines_ref[:, EXTRA + tile * rows : EXTRA + (tile + 1) * rows].reshape(sources * rows, LANES).T
        for tile in range(tiles)
    ]
    picked = jnp.sum(lines_ref[:, :EXTRA].astype(F32), axis=0)
    pieces = L // LANES
    skewed = []
    for part in range(2):
        spread = [jnp.broadcast_to(picked[part * pieces + t][None], (LANES, LANES)) for t in range(pieces)]
        skewed.append(pltpu.roll(jnp.concatenate(spread, axis=1), 0, 1, stride=1, stride_axis=0))
    for apart in range(1 - columns, columns):
        at = apart % pieces * LANES
        straight, crossed = (skewed[part][:, at : at + LANES] for part in range(2))
        for target, pair in enumerate(((straight, crossed), (-crossed, straight))):
            slot = (apart + columns - 1) * 2 + target
            for part in range(2):
                columns_held[slot, pl.ds(part, LANES, stride=2), :] = pair[part]
            block = columns_held[slot].astype(BF)
            for column in range(columns):
                line = column - apart
                if 0 <= line < columns:
                    lane = target * pulses + column * LANES
                    taps[2 * line * LANES : 2 * (line + 1) * LANES, lane : lane + LANES] = block
    copies = []
    spans = [(0, LANES // 2), (LANES // 2, LANES // 2)] + [(tile * LANES, LANES) for tile in range(1, tiles)]
    for at, (first, bins) in enumerate(spans):
        block = turned[first // LANES][first % LANES : first % LANES + bins]
        focused = jnp.dot(block, taps[...], preferred_element_type=F32)
        start = first * 2 * columns
        for part in range(2):
            for column in range(columns):
                lane = part * pulses + column * LANES
                made[pl.ds(start + 2 * column + part, bins, stride=2 * columns), :] = focused[:, lane : lane + LANES]
        into = pl.ds(start, bins * 2 * columns)
        copies.append(pltpu.make_async_copy(made.at[into], out_ref.at[into], sems.at[at]))
        copies[-1].start()
    for copy in copies:
        copy.wait()


def toeplitz(diagonal_taps, size):
    span_size = 2 * size - 1
    reversed_taps = diagonal_taps[..., ::-1]
    shifted = jnp.concatenate(
        [reversed_taps[..., size - 1 :], reversed_taps[..., : size - 1]], axis=-1
    )
    reps = (1,) * (shifted.ndim - 1) + (size,)
    tiled_flat = jnp.tile(shifted, reps)[..., : size * (span_size - 1)]
    return tiled_flat.reshape(shifted.shape[:-1] + (size, span_size - 1))[..., :size]


def tap_blocks(tap_values, size):
    block_total = tap_values.shape[1] // size + 1
    padded_taps = jnp.pad(tap_values, ((0, 0), (size, 2 * size)))
    matrices = []
    for offset_block in range(block_total):
        first_tap = offset_block * size + 1
        parts = toeplitz(padded_taps[:, first_tap : first_tap + 2 * size - 1], size)
        real_part = parts[0]
        imag_part = parts[1]
        matrices.append(
            jnp.stack([jnp.stack([real_part, -imag_part]), jnp.stack([imag_part, real_part])])
        )
    return jnp.stack(matrices)


def correlate(blocked, matrices, output_count):
    summed = jnp.zeros((blocked.shape[0], 2, output_count, blocked.shape[3]), F32)
    for offset_block in range(matrices.shape[0]):
        piece_rows = blocked[:, :, offset_block : offset_block + output_count, :]
        summed = summed + jnp.einsum(
            "rcib,cdbn->rdin", piece_rows, matrices[offset_block], preferred_element_type=F32
        )
    return summed


def focus_long(range_lines, reference_row):
    block_size = L // 2
    bin_count, _, total_pulses = range_lines.shape
    block_count = total_pulses // block_size
    blocked = range_lines.reshape(bin_count, 2, block_count, block_size)
    blocked = jnp.pad(blocked, ((0, 0), (0, 0), (1, 1), (0, 0)))
    focused = correlate(blocked, tap_blocks(reference_row, block_size), block_count)
    return focused.reshape(1, bin_count, 2, total_pulses)


def call(kernel, outs, specs, scratch=(), vmem=24, flops=1000):
    space = {"s": pltpu.SMEM, "v": pltpu.VMEM, "a": pl.ANY}
    blocks = [pl.BlockSpec(memory_space=space[kind]) for kind in specs]
    return pl.pallas_call(
        kernel,
        out_shape=outs,
        in_specs=blocks[: -len(outs)],
        out_specs=tuple(blocks[-len(outs) :]),
        scratch_shapes=list(scratch),
        compiler_params=pltpu.CompilerParams(vmem_limit_bytes=int(vmem * 2**20)),
        cost_estimate=pl.CostEstimate(flops=flops, bytes_accessed=1000, transcendentals=0),
    )


def on_device(raw_echo, chirp_replica, azimuth_refs, migration_index, window_start):
    pulses = raw_echo.shape[0]
    segment_devices = lax.axis_size("sa")
    pulse_devices = lax.axis_size("pa")
    tap_count = chirp_replica.shape[1]
    kept_width = R // segment_devices
    bin_count = kept_width // pulse_devices
    total_pulses = pulses * pulse_devices
    half = kept_width // LANES
    tap_tiles = tap_count // LANES + 2
    span = half + tap_tiles - 1

    rows = 2 * pulses
    shape = jax.ShapeDtypeStruct
    token = shape((8, LANES), F32)
    short = bin_count % LANES == 0 and total_pulses == L // 2

    targets = pulse_devices if short else half // 8
    slot = half // targets * rows

    tail, turn = call(
        tail_kernel,
        (shape((half, rows, LANES), BF), token),
        "avv",
        [pltpu.VMEM((pulses, 2, (half + 8) * LANES), BF), pltpu.SemaphoreType.DMA((4,))],
        53,
    )(raw_echo)
    tail = lax.ppermute(tail, "sa", [(0, 1), (1, 3)])
    head, turn = call(head_kernel, (shape((span - half + 16, rows, LANES), BF), token), "vvvv")(turn, raw_echo)
    head = lax.ppermute(head, "sa", [(2, 3)])
    taps, own_rows, turn = call(
        prep_kernel,
        (shape((tap_tiles * LANES, 2 * LANES), BF), shape((pulse_devices, 2 * EXTRA, LANES), BF), token),
        "vsvvvvvv",
    )(turn, window_start, migration_index, chirp_replica, azimuth_refs)
    near, turn = call(
        ahead_kernel,
        (shape((targets, slot, LANES), BF), token),
        "vsvvvv",
        [pltpu.VMEM((span, rows, LANES), BF)],
    )(turn, window_start, raw_echo, taps)
    near = lax.ppermute(near, "sa", [(1, 2)])
    extra = own_rows if short else jnp.zeros((targets, 2 * EXTRA, LANES), BF)
    made = shape((targets, slot + EXTRA, LANES), BF)
    (early,) = call(
        early_kernel,
        (made,),
        "vsvvvvvv",
        [pltpu.VMEM((span + 16, rows, LANES), BF)],
        flops=10**10,
    )(turn, window_start, raw_echo, tail, head, taps, extra)
    (compressed,) = call(late_kernel, (made,), "vvvv")(near, extra, early)

    if not short:
        kept = compressed[:, EXTRA:].reshape(half, pulses, 2, LANES).transpose(0, 3, 2, 1)
        outgoing = kept.reshape(pulse_devices, bin_count, 2, pulses)
        turned = lax.all_to_all(outgoing, "pa", split_axis=0, concat_axis=3, tiled=True)
        rows_in = lax.all_to_all(own_rows, "pa", split_axis=0, concat_axis=0, tiled=True)
        reference_row = jnp.sum(rows_in[:, :8].astype(F32), axis=0).astype(BF).reshape(2, L)
        reference_row = jnp.roll(reference_row, -(L // 2 + 1), axis=1)[:, ::-1]
        return focus_long(turned[0], reference_row)

    lines = lax.all_to_all(compressed, "pa", split_axis=0, concat_axis=0, tiled=True)
    width = 2 * total_pulses
    (focused,) = call(
        azimuth_kernel,
        (shape((bin_count * width // LANES, LANES), F32),),
        "va",
        [
            pltpu.VMEM((width // LANES * 2 - 1, 2 * LANES, LANES), F32),
            pltpu.VMEM((width, width), BF),
            pltpu.VMEM((bin_count * width // LANES + 8, LANES), F32),
            pltpu.SemaphoreType.DMA((bin_count // LANES + 1,)),
        ],
    )(lines)
    focused = focused.reshape(1, bin_count, total_pulses // LANES, 2, LANES).swapaxes(2, 3)
    return focused.reshape(1, bin_count, 2, total_pulses)


def solution(mesh):
    placed = (P("pa", None, "sa"), P(), P("pa", None, None), P(), P())
    return jax.shard_map(
        on_device, mesh=mesh, in_specs=placed, out_specs=P("sa", "pa", None, None), check_vma=False
    )
```
